32 devices in a mesh: ctx: 8 (over z, core), tp: 4 (over y, x).
Axes of the slice: x: 2, y: 2, z: 4, core: 2. Of those that a mesh axis runs over, the one named last changes fastest.
Arguments:
- inputs: bfloat16 [2, 2, 2048, 2048], P(None, None, 'ctx'), may hold values from -6 to 6
- segments: int32 [2, 2, 2048], replicated, may hold values from 0 to 15, as said below
- keep_mask: int32 [2, 2, 2048], replicated, may hold values 0 or 1
- first_gain: float32 [2048], replicated, may hold values from 0.25 to 1.75
- first_shift: float32 [2048], replicated, may hold values from -4 to 4
- proj_weight: bfloat16 [2048, 3, 2048], P(None, None, 'tp'), may hold values from -0.125 to 0.125
- proj_bias: float32 [2, 2048], P(None, 'tp'), may hold values from -4 to 4
- mixer_weight: bfloat16 [2048, 2048], P('tp'), may hold values from -0.75 to 0.75
- mixer_bias: float32 [2048], replicated, may hold values from -4 to 4
- second_gain: float32 [2048], replicated, may hold values from 0.25 to 1.75
- second_shift: float32 [2048], replicated, may hold values from -4 to 4
- up_weight: bfloat16 [2048, 8192], P(None, 'tp'), may hold values from -0.125 to 0.125
- up_bias: float32 [8192], P('tp'), may hold values from -4 to 4
- down_weight: bfloat16 [8192, 2048], P('tp'), may hold values from -0.1875 to 0.1875
- down_bias: float32 [2048], replicated, may hold values from -4 to 4
- out_cotangent: bfloat16 [2, 2, 2048, 2048], P(None, None, 'ctx'), may hold values from -6 to 6
Outputs:
- outputs: bfloat16 [2, 2, 2048, 2048], P(None, None, 'ctx')
- input_grad: float32 [2, 2, 2048, 2048], P(None, None, 'ctx')
- first_gain_grad: float32 [2048], P('ctx')
- first_shift_grad: float32 [2048], P('ctx')
- proj_weight_grad: float32 [2048, 3, 2048], P('ctx', None, 'tp')
- proj_bias_grad: float32 [2, 2048], P(None, ('tp', 'ctx'))
- mixer_weight_grad: float32 [2048, 2048], P('tp', 'ctx')
- mixer_bias_grad: float32 [2048], P('ctx')
- second_gain_grad: float32 [2048], P('ctx')
- second_shift_grad: float32 [2048], P('ctx')
- up_weight_grad: float32 [2048, 8192], P('ctx', 'tp')
- up_bias_grad: float32 [8192], P(('tp', 'ctx'))
- down_weight_grad: float32 [8192, 2048], P('tp', 'ctx')
- down_bias_grad: float32 [2048], P('ctx')
The draws below stay inside these ranges and needn't reach their ends.
Inputs may be any that keep to these rules, and one draw needn't show every extreme that they name: `segments`: document numbers never fall along a sequence; document 0 starts at position 0 and covers at least the first half of each sequence; the last position holds 15.
All inputs are finite; a program needn't handle non-finite values.
Results may differ from the reference program's by a relative error of at most 0.03.
Values may be sent and summed in bfloat16 or wider, within the bound.
No kernel may reach another device: no remote copies, remote signals or barrier semaphores. Data moves between devices by JAX's collectives and lax.ppermute only.
A program may use at most 256 MiB of HBM per device.

```python
import math
from functools import partial
import jax
import jax.numpy as jnp
from jax import lax

D = 2048
HEADS = 16
HD = 128
FF = 8192
MB = 2
SEQS = 2
DOCS = 16
SEQ = 2048
N_CTX = 8


def draw_segments(key, part):
    key = jax.random.fold_in(key, 11)
    row_keys = jax.random.split(key, MB * SEQS)

    def one_row(row_key):
        first_key, second_key = jax.random.split(row_key)
        first_len = SEQ // 2 + jax.random.randint(first_key, (), 0, SEQ // 4 + 1, dtype=jnp.int32)
        rest_len = SEQ - first_len
        uniform_int = jax.random.randint(second_key, (DOCS - 2,), 0, 1024, dtype=jnp.int32)
        cubed = uniform_int * uniform_int // 1024 * uniform_int // 1024
        cut_points = first_len + 1 + (rest_len - 1) * cubed // 1024
        position_ids = jnp.arange(SEQ, dtype=jnp.int32)
        after_first = (position_ids >= first_len).astype(jnp.int32)
        past_cuts = jnp.sum((position_ids[:, None] >= cut_points[None, :]).astype(jnp.int32), axis=1)
        return after_first + past_cuts
    return jax.vmap(one_row)(row_keys).reshape(MB, SEQS, SEQ)


def touch_ends(entries, own_key, smallest, largest):
    extent = entries.shape
    spot = [jax.random.randint(jax.random.fold_in(own_key, axis), (), 0, extent[axis]) for axis in range(len(extent))]
    entries = entries.at[tuple(spot)].set(smallest)
    longest = extent.index(max(extent))
    spot[longest] = (spot[longest] + 1) % extent[longest]
    return entries.at[tuple(spot)].set(largest)


def steps_of(rng, shape, shards, least, high):
    loudness = 1.0
    for dim, parts in shards:
        steps = jax.random.uniform(jax.random.fold_in(jax.random.fold_in(rng, 6), dim), (parts,), jnp.float32, least / len(shards), high / len(shards))
        loudness = loudness * jnp.repeat(jnp.exp(steps), shape[dim] // parts).reshape((-1,) + (1,) * (len(shape) - 1 - dim))
    return loudness


def centred(key, dims, width, reach, cuts=(), kind=jnp.bfloat16):
    values = width * jax.random.normal(key, dims, jnp.float32)
    if cuts:
        values = values * steps_of(key, dims, cuts, -0.22, 0.18)
    return jnp.clip(values, -reach, reach).astype(kind)


def setup_inputs(seed: int = 0) -> dict:
    streams_of = jax.random.split(jax.random.key(seed), 17)
    inputs = centred(streams_of[0], (MB, SEQS, SEQ, D), 1.0, 6.0, ((2, 8),))
    segments = draw_segments(jax.random.fold_in(streams_of[16], 71), 0)
    keep_mask = touch_ends((jax.random.randint(streams_of[2], (MB, SEQS, SEQ), 0, 8) < 7).astype(jnp.int32), jax.random.fold_in(streams_of[2], 1), 0, 1)
    first_gain = jnp.clip(1.0 + 0.15 * jax.random.normal(streams_of[3], (D,), jnp.float32), 0.25, 1.75)
    first_shift = centred(streams_of[4], (D,), 0.3, 4.0, (), jnp.float32)
    proj_weight = centred(streams_of[5], (D, 3, HEADS * HD), D ** -0.5, 0.125, ((2, 4),))
    proj_bias = centred(streams_of[6], (2, HEADS * HD), 0.3, 4.0, ((1, 4),), jnp.float32)
    mixer_weight = centred(streams_of[7], (HEADS * HD, D), (HEADS * HD // 32) ** -0.5, 0.75, ((0, 4),))
    mixer_bias = centred(streams_of[8], (D,), 0.3, 4.0, (), jnp.float32)
    second_gain = jnp.clip(1.0 + 0.15 * jax.random.normal(streams_of[9], (D,), jnp.float32), 0.25, 1.75)
    second_shift = centred(streams_of[10], (D,), 0.3, 4.0, (), jnp.float32)
    up_weight = centred(streams_of[11], (D, FF), D ** -0.5, 0.125, ((1, 4),))
    up_bias = centred(streams_of[12], (FF,), 0.3, 4.0, ((0, 4),), jnp.float32)
    down_weight = centred(streams_of[13], (FF, D), (FF // 8) ** -0.5, 0.1875, ((0, 4),))
    down_bias = centred(streams_of[14], (D,), 0.3, 4.0, (), jnp.float32)
    out_cotangent = centred(streams_of[15], (MB, SEQS, SEQ, D), 1.0, 6.0, ((2, 8),))
    return dict(inputs=inputs, segments=segments, keep_mask=keep_mask, first_gain=first_gain, first_shift=first_shift, proj_weight=proj_weight, proj_bias=proj_bias, mixer_weight=mixer_weight, mixer_bias=mixer_bias, second_gain=second_gain, second_shift=second_shift, up_weight=up_weight, up_bias=up_bias, down_weight=down_weight, down_bias=down_bias, out_cotangent=out_cotangent)


@jax.custom_vjp
def low(v):
    return lax.optimization_barrier(v.astype(jnp.bfloat16)).astype(jnp.float32)

@jax.custom_vjp
def low_back(v):
    return v

def low_keep(v):
    return (low(v), None)

def low_pass(kept, grad):
    return (grad,)

def back_keep(v):
    return (v, None)

def back_low(kept, grad):
    return (low(grad),)
low.defvjp(low_keep, low_pass)
low_back.defvjp(back_keep, back_low)

def storage_order(values, part_count):
    leading = values.shape[:-1]
    blocks = values.reshape(leading + (2 * part_count, -1))
    front_half = blocks[..., :part_count, :]
    back_half = jnp.flip(blocks[..., part_count:, :], axis=-2)
    return jnp.stack([front_half, back_half], axis=-2).reshape(leading + (-1,))

def layer_norm(values, norm_gain, norm_shift):
    center = values - lax.optimization_barrier(jnp.mean(values, axis=-1, keepdims=True))
    spread = lax.optimization_barrier(jnp.mean(center * center, axis=-1, keepdims=True))
    return center * lax.rsqrt(spread + 1e-05) * norm_gain + norm_shift

def attention(queries, key_rows, value_rows, places, seg_ids, keep_flags):
    seq_count, seq_len, head_count, head_size = queries.shape
    block_rows = math.gcd(seq_len, 512)
    block_count = seq_len // block_rows
    scaler = 1.0 / math.sqrt(head_size)
    highest = lax.Precision.HIGHEST

    def one_block(number):
        row_index = number // block_count
        start = number % block_count * block_rows
        query_seq = lax.dynamic_index_in_dim(queries, row_index, 0, False)
        query_blk = lax.dynamic_slice_in_dim(query_seq, start, block_rows, 0)
        key_seq = lax.dynamic_index_in_dim(key_rows, row_index, 0, False)
        value_seq = lax.dynamic_index_in_dim(value_rows, row_index, 0, False)
        seg_row = lax.dynamic_index_in_dim(seg_ids, row_index, 0, False)
        keep_row = lax.dynamic_index_in_dim(keep_flags, row_index, 0, False)
        my_places = lax.dynamic_slice_in_dim(places, start, block_rows, 0)
        my_seg = lax.dynamic_slice_in_dim(seg_row, start, block_rows, 0)
        itself = places[None, :] == my_places[:, None]
        allowed = (places[None, :] <= my_places[:, None]) & (seg_row[None, :] == my_seg[:, None]) & ((keep_row[None, :] > 0) | itself)
        scores = low_back(jnp.einsum('qhd,khd->hqk', query_blk, key_seq, precision=highest) * scaler)
        scores = jnp.where(allowed[None], scores, -1000000000.0)
        top = lax.optimization_barrier(jnp.max(scores, axis=-1, keepdims=True))
        raised = jnp.exp(scores - top)
        probs = raised / lax.optimization_barrier(jnp.sum(raised, axis=-1, keepdims=True))
        return jnp.einsum('hqk,khd->qhd', low(probs), value_seq, precision=highest)
    numbers = jnp.arange(seq_count * block_count, dtype=jnp.int32)
    result = lax.map(jax.checkpoint(one_block), numbers)
    return result.reshape(seq_count, seq_len, head_count * head_size)

def forward(seg_ids, keep_flags, places, x_in, first_gain, first_shift, proj_weight, proj_bias, mixer_weight, mixer_bias, second_gain, second_shift, up_weight, up_bias, down_weight, down_bias):
    highest = lax.Precision.HIGHEST
    seq_count, seq_len, model_width = x_in.shape
    normed_one = low(layer_norm(x_in, first_gain, first_shift))
    bias_three = jnp.stack([proj_bias[0], jnp.zeros_like(proj_bias[0]), proj_bias[1]])
    proj = jnp.einsum('std,dcn->stcn', normed_one, proj_weight, precision=highest) + bias_three
    proj = low(low_back(proj))
    queries = proj[:, :, 0].reshape(seq_count, seq_len, HEADS, HD)
    key_rows = proj[:, :, 1].reshape(seq_count, seq_len, HEADS, HD)
    value_rows = proj[:, :, 2].reshape(seq_count, seq_len, HEADS, HD)
    heads_out = attention(queries, key_rows, value_rows, places, seg_ids, keep_flags)
    heads_out = low(low_back(heads_out))
    mixed = low_back(jnp.einsum('stn,nd->std', heads_out, mixer_weight, precision=highest) + mixer_bias)
    resid = x_in + mixed
    normed_two = low(layer_norm(resid, second_gain, second_shift))
    pre_act = low_back(jnp.einsum('std,df->stf', normed_two, up_weight, precision=highest) + up_bias)
    act = low(jax.nn.gelu(pre_act, approximate=False))
    feed = low_back(jnp.einsum('stf,fd->std', act, down_weight, precision=highest) + down_bias)
    return resid + feed

def reference(inputs, segments, keep_mask, first_gain, first_shift, proj_weight, proj_bias, mixer_weight, mixer_bias, second_gain, second_shift, up_weight, up_bias, down_weight, down_bias, out_cotangent):
    places = storage_order(jnp.arange(SEQ, dtype=jnp.int32), N_CTX)
    seg_store = storage_order(segments, N_CTX)
    keep_store = storage_order(keep_mask, N_CTX)
    params = (first_gain.astype(jnp.float32), first_shift.astype(jnp.float32), proj_weight.astype(jnp.float32), proj_bias.astype(jnp.float32), mixer_weight.astype(jnp.float32), mixer_bias.astype(jnp.float32), second_gain.astype(jnp.float32), second_shift.astype(jnp.float32), up_weight.astype(jnp.float32), up_bias.astype(jnp.float32), down_weight.astype(jnp.float32), down_bias.astype(jnp.float32))

    def micro_step(totals_now, scanned):
        x_now, cot_now, seg_now, keep_now = scanned
        out_now, pull_back = jax.vjp(partial(forward, seg_now, keep_now, places), x_now.astype(jnp.float32), *params)
        gradients = pull_back(cot_now.astype(jnp.float32))
        totals_now = tuple((earlier + adding for earlier, adding in zip(totals_now, gradients[1:])))
        return (totals_now, (out_now.astype(jnp.bfloat16), gradients[0]))
    starting = tuple((jnp.zeros_like(item) for item in params))
    totals, stacked = lax.scan(micro_step, starting, (inputs, out_cotangent, seg_store, keep_store))
    return (stacked[0], stacked[1], totals[0], totals[1], totals[2], totals[3], totals[4], totals[5], totals[6], totals[7], totals[8], totals[9], totals[10], totals[11])
```

```python
import math

import jax
import jax.numpy as jnp
from jax import lax
from jax.experimental import pallas as pl
from jax.experimental.pallas import tpu as pltpu
from jax.sharding import PartitionSpec as P

HD = 128


def storage_order(values, part_count):
    leading = values.shape[:-1]
    blocks = values.reshape(leading + (2 * part_count, -1))
    front_half = blocks[..., :part_count, :]
    back_half = jnp.flip(blocks[..., part_count:, :], axis=-2)
    return jnp.stack([front_half, back_half], axis=-2).reshape(leading + (-1,))


def layer_norm(values, norm_gain, norm_shift):
    center = values - jnp.mean(values, axis=-1, keepdims=True)
    spread = jnp.mean(center * center, axis=-1, keepdims=True)
    return center * lax.rsqrt(spread + 1e-05) * norm_gain + norm_shift


def gelu_exact(values):
    return jax.nn.gelu(values, approximate=False)


def split_heads(rows, heads_here):
    return rows.reshape(rows.shape[0], rows.shape[1], heads_here, -1)


def scores_of(queries, key_all, allowed, heads_here, scaler):
    raw = (
        jnp.einsum(
            "sqhd,skhd->shqk",
            split_heads(queries, heads_here),
            split_heads(key_all, heads_here),
            preferred_element_type=jnp.float32,
        )
        * scaler
    )
    return jnp.where(allowed[:, None], raw, -1000000000.0)


def attend(queries, key_all, value_all, allowed, heads_here, scaler):
    masked = scores_of(queries, key_all, allowed, heads_here, scaler)
    top = jnp.max(masked, axis=-1, keepdims=True)
    raised = jnp.exp(masked - top)
    totals = jnp.sum(raised, axis=-1, keepdims=True)
    probs = raised / totals
    mixed = jnp.einsum(
        "shqk,skhd->sqhd",
        probs.astype(jnp.bfloat16),
        split_heads(value_all, heads_here),
        preferred_element_type=jnp.float32,
    )
    return (mixed.reshape(queries.shape), top + jnp.log(totals))


def attend_back(queries, key_all, value_all, allowed, log_total, grad_heads, heads_here, scaler):
    masked = scores_of(queries, key_all, allowed, heads_here, scaler)
    probs = jnp.exp(masked - log_total)
    grad_four = split_heads(grad_heads, heads_here)
    grad_value = jnp.einsum(
        "shqk,sqhd->skhd", probs.astype(jnp.bfloat16), grad_four, preferred_element_type=jnp.float32
    )
    grad_probs = jnp.einsum(
        "sqhd,skhd->shqk",
        grad_four,
        split_heads(value_all, heads_here),
        preferred_element_type=jnp.float32,
    )
    inner_sum = jnp.sum(probs * grad_probs, axis=-1, keepdims=True)
    grad_scores = (probs * (grad_probs - inner_sum)).astype(jnp.bfloat16)
    grad_query = (
        jnp.einsum(
            "shqk,skhd->sqhd",
            grad_scores,
            split_heads(key_all, heads_here),
            preferred_element_type=jnp.float32,
        )
        * scaler
    )
    grad_key = (
        jnp.einsum(
            "shqk,sqhd->skhd",
            grad_scores,
            split_heads(queries, heads_here),
            preferred_element_type=jnp.float32,
        )
        * scaler
    )
    return (
        grad_query.reshape(queries.shape),
        grad_key.reshape(key_all.shape),
        grad_value.reshape(value_all.shape),
    )


def reduce_grads(grads):
    return (
        lax.psum_scatter(
            grads[0].astype(jnp.bfloat16), "ctx", scatter_dimension=0, tiled=True
        ).astype(jnp.float32),
        lax.psum_scatter(
            grads[1].astype(jnp.bfloat16), "ctx", scatter_dimension=0, tiled=True
        ).astype(jnp.float32),
        lax.psum_scatter(
            grads[2].astype(jnp.bfloat16), "ctx", scatter_dimension=0, tiled=True
        ).astype(jnp.float32),
        lax.psum_scatter(
            grads[3].astype(jnp.bfloat16), "ctx", scatter_dimension=1, tiled=True
        ).astype(jnp.float32),
        lax.psum_scatter(
            grads[4].astype(jnp.bfloat16), "ctx", scatter_dimension=1, tiled=True
        ).astype(jnp.float32),
        lax.psum_scatter(
            grads[5].astype(jnp.bfloat16), "ctx", scatter_dimension=0, tiled=True
        ).astype(jnp.float32),
        lax.psum_scatter(
            grads[6].astype(jnp.bfloat16), "ctx", scatter_dimension=0, tiled=True
        ).astype(jnp.float32),
        lax.psum_scatter(
            grads[7].astype(jnp.bfloat16), "ctx", scatter_dimension=0, tiled=True
        ).astype(jnp.float32),
        lax.psum_scatter(
            grads[8].astype(jnp.bfloat16), "ctx", scatter_dimension=0, tiled=True
        ).astype(jnp.float32),
        lax.psum_scatter(
            grads[9].astype(jnp.bfloat16), "ctx", scatter_dimension=0, tiled=True
        ).astype(jnp.float32),
        lax.psum_scatter(
            grads[10].astype(jnp.bfloat16), "ctx", scatter_dimension=1, tiled=True
        ).astype(jnp.float32),
        lax.psum_scatter(
            grads[11].astype(jnp.bfloat16), "ctx", scatter_dimension=0, tiled=True
        ).astype(jnp.float32),
    )


def per_device(
    inputs,
    segments,
    keep_mask,
    first_gain,
    first_shift,
    proj_weight,
    proj_bias,
    mixer_weight,
    mixer_bias,
    second_gain,
    second_shift,
    up_weight,
    up_bias,
    down_weight,
    down_bias,
    out_cotangent,
):
    ctx_count = lax.axis_size("ctx")
    micro_count, seq_count, tok_len, model_width = inputs.shape
    inner_width = proj_bias.shape[1]
    heads_here = inner_width // HD
    scaler = 1.0 / math.sqrt(HD)
    seq_len = tok_len * ctx_count
    places = storage_order(jnp.arange(seq_len, dtype=jnp.int32), ctx_count)
    offset = lax.axis_index("ctx") * tok_len
    my_places = lax.dynamic_slice_in_dim(places, offset, tok_len, 0)
    seg_store = storage_order(segments, ctx_count)
    keep_store = storage_order(keep_mask, ctx_count)
    proj_flat = proj_weight.reshape(model_width, 3 * inner_width)
    bias_three = jnp.stack([proj_bias[0], jnp.zeros_like(proj_bias[0]), proj_bias[1]])
    causal = places[None, :] <= my_places[:, None]
    itself = places[None, :] == my_places[:, None]
    shaped_like = (
        first_gain,
        first_shift,
        proj_weight,
        proj_bias,
        mixer_weight,
        mixer_bias,
        second_gain,
        second_shift,
        up_weight,
        up_bias,
        down_weight,
        down_bias,
    )
    running = tuple((jnp.zeros(item.shape, jnp.float32) for item in shaped_like))
    out_list = []
    grad_list = []
    for micro_index in range(micro_count):
        x_now = inputs[micro_index].astype(jnp.float32)
        seg_keys = seg_store[micro_index]
        seg_mine = lax.dynamic_slice_in_dim(seg_keys, offset, tok_len, 1)
        visible = (keep_store[micro_index] > 0)[:, None, :] | itself[None]
        allowed = causal[None] & (seg_keys[:, None, :] == seg_mine[:, :, None]) & visible
        normed_one = layer_norm(x_now, first_gain, first_shift).astype(jnp.bfloat16)
        projected = jnp.einsum(
            "std,dc->stc", normed_one, proj_flat, preferred_element_type=jnp.float32
        )
        projected = (projected.reshape(seq_count, tok_len, 3, inner_width) + bias_three).astype(
            jnp.bfloat16
        )
        queries = projected[:, :, 0]
        key_here = projected[:, :, 1]
        value_here = projected[:, :, 2]
        key_all, value_all = (
            lax.all_gather(key_here, "ctx", axis=1, tiled=True),
            lax.all_gather(value_here, "ctx", axis=1, tiled=True),
        )
        heads_out, log_total = attend(queries, key_all, value_all, allowed, heads_here, scaler)
        heads_low = heads_out.astype(jnp.bfloat16)
        mixed_part = jnp.einsum(
            "stn,nd->std", heads_low, mixer_weight, preferred_element_type=jnp.float32
        )
        resid = (
            x_now + lax.psum(mixed_part.astype(jnp.bfloat16), "tp").astype(jnp.float32) + mixer_bias
        )
        normed_two = layer_norm(resid, second_gain, second_shift).astype(jnp.bfloat16)
        pre_act = (
            jnp.einsum("std,df->stf", normed_two, up_weight, preferred_element_type=jnp.float32)
            + up_bias
        )
        act_low = gelu_exact(pre_act).astype(jnp.bfloat16)
        feed_part = jnp.einsum(
            "stf,fd->std", act_low, down_weight, preferred_element_type=jnp.float32
        )
        feed = lax.psum(feed_part.astype(jnp.bfloat16), "tp").astype(jnp.float32) + down_bias
        out_list.append((resid + feed).astype(jnp.bfloat16))
        cot_low = out_cotangent[micro_index]
        cot_full = cot_low.astype(jnp.float32)
        down_bias_part = jnp.sum(cot_full, axis=(0, 1))
        down_part = jnp.einsum("stf,std->fd", act_low, cot_low, preferred_element_type=jnp.float32)
        grad_act = jnp.einsum(
            "std,fd->stf", cot_low, down_weight, preferred_element_type=jnp.float32
        )
        grad_pre = jax.vjp(gelu_exact, pre_act)[1](grad_act)[0].astype(jnp.bfloat16)
        up_part = jnp.einsum(
            "std,stf->df", normed_two, grad_pre, preferred_element_type=jnp.float32
        )
        up_bias_part = jnp.sum(grad_pre.astype(jnp.float32), axis=(0, 1))
        grad_two_part = jnp.einsum(
            "stf,df->std", grad_pre, up_weight, preferred_element_type=jnp.float32
        )
        grad_two = lax.psum(grad_two_part.astype(jnp.bfloat16), "tp").astype(jnp.float32)
        resid_part, second_gain_part, second_shift_part = jax.vjp(
            layer_norm, resid, second_gain, second_shift
        )[1](grad_two)
        grad_resid = cot_full + resid_part
        grad_mix = grad_resid.astype(jnp.bfloat16)
        mixer_bias_part = jnp.sum(grad_mix.astype(jnp.float32), axis=(0, 1))
        mixer_part = jnp.einsum(
            "stn,std->nd", heads_low, grad_mix, preferred_element_type=jnp.float32
        )
        grad_heads = jnp.einsum(
            "std,nd->stn", grad_mix, mixer_weight, preferred_element_type=jnp.float32
        ).astype(jnp.bfloat16)
        key_back, value_back = (key_all, value_all)
        grad_query, grad_key, grad_value = attend_back(
            queries, key_back, value_back, allowed, log_total, grad_heads, heads_here, scaler
        )
        key_share, value_share = (
            lax.psum_scatter(
                grad_key.astype(jnp.bfloat16), "ctx", scatter_dimension=1, tiled=True
            ).astype(jnp.float32),
            lax.psum_scatter(
                grad_value.astype(jnp.bfloat16), "ctx", scatter_dimension=1, tiled=True
            ).astype(jnp.float32),
        )
        grad_proj = jnp.stack([grad_query, key_share, value_share], axis=2).astype(jnp.bfloat16)
        proj_part = jnp.einsum(
            "std,stcn->dcn", normed_one, grad_proj, preferred_element_type=jnp.float32
        )
        proj_sums = jnp.sum(grad_proj.astype(jnp.float32), axis=(0, 1))
        proj_bias_part = jnp.stack([proj_sums[0], proj_sums[2]])
        grad_one_part = jnp.einsum(
            "stc,dc->std",
            grad_proj.reshape(seq_count, tok_len, 3 * inner_width),
            proj_flat,
            preferred_element_type=jnp.float32,
        )
        grad_one = lax.psum(grad_one_part.astype(jnp.bfloat16), "tp").astype(jnp.float32)
        input_part, first_gain_part, first_shift_part = jax.vjp(
            layer_norm, x_now, first_gain, first_shift
        )[1](grad_one)
        grad_list.append(grad_resid + input_part)
        batch_grads = (
            first_gain_part,
            first_shift_part,
            proj_part,
            proj_bias_part,
            mixer_part,
            mixer_bias_part,
            second_gain_part,
            second_shift_part,
            up_part,
            up_bias_part,
            down_part,
            down_bias_part,
        )
        running = tuple((earlier + adding for earlier, adding in zip(running, batch_grads)))
    final = reduce_grads(running)
    return (
        jnp.stack(out_list),
        jnp.stack(grad_list),
        final[0],
        final[1],
        final[2],
        final[3],
        final[4],
        final[5],
        final[6],
        final[7],
        final[8],
        final[9],
        final[10],
        final[11],
    )


BF = jnp.bfloat16
F32 = jnp.float32
LOG2E = 1.4426950408889634
LOW = -1e30
ORDERS = ((1, 2), (2, 1))


def xor_permute(values, axis, step):
    count = lax.axis_size(axis)
    return lax.ppermute(values, axis, [(i, i ^ step) for i in range(count)])


def sds(shape, dtype=BF):
    return jax.ShapeDtypeStruct(tuple(shape), dtype)


def run_kernel(body, outs, args, flops=0, exps=0, scratch=(), limit=48, name=None):
    specs = []
    moved = 0
    for arg in args:
        if arg.dtype == jnp.int32 and arg.size <= 8:
            specs.append(pl.BlockSpec(memory_space=pltpu.SMEM))
        else:
            specs.append(pl.BlockSpec(memory_space=pltpu.VMEM))
            moved += arg.size * arg.dtype.itemsize
    moved += sum(math.prod(o.shape) * o.dtype.itemsize for o in outs)
    return pl.pallas_call(
        body,
        out_shape=tuple(outs),
        in_specs=specs,
        out_specs=tuple(pl.BlockSpec(memory_space=pltpu.VMEM) for _ in outs),
        scratch_shapes=list(scratch),
        compiler_params=pltpu.CompilerParams(vmem_limit_bytes=limit << 20),
        cost_estimate=pl.CostEstimate(
            flops=flops, bytes_accessed=moved, transcendentals=exps
        ),
        name=name,
    )(*args)


def rows_at(start, count):
    return pl.ds(pl.multiple_of(start, count), count)


def shard_reduce(messages):
    sums = []
    for part, (first, second) in enumerate(ORDERS):
        send, keep = messages[2 * part], messages[2 * part + 1]
        got = xor_permute(send, "tp", first)
        middle = (keep[1].astype(F32) + got[1].astype(F32)).astype(BF)
        sums += [keep, got, xor_permute(middle, "tp", second)]
    return sums


def shard_gather(halves):
    pieces = []
    for part, (first, second) in enumerate(ORDERS):
        near = xor_permute(halves[part], "tp", first)
        far = xor_permute(jnp.stack([halves[part], near]), "tp", second)
        pieces += [halves[part], near, far]
    return pieces


def total_of(refs):
    halves = []
    for part in range(2):
        keep, got, late = refs[3 * part : 3 * part + 3]
        halves.append(
            keep[0].astype(F32) + got[0].astype(F32) + late[...].astype(F32)
        )
    return jnp.concatenate(halves, axis=0)


def place_gathered(store, tp_here, refs, size):
    half = size // 2
    for part, (first, second) in enumerate(ORDERS):
        mine, near, far = refs[3 * part : 3 * part + 3]
        parts = ((0, mine[...]), (first, near[...]), (second, far[0]), (first | second, far[1]))
        for step, value in parts:
            store(rows_at((tp_here ^ step) * size + part * half, half), value)


def emit_messages(load, tp_here, refs, size):
    half = size // 2
    for part, (first, second) in enumerate(ORDERS):
        send, keep = refs[2 * part], refs[2 * part + 1]
        for ref, steps in ((send, (first, first | second)), (keep, (0, second))):
            for place, step in enumerate(steps):
                ref[place] = load(rows_at((tp_here ^ step) * size + part * half, half))


def message_shapes(half, width):
    return [sds((2, half, width)) for _ in range(4)]


def exchange(local, cross, first, second, third):
    got = [
        xor_permute(item, "ctx", 2 * (place + 1))
        for place, item in enumerate((first, second, third))
    ]
    packed = jnp.stack([cross] + [item[1] for item in got])
    return [local] + got + [xor_permute(packed, "ctx", 1)]


def exchanged(refs, here):
    local, first, second, third, packed = refs
    return (
        (here, local[...]),
        (here ^ 1, packed[0]),
        (here ^ 2, first[0]),
        (here ^ 3, packed[1]),
        (here ^ 4, second[0]),
        (here ^ 5, packed[2]),
        (here ^ 6, third[0]),
        (here ^ 7, packed[3]),
    )


def emit_exchange(load, here, refs):
    local, cross, first, second, third = refs
    local[...] = load(here)
    cross[...] = load(here ^ 1)
    for place, ref in enumerate((first, second, third)):
        other = here ^ (2 * (place + 1))
        ref[0] = load(other)
        ref[1] = load(other ^ 1)


def exchange_shapes(rows, width):
    return [sds((rows, width)), sds((rows, width))] + [sds((2, rows, width))] * 3


def normalized(values):
    center = values - jnp.mean(values, axis=-1, keepdims=True)
    spread = jnp.mean(center * center, axis=-1, keepdims=True)
    root = lax.rsqrt(spread + 1e-05)
    return center * root, root


def norm_back(values, gain, grad):
    unit, root = normalized(values)
    scaled = grad * gain
    back = root * (
        scaled
        - jnp.mean(scaled, axis=-1, keepdims=True)
        - unit * jnp.mean(scaled * unit, axis=-1, keepdims=True)
    )
    gain_sum = jnp.sum(grad * unit, axis=0, keepdims=True)
    shift_sum = jnp.sum(grad, axis=0, keepdims=True)
    return back, gain_sum, shift_sum


def dot(left, right):
    return jnp.dot(left, right, preferred_element_type=F32)


def dot_nt(left, right):
    return lax.dot_general(left, right, (((1,), (1,)), ((), ())), preferred_element_type=F32)


def dot_tn(left, right):
    return lax.dot_general(left, right, (((0,), (0,)), ((), ())), preferred_element_type=F32)


def project(here, x_rows, gain, shift, weight, bias, tok_len):
    rows, width = x_rows.shape
    inner = weight.shape[2]
    heads = inner // HD

    def body(here_ref, x_ref, gain_ref, shift_ref, weight_ref, bias_ref, *rest):
        norm_ref, outs, held = rest[0], rest[1:6], rest[6]
        unit, _ = normalized(x_ref[...].astype(F32))
        norm_ref[...] = (unit * gain_ref[...] + shift_ref[...]).astype(BF)
        for part in range(3):
            value = dot(norm_ref[...], weight_ref[part]) + bias_ref[part : part + 1]
            value = value.astype(BF)
            for head in range(heads):
                held[head, :, part * HD : (part + 1) * HD] = value[:, head * HD : (head + 1) * HD]

        def load(unit_id):
            return held[unit_id % heads, rows_at(unit_id // heads * tok_len, tok_len), :]

        emit_exchange(load, here_ref[0], outs)

    return run_kernel(
        body,
        [sds((rows, width))] + exchange_shapes(tok_len, 3 * HD),
        [here, x_rows, gain, shift, weight, bias],
        flops=6 * rows * width * inner,
        scratch=[pltpu.VMEM((heads, rows, 3 * HD), BF)],
        name="project",
    )


def rows_of_device(device, block, blocks):
    return (
        rows_at(device * block, block),
        rows_at((blocks - 1 - device) * block, block),
    )


def attention(here, received, seg_column, key_row, heads):
    tok_len = received[0].shape[0]
    block = tok_len // 2
    seq_len = seg_column.shape[1]
    blocks = seq_len // block
    step = 256
    factor = LOG2E / math.sqrt(HD)

    def body(here_ref, *rest):
        refs, seg_ref, key_ref = rest[:5], rest[5], rest[6]
        outs, lse_ref = rest[7:12], rest[12]
        q_all, k_turned, v_all, mixed = rest[13:]
        me = here_ref[0]
        seq = me // heads
        for device, value in exchanged(refs, me):
            for half, place in enumerate(rows_of_device(device, block, blocks)):
                rows = value[half * block : (half + 1) * block]
                q_all[place] = rows[:, :HD]
                k_turned[:, place] = rows[:, HD : 2 * HD].T
                v_all[place] = rows[:, 2 * HD :]
        for number in range(seq_len // step):
            start, stop = number * step, (number + 1) * step
            segs = seg_ref[seq, start:stop]
            scores = dot(q_all[start:stop], k_turned[:, :stop]) * factor
            scores = masked(scores, segs, key_ref, seq, start, stop)
            top = jnp.max(scores, axis=-1, keepdims=True)
            raised = jnp.exp2(scores - top)
            total = jnp.sum(raised, axis=-1, keepdims=True)
            out = dot(raised.astype(BF), v_all[:stop]) / total
            mixed[start:stop] = out.astype(BF)
            lse_ref[start:stop] = top + jnp.log2(total)

        def load(device):
            return jnp.concatenate(
                [mixed[place] for place in rows_of_device(device, block, blocks)], axis=0
            )

        emit_exchange(load, me, outs)

    return run_kernel(
        body,
        exchange_shapes(tok_len, HD) + [sds((seq_len, 1), F32)],
        [here] + list(received) + [seg_column, key_row],
        flops=2 * 2 * seq_len * seq_len * HD,
        exps=seq_len * seq_len // 2,
        scratch=[
            pltpu.VMEM((seq_len, HD), BF),
            pltpu.VMEM((HD, seq_len), BF),
            pltpu.VMEM((seq_len, HD), BF),
            pltpu.VMEM((seq_len, HD), BF),
        ],
        name="attention",
    )


def masked(scores, segs, key_ref, seq, start, stop):
    size = stop - start
    row = lax.broadcasted_iota(jnp.int32, (size, size), 0)
    column = lax.broadcasted_iota(jnp.int32, (size, size), 1)
    same = segs == key_ref[seq, :, start:stop]
    seen = (same & (column < row)) | (column == row)
    corner = jnp.where(seen, scores[:, start:], LOW)
    if start == 0:
        return corner
    left = jnp.where(segs == key_ref[seq, :, :start], scores[:, :start], LOW)
    return jnp.concatenate([left, corner], axis=1)


def attention_back(here, received, grads, seg_column, key_row, lse, heads):
    tok_len = received[0].shape[0]
    block = tok_len // 2
    seq_len = seg_column.shape[1]
    blocks = seq_len // block
    step = 256
    scaler = 1.0 / math.sqrt(HD)

    def body(here_ref, *rest):
        refs, grad_refs = rest[:5], rest[5:10]
        seg_ref, key_ref, lse_ref = rest[10:13]
        outs = rest[13:18]
        q_all, k_all, k_turned, v_turned, g_all, result, dk_turned, dv_turned = rest[18:]
        me = here_ref[0]
        seq = me // heads
        for device, value in exchanged(refs, me):
            for half, place in enumerate(rows_of_device(device, block, blocks)):
                rows = value[half * block : (half + 1) * block]
                q_all[place] = rows[:, :HD]
                k_all[place] = rows[:, HD : 2 * HD]
                k_turned[:, place] = rows[:, HD : 2 * HD].T
                v_turned[:, place] = rows[:, 2 * HD :].T
        for device, value in exchanged(grad_refs, me):
            for half, place in enumerate(rows_of_device(device, block, blocks)):
                g_all[place] = value[half * block : (half + 1) * block]
        last = seq_len // step - 1
        for number in range(last, -1, -1):
            start, stop = number * step, (number + 1) * step
            segs = seg_ref[seq, start:stop]
            query, grad = q_all[start:stop], g_all[start:stop]
            scores = dot(query, k_turned[:, :stop]) * (scaler * LOG2E)
            scores = masked(scores, segs, key_ref, seq, start, stop)
            probs = jnp.exp2(scores - lse_ref[start:stop])
            grad_probs = dot(grad, v_turned[:, :stop])
            inner = jnp.sum(probs * grad_probs, axis=-1, keepdims=True)
            grad_scores = (probs * (grad_probs - inner)).astype(BF)
            dv_part = dot_tn(grad, probs.astype(BF))
            dk_part = dot_tn(query, grad_scores)
            if number == last:
                dv_turned[...] = dv_part
                dk_turned[...] = dk_part
            else:
                dv_turned[:, :stop] += dv_part
                dk_turned[:, :stop] += dk_part
            dq = dot(grad_scores, k_all[:stop]) * scaler
            result[start:stop, :HD] = dq.astype(BF)
        for number in range(last + 1):
            start, stop = number * step, (number + 1) * step
            result[start:stop, HD : 2 * HD] = (dk_turned[:, start:stop] * scaler).T.astype(BF)
            result[start:stop, 2 * HD :] = dv_turned[:, start:stop].T.astype(BF)

        def load(device):
            return jnp.concatenate(
                [result[place] for place in rows_of_device(device, block, blocks)], axis=0
            )

        emit_exchange(load, me, outs)

    return run_kernel(
        body,
        exchange_shapes(tok_len, 3 * HD),
        [here] + list(received) + list(grads) + [seg_column, key_row, lse],
        flops=5 * 2 * seq_len * seq_len * HD // 2,
        exps=seq_len * seq_len // 2,
        scratch=[
            pltpu.VMEM((seq_len, HD), BF),
            pltpu.VMEM((seq_len, HD), BF),
            pltpu.VMEM((HD, seq_len), BF),
            pltpu.VMEM((HD, seq_len), BF),
            pltpu.VMEM((seq_len, HD), BF),
            pltpu.VMEM((seq_len, 3 * HD), BF),
            pltpu.VMEM((HD, seq_len), F32),
            pltpu.VMEM((HD, seq_len), F32),
        ],
        name="attention_back",
    )


def mix_heads(here, tp_here, received, weight, heads):
    tok_len = received[0].shape[0]
    inner, width = weight.shape
    rows = len_units(received) * tok_len // heads
    size = rows // 4

    def body(here_ref, tp_ref, *rest):
        refs, weight_ref = rest[:5], rest[5]
        heads_ref, outs, held = rest[6], rest[7:11], rest[11]
        for unit_id, value in exchanged(refs, here_ref[0]):
            column = pl.multiple_of(unit_id % heads * HD, HD)
            heads_ref[rows_at(unit_id // heads * tok_len, tok_len), pl.ds(column, HD)] = value
        for start in range(0, width, 512):
            held[:, start : start + 512] = dot(
                heads_ref[...], weight_ref[:, start : start + 512]
            ).astype(BF)
        emit_messages(lambda place: held[place, :], tp_ref[0], outs, size)

    return run_kernel(
        body,
        [sds((rows, inner))] + message_shapes(size // 2, width),
        [here, tp_here] + list(received) + [weight],
        flops=2 * rows * inner * width,
        scratch=[pltpu.VMEM((rows, width), BF)],
        name="mix_heads",
    )


def len_units(received):
    return 2 * received[-1].shape[0]


def second_norm(tp_here, sums, x_rows, mixer_bias, gain, shift):
    rows, width = x_rows.shape
    size = rows // 4

    def body(tp_ref, *rest):
        refs, x_ref, bias_ref, gain_ref, shift_ref = rest[:6], *rest[6:10]
        resid_ref, low_ref, high_ref = rest[10:]
        mine = x_ref[rows_at(tp_ref[0] * size, size), :].astype(F32)
        resid = mine + total_of(refs) + bias_ref[...]
        resid_ref[...] = resid
        unit, _ = normalized(resid)
        value = (unit * gain_ref[...] + shift_ref[...]).astype(BF)
        low_ref[...] = value[: size // 2]
        high_ref[...] = value[size // 2 :]

    return run_kernel(
        body,
        [sds((size, width), F32)] + [sds((size // 2, width))] * 2,
        [tp_here] + list(sums) + [x_rows, mixer_bias, gain, shift],
        name="second_norm",
    )


def erf_of(value):
    return lax.erf(value)


def feed_forward(tp_here, pieces, cot, up_weight, up_bias, down_weight):
    rows, width = cot.shape
    hidden = up_weight.shape[1]
    size = rows // 4
    step = 256
    count = hidden // step

    def body(tp_ref, *rest):
        refs, cot_ref, up_ref, bias_ref, down_ref = rest[:6], *rest[6:10]
        norm_ref, act_ref, pre_ref, sum_ref = rest[10:14]
        feed_outs, grad_outs = rest[14:18], rest[18:22]
        feed, grad = rest[22:]
        number = pl.program_id(0)

        @pl.when(number == 0)
        def _():
            def store(place, value):
                norm_ref[place, :] = value

            place_gathered(store, tp_ref[0], refs, size)

        pre = dot(norm_ref[...], up_ref[...]) + bias_ref[...]
        grad_act = dot_nt(cot_ref[...], down_ref[...])
        spread = 0.5 + 0.5 * erf_of(pre * math.sqrt(0.5))
        dense = jnp.exp(-0.5 * pre * pre) * (1.0 / math.sqrt(2.0 * math.pi))
        act = (pre * spread).astype(BF)
        grad_pre = (grad_act * (spread + pre * dense)).astype(BF)
        act_ref[...] = act
        pre_ref[...] = grad_pre
        sum_ref[...] = jnp.sum(grad_pre.astype(F32), axis=0, keepdims=True)
        feed_part = dot(act, down_ref[...])
        grad_part = dot_nt(grad_pre, up_ref[...])

        @pl.when(number == 0)
        def _():
            feed[...] = feed_part
            grad[...] = grad_part

        @pl.when(number > 0)
        def _():
            feed[...] += feed_part
            grad[...] += grad_part

        @pl.when(number == count - 1)
        def _():
            emit_messages(lambda at: feed[at, :].astype(BF), tp_ref[0], feed_outs, size)
            emit_messages(lambda at: grad[at, :].astype(BF), tp_ref[0], grad_outs, size)

    whole = lambda *shape: pl.BlockSpec(shape, lambda i: (0,) * len(shape))
    in_specs = (
        [pl.BlockSpec(memory_space=pltpu.SMEM)]
        + [whole(*piece.shape) for piece in pieces]
        + [
            whole(rows, width),
            pl.BlockSpec((width, step), lambda i: (0, i)),
            pl.BlockSpec((1, step), lambda i: (0, i)),
            pl.BlockSpec((step, width), lambda i: (i, 0)),
        ]
    )
    out_specs = (
        [
            whole(rows, width),
            pl.BlockSpec((rows, step), lambda i: (0, i)),
            pl.BlockSpec((rows, step), lambda i: (0, i)),
            pl.BlockSpec((1, step), lambda i: (0, i)),
        ]
        + [whole(2, size // 2, width)] * 8
    )
    outs = (
        [sds((rows, width)), sds((rows, hidden)), sds((rows, hidden)), sds((1, hidden), F32)]
        + message_shapes(size // 2, width)
        + message_shapes(size // 2, width)
    )
    return pl.pallas_call(
        body,
        grid=(count,),
        out_shape=tuple(outs),
        in_specs=in_specs,
        out_specs=tuple(out_specs),
        scratch_shapes=[pltpu.VMEM((rows, width), F32), pltpu.VMEM((rows, width), F32)],
        compiler_params=pltpu.CompilerParams(vmem_limit_bytes=56 << 20),
        cost_estimate=pl.CostEstimate(
            flops=8 * rows * width * hidden,
            bytes_accessed=4 * width * hidden + 20 * rows * width,
            transcendentals=2 * rows * hidden,
        ),
        name="feed_forward",
    )(tp_here, *pieces, cot, up_weight, up_bias, down_weight)


def second_norm_back(tp_here, sums, resid, cot, gain):
    size, width = resid.shape

    def body(tp_ref, *rest):
        refs, resid_ref, cot_ref, gain_ref = rest[:6], *rest[6:9]
        grad_ref, low_ref, high_ref, gain_out, shift_out = rest[9:]
        back, gain_sum, shift_sum = norm_back(resid_ref[...], gain_ref[...], total_of(refs))
        grad = back + cot_ref[rows_at(tp_ref[0] * size, size), :].astype(F32)
        grad_ref[...] = grad
        low = grad.astype(BF)
        low_ref[...] = low[: size // 2]
        high_ref[...] = low[size // 2 :]
        gain_out[...] = gain_sum
        shift_out[...] = shift_sum

    return run_kernel(
        body,
        [sds((size, width), F32)]
        + [sds((size // 2, width))] * 2
        + [sds((1, width), F32)] * 2,
        [tp_here] + list(sums) + [resid, cot, gain],
        name="second_norm_back",
    )


def first_norm_back(tp_here, sums, x_rows, grad_resid, gain):
    size, width = grad_resid.shape

    def body(tp_ref, *rest):
        refs, x_ref, grad_ref, gain_ref = rest[:6], *rest[6:9]
        low_ref, high_ref, gain_out, shift_out = rest[9:]
        mine = x_ref[rows_at(tp_ref[0] * size, size), :].astype(F32)
        back, gain_sum, shift_sum = norm_back(mine, gain_ref[...], total_of(refs))
        low = (back + grad_ref[...]).astype(BF)
        low_ref[...] = low[: size // 2]
        high_ref[...] = low[size // 2 :]
        gain_out[...] = gain_sum
        shift_out[...] = shift_sum

    return run_kernel(
        body,
        [sds((size // 2, width))] * 2 + [sds((1, width), F32)] * 2,
        [tp_here] + list(sums) + [x_rows, grad_resid, gain],
        name="first_norm_back",
    )


def finish_output(sums, resid, bias):
    size, width = resid.shape

    def body(*rest):
        refs, resid_ref, bias_ref, low_ref, high_ref = rest[:6], *rest[6:]
        value = (resid_ref[...] + total_of(refs) + bias_ref[...]).astype(BF)
        low_ref[...] = value[: size // 2]
        high_ref[...] = value[size // 2 :]

    return run_kernel(
        body,
        [sds((size // 2, width))] * 2,
        list(sums) + [resid, bias],
        name="finish_output",
    )


def heads_back(here, tp_here, pieces, weight, tok_len):
    inner, width = weight.shape
    heads = inner // HD
    size = 2 * pieces[0].shape[0]
    rows = 4 * size

    def body(here_ref, tp_ref, *rest):
        refs, weight_ref = rest[:6], rest[6]
        mix_ref, sum_ref, outs, held = rest[7], rest[8], rest[9:14], rest[14]

        def store(place, value):
            mix_ref[place, :] = value

        place_gathered(store, tp_ref[0], refs, size)
        sum_ref[...] = jnp.sum(mix_ref[...].astype(F32), axis=0, keepdims=True)
        value = dot_nt(mix_ref[...], weight_ref[...]).astype(BF)
        for head in range(heads):
            held[head] = value[:, head * HD : (head + 1) * HD]

        def load(unit_id):
            return held[unit_id % heads, rows_at(unit_id // heads * tok_len, tok_len), :]

        emit_exchange(load, here_ref[0], outs)

    return run_kernel(
        body,
        [sds((rows, width)), sds((1, width), F32)] + exchange_shapes(tok_len, HD),
        [here, tp_here] + list(pieces) + [weight],
        flops=2 * rows * inner * width,
        scratch=[pltpu.VMEM((heads, rows, HD), BF)],
        name="heads_back",
    )


def project_back(here, tp_here, received, weight):
    tok_len = received[0].shape[0]
    _, width, inner = weight.shape
    heads = inner // HD
    rows = len_units(received) * tok_len // heads
    size = rows // 4

    def body(here_ref, tp_ref, *rest):
        refs, weight_ref = rest[:5], rest[5]
        proj_ref, sum_ref, outs, held = rest[6], rest[7], rest[8:12], rest[12]
        for unit_id, value in exchanged(refs, here_ref[0]):
            place = rows_at(unit_id // heads * tok_len, tok_len)
            for part in range(3):
                column = pl.multiple_of(part * inner + unit_id % heads * HD, HD)
                proj_ref[place, pl.ds(column, HD)] = value[:, part * HD : (part + 1) * HD]
        sum_ref[...] = jnp.sum(proj_ref[...].astype(F32), axis=0, keepdims=True)
        for start in range(0, width, 512):
            value = dot_nt(proj_ref[:, :inner], weight_ref[0, start : start + 512])
            for part in range(1, 3):
                value += dot_nt(
                    proj_ref[:, part * inner : (part + 1) * inner],
                    weight_ref[part, start : start + 512],
                )
            held[:, start : start + 512] = value.astype(BF)
        emit_messages(lambda place: held[place, :], tp_ref[0], outs, size)

    return run_kernel(
        body,
        [sds((rows, 3 * inner)), sds((1, 3 * inner), F32)] + message_shapes(size // 2, width),
        [here, tp_here] + list(received) + [weight],
        flops=6 * rows * inner * width,
        scratch=[pltpu.VMEM((rows, width), BF)],
        name="project_back",
    )


def assemble(tp_here, pieces, earlier, index, count, dtype):
    half, width = pieces[0].shape
    size = 2 * half
    rows = 4 * size

    def body(tp_ref, *rest):
        refs, out_ref = rest[:6], rest[-1]

        def store(place, value):
            out_ref[0, place, :] = value.astype(dtype)

        place_gathered(store, tp_ref[0], refs, size)

    args = [tp_here] + list(pieces)
    in_specs = [pl.BlockSpec(memory_space=pltpu.SMEM)] + [
        pl.BlockSpec(piece.shape, lambda i, n=piece.ndim: (0,) * n) for piece in pieces
    ]
    aliases = {}
    if earlier is not None:
        aliases = {len(args): 0}
        args.append(earlier)
        in_specs.append(pl.BlockSpec(memory_space=pl.ANY))
    return pl.pallas_call(
        body,
        grid=(1,),
        out_shape=sds((count, rows, width), dtype),
        in_specs=in_specs,
        out_specs=pl.BlockSpec((1, rows, width), lambda i: (index, 0, 0)),
        input_output_aliases=aliases,
        compiler_params=pltpu.CompilerParams(vmem_limit_bytes=32 << 20),
        cost_estimate=pl.CostEstimate(
            flops=0, bytes_accessed=rows * width * 6, transcendentals=0
        ),
        name="assemble",
    )(*args)


def weight_grad(lefts, rights, step=512):
    count = len(lefts)
    rows, tall = lefts[0].shape
    wide = rights[0].shape[1]
    step = min(step, tall)

    def body(*rest):
        left_refs, right_refs, out_ref = rest[:count], rest[count : 2 * count], rest[-1]
        value = dot_tn(left_refs[0][...], right_refs[0][...])
        for place in range(1, count):
            value += dot_tn(left_refs[place][...], right_refs[place][...])
        out_ref[...] = value.astype(BF)

    return pl.pallas_call(
        body,
        grid=(tall // step,),
        out_shape=sds((tall, wide)),
        in_specs=[pl.BlockSpec((rows, step), lambda i: (0, i))] * count
        + [pl.BlockSpec((rows, wide), lambda i: (0, 0))] * count,
        out_specs=pl.BlockSpec((step, wide), lambda i: (i, 0)),
        compiler_params=pltpu.CompilerParams(vmem_limit_bytes=48 << 20),
        cost_estimate=pl.CostEstimate(
            flops=2 * count * rows * tall * wide,
            bytes_accessed=2 * (count * rows * (tall + wide) + tall * wide),
            transcendentals=0,
        ),
        name="weight_grad",
    )(*lefts, *rights)


def small_sums(values):
    here = lax.axis_index("ctx")
    step = values.shape[0] // 2
    while step:
        pair = values.reshape((2, step) + values.shape[1:])
        bit = (here // step) % 2
        keep = lax.dynamic_index_in_dim(pair, bit, 0, False)
        send = lax.dynamic_index_in_dim(pair, 1 - bit, 0, False)
        values = keep + xor_permute(send, "ctx", step)
        step //= 2
    return values[0]


def per_device_exchanged(
    inputs,
    segments,
    keep_mask,
    first_gain,
    first_shift,
    proj_weight,
    proj_bias,
    mixer_weight,
    mixer_bias,
    second_gain,
    second_shift,
    up_weight,
    up_bias,
    down_weight,
    down_bias,
    out_cotangent,
):
    ctx_count = lax.axis_size("ctx")
    micro_count, seq_count, tok_len, width = inputs.shape
    inner = proj_bias.shape[1]
    heads = inner // HD
    rows = seq_count * tok_len
    here = lax.axis_index("ctx").astype(jnp.int32).reshape(1)
    tp_here = lax.axis_index("tp").astype(jnp.int32).reshape(1)
    weight_three = jnp.transpose(proj_weight, (1, 0, 2))
    bias_three = jnp.stack([proj_bias[0], jnp.zeros_like(proj_bias[0]), proj_bias[1]])
    x_all = inputs.reshape(micro_count, rows, width)
    cot_all = out_cotangent.reshape(micro_count, rows, width)
    key_rows = jnp.where(keep_mask > 0, segments, -1)[:, :, None, :]
    seg_columns = segments[:, :, :, None]
    gain_one, shift_one = first_gain[None], first_shift[None]
    gain_two, shift_two = second_gain[None], second_shift[None]
    mix_bias, low_bias, high_bias = mixer_bias[None], down_bias[None], up_bias[None]
    micro = range(micro_count)

    norm_one, received, lses, heads_low, resids = [], [], [], [], []
    for index in micro:
        normed, *sent = project(
            here, x_all[index], gain_one, shift_one, weight_three, bias_three, tok_len
        )
        norm_one.append(normed)
        received.append(exchange(*sent))
    gathered_two = []
    for index in micro:
        *sent, lse = attention(here, received[index], seg_columns[index], key_rows[index], heads)
        lses.append(lse)
        mixed, *messages = mix_heads(here, tp_here, exchange(*sent), mixer_weight, heads)
        heads_low.append(mixed)
        resid, low, high = second_norm(
            tp_here, shard_reduce(messages), x_all[index], mix_bias, gain_two, shift_two
        )
        resids.append(resid)
        gathered_two.append(shard_gather((low, high)))
    norm_two, acts, grad_pres, up_sums, feeds, grad_twos = [], [], [], [], [], []
    for index in micro:
        normed, act, grad_pre, up_sum, *messages = feed_forward(
            tp_here, gathered_two[index], cot_all[index], up_weight, high_bias, down_weight
        )
        norm_two.append(normed)
        acts.append(act)
        grad_pres.append(grad_pre)
        up_sums.append(up_sum)
        feeds.append(messages[:4])
        grad_twos.append(messages[4:])
    grad_resids, gain_twos, shift_twos, gathered_mix = [], [], [], []
    for index in micro:
        grad_resid, low, high, gain_sum, shift_sum = second_norm_back(
            tp_here, shard_reduce(grad_twos[index]), resids[index], cot_all[index], gain_two
        )
        grad_resids.append(grad_resid)
        gain_twos.append(gain_sum)
        shift_twos.append(shift_sum)
        gathered_mix.append(shard_gather((low, high)))

    def scattered(part, dim):
        return lax.psum_scatter(part, "ctx", scatter_dimension=dim, tiled=True).astype(F32)

    cots = [cot_all[index] for index in micro]
    down_grad = scattered(weight_grad(acts, cots), 1)
    up_grad = scattered(weight_grad(norm_two, grad_pres), 0)

    grad_mixes, mix_sums, grad_projs, proj_sums, gain_ones, shift_ones = [], [], [], [], [], []
    input_grad = None
    outputs = None
    for index in micro:
        grad_mix, mix_sum, *sent = heads_back(
            here, tp_here, gathered_mix[index], mixer_weight, tok_len
        )
        grad_mixes.append(grad_mix)
        mix_sums.append(mix_sum)
        sent = attention_back(
            here,
            received[index],
            exchange(*sent),
            seg_columns[index],
            key_rows[index],
            lses[index],
            heads,
        )
        grad_proj, proj_sum, *messages = project_back(
            here, tp_here, exchange(*sent), weight_three
        )
        grad_projs.append(grad_proj)
        proj_sums.append(proj_sum)
        low, high, gain_sum, shift_sum = first_norm_back(
            tp_here, shard_reduce(messages), x_all[index], grad_resids[index], gain_one
        )
        gain_ones.append(gain_sum)
        shift_ones.append(shift_sum)
        input_grad = assemble(
            tp_here, shard_gather((low, high)), input_grad, index, micro_count, F32
        )
    for index in micro:
        halves = finish_output(shard_reduce(feeds[index]), resids[index], low_bias)
        outputs = assemble(tp_here, shard_gather(halves), outputs, index, micro_count, BF)
    mixer_grad = scattered(weight_grad(heads_low, grad_mixes), 1)
    proj_grad = scattered(weight_grad(norm_one, grad_projs), 0)

    def over_micro(items):
        return sum(items[1:], items[0]).reshape(ctx_count, -1)

    cot_sum = jnp.sum(out_cotangent.astype(F32), axis=(0, 1, 2)).reshape(ctx_count, -1)
    proj_sum = sum(proj_sums[1:], proj_sums[0]).reshape(3, ctx_count, -1)
    pair_sum = jnp.concatenate([proj_sum[0], proj_sum[2]], axis=1)
    share = cot_sum.shape[1]
    pair_sum = jnp.pad(pair_sum, ((0, 0), (0, share - pair_sum.shape[1])))
    kinds = [
        over_micro(gain_ones),
        over_micro(shift_ones),
        over_micro(gain_twos),
        over_micro(shift_twos),
        over_micro(mix_sums),
        cot_sum,
        over_micro(up_sums),
        pair_sum,
    ]
    small = small_sums(jnp.stack(kinds, axis=1))
    norms = small[:4]
    for step in (1, 2):
        norms = norms + xor_permute(norms, "tp", step)
    proj_bias_grad = small[7, : 2 * inner // ctx_count].reshape(2, -1)
    return (
        outputs.reshape(inputs.shape),
        input_grad.reshape(inputs.shape),
        norms[0],
        norms[1],
        proj_grad.reshape(width // ctx_count, 3, inner),
        proj_bias_grad,
        mixer_grad,
        small[4],
        norms[2],
        norms[3],
        up_grad,
        small[6],
        down_grad,
        small[5],
    )


def plan_for(mesh):
    sizes = dict(mesh.shape)

    def chosen(*args):
        seq_count, width = args[0].shape[1], args[0].shape[3]
        units = seq_count * args[6].shape[1] // HD
        fits = sizes["ctx"] == 8 and sizes["tp"] == 4 and units == sizes["ctx"]
        fits = fits and args[12].shape[0] == width
        return (per_device_exchanged if fits else per_device)(*args)

    return chosen


def solution(mesh):
    in_specs = (
        P(None, None, "ctx", None),
        P(),
        P(),
        P(),
        P(),
        P(None, None, "tp"),
        P(None, "tp"),
        P("tp", None),
        P(),
        P(),
        P(),
        P(None, "tp"),
        P("tp"),
        P("tp", None),
        P(),
        P(None, None, "ctx", None),
    )
    out_specs = (
        P(None, None, "ctx", None),
        P(None, None, "ctx", None),
        P("ctx"),
        P("ctx"),
        P("ctx", None, "tp"),
        P(None, ("tp", "ctx")),
        P("tp", "ctx"),
        P("ctx"),
        P("ctx"),
        P("ctx"),
        P("ctx", "tp"),
        P(("tp", "ctx")),
        P("tp", "ctx"),
        P("ctx"),
    )
    return jax.shard_map(
        plan_for(mesh), mesh=mesh, in_specs=in_specs, out_specs=out_specs, check_vma=False
    )
```

```python
import math

import jax
import jax.numpy as jnp
from jax import lax
from jax.experimental import pallas as pl
from jax.experimental.pallas import tpu as pltpu
from jax.sharding import PartitionSpec as P

HD = 128


def storage_order(values, part_count):
    leading = values.shape[:-1]
    blocks = values.reshape(leading + (2 * part_count, -1))
    front_half = blocks[..., :part_count, :]
    back_half = jnp.flip(blocks[..., part_count:, :], axis=-2)
    return jnp.stack([front_half, back_half], axis=-2).reshape(leading + (-1,))


def layer_norm(values, norm_gain, norm_shift):
    center = values - jnp.mean(values, axis=-1, keepdims=True)
    spread = jnp.mean(center * center, axis=-1, keepdims=True)
    return center * lax.rsqrt(spread + 1e-05) * norm_gain + norm_shift


def gelu_exact(values):
    return jax.nn.gelu(values, approximate=False)


def split_heads(rows, heads_here):
    return rows.reshape(rows.shape[0], rows.shape[1], heads_here, -1)


def scores_of(queries, key_all, allowed, heads_here, scaler):
    raw = (
        jnp.einsum(
            "sqhd,skhd->shqk",
            split_heads(queries, heads_here),
            split_heads(key_all, heads_here),
            preferred_element_type=jnp.float32,
        )
        * scaler
    )
    return jnp.where(allowed[:, None], raw, -1000000000.0)


def attend(queries, key_all, value_all, allowed, heads_here, scaler):
    masked = scores_of(queries, key_all, allowed, heads_here, scaler)
    top = jnp.max(masked, axis=-1, keepdims=True)
    raised = jnp.exp(masked - top)
    totals = jnp.sum(raised, axis=-1, keepdims=True)
    probs = raised / totals
    mixed = jnp.einsum(
        "shqk,skhd->sqhd",
        probs.astype(jnp.bfloat16),
        split_heads(value_all, heads_here),
        preferred_element_type=jnp.float32,
    )
    return (mixed.reshape(queries.shape), top + jnp.log(totals))


def attend_back(queries, key_all, value_all, allowed, log_total, grad_heads, heads_here, scaler):
    masked = scores_of(queries, key_all, allowed, heads_here, scaler)
    probs = jnp.exp(masked - log_total)
    grad_four = split_heads(grad_heads, heads_here)
    grad_value = jnp.einsum(
        "shqk,sqhd->skhd", probs.astype(jnp.bfloat16), grad_four, preferred_element_type=jnp.float32
    )
    grad_probs = jnp.einsum(
        "sqhd,skhd->shqk",
        grad_four,
        split_heads(value_all, heads_here),
        preferred_element_type=jnp.float32,
    )
    inner_sum = jnp.sum(probs * grad_probs, axis=-1, keepdims=True)
    grad_scores = (probs * (grad_probs - inner_sum)).astype(jnp.bfloat16)
    grad_query = (
        jnp.einsum(
            "shqk,skhd->sqhd",
            grad_scores,
            split_heads(key_all, heads_here),
            preferred_element_type=jnp.float32,
        )
        * scaler
    )
    grad_key = (
        jnp.einsum(
            "shqk,sqhd->skhd",
            grad_scores,
            split_heads(queries, heads_here),
            preferred_element_type=jnp.float32,
        )
        * scaler
    )
    return (
        grad_query.reshape(queries.shape),
        grad_key.reshape(key_all.shape),
        grad_value.reshape(value_all.shape),
    )


def reduce_grads(grads):
    return (
        lax.psum_scatter(
            grads[0].astype(jnp.bfloat16), "ctx", scatter_dimension=0, tiled=True
        ).astype(jnp.float32),
        lax.psum_scatter(
            grads[1].astype(jnp.bfloat16), "ctx", scatter_dimension=0, tiled=True
        ).astype(jnp.float32),
        lax.psum_scatter(
            grads[2].astype(jnp.bfloat16), "ctx", scatter_dimension=0, tiled=True
        ).astype(jnp.float32),
        lax.psum_scatter(
            grads[3].astype(jnp.bfloat16), "ctx", scatter_dimension=1, tiled=True
        ).astype(jnp.float32),
        lax.psum_scatter(
            grads[4].astype(jnp.bfloat16), "ctx", scatter_dimension=1, tiled=True
        ).astype(jnp.float32),
        lax.psum_scatter(
            grads[5].astype(jnp.bfloat16), "ctx", scatter_dimension=0, tiled=True
        ).astype(jnp.float32),
        lax.psum_scatter(
            grads[6].astype(jnp.bfloat16), "ctx", scatter_dimension=0, tiled=True
        ).astype(jnp.float32),
        lax.psum_scatter(
            grads[7].astype(jnp.bfloat16), "ctx", scatter_dimension=0, tiled=True
        ).astype(jnp.float32),
        lax.psum_scatter(
            grads[8].astype(jnp.bfloat16), "ctx", scatter_dimension=0, tiled=True
        ).astype(jnp.float32),
        lax.psum_scatter(
            grads[9].astype(jnp.bfloat16), "ctx", scatter_dimension=0, tiled=True
        ).astype(jnp.float32),
        lax.psum_scatter(
            grads[10].astype(jnp.bfloat16), "ctx", scatter_dimension=1, tiled=True
        ).astype(jnp.float32),
        lax.psum_scatter(
            grads[11].astype(jnp.bfloat16), "ctx", scatter_dimension=0, tiled=True
        ).astype(jnp.float32),
    )


def per_device(
    inputs,
    segments,
    keep_mask,
    first_gain,
    first_shift,
    proj_weight,
    proj_bias,
    mixer_weight,
    mixer_bias,
    second_gain,
    second_shift,
    up_weight,
    up_bias,
    down_weight,
    down_bias,
    out_cotangent,
):
    ctx_count = lax.axis_size("ctx")
    micro_count, seq_count, tok_len, model_width = inputs.shape
    inner_width = proj_bias.shape[1]
    heads_here = inner_width // HD
    scaler = 1.0 / math.sqrt(HD)
    seq_len = tok_len * ctx_count
    places = storage_order(jnp.arange(seq_len, dtype=jnp.int32), ctx_count)
    offset = lax.axis_index("ctx") * tok_len
    my_places = lax.dynamic_slice_in_dim(places, offset, tok_len, 0)
    seg_store = storage_order(segments, ctx_count)
    keep_store = storage_order(keep_mask, ctx_count)
    proj_flat = proj_weight.reshape(model_width, 3 * inner_width)
    bias_three = jnp.stack([proj_bias[0], jnp.zeros_like(proj_bias[0]), proj_bias[1]])
    causal = places[None, :] <= my_places[:, None]
    itself = places[None, :] == my_places[:, None]
    shaped_like = (
        first_gain,
        first_shift,
        proj_weight,
        proj_bias,
        mixer_weight,
        mixer_bias,
        second_gain,
        second_shift,
        up_weight,
        up_bias,
        down_weight,
        down_bias,
    )
    running = tuple((jnp.zeros(item.shape, jnp.float32) for item in shaped_like))
    out_list = []
    grad_list = []
    for micro_index in range(micro_count):
        x_now = inputs[micro_index].astype(jnp.float32)
        seg_keys = seg_store[micro_index]
        seg_mine = lax.dynamic_slice_in_dim(seg_keys, offset, tok_len, 1)
        visible = (keep_store[micro_index] > 0)[:, None, :] | itself[None]
        allowed = causal[None] & (seg_keys[:, None, :] == seg_mine[:, :, None]) & visible
        normed_one = layer_norm(x_now, first_gain, first_shift).astype(jnp.bfloat16)
        projected = jnp.einsum(
            "std,dc->stc", normed_one, proj_flat, preferred_element_type=jnp.float32
        )
        projected = (projected.reshape(seq_count, tok_len, 3, inner_width) + bias_three).astype(
            jnp.bfloat16
        )
        queries = projected[:, :, 0]
        key_here = projected[:, :, 1]
        value_here = projected[:, :, 2]
        key_all, value_all = (
            lax.all_gather(key_here, "ctx", axis=1, tiled=True),
            lax.all_gather(value_here, "ctx", axis=1, tiled=True),
        )
        heads_out, log_total = attend(queries, key_all, value_all, allowed, heads_here, scaler)
        heads_low = heads_out.astype(jnp.bfloat16)
        mixed_part = jnp.einsum(
            "stn,nd->std", heads_low, mixer_weight, preferred_element_type=jnp.float32
        )
        resid = (
            x_now + lax.psum(mixed_part.astype(jnp.bfloat16), "tp").astype(jnp.float32) + mixer_bias
        )
        normed_two = layer_norm(resid, second_gain, second_shift).astype(jnp.bfloat16)
        pre_act = (
            jnp.einsum("std,df->stf", normed_two, up_weight, preferred_element_type=jnp.float32)
            + up_bias
        )
        act_low = gelu_exact(pre_act).astype(jnp.bfloat16)
        feed_part = jnp.einsum(
            "stf,fd->std", act_low, down_weight, preferred_element_type=jnp.float32
        )
        feed = lax.psum(feed_part.astype(jnp.bfloat16), "tp").astype(jnp.float32) + down_bias
        out_list.append((resid + feed).astype(jnp.bfloat16))
        cot_low = out_cotangent[micro_index]
        cot_full = cot_low.astype(jnp.float32)
        down_bias_part = jnp.sum(cot_full, axis=(0, 1))
        down_part = jnp.einsum("stf,std->fd", act_low, cot_low, preferred_element_type=jnp.float32)
        grad_act = jnp.einsum(
            "std,fd->stf", cot_low, down_weight, preferred_element_type=jnp.float32
        )
        grad_pre = jax.vjp(gelu_exact, pre_act)[1](grad_act)[0].astype(jnp.bfloat16)
        up_part = jnp.einsum(
            "std,stf->df", normed_two, grad_pre, preferred_element_type=jnp.float32
        )
        up_bias_part = jnp.sum(grad_pre.astype(jnp.float32), axis=(0, 1))
        grad_two_part = jnp.einsum(
            "stf,df->std", grad_pre, up_weight, preferred_element_type=jnp.float32
        )
        grad_two = lax.psum(grad_two_part.astype(jnp.bfloat16), "tp").astype(jnp.float32)
        resid_part, second_gain_part, second_shift_part = jax.vjp(
            layer_norm, resid, second_gain, second_shift
        )[1](grad_two)
        grad_resid = cot_full + resid_part
        grad_mix = grad_resid.astype(jnp.bfloat16)
        mixer_bias_part = jnp.sum(grad_mix.astype(jnp.float32), axis=(0, 1))
        mixer_part = jnp.einsum(
            "stn,std->nd", heads_low, grad_mix, preferred_element_type=jnp.float32
        )
        grad_heads = jnp.einsum(
            "std,nd->stn", grad_mix, mixer_weight, preferred_element_type=jnp.float32
        ).astype(jnp.bfloat16)
        key_back, value_back = (key_all, value_all)
        grad_query, grad_key, grad_value = attend_back(
            queries, key_back, value_back, allowed, log_total, grad_heads, heads_here, scaler
        )
        key_share, value_share = (
            lax.psum_scatter(
                grad_key.astype(jnp.bfloat16), "ctx", scatter_dimension=1, tiled=True
            ).astype(jnp.float32),
            lax.psum_scatter(
                grad_value.astype(jnp.bfloat16), "ctx", scatter_dimension=1, tiled=True
            ).astype(jnp.float32),
        )
        grad_proj = jnp.stack([grad_query, key_share, value_share], axis=2).astype(jnp.bfloat16)
        proj_part = jnp.einsum(
            "std,stcn->dcn", normed_one, grad_proj, preferred_element_type=jnp.float32
        )
        proj_sums = jnp.sum(grad_proj.astype(jnp.float32), axis=(0, 1))
        proj_bias_part = jnp.stack([proj_sums[0], proj_sums[2]])
        grad_one_part = jnp.einsum(
            "stc,dc->std",
            grad_proj.reshape(seq_count, tok_len, 3 * inner_width),
            proj_flat,
            preferred_element_type=jnp.float32,
        )
        grad_one = lax.psum(grad_one_part.astype(jnp.bfloat16), "tp").astype(jnp.float32)
        input_part, first_gain_part, first_shift_part = jax.vjp(
            layer_norm, x_now, first_gain, first_shift
        )[1](grad_one)
        grad_list.append(grad_resid + input_part)
        batch_grads = (
            first_gain_part,
            first_shift_part,
            proj_part,
            proj_bias_part,
            mixer_part,
            mixer_bias_part,
            second_gain_part,
            second_shift_part,
            up_part,
            up_bias_part,
            down_part,
            down_bias_part,
        )
        running = tuple((earlier + adding for earlier, adding in zip(running, batch_grads)))
    final = reduce_grads(running)
    return (
        jnp.stack(out_list),
        jnp.stack(grad_list),
        final[0],
        final[1],
        final[2],
        final[3],
        final[4],
        final[5],
        final[6],
        final[7],
        final[8],
        final[9],
        final[10],
        final[11],
    )


BF = jnp.bfloat16
F32 = jnp.float32
LOG2E = 1.4426950408889634
LOW = -1e30
ORDERS = ((1, 2), (2, 1))
COST_SHARE = 1.0


def xor_permute(values, axis, step):
    count = lax.axis_size(axis)
    return lax.ppermute(values, axis, [(i, i ^ step) for i in range(count)])


def sds(shape, dtype=BF):
    return jax.ShapeDtypeStruct(tuple(shape), dtype)


def cost(flops, moved, exps=0):
    return pl.CostEstimate(
        flops=int(flops * COST_SHARE),
        bytes_accessed=int(moved * COST_SHARE),
        transcendentals=int(exps * COST_SHARE),
    )


HBM = pltpu.MemorySpace.HBM


def launch(
    body, args, in_specs, outs, out_specs, scratch, limit, cost, name, after, grid=(), aliases=None
):
    first, last = len(after), len(after) + len(args) + len(outs)

    def inner(*refs):
        body(*refs[first:last], *refs[last + 1 :])

    token = pl.BlockSpec(memory_space=HBM)
    *results, done = pl.pallas_call(
        inner,
        grid=grid,
        out_shape=(*outs, sds((8, 128), F32)),
        in_specs=[token] * first + list(in_specs),
        out_specs=(*out_specs, token),
        scratch_shapes=list(scratch),
        input_output_aliases={first + key: value for key, value in (aliases or {}).items()},
        compiler_params=pltpu.CompilerParams(vmem_limit_bytes=limit),
        cost_estimate=cost,
        name=name,
    )(*after, *args)
    return results, (done,)


class Part:
    def __init__(self, array, index):
        self.array, self.index = array, index
        self.shape, self.dtype = array.shape[1:], array.dtype

    def spec(self):
        index, rest = self.index, (0,) * len(self.shape)
        return pl.BlockSpec((None,) + self.shape, lambda *_: (index,) + rest)


def operands_of(args):
    arrays = [arg.array if isinstance(arg, Part) else arg for arg in args]
    return [
        array if array.dtype == jnp.int32 else pltpu.with_memory_space_constraint(array, HBM)
        for array in arrays
    ]


class Part:
    def __init__(self, array, index):
        self.array, self.index = array, index
        self.shape, self.dtype = array.shape[1:], array.dtype

    def spec(self):
        index, rest = self.index, (0,) * len(self.shape)
        return pl.BlockSpec((None,) + self.shape, lambda *_: (index,) + rest)


def operands_of(args):
    arrays = [arg.array if isinstance(arg, Part) else arg for arg in args]
    return [
        array if array.dtype == jnp.int32 else pltpu.with_memory_space_constraint(array, HBM)
        for array in arrays
    ]


def run_kernel(body, outs, args, flops=0, exps=0, scratch=(), limit=8, name=None, after=(), in_hbm=()):
    specs = []
    moved = 0
    for place, arg in enumerate(args):
        if arg.dtype == jnp.int32 and math.prod(arg.shape) <= 8:
            specs.append(pl.BlockSpec(memory_space=pltpu.SMEM))
        elif place in in_hbm:
            specs.append(pl.BlockSpec(memory_space=pl.ANY))
        else:
            specs.append(pl.BlockSpec(memory_space=pltpu.VMEM))
            moved += math.prod(arg.shape) * arg.dtype.itemsize
    moved += sum(math.prod(o.shape) * o.dtype.itemsize for o in outs)
    kept = [item for item in scratch if item.dtype in (BF, F32)]
    held = moved + sum(math.prod(item.shape) * item.dtype.itemsize for item in kept)
    return launch(
        body,
        args,
        specs,
        outs,
        [pl.BlockSpec(memory_space=pltpu.VMEM) for _ in outs],
        scratch,
        held + (limit << 20),
        cost(flops, moved, exps),
        name,
        after,
    )


def whole_of(shape):
    return pl.BlockSpec(shape, lambda *_, n=len(shape): (0,) * n)


def rows_at(start, count):
    return pl.ds(pl.multiple_of(start, count), count)


def held_until(items, after):
    held, _ = lax.optimization_barrier((items, after))
    return held, after


def reduce_first(messages):
    return [
        (messages[2 * part + 1], xor_permute(messages[2 * part], "tp", first))
        for part, (first, _) in enumerate(ORDERS)
    ]


def reduce_second(state, after=()):
    middle_shape = state[0][0].shape[:-3] + state[0][0].shape[-2:]

    def body(*refs):
        for part in range(2):
            keep, got = refs[2 * part : 2 * part + 2]
            value = keep[..., 1, :, :].astype(F32) + got[..., 1, :, :].astype(F32)
            refs[4 + part][...] = value.astype(BF)

    middles, done = run_kernel(
        body,
        [sds(middle_shape)] * 2,
        [item for pair in state for item in pair],
        after=after,
        name="reduce_middle",
        limit=3,
    )
    sums = []
    for part, (_, second) in enumerate(ORDERS):
        sums += [*state[part], xor_permute(middles[part], "tp", second)]
    return sums, done


def reduce_direct(messages):
    mine, *sent = messages
    return [mine] + [xor_permute(item, "tp", 1 + step) for step, item in enumerate(sent)]


def gather_first(halves):
    return [
        (halves[part], xor_permute(halves[part], "tp", first))
        for part, (first, _) in enumerate(ORDERS)
    ]


def gather_second(state, after=()):
    half = state[0][0].shape
    pair_shape = half[:-2] + (2,) + half[-2:]

    def body(*refs):
        for part in range(2):
            for place in range(2):
                refs[4 + part][..., place, :, :] = refs[2 * part + place][...]

    pairs, done = run_kernel(
        body,
        [sds(pair_shape)] * 2,
        [item for pair in state for item in pair],
        after=after,
        name="gather_middle",
        limit=3,
    )
    pieces = []
    for part, (_, second) in enumerate(ORDERS):
        pieces += [*state[part], xor_permute(pairs[part], "tp", second)]
    return pieces, done


def gather_direct(mine):
    return [mine] + [xor_permute(mine, "tp", step) for step in (1, 2, 3)]


def total_of(refs):
    if len(refs) == 4:
        return sum([ref[...].astype(F32) for ref in refs[1:]], refs[0][...].astype(F32))
    halves = []
    for part in range(2):
        keep, got, late = refs[3 * part : 3 * part + 3]
        halves.append(
            keep[0].astype(F32) + got[0].astype(F32) + late[...].astype(F32)
        )
    return jnp.concatenate(halves, axis=0)


def place_gathered(store, tp_here, refs, size):
    if len(refs) == 4:
        for step, ref in enumerate(refs):
            store(rows_at((tp_here ^ step) * size, size), ref[...])
        return
    half = size // 2
    for part, (first, second) in enumerate(ORDERS):
        mine, near, far = refs[3 * part : 3 * part + 3]
        parts = ((0, mine[...]), (first, near[...]), (second, far[0]), (first | second, far[1]))
        for step, value in parts:
            store(rows_at((tp_here ^ step) * size + part * half, half), value)


def emit_messages(load, tp_here, refs, size):
    if refs[0].shape[-2] == size:
        for step, ref in enumerate(refs):
            ref[...] = load(rows_at((tp_here ^ step) * size, size))
        return
    half = size // 2
    for part, (first, second) in enumerate(ORDERS):
        send, keep = refs[2 * part], refs[2 * part + 1]
        for ref, steps in ((send, (first, first | second)), (keep, (0, second))):
            for place, step in enumerate(steps):
                ref[place] = load(rows_at((tp_here ^ step) * size + part * half, half))


def emit_shard(value, refs):
    rows = value.shape[0] // len(refs)
    for place, ref in enumerate(refs):
        ref[...] = value[place * rows : (place + 1) * rows]


def shard_shapes(size, width, direct=False):
    return [sds((size, width))] if direct else [sds((size // 2, width))] * 2


def message_shapes(half, width, direct=False):
    return [sds((2 * half, width) if direct else (2, half, width))] * 4


def exchange_chips(local, cross, first, second, third):
    got = [
        xor_permute(item, "ctx", 2 * (place + 1))
        for place, item in enumerate((first, second, third))
    ]
    return [local, cross] + got


def exchange_cores(state, after):
    local, cross, *got = state

    lead = cross.shape[:-2]

    def body(cross_ref, first_ref, second_ref, third_ref, out_ref):
        out_ref[..., 0, :, :] = cross_ref[...]
        for place, ref in enumerate((first_ref, second_ref, third_ref)):
            out_ref[..., place + 1, :, :] = ref[..., 1, :, :]

    (packed,), done = run_kernel(
        body, [sds(lead + (4,) + cross.shape[-2:])], [cross] + got, after=after, limit=2, name="pack"
    )
    return [local] + got + [xor_permute(packed, "ctx", 1)], done


def exchanged(refs, here):
    local, first, second, third, packed = refs
    return (
        (here, local[...]),
        (here ^ 1, packed[0]),
        (here ^ 2, first[0]),
        (here ^ 3, packed[1]),
        (here ^ 4, second[0]),
        (here ^ 5, packed[2]),
        (here ^ 6, third[0]),
        (here ^ 7, packed[3]),
    )


def emit_exchange(load, here, refs):
    local, cross, first, second, third = refs
    local[...] = load(here)
    cross[...] = load(here ^ 1)
    for place, ref in enumerate((first, second, third)):
        other = here ^ (2 * (place + 1))
        ref[0] = load(other)
        ref[1] = load(other ^ 1)


def exchange_shapes(rows, width):
    return [sds((rows, width)), sds((rows, width))] + [sds((2, rows, width))] * 3


def normalized(values):
    center = values - jnp.mean(values, axis=-1, keepdims=True)
    spread = jnp.mean(center * center, axis=-1, keepdims=True)
    root = lax.rsqrt(spread + 1e-05)
    return center * root, root


def norm_back(values, gain, grad):
    unit, root = normalized(values)
    scaled = grad * gain
    back = root * (
        scaled
        - jnp.mean(scaled, axis=-1, keepdims=True)
        - unit * jnp.mean(scaled * unit, axis=-1, keepdims=True)
    )
    gain_sum = jnp.sum(grad * unit, axis=0, keepdims=True)
    shift_sum = jnp.sum(grad, axis=0, keepdims=True)
    return back, gain_sum, shift_sum


def dot(left, right):
    return jnp.dot(left, right, preferred_element_type=F32)


def dot_nt(left, right):
    return lax.dot_general(left, right, (((1,), (1,)), ((), ())), preferred_element_type=F32)


def dot_tn(left, right):
    return lax.dot_general(left, right, (((0,), (0,)), ((), ())), preferred_element_type=F32)


def project(here, x_all, index, gain, shift, weight, bias, tok_len, after=()):
    _, rows, width = x_all.shape
    inner = weight.shape[2]
    heads = inner // HD

    def body(here_ref, x_ref, gain_ref, shift_ref, weight_hbm, bias_ref, *rest):
        norm_ref, outs, (held, weight_ref, x_held, sems) = rest[0], rest[1:6], rest[6:]
        fetch = pltpu.make_async_copy(x_ref.at[index], x_held, sems.at[3])
        fetch.start()
        copies = [
            pltpu.make_async_copy(weight_hbm.at[part], weight_ref.at[part], sems.at[part])
            for part in range(3)
        ]
        for copy in copies:
            copy.start()
        fetch.wait()
        unit, _ = normalized(x_held[...].astype(F32))
        norm_ref[...] = (unit * gain_ref[...] + shift_ref[...]).astype(BF)
        for part in range(3):
            copies[part].wait()
            value = dot(norm_ref[...], weight_ref[part]) + bias_ref[part : part + 1]
            value = value.astype(BF)
            for head in range(heads):
                held[head, :, part * HD : (part + 1) * HD] = value[:, head * HD : (head + 1) * HD]

        def load(unit_id):
            return held[unit_id % heads, rows_at(unit_id // heads * tok_len, tok_len), :]

        emit_exchange(load, here_ref[0], outs)

    return run_kernel(
        body,
        [sds((rows, width))] + exchange_shapes(tok_len, 3 * HD),
        [here, x_all, gain, shift, weight, bias],
        flops=6 * rows * width * inner,
        scratch=[
            pltpu.VMEM((heads, rows, 3 * HD), BF),
            pltpu.VMEM(weight.shape, BF),
            pltpu.VMEM((rows, width), BF),
            pltpu.SemaphoreType.DMA((4,)),
        ],
        name="project",
        limit=14,
        after=after,
        in_hbm=(1, 4),
    )


def rows_of_device(device, block, blocks):
    return (
        rows_at(device * block, block),
        rows_at((blocks - 1 - device) * block, block),
    )


def attention(here, received, seg_row, key_row, heads, after=()):
    tok_len = received[0].shape[0]
    block = tok_len // 2
    seq_len = seg_row.shape[2]
    blocks = seq_len // block
    step = 256
    factor = LOG2E / math.sqrt(HD)

    def body(here_ref, *rest):
        refs, seg_ref, key_ref = rest[:5], rest[5], rest[6]
        outs, lse_ref = rest[7:12], rest[12]
        q_all, k_turned, v_all, mixed = rest[13:]
        me = here_ref[0]
        seq = me // heads
        for device, value in exchanged(refs, me):
            for half, place in enumerate(rows_of_device(device, block, blocks)):
                rows = value[half * block : (half + 1) * block]
                q_all[place] = rows[:, :HD]
                k_turned[:, place] = rows[:, HD : 2 * HD].T
                v_all[place] = rows[:, 2 * HD :]
        for number in range(seq_len // step):
            start, stop = number * step, (number + 1) * step
            segs = as_column(seg_ref[seq, :, start:stop])
            scores = dot(q_all[start:stop], k_turned[:, :stop]) * factor
            scores = masked(scores, segs, key_ref, seq, start, stop)
            top = jnp.max(scores, axis=-1, keepdims=True)
            raised = jnp.exp2(scores - top)
            total = jnp.sum(raised, axis=-1, keepdims=True)
            out = dot(raised.astype(BF), v_all[:stop]) / total
            mixed[start:stop] = out.astype(BF)
            lse_ref[start:stop] = top + jnp.log2(total)

        def load(device):
            return jnp.concatenate(
                [mixed[place] for place in rows_of_device(device, block, blocks)], axis=0
            )

        emit_exchange(load, me, outs)

    return run_kernel(
        body,
        exchange_shapes(tok_len, HD) + [sds((seq_len, 1), F32)],
        [here] + list(received) + [seg_row, key_row],
        flops=2 * 2 * seq_len * seq_len * HD,
        exps=seq_len * seq_len // 2,
        scratch=[
            pltpu.VMEM((seq_len, HD), BF),
            pltpu.VMEM((HD, seq_len), BF),
            pltpu.VMEM((seq_len, HD), BF),
            pltpu.VMEM((seq_len, HD), BF),
        ],
        after=after,
        name="attention",
        limit=16,
    )


def as_column(row):
    return jnp.broadcast_to(row, (128, row.shape[1])).T[:, :1]


def masked(scores, segs, key_ref, seq, start, stop):
    size = stop - start
    row = lax.broadcasted_iota(jnp.int32, (size, size), 0)
    column = lax.broadcasted_iota(jnp.int32, (size, size), 1)
    same = segs == key_ref[seq, :, start:stop]
    seen = (same & (column < row)) | (column == row)
    corner = jnp.where(seen, scores[:, start:], LOW)
    if start == 0:
        return corner
    left = jnp.where(segs == key_ref[seq, :, :start], scores[:, :start], LOW)
    return jnp.concatenate([left, corner], axis=1)


def attention_back(
    here, received, grads, seg_row, key_row, lse, heads, earlier, index, count, after=()
):
    tok_len = received[0].shape[0]
    block = tok_len // 2
    seq_len = seg_row.shape[2]
    blocks = seq_len // block
    step = 256
    scaler = 1.0 / math.sqrt(HD)

    def body(here_ref, *rest):
        refs, grad_refs = rest[:5], rest[5:10]
        seg_ref, key_ref, lse_ref = rest[10:13]
        rest = rest[13 + len(earlier) :]
        outs = [ref.at[0] for ref in rest[:5]]
        q_all, k_all, k_turned, v_turned, g_all, result, dk_turned, dv_turned = rest[5:]
        me = here_ref[0]
        seq = me // heads
        for device, value in exchanged(refs, me):
            for half, place in enumerate(rows_of_device(device, block, blocks)):
                rows = value[half * block : (half + 1) * block]
                q_all[place] = rows[:, :HD]
                k_all[place] = rows[:, HD : 2 * HD]
                k_turned[:, place] = rows[:, HD : 2 * HD].T
                v_turned[:, place] = rows[:, 2 * HD :].T
        for device, value in exchanged(grad_refs, me):
            for half, place in enumerate(rows_of_device(device, block, blocks)):
                g_all[place] = value[half * block : (half + 1) * block]
        last = seq_len // step - 1
        for number in range(last, -1, -1):
            start, stop = number * step, (number + 1) * step
            segs = as_column(seg_ref[seq, :, start:stop])
            query, grad = q_all[start:stop], g_all[start:stop]
            scores = dot(query, k_turned[:, :stop]) * (scaler * LOG2E)
            scores = masked(scores, segs, key_ref, seq, start, stop)
            probs = jnp.exp2(scores - lse_ref[start:stop])
            grad_probs = dot(grad, v_turned[:, :stop])
            inner = jnp.sum(probs * grad_probs, axis=-1, keepdims=True)
            grad_scores = (probs * (grad_probs - inner)).astype(BF)
            dv_part = dot_tn(grad, probs.astype(BF))
            dk_part = dot_tn(query, grad_scores)
            if number == last:
                dv_turned[...] = dv_part
                dk_turned[...] = dk_part
            else:
                dv_turned[:, :stop] += dv_part
                dk_turned[:, :stop] += dk_part
            dq = dot(grad_scores, k_all[:stop]) * scaler
            result[start:stop, :HD] = dq.astype(BF)
        for number in range(last + 1):
            start, stop = number * step, (number + 1) * step
            result[start:stop, HD : 2 * HD] = (dk_turned[:, start:stop] * scaler).T.astype(BF)
            result[start:stop, 2 * HD :] = dv_turned[:, start:stop].T.astype(BF)

        def load(device):
            return jnp.concatenate(
                [result[place] for place in rows_of_device(device, block, blocks)], axis=0
            )

        emit_exchange(load, me, outs)

    shapes = exchange_shapes(tok_len, 3 * HD)
    args = [here, *received, *grads, seg_row, key_row, lse, *earlier]
    first = len(args) - len(earlier)
    return launch(
        body,
        operands_of(args),
        [pl.BlockSpec(memory_space=pltpu.SMEM)]
        + [whole_of(item.shape) for item in args[1:first]]
        + [pl.BlockSpec(memory_space=pl.ANY) for _ in earlier],
        [sds((count,) + item.shape) for item in shapes],
        [
            pl.BlockSpec((1,) + item.shape, lambda i, n=len(item.shape): (index,) + (0,) * n)
            for item in shapes
        ],
        [
            pltpu.VMEM((seq_len, HD), BF),
            pltpu.VMEM((seq_len, HD), BF),
            pltpu.VMEM((HD, seq_len), BF),
            pltpu.VMEM((HD, seq_len), BF),
            pltpu.VMEM((seq_len, HD), BF),
            pltpu.VMEM((seq_len, 3 * HD), BF),
            pltpu.VMEM((HD, seq_len), F32),
            pltpu.VMEM((HD, seq_len), F32),
        ],
        36 << 20,
        cost(5 * seq_len * seq_len * HD, 12 * seq_len * HD),
        "attention_back",
        after,
        grid=(1,),
        aliases={first + number: number for number in range(len(earlier))},
    )


def mix_heads(here, tp_here, received, weight, heads, direct, after=()):
    tok_len = received[0].shape[0]
    inner, width = weight.shape
    rows = len_units(received) * tok_len // heads
    size = rows // 4

    def body(here_ref, tp_ref, *rest):
        refs, weight_ref = rest[:5], rest[5]
        heads_ref, outs, held = rest[6], rest[7:11], rest[11]
        for unit_id, value in exchanged(refs, here_ref[0]):
            column = pl.multiple_of(unit_id % heads * HD, HD)
            heads_ref[rows_at(unit_id // heads * tok_len, tok_len), pl.ds(column, HD)] = value
        for start in range(0, width, 512):
            held[:, start : start + 512] = dot(
                heads_ref[...], weight_ref[:, start : start + 512]
            ).astype(BF)
        emit_messages(lambda place: held[place, :], tp_ref[0], outs, size)

    return run_kernel(
        body,
        [sds((rows, inner))] + message_shapes(size // 2, width, direct),
        [here, tp_here] + list(received) + [weight],
        flops=2 * rows * inner * width,
        scratch=[pltpu.VMEM((rows, width), BF)],
        after=after,
        name="mix_heads",
        limit=6,
    )


def len_units(received):
    return 2 * received[-1].shape[0]


def second_norm(sums, x_mine, mixer_bias, gain, shift, direct, after=()):
    size, width = x_mine.shape
    count = len(sums)

    def body(*rest):
        refs, (x_ref, bias_ref, gain_ref, shift_ref) = rest[:count], rest[count : count + 4]
        resid_ref, outs = rest[count + 4], rest[count + 5 :]
        resid = x_ref[...].astype(F32) + total_of(refs) + bias_ref[...]
        resid_ref[...] = resid
        unit, _ = normalized(resid)
        emit_shard((unit * gain_ref[...] + shift_ref[...]).astype(BF), outs)

    return run_kernel(
        body,
        [sds((size, width), F32)] + shard_shapes(size, width, direct),
        list(sums) + [x_mine, mixer_bias, gain, shift],
        name="second_norm",
        limit=8,
        after=after,
    )


def feed_forward(
    tp_here, pieces, cot, up_weight, up_bias, down_weight, earlier, index, count, direct, after=()
):
    rows, width = cot.shape
    hidden = up_weight.shape[1]
    size = rows // 4
    step = 512
    blocks = hidden // step

    def body(tp_ref, *rest):
        refs, rest = rest[: len(pieces)], rest[len(pieces) :]
        cot_ref, up_hbm, bias_ref, down_hbm = rest[:4]
        rest = rest[4 + len(earlier) :]
        norm_ref, act_ref, pre_ref, sum_ref, cot_sum_ref = rest[:5]
        feed_outs, grad_outs = rest[5:9], rest[9:13]
        up, down, held, sems = rest[13:]

        def part(number):
            return pl.ds(pl.multiple_of(number * step, step), step)

        def copies(number):
            place = part(number)
            return (
                pltpu.make_async_copy(up_hbm.at[:, place], up.at[:, place], sems.at[0, number]),
                pltpu.make_async_copy(down_hbm.at[place, :], down.at[place, :], sems.at[1, number]),
            )

        for number in range(blocks):
            for copy in copies(number):
                copy.start()

        def store(place, value):
            norm_ref[place, :] = value

        place_gathered(store, tp_ref[0], refs, size)
        cot_sum_ref[...] = jnp.sum(cot_ref[...].astype(F32), axis=0, keepdims=True)

        @pl.loop(0, blocks)
        def _(number):
            for copy in copies(number):
                copy.wait()
            place = part(number)
            pre = dot(norm_ref[...], up[:, place]) + bias_ref[:, place]
            grad_act = dot_nt(cot_ref[...], down[place, :])
            spread = 0.5 + 0.5 * lax.erf(pre * math.sqrt(0.5))
            dense = jnp.exp(-0.5 * pre * pre) * (1.0 / math.sqrt(2.0 * math.pi))
            act_ref[:, place] = (pre * spread).astype(BF)
            grad_pre = (grad_act * (spread + pre * dense)).astype(BF)
            pre_ref[:, place] = grad_pre
            sum_ref[:, place] = jnp.sum(grad_pre.astype(F32), axis=0, keepdims=True)

        @pl.loop(0, width // step)
        def _(number):
            place = part(number)
            held[:, place] = dot_nt(pre_ref[...], up[place, :]).astype(BF)

        emit_messages(lambda at: held[at, :], tp_ref[0], grad_outs, size)

        @pl.loop(0, width // step)
        def _(number):
            place = part(number)
            held[:, place] = dot(act_ref[...], down[:, place]).astype(BF)

        emit_messages(lambda at: held[at, :], tp_ref[0], [ref.at[0] for ref in feed_outs], size)

    message = (2, size // 2, width)
    args = [tp_here, *pieces, cot, up_weight, up_bias, down_weight, *earlier]
    first = len(args) - len(earlier)
    outs = [
        sds((rows, width)),
        sds((rows, hidden)),
        sds((rows, hidden)),
        sds((1, hidden), F32),
        sds((1, width), F32),
    ]
    messages = message_shapes(size // 2, width, direct)
    return launch(
        body,
        operands_of(args),
        [pl.BlockSpec(memory_space=pltpu.SMEM)]
        + [whole_of(piece.shape) for piece in pieces]
        + [cot.spec(), pl.BlockSpec(memory_space=pl.ANY), whole_of(up_bias.shape)]
        + [pl.BlockSpec(memory_space=pl.ANY)] * (1 + len(earlier)),
        outs + [sds((count,) + message)] * 4 + messages,
        [whole_of(item.shape) for item in outs]
        + [pl.BlockSpec((1,) + message, lambda i: (index, 0, 0, 0))] * 4
        + [whole_of(item.shape) for item in messages],
        [
            pltpu.VMEM((width, hidden), BF),
            pltpu.VMEM((hidden, width), BF),
            pltpu.VMEM((rows, width), BF),
            pltpu.SemaphoreType.DMA((2, blocks)),
        ],
        50 << 20,
        cost(8 * rows * width * hidden, 4 * width * hidden + 20 * rows * width),
        "feed_forward",
        after,
        grid=(1,),
        aliases={first + number: 5 + number for number in range(len(earlier))},
    )


def second_norm_back(sums, resid, cot_mine, gain, direct, after=()):
    size, width = resid.shape
    count = len(sums)

    def body(*rest):
        refs, (resid_ref, cot_ref, gain_ref) = rest[:count], rest[count : count + 3]
        grad_ref, gain_out, shift_out, *outs = rest[count + 3 :]
        back, gain_sum, shift_sum = norm_back(resid_ref[...], gain_ref[...], total_of(refs))
        grad = back + cot_ref[...].astype(F32)
        grad_ref[...] = grad
        emit_shard(grad.astype(BF), outs)
        gain_out[...] = gain_sum
        shift_out[...] = shift_sum

    return run_kernel(
        body,
        [sds((size, width), F32)]
        + [sds((1, width), F32)] * 2
        + shard_shapes(size, width, direct),
        list(sums) + [resid, cot_mine, gain],
        name="second_norm_back",
        limit=10,
        after=after,
    )


def first_norm_back(sums, x_mine, grad_resids, gain, after=()):
    count = len(x_mine)
    size, width = grad_resids[0].shape

    def body(*rest):
        refs, rest = rest[:6], rest[6:]
        x_refs, grad_refs, gain_ref = rest[:count], rest[count : 2 * count], rest[2 * count]
        gain_out, shift_out, *outs = rest[2 * count + 1 :]
        for index in range(count):
            back, gain_sum, shift_sum = norm_back(
                x_refs[index][...].astype(F32),
                gain_ref[...],
                total_of([ref.at[index] for ref in refs]),
            )
            emit_shard(
                (back + grad_refs[index][...]).astype(BF), [ref.at[index] for ref in outs]
            )
            gain_out[...] = gain_sum if index == 0 else gain_out[...] + gain_sum
            shift_out[...] = shift_sum if index == 0 else shift_out[...] + shift_sum

    return run_kernel(
        body,
        [sds((1, width), F32)] * 2
        + [sds((count,) + item.shape) for item in shard_shapes(size, width)],
        list(sums) + list(x_mine) + list(grad_resids) + [gain],
        name="first_norm_back",
        limit=10,
        after=after,
    )


def finish_outputs(sums, resids, bias, after=()):
    size, width = resids[0].shape
    half = size // 2
    count = len(resids)

    def body(*rest):
        refs, resid_refs, bias_ref = rest[:6], rest[6 : 6 + count], rest[6 + count]
        low_ref, high_ref = rest[7 + count :]
        for index in range(count):
            ours = [ref.at[index] for ref in refs]
            value = (resid_refs[index][...] + total_of(ours) + bias_ref[...]).astype(BF)
            low_ref[index] = value[:half]
            high_ref[index] = value[half:]

    return run_kernel(
        body,
        [sds((count, half, width))] * 2,
        list(sums) + list(resids) + [bias],
        after=after,
        name="finish_outputs",
        limit=8,
    )


def assemble_outputs(tp_here, pieces, dtype, after=()):
    count, half, width = pieces[0].shape
    size = 2 * half
    rows = 4 * size

    def block_of(shape):
        return pl.BlockSpec((1,) + shape[1:], lambda i, n=len(shape) - 1: (i,) + (0,) * n)

    def body(tp_ref, *rest):
        refs, out_ref = rest[:6], rest[6]

        def store(place, value):
            out_ref[0, place, :] = value.astype(dtype)

        place_gathered(store, tp_ref[0], [ref.at[0] for ref in refs], size)

    results, done = launch(
        body,
        [tp_here] + list(pieces),
        [pl.BlockSpec(memory_space=pltpu.SMEM)] + [block_of(piece.shape) for piece in pieces],
        [HBM((count, rows, width), dtype)],
        [block_of((count, rows, width))],
        (),
        24 << 20,
        cost(0, count * rows * width * 6),
        "assemble_outputs",
        after,
        grid=(count,),
    )
    return results[0], done


def widen(part, turned, after=()):
    rows, wide = part.shape

    def body(part_ref, out_ref):
        value = part_ref[...].astype(F32)
        out_ref[...] = value.T if turned else value

    shape = (wide, rows) if turned else (rows, wide)
    return run_kernel(body, [sds(shape, F32)], [part], after=after, name="widen", limit=6)


def widen_last(part, inner, after=()):
    rows, _ = part.shape

    def body(part_ref, proj_ref, mixer_ref):
        for number in range(3):
            place = slice(number * inner, (number + 1) * inner)
            proj_ref[number] = part_ref[:, place].astype(F32)
        mixer_ref[...] = part_ref[:, 3 * inner :].astype(F32).T

    return run_kernel(
        body,
        [sds((3, rows, inner), F32), sds((inner, rows), F32)],
        [part],
        after=after,
        name="widen",
        limit=6,
    )


def heads_back(here, tp_here, pieces, weight, tok_len, after=()):
    inner, width = weight.shape
    heads = inner // HD
    count = len(pieces)
    size = pieces[0].shape[0] * (1 if count == 4 else 2)
    rows = 4 * size

    def body(here_ref, tp_ref, *rest):
        refs, weight_ref, rest = rest[:count], rest[count], rest[count + 1 :]
        mix_ref, sum_ref, outs, held = rest[0], rest[1], rest[2:7], rest[7]

        def store(place, value):
            mix_ref[place, :] = value

        place_gathered(store, tp_ref[0], refs, size)
        sum_ref[...] = jnp.sum(mix_ref[...].astype(F32), axis=0, keepdims=True)
        value = dot_nt(mix_ref[...], weight_ref[...]).astype(BF)
        for head in range(heads):
            held[head] = value[:, head * HD : (head + 1) * HD]

        def load(unit_id):
            return held[unit_id % heads, rows_at(unit_id // heads * tok_len, tok_len), :]

        emit_exchange(load, here_ref[0], outs)

    return run_kernel(
        body,
        [sds((rows, width)), sds((1, width), F32)] + exchange_shapes(tok_len, HD),
        [here, tp_here] + list(pieces) + [weight],
        flops=2 * rows * inner * width,
        scratch=[pltpu.VMEM((heads, rows, HD), BF)],
        after=after,
        name="heads_back",
        limit=8,
    )


def project_back(here, tp_here, received, weight, after=()):
    count, tok_len, _ = received[0].shape
    _, width, inner = weight.shape
    heads = inner // HD
    rows = 2 * received[-1].shape[1] * tok_len // heads
    size = rows // 4

    def body(here_ref, tp_ref, *rest):
        refs, weight_ref, rest = rest[:5], rest[5], rest[6:]
        proj_refs, sum_ref, outs, held = rest[:count], rest[count], rest[-5:-1], rest[-1]
        for index, proj_ref in enumerate(proj_refs):
            for unit_id, value in exchanged([ref.at[index] for ref in refs], here_ref[0]):
                place = rows_at(unit_id // heads * tok_len, tok_len)
                for part in range(3):
                    column = pl.multiple_of(part * inner + unit_id % heads * HD, HD)
                    proj_ref[place, pl.ds(column, HD)] = value[:, part * HD : (part + 1) * HD]
            part_sum = jnp.sum(proj_ref[...].astype(F32), axis=0, keepdims=True)
            sum_ref[...] = part_sum if index == 0 else sum_ref[...] + part_sum
            for start in range(0, width, 512):
                value = dot_nt(proj_ref[:, :inner], weight_ref[0, start : start + 512])
                for part in range(1, 3):
                    value += dot_nt(
                        proj_ref[:, part * inner : (part + 1) * inner],
                        weight_ref[part, start : start + 512],
                    )
                held[:, start : start + 512] = value.astype(BF)
            emit_messages(
                lambda place: held[place, :], tp_ref[0], [ref.at[index] for ref in outs], size
            )

    return run_kernel(
        body,
        [sds((rows, 3 * inner))] * count
        + [sds((1, 3 * inner), F32)]
        + [sds((count,) + item.shape) for item in message_shapes(size // 2, width)],
        [here, tp_here] + list(received) + [weight],
        flops=6 * count * rows * inner * width,
        scratch=[pltpu.VMEM((rows, width), BF)],
        name="project_back",
        limit=10,
        after=after,
    )


def weight_grad(groups, step=512, after=()):
    count = len(groups[0][0])
    rows, tall = groups[0][0][0].shape
    widths = [rights[0].shape[1] for _, rights in groups]
    step = min(step, tall)

    def body(*refs):
        out_ref = refs[-1]
        start = 0
        for place, wide in enumerate(widths):
            ours = refs[2 * count * place : 2 * count * (place + 1)]
            value = dot_tn(ours[0][...], ours[count][...])
            for number in range(1, count):
                value += dot_tn(ours[number][...], ours[count + number][...])
            out_ref[:, start : start + wide] = value.astype(BF)
            start += wide

    in_specs = []
    args = []
    for (lefts, rights), wide in zip(groups, widths):
        for item in lefts:
            if isinstance(item, Part):
                in_specs.append(
                    pl.BlockSpec((None, rows, step), lambda i, k=item.index: (k, 0, i))
                )
            else:
                in_specs.append(pl.BlockSpec((rows, step), lambda i: (0, i)))
        in_specs += [pl.BlockSpec((rows, wide), lambda i: (0, 0))] * count
        args += list(lefts) + list(rights)
    total = sum(widths)
    results, done = launch(
        body,
        operands_of(args),
        in_specs,
        [HBM((tall, total), BF)],
        [pl.BlockSpec((step, total), lambda i: (i, 0))],
        (),
        30 << 20,
        cost(
            2 * count * rows * tall * total,
            2 * (count * rows * (tall * len(groups) + total) + tall * total),
        ),
        "weight_grad",
        after,
        grid=(tall // step,),
    )
    return results[0], done


def small_sums(values):
    here = lax.axis_index("ctx")
    step = values.shape[0] // 2
    while step:
        pair = values.reshape((2, step) + values.shape[1:])
        bit = (here // step) % 2
        keep = lax.dynamic_index_in_dim(pair, bit, 0, False)
        send = lax.dynamic_index_in_dim(pair, 1 - bit, 0, False)
        values = keep + xor_permute(send, "ctx", step)
        step //= 2
    return values[0]


def per_device_exchanged(
    inputs,
    segments,
    keep_mask,
    first_gain,
    first_shift,
    proj_weight,
    proj_bias,
    mixer_weight,
    mixer_bias,
    second_gain,
    second_shift,
    up_weight,
    up_bias,
    down_weight,
    down_bias,
    out_cotangent,
):
    ctx_count = lax.axis_size("ctx")
    micro_count, seq_count, tok_len, width = inputs.shape
    inner = proj_bias.shape[1]
    heads = inner // HD
    rows = seq_count * tok_len
    here = lax.axis_index("ctx").astype(jnp.int32).reshape(1)
    tp_here = lax.axis_index("tp").astype(jnp.int32).reshape(1)
    weight_three = jnp.transpose(proj_weight, (1, 0, 2))
    bias_three = jnp.stack([proj_bias[0], jnp.zeros_like(proj_bias[0]), proj_bias[1]])
    x_all = inputs.reshape(micro_count, rows, width)
    cot_all = out_cotangent.reshape(micro_count, rows, width)
    key_rows = jnp.where(keep_mask > 0, segments, -1)[:, :, None, :]
    gain_one, shift_one = first_gain[None], first_shift[None]
    gain_two, shift_two = second_gain[None], second_shift[None]
    mix_bias, low_bias, high_bias = mixer_bias[None], down_bias[None], up_bias[None]
    micro = range(micro_count)

    key_rows = [key_rows[index] for index in micro]
    seg_rows = [segments[index][:, None, :] for index in micro]
    cots = [Part(cot_all, index) for index in micro]
    size = rows // lax.axis_size("tp")
    start = tp_here[0] * size
    x_mine = [lax.dynamic_slice(x_all, (index, start, 0), (1, size, width))[0] for index in micro]
    cot_mine = [
        lax.dynamic_slice(cot_all, (index, start, 0), (1, size, width))[0] for index in micro
    ]

    def scattered(part):
        return lax.psum_scatter(part, "ctx", scatter_dimension=0, tiled=True)

    norm_one, received, lses, heads_low, resids = [], [], [], [], []

    def project_micro(index, done):
        (normed, *sent), done = project(
            here, x_all, index, gain_one, shift_one, weight_three, bias_three, tok_len, after=done
        )
        norm_one.append(normed)
        return exchange_chips(*sent), done

    def attend_micro(index, got, done):
        received.append(got)
        (*sent, lse), done = attention(
            here, got, seg_rows[index], key_rows[index], heads, after=done
        )
        lses.append(lse)
        return exchange_chips(*sent), done

    def mix_micro(got, direct, done):
        (mixed, *messages), done = mix_heads(
            here, tp_here, got, mixer_weight, heads, direct, after=done
        )
        heads_low.append(mixed)
        return messages, done

    def norm_micro(index, sums, direct, done):
        (resid, *shard), done = second_norm(
            sums, x_mine[index], mix_bias, gain_two, shift_two, direct, after=done
        )
        resids.append(resid)
        return shard if direct else gather_first(shard), done

    norm_two, acts, grad_pres, up_sums, cot_sums = [], [], [], [], []

    def feed_micro(index, pieces, feeds, done):
        (normed, act, grad_pre, up_sum, cot_sum, *messages), done = feed_forward(
            tp_here,
            pieces,
            cots[index],
            up_weight,
            high_bias,
            down_weight,
            feeds,
            index,
            micro_count,
            True,
            after=done,
        )
        norm_two.append(normed)
        acts.append(act)
        grad_pres.append(grad_pre)
        up_sums.append(up_sum)
        cot_sums.append(cot_sum)
        return messages[:4], reduce_direct(messages[4:]), done

    grad_resids, gain_twos, shift_twos = [], [], []
    grad_mixes, mix_sums, states = [], [], []

    def norm_back_micro(index, sums, done):
        (grad_resid, gain_sum, shift_sum, *shard), done = second_norm_back(
            sums, resids[index], cot_mine[index], gain_two, False, after=done
        )
        grad_resids.append(grad_resid)
        gain_twos.append(gain_sum)
        shift_twos.append(shift_sum)
        return gather_first(shard), done

    def heads_back_micro(index, pieces, done):
        (grad_mix, mix_sum, *sent), done = heads_back(
            here, tp_here, pieces, mixer_weight, tok_len, after=done
        )
        grad_mixes.append(grad_mix)
        mix_sums.append(mix_sum)
        states.append(exchange_chips(*sent))
        return done

    def attend_back_micro(index, got, earlier, done):
        return attention_back(
            here,
            received[index],
            got,
            seg_rows[index],
            key_rows[index],
            lses[index],
            heads,
            earlier,
            index,
            micro_count,
            after=done,
        )

    state_a, done = project_micro(0, ())
    state_b, done = project_micro(1, done)
    got, done = exchange_cores(state_a, done)
    state_a, done = attend_micro(0, got, done)
    got, done = exchange_cores(state_b, done)
    state_b, done = attend_micro(1, got, done)
    got, done = exchange_cores(state_a, done)
    messages, done = mix_micro(got, False, done)
    sums_a, done = reduce_second(reduce_first(messages), done)
    state_a, done = norm_micro(0, sums_a, False, done)
    got, done = exchange_cores(state_b, done)
    messages, done = mix_micro(got, False, done)
    state_b = reduce_first(messages)
    pieces_a, done = gather_second(state_a, done)
    sums_b, done = reduce_second(state_b, done)
    state_b, done = norm_micro(1, sums_b, True, done)
    pieces_b = gather_direct(state_b[0])
    feeds, sums_a, done = feed_micro(0, pieces_a, [], done)
    feeds, sums_b, done = feed_micro(1, pieces_b, feeds, done)
    state_a, done = norm_back_micro(0, sums_a, done)
    down_part, done = weight_grad([(cots, acts)], after=done)
    pieces_a, done = gather_second(state_a, done)
    (down_part,), done = held_until([down_part], done)
    down_grad = scattered(down_part)
    up_part, done = weight_grad([(norm_two, grad_pres)], after=done)
    done = heads_back_micro(0, pieces_a, done)
    state_b, done = norm_back_micro(1, sums_b, done)
    got_a, done = exchange_cores(states[0], done)
    pieces_b, done = gather_second(state_b, done)
    done = heads_back_micro(1, pieces_b, done)
    feeds, done = held_until(feeds, done)
    state_feed = reduce_first(feeds)
    sent, done = attend_back_micro(0, got_a, [], done)
    got_b, done = exchange_cores(states[1], done)
    sums_feed, done = reduce_second(state_feed, done)
    sent, done = attend_back_micro(1, got_b, sent, done)
    state_back = exchange_chips(*sent)
    halves, done = finish_outputs(sums_feed, resids, low_bias, after=done)
    state_out = gather_first(halves)
    got, done = exchange_cores(state_back, done)
    (up_part,), done = held_until([up_part], done)
    up_grad = scattered(up_part)
    (*grad_projs, proj_sum, first, second, third, fourth), done = project_back(
        here, tp_here, got, weight_three, after=done
    )
    state_one = reduce_first((first, second, third, fourth))
    last_part, done = weight_grad(
        [(norm_one, grad_projs), (grad_mixes, heads_low)], after=done
    )
    pieces_out, done = gather_second(state_out, done)
    (last_part,), done = held_until([last_part], done)
    last_grad = scattered(last_part)
    sums_one, done = reduce_second(state_one, done)
    (gain_sum, shift_sum, *halves), done = first_norm_back(
        sums_one, x_mine, grad_resids, gain_one, after=done
    )
    outputs, done = assemble_outputs(tp_here, pieces_out, BF, after=done)
    gain_ones, shift_ones, proj_sums = [gain_sum], [shift_sum], [proj_sum]
    pieces_in, done = gather_second(gather_first(halves), done)
    input_grad, done = assemble_outputs(tp_here, pieces_in, F32, after=done)
    (down_grad,), done = widen(down_grad, True, after=done)
    (up_grad,), done = widen(up_grad, False, after=done)
    (proj_grad, mixer_grad), done = widen_last(last_grad, inner, after=done)
    proj_grad = jnp.transpose(proj_grad, (1, 0, 2))

    def over_micro(items):
        return sum(items[1:], items[0]).reshape(ctx_count, -1)

    proj_sum = sum(proj_sums[1:], proj_sums[0]).reshape(3, ctx_count, -1)
    pair_sum = jnp.concatenate([proj_sum[0], proj_sum[2]], axis=1)
    share = width // ctx_count
    pair_sum = jnp.pad(pair_sum, ((0, 0), (0, share - pair_sum.shape[1])))
    kinds = [
        over_micro(gain_ones),
        over_micro(shift_ones),
        over_micro(gain_twos),
        over_micro(shift_twos),
        over_micro(mix_sums),
        over_micro(cot_sums),
        over_micro(up_sums),
        pair_sum,
    ]
    small = small_sums(jnp.stack(kinds, axis=1))
    norms = small[:4]
    for step in (1, 2):
        norms = norms + xor_permute(norms, "tp", step)
    proj_bias_grad = small[7, : 2 * inner // ctx_count].reshape(2, -1)
    return (
        outputs.reshape(inputs.shape),
        input_grad.reshape(inputs.shape),
        norms[0],
        norms[1],
        proj_grad,
        proj_bias_grad,
        mixer_grad,
        small[4],
        norms[2],
        norms[3],
        up_grad,
        small[6],
        down_grad,
        small[5],
    )


def plan_for(mesh):
    sizes = dict(mesh.shape)

    def chosen(*args):
        micro, seq_count, _, width = args[0].shape
        units = seq_count * args[6].shape[1] // HD
        fits = sizes["ctx"] == 8 and sizes["tp"] == 4 and units == sizes["ctx"]
        fits = fits and args[12].shape[0] == width and micro == 2
        return (per_device_exchanged if fits else per_device)(*args)

    return chosen


def solution(mesh):
    in_specs = (
        P(None, None, "ctx", None),
        P(),
        P(),
        P(),
        P(),
        P(None, None, "tp"),
        P(None, "tp"),
        P("tp", None),
        P(),
        P(),
        P(),
        P(None, "tp"),
        P("tp"),
        P("tp", None),
        P(),
        P(None, None, "ctx", None),
    )
    out_specs = (
        P(None, None, "ctx", None),
        P(None, None, "ctx", None),
        P("ctx"),
        P("ctx"),
        P("ctx", None, "tp"),
        P(None, ("tp", "ctx")),
        P("tp", "ctx"),
        P("ctx"),
        P("ctx"),
        P("ctx"),
        P("ctx", "tp"),
        P(("tp", "ctx")),
        P("tp", "ctx"),
        P("ctx"),
    )
    return jax.shard_map(
        plan_for(mesh), mesh=mesh, in_specs=in_specs, out_specs=out_specs, check_vma=False
    )
```

```python
import math

import jax
import jax.numpy as jnp
from jax import lax
from jax.experimental import pallas as pl
from jax.experimental.pallas import tpu as pltpu
from jax.sharding import PartitionSpec as P

HD = 128


def storage_order(values, part_count):
    leading = values.shape[:-1]
    blocks = values.reshape(leading + (2 * part_count, -1))
    front_half = blocks[..., :part_count, :]
    back_half = jnp.flip(blocks[..., part_count:, :], axis=-2)
    return jnp.stack([front_half, back_half], axis=-2).reshape(leading + (-1,))


def layer_norm(values, norm_gain, norm_shift):
    center = values - jnp.mean(values, axis=-1, keepdims=True)
    spread = jnp.mean(center * center, axis=-1, keepdims=True)
    return center * lax.rsqrt(spread + 1e-05) * norm_gain + norm_shift


def gelu_exact(values):
    return jax.nn.gelu(values, approximate=False)


def split_heads(rows, heads_here):
    return rows.reshape(rows.shape[0], rows.shape[1], heads_here, -1)


def scores_of(queries, key_all, allowed, heads_here, scaler):
    raw = (
        jnp.einsum(
            "sqhd,skhd->shqk",
            split_heads(queries, heads_here),
            split_heads(key_all, heads_here),
            preferred_element_type=jnp.float32,
        )
        * scaler
    )
    return jnp.where(allowed[:, None], raw, -1000000000.0)


def attend(queries, key_all, value_all, allowed, heads_here, scaler):
    masked = scores_of(queries, key_all, allowed, heads_here, scaler)
    top = jnp.max(masked, axis=-1, keepdims=True)
    raised = jnp.exp(masked - top)
    totals = jnp.sum(raised, axis=-1, keepdims=True)
    probs = raised / totals
    mixed = jnp.einsum(
        "shqk,skhd->sqhd",
        probs.astype(jnp.bfloat16),
        split_heads(value_all, heads_here),
        preferred_element_type=jnp.float32,
    )
    return (mixed.reshape(queries.shape), top + jnp.log(totals))


def attend_back(queries, key_all, value_all, allowed, log_total, grad_heads, heads_here, scaler):
    masked = scores_of(queries, key_all, allowed, heads_here, scaler)
    probs = jnp.exp(masked - log_total)
    grad_four = split_heads(grad_heads, heads_here)
    grad_value = jnp.einsum(
        "shqk,sqhd->skhd", probs.astype(jnp.bfloat16), grad_four, preferred_element_type=jnp.float32
    )
    grad_probs = jnp.einsum(
        "sqhd,skhd->shqk",
        grad_four,
        split_heads(value_all, heads_here),
        preferred_element_type=jnp.float32,
    )
    inner_sum = jnp.sum(probs * grad_probs, axis=-1, keepdims=True)
    grad_scores = (probs * (grad_probs - inner_sum)).astype(jnp.bfloat16)
    grad_query = (
        jnp.einsum(
            "shqk,skhd->sqhd",
            grad_scores,
            split_heads(key_all, heads_here),
            preferred_element_type=jnp.float32,
        )
        * scaler
    )
    grad_key = (
        jnp.einsum(
            "shqk,sqhd->skhd",
            grad_scores,
            split_heads(queries, heads_here),
            preferred_element_type=jnp.float32,
        )
        * scaler
    )
    return (
        grad_query.reshape(queries.shape),
        grad_key.reshape(key_all.shape),
        grad_value.reshape(value_all.shape),
    )


def reduce_grads(grads):
    return (
        lax.psum_scatter(
            grads[0].astype(jnp.bfloat16), "ctx", scatter_dimension=0, tiled=True
        ).astype(jnp.float32),
        lax.psum_scatter(
            grads[1].astype(jnp.bfloat16), "ctx", scatter_dimension=0, tiled=True
        ).astype(jnp.float32),
        lax.psum_scatter(
            grads[2].astype(jnp.bfloat16), "ctx", scatter_dimension=0, tiled=True
        ).astype(jnp.float32),
        lax.psum_scatter(
            grads[3].astype(jnp.bfloat16), "ctx", scatter_dimension=1, tiled=True
        ).astype(jnp.float32),
        lax.psum_scatter(
            grads[4].astype(jnp.bfloat16), "ctx", scatter_dimension=1, tiled=True
        ).astype(jnp.float32),
        lax.psum_scatter(
            grads[5].astype(jnp.bfloat16), "ctx", scatter_dimension=0, tiled=True
        ).astype(jnp.float32),
        lax.psum_scatter(
            grads[6].astype(jnp.bfloat16), "ctx", scatter_dimension=0, tiled=True
        ).astype(jnp.float32),
        lax.psum_scatter(
            grads[7].astype(jnp.bfloat16), "ctx", scatter_dimension=0, tiled=True
        ).astype(jnp.float32),
        lax.psum_scatter(
            grads[8].astype(jnp.bfloat16), "ctx", scatter_dimension=0, tiled=True
        ).astype(jnp.float32),
        lax.psum_scatter(
            grads[9].astype(jnp.bfloat16), "ctx", scatter_dimension=0, tiled=True
        ).astype(jnp.float32),
        lax.psum_scatter(
            grads[10].astype(jnp.bfloat16), "ctx", scatter_dimension=1, tiled=True
        ).astype(jnp.float32),
        lax.psum_scatter(
            grads[11].astype(jnp.bfloat16), "ctx", scatter_dimension=0, tiled=True
        ).astype(jnp.float32),
    )


def per_device(
    inputs,
    segments,
    keep_mask,
    first_gain,
    first_shift,
    proj_weight,
    proj_bias,
    mixer_weight,
    mixer_bias,
    second_gain,
    second_shift,
    up_weight,
    up_bias,
    down_weight,
    down_bias,
    out_cotangent,
):
    ctx_count = lax.axis_size("ctx")
    micro_count, seq_count, tok_len, model_width = inputs.shape
    inner_width = proj_bias.shape[1]
    heads_here = inner_width // HD
    scaler = 1.0 / math.sqrt(HD)
    seq_len = tok_len * ctx_count
    places = storage_order(jnp.arange(seq_len, dtype=jnp.int32), ctx_count)
    offset = lax.axis_index("ctx") * tok_len
    my_places = lax.dynamic_slice_in_dim(places, offset, tok_len, 0)
    seg_store = storage_order(segments, ctx_count)
    keep_store = storage_order(keep_mask, ctx_count)
    proj_flat = proj_weight.reshape(model_width, 3 * inner_width)
    bias_three = jnp.stack([proj_bias[0], jnp.zeros_like(proj_bias[0]), proj_bias[1]])
    causal = places[None, :] <= my_places[:, None]
    itself = places[None, :] == my_places[:, None]
    shaped_like = (
        first_gain,
        first_shift,
        proj_weight,
        proj_bias,
        mixer_weight,
        mixer_bias,
        second_gain,
        second_shift,
        up_weight,
        up_bias,
        down_weight,
        down_bias,
    )
    running = tuple((jnp.zeros(item.shape, jnp.float32) for item in shaped_like))
    out_list = []
    grad_list = []
    for micro_index in range(micro_count):
        x_now = inputs[micro_index].astype(jnp.float32)
        seg_keys = seg_store[micro_index]
        seg_mine = lax.dynamic_slice_in_dim(seg_keys, offset, tok_len, 1)
        visible = (keep_store[micro_index] > 0)[:, None, :] | itself[None]
        allowed = causal[None] & (seg_keys[:, None, :] == seg_mine[:, :, None]) & visible
        normed_one = layer_norm(x_now, first_gain, first_shift).astype(jnp.bfloat16)
        projected = jnp.einsum(
            "std,dc->stc", normed_one, proj_flat, preferred_element_type=jnp.float32
        )
        projected = (projected.reshape(seq_count, tok_len, 3, inner_width) + bias_three).astype(
            jnp.bfloat16
        )
        queries = projected[:, :, 0]
        key_here = projected[:, :, 1]
        value_here = projected[:, :, 2]
        key_all, value_all = (
            lax.all_gather(key_here, "ctx", axis=1, tiled=True),
            lax.all_gather(value_here, "ctx", axis=1, tiled=True),
        )
        heads_out, log_total = attend(queries, key_all, value_all, allowed, heads_here, scaler)
        heads_low = heads_out.astype(jnp.bfloat16)
        mixed_part = jnp.einsum(
            "stn,nd->std", heads_low, mixer_weight, preferred_element_type=jnp.float32
        )
        resid = (
            x_now + lax.psum(mixed_part.astype(jnp.bfloat16), "tp").astype(jnp.float32) + mixer_bias
        )
        normed_two = layer_norm(resid, second_gain, second_shift).astype(jnp.bfloat16)
        pre_act = (
            jnp.einsum("std,df->stf", normed_two, up_weight, preferred_element_type=jnp.float32)
            + up_bias
        )
        act_low = gelu_exact(pre_act).astype(jnp.bfloat16)
        feed_part = jnp.einsum(
            "stf,fd->std", act_low, down_weight, preferred_element_type=jnp.float32
        )
        feed = lax.psum(feed_part.astype(jnp.bfloat16), "tp").astype(jnp.float32) + down_bias
        out_list.append((resid + feed).astype(jnp.bfloat16))
        cot_low = out_cotangent[micro_index]
        cot_full = cot_low.astype(jnp.float32)
        down_bias_part = jnp.sum(cot_full, axis=(0, 1))
        down_part = jnp.einsum("stf,std->fd", act_low, cot_low, preferred_element_type=jnp.float32)
        grad_act = jnp.einsum(
            "std,fd->stf", cot_low, down_weight, preferred_element_type=jnp.float32
        )
        grad_pre = jax.vjp(gelu_exact, pre_act)[1](grad_act)[0].astype(jnp.bfloat16)
        up_part = jnp.einsum(
            "std,stf->df", normed_two, grad_pre, preferred_element_type=jnp.float32
        )
        up_bias_part = jnp.sum(grad_pre.astype(jnp.float32), axis=(0, 1))
        grad_two_part = jnp.einsum(
            "stf,df->std", grad_pre, up_weight, preferred_element_type=jnp.float32
        )
        grad_two = lax.psum(grad_two_part.astype(jnp.bfloat16), "tp").astype(jnp.float32)
        resid_part, second_gain_part, second_shift_part = jax.vjp(
            layer_norm, resid, second_gain, second_shift
        )[1](grad_two)
        grad_resid = cot_full + resid_part
        grad_mix = grad_resid.astype(jnp.bfloat16)
        mixer_bias_part = jnp.sum(grad_mix.astype(jnp.float32), axis=(0, 1))
        mixer_part = jnp.einsum(
            "stn,std->nd", heads_low, grad_mix, preferred_element_type=jnp.float32
        )
        grad_heads = jnp.einsum(
            "std,nd->stn", grad_mix, mixer_weight, preferred_element_type=jnp.float32
        ).astype(jnp.bfloat16)
        key_back, value_back = (key_all, value_all)
        grad_query, grad_key, grad_value = attend_back(
            queries, key_back, value_back, allowed, log_total, grad_heads, heads_here, scaler
        )
        key_share, value_share = (
            lax.psum_scatter(
                grad_key.astype(jnp.bfloat16), "ctx", scatter_dimension=1, tiled=True
            ).astype(jnp.float32),
            lax.psum_scatter(
                grad_value.astype(jnp.bfloat16), "ctx", scatter_dimension=1, tiled=True
            ).astype(jnp.float32),
        )
        grad_proj = jnp.stack([grad_query, key_share, value_share], axis=2).astype(jnp.bfloat16)
        proj_part = jnp.einsum(
            "std,stcn->dcn", normed_one, grad_proj, preferred_element_type=jnp.float32
        )
        proj_sums = jnp.sum(grad_proj.astype(jnp.float32), axis=(0, 1))
        proj_bias_part = jnp.stack([proj_sums[0], proj_sums[2]])
        grad_one_part = jnp.einsum(
            "stc,dc->std",
            grad_proj.reshape(seq_count, tok_len, 3 * inner_width),
            proj_flat,
            preferred_element_type=jnp.float32,
        )
        grad_one = lax.psum(grad_one_part.astype(jnp.bfloat16), "tp").astype(jnp.float32)
        input_part, first_gain_part, first_shift_part = jax.vjp(
            layer_norm, x_now, first_gain, first_shift
        )[1](grad_one)
        grad_list.append(grad_resid + input_part)
        batch_grads = (
            first_gain_part,
            first_shift_part,
            proj_part,
            proj_bias_part,
            mixer_part,
            mixer_bias_part,
            second_gain_part,
            second_shift_part,
            up_part,
            up_bias_part,
            down_part,
            down_bias_part,
        )
        running = tuple((earlier + adding for earlier, adding in zip(running, batch_grads)))
    final = reduce_grads(running)
    return (
        jnp.stack(out_list),
        jnp.stack(grad_list),
        final[0],
        final[1],
        final[2],
        final[3],
        final[4],
        final[5],
        final[6],
        final[7],
        final[8],
        final[9],
        final[10],
        final[11],
    )


BF = jnp.bfloat16
F32 = jnp.float32
LOG2E = 1.4426950408889634
LOW = -1e30
ORDERS = ((1, 2), (2, 1))
COST_SHARE = 1.0


def xor_permute(values, axis, step):
    count = lax.axis_size(axis)
    return lax.ppermute(values, axis, [(i, i ^ step) for i in range(count)])


def sds(shape, dtype=BF):
    return jax.ShapeDtypeStruct(tuple(shape), dtype)


def cost(flops, moved, exps=0):
    return pl.CostEstimate(
        flops=int(flops * COST_SHARE),
        bytes_accessed=int(moved * COST_SHARE),
        transcendentals=int(exps * COST_SHARE),
    )


HBM = pltpu.MemorySpace.HBM


def launch(
    body,
    args,
    in_specs,
    outs,
    out_specs,
    scratch,
    limit,
    cost,
    name,
    after,
    grid=(),
    aliases=None,
    scalars=(),
):
    first, last = len(after), len(after) + len(args) + len(outs)

    def inner(*refs):
        fixed, refs = refs[: len(scalars)], refs[len(scalars) :]
        body(*fixed, *refs[first:last], *refs[last + 1 :])

    token = pl.BlockSpec(memory_space=HBM)
    *results, done = pl.pallas_call(
        inner,
        grid_spec=pltpu.PrefetchScalarGridSpec(
            num_scalar_prefetch=len(scalars),
            grid=grid,
            in_specs=[token] * first + list(in_specs),
            out_specs=(*out_specs, token),
            scratch_shapes=list(scratch),
        ),
        out_shape=(*outs, sds((8, 128), F32)),
        input_output_aliases={first + key: value for key, value in (aliases or {}).items()},
        compiler_params=pltpu.CompilerParams(vmem_limit_bytes=limit),
        cost_estimate=cost,
        name=name,
    )(*scalars, *after, *args)
    return results, (done,)


class Part:
    def __init__(self, array, index):
        self.array, self.index = array, index
        self.shape, self.dtype = array.shape[1:], array.dtype

    def spec(self):
        index, rest = self.index, (0,) * len(self.shape)
        return pl.BlockSpec((None,) + self.shape, lambda *_: (index,) + rest)


def operands_of(args):
    arrays = [arg.array if isinstance(arg, Part) else arg for arg in args]
    return [
        array if array.dtype == jnp.int32 else pltpu.with_memory_space_constraint(array, HBM)
        for array in arrays
    ]


class Part:
    def __init__(self, array, index):
        self.array, self.index = array, index
        self.shape, self.dtype = array.shape[1:], array.dtype

    def spec(self):
        index, rest = self.index, (0,) * len(self.shape)
        return pl.BlockSpec((None,) + self.shape, lambda *_: (index,) + rest)


def operands_of(args):
    arrays = [arg.array if isinstance(arg, Part) else arg for arg in args]
    return [
        array if array.dtype == jnp.int32 else pltpu.with_memory_space_constraint(array, HBM)
        for array in arrays
    ]


def run_kernel(body, outs, args, flops=0, exps=0, scratch=(), limit=8, name=None, after=(), in_hbm=()):
    specs = []
    moved = 0
    for place, arg in enumerate(args):
        if arg.dtype == jnp.int32 and math.prod(arg.shape) <= 8:
            specs.append(pl.BlockSpec(memory_space=pltpu.SMEM))
        elif place in in_hbm:
            specs.append(pl.BlockSpec(memory_space=HBM))
        else:
            specs.append(pl.BlockSpec(memory_space=pltpu.VMEM))
            moved += math.prod(arg.shape) * arg.dtype.itemsize
    moved += sum(math.prod(o.shape) * o.dtype.itemsize for o in outs)
    kept = [item for item in scratch if item.dtype in (BF, F32)]
    held = moved + sum(math.prod(item.shape) * item.dtype.itemsize for item in kept)
    return launch(
        body,
        args,
        specs,
        outs,
        [pl.BlockSpec(memory_space=pltpu.VMEM) for _ in outs],
        scratch,
        held + (limit << 20),
        cost(flops, moved, exps),
        name,
        after,
    )


def whole_of(shape):
    return pl.BlockSpec(shape, lambda *_, n=len(shape): (0,) * n)


def rows_at(start, count):
    return pl.ds(pl.multiple_of(start, count), count)


def reduce_first(messages):
    return [
        (messages[2 * part + 1], xor_permute(messages[2 * part], "tp", first))
        for part, (first, _) in enumerate(ORDERS)
    ]


def reduce_second(state, after=()):
    middle_shape = state[0][0].shape[:-3] + state[0][0].shape[-2:]

    def body(*refs):
        for part in range(2):
            keep, got = refs[2 * part : 2 * part + 2]
            value = keep[..., 1, :, :].astype(F32) + got[..., 1, :, :].astype(F32)
            refs[4 + part][...] = value.astype(BF)

    middles, done = run_kernel(
        body,
        [sds(middle_shape)] * 2,
        [item for pair in state for item in pair],
        after=after,
        name="reduce_middle",
        limit=3,
    )
    sums = []
    for part, (_, second) in enumerate(ORDERS):
        sums += [*state[part], xor_permute(middles[part], "tp", second)]
    return sums, done


def reduce_direct(messages):
    mine, *sent = messages
    return [mine] + [xor_permute(item, "tp", 1 + step) for step, item in enumerate(sent)]


def gather_first(halves):
    return [
        (halves[part], xor_permute(halves[part], "tp", first))
        for part, (first, _) in enumerate(ORDERS)
    ]


def gather_second(state, after=()):
    half = state[0][0].shape
    pair_shape = half[:-2] + (2,) + half[-2:]

    def body(*refs):
        for part in range(2):
            for place in range(2):
                refs[4 + part][..., place, :, :] = refs[2 * part + place][...]

    pairs, done = run_kernel(
        body,
        [sds(pair_shape)] * 2,
        [item for pair in state for item in pair],
        after=after,
        name="gather_middle",
        limit=3,
    )
    pieces = []
    for part, (_, second) in enumerate(ORDERS):
        pieces += [*state[part], xor_permute(pairs[part], "tp", second)]
    return pieces, done


def gather_direct(mine):
    return [mine] + [xor_permute(mine, "tp", step) for step in (1, 2, 3)]


def total_of(refs):
    if len(refs) == 4:
        return sum([ref[...].astype(F32) for ref in refs[1:]], refs[0][...].astype(F32))
    halves = []
    for part in range(2):
        keep, got, late = refs[3 * part : 3 * part + 3]
        halves.append(
            keep[0].astype(F32) + got[0].astype(F32) + late[...].astype(F32)
        )
    return jnp.concatenate(halves, axis=0)


def place_gathered(store, tp_here, refs, size):
    if len(refs) == 4:
        for step, ref in enumerate(refs):
            store(rows_at((tp_here ^ step) * size, size), ref[...])
        return
    half = size // 2
    for part, (first, second) in enumerate(ORDERS):
        mine, near, far = refs[3 * part : 3 * part + 3]
        parts = ((0, mine[...]), (first, near[...]), (second, far[0]), (first | second, far[1]))
        for step, value in parts:
            store(rows_at((tp_here ^ step) * size + part * half, half), value)


def emit_messages(load, tp_here, refs, size):
    if refs[0].shape[-2] == size:
        for step, ref in enumerate(refs):
            ref[...] = load(rows_at((tp_here ^ step) * size, size))
        return
    half = size // 2
    for part, (first, second) in enumerate(ORDERS):
        send, keep = refs[2 * part], refs[2 * part + 1]
        for ref, steps in ((send, (first, first | second)), (keep, (0, second))):
            for place, step in enumerate(steps):
                ref[place] = load(rows_at((tp_here ^ step) * size + part * half, half))


def emit_shard(value, refs):
    rows = value.shape[0] // len(refs)
    for place, ref in enumerate(refs):
        ref[...] = value[place * rows : (place + 1) * rows]


def shard_shapes(size, width, direct=False):
    return [sds((size, width))] if direct else [sds((size // 2, width))] * 2


def message_shapes(half, width, direct=False):
    return [sds((2 * half, width) if direct else (2, half, width))] * 4


def exchange_chips(local, cross, first, second, third):
    got = [
        xor_permute(item, "ctx", 2 * (place + 1))
        for place, item in enumerate((first, second, third))
    ]
    return [local, cross] + got


def exchange_cores(state, after):
    local, cross, *got = state

    lead = cross.shape[:-2]

    def body(cross_ref, first_ref, second_ref, third_ref, out_ref):
        out_ref[..., 0, :, :] = cross_ref[...]
        for place, ref in enumerate((first_ref, second_ref, third_ref)):
            out_ref[..., place + 1, :, :] = ref[..., 1, :, :]

    (packed,), done = run_kernel(
        body, [sds(lead + (4,) + cross.shape[-2:])], [cross] + got, after=after, limit=2, name="pack"
    )
    return [local] + got + [xor_permute(packed, "ctx", 1)], done


def exchanged(refs, here):
    local, first, second, third, packed = refs
    return (
        (here, local[...]),
        (here ^ 1, packed[0]),
        (here ^ 2, first[0]),
        (here ^ 3, packed[1]),
        (here ^ 4, second[0]),
        (here ^ 5, packed[2]),
        (here ^ 6, third[0]),
        (here ^ 7, packed[3]),
    )


def emit_exchange(load, here, refs):
    local, cross, first, second, third = refs
    local[...] = load(here)
    cross[...] = load(here ^ 1)
    for place, ref in enumerate((first, second, third)):
        other = here ^ (2 * (place + 1))
        ref[0] = load(other)
        ref[1] = load(other ^ 1)


def exchange_shapes(rows, width):
    return [sds((rows, width)), sds((rows, width))] + [sds((2, rows, width))] * 3


def normalized(values):
    center = values - jnp.mean(values, axis=-1, keepdims=True)
    spread = jnp.mean(center * center, axis=-1, keepdims=True)
    root = lax.rsqrt(spread + 1e-05)
    return center * root, root


def norm_back(values, gain, grad):
    unit, root = normalized(values)
    scaled = grad * gain
    back = root * (
        scaled
        - jnp.mean(scaled, axis=-1, keepdims=True)
        - unit * jnp.mean(scaled * unit, axis=-1, keepdims=True)
    )
    gain_sum = jnp.sum(grad * unit, axis=0, keepdims=True)
    shift_sum = jnp.sum(grad, axis=0, keepdims=True)
    return back, gain_sum, shift_sum


def dot(left, right):
    return jnp.dot(left, right, preferred_element_type=F32)


def dot_nt(left, right):
    return lax.dot_general(left, right, (((1,), (1,)), ((), ())), preferred_element_type=F32)


def dot_tn(left, right):
    return lax.dot_general(left, right, (((0,), (0,)), ((), ())), preferred_element_type=F32)


def project(here, x_all, index, gain, shift, weight, bias, tok_len, after=()):
    _, rows, width = x_all.shape
    inner = weight.shape[2]
    heads = inner // HD

    def body(here_ref, x_ref, gain_ref, shift_ref, weight_hbm, bias_ref, *rest):
        norm_ref, outs, (held, weight_ref, x_held, sems) = rest[0], rest[1:6], rest[6:]
        fetch = pltpu.make_async_copy(x_ref.at[index], x_held, sems.at[3])
        fetch.start()
        copies = [
            pltpu.make_async_copy(weight_hbm.at[part], weight_ref.at[part], sems.at[part])
            for part in range(3)
        ]
        for copy in copies:
            copy.start()
        fetch.wait()
        unit, _ = normalized(x_held[...].astype(F32))
        norm_ref[...] = (unit * gain_ref[...] + shift_ref[...]).astype(BF)
        for part in range(3):
            copies[part].wait()
            value = dot(norm_ref[...], weight_ref[part]) + bias_ref[part : part + 1]
            value = value.astype(BF)
            for head in range(heads):
                held[head, :, part * HD : (part + 1) * HD] = value[:, head * HD : (head + 1) * HD]

        def load(unit_id):
            return held[unit_id % heads, rows_at(unit_id // heads * tok_len, tok_len), :]

        emit_exchange(load, here_ref[0], outs)

    return run_kernel(
        body,
        [sds((rows, width))] + exchange_shapes(tok_len, 3 * HD),
        [here, x_all, gain, shift, weight, bias],
        flops=6 * rows * width * inner,
        scratch=[
            pltpu.VMEM((heads, rows, 3 * HD), BF),
            pltpu.VMEM(weight.shape, BF),
            pltpu.VMEM((rows, width), BF),
            pltpu.SemaphoreType.DMA((4,)),
        ],
        name="project",
        limit=14,
        after=after,
        in_hbm=(1, 4),
    )


def rows_of_device(device, block, blocks):
    return (
        rows_at(device * block, block),
        rows_at((blocks - 1 - device) * block, block),
    )


def attention(here, received, seg_row, key_row, heads, after=()):
    tok_len = received[0].shape[0]
    block = tok_len // 2
    seq_len = seg_row.shape[2]
    blocks = seq_len // block
    step = 256
    factor = LOG2E / math.sqrt(HD)

    def body(here_ref, *rest):
        refs, seg_ref, key_ref = rest[:5], rest[5], rest[6]
        outs, lse_ref = rest[7:12], rest[12]
        q_all, k_turned, v_all, mixed = rest[13:]
        me = here_ref[0]
        seq = me // heads
        for device, value in exchanged(refs, me):
            for half, place in enumerate(rows_of_device(device, block, blocks)):
                rows = value[half * block : (half + 1) * block]
                q_all[place] = rows[:, :HD]
                k_turned[:, place] = rows[:, HD : 2 * HD].T
                v_all[place] = rows[:, 2 * HD :]
        for number in range(seq_len // step):
            start, stop = number * step, (number + 1) * step
            segs = as_column(seg_ref[seq, :, start:stop])
            scores = dot(q_all[start:stop], k_turned[:, :stop]) * factor
            scores = masked(scores, segs, key_ref, seq, start, stop)
            top = jnp.max(scores, axis=-1, keepdims=True)
            raised = jnp.exp2(scores - top)
            total = jnp.sum(raised, axis=-1, keepdims=True)
            out = dot(raised.astype(BF), v_all[:stop]) / total
            mixed[start:stop] = out.astype(BF)
            lse_ref[start:stop] = top + jnp.log2(total)

        def load(device):
            return jnp.concatenate(
                [mixed[place] for place in rows_of_device(device, block, blocks)], axis=0
            )

        emit_exchange(load, me, outs)

    return run_kernel(
        body,
        exchange_shapes(tok_len, HD) + [sds((seq_len, 1), F32)],
        [here] + list(received) + [seg_row, key_row],
        flops=2 * 2 * seq_len * seq_len * HD,
        exps=seq_len * seq_len // 2,
        scratch=[
            pltpu.VMEM((seq_len, HD), BF),
            pltpu.VMEM((HD, seq_len), BF),
            pltpu.VMEM((seq_len, HD), BF),
            pltpu.VMEM((seq_len, HD), BF),
        ],
        after=after,
        name="attention",
        limit=16,
    )


def as_column(row):
    return jnp.broadcast_to(row, (128, row.shape[1])).T[:, :1]


def masked(scores, segs, key_ref, seq, start, stop):
    size = stop - start
    row = lax.broadcasted_iota(jnp.int32, (size, size), 0)
    column = lax.broadcasted_iota(jnp.int32, (size, size), 1)
    same = segs == key_ref[seq, :, start:stop]
    seen = (same & (column < row)) | (column == row)
    corner = jnp.where(seen, scores[:, start:], LOW)
    if start == 0:
        return corner
    left = jnp.where(segs == key_ref[seq, :, :start], scores[:, :start], LOW)
    return jnp.concatenate([left, corner], axis=1)


def attention_back(
    here, received, grads, seg_row, key_row, lse, heads, earlier, index, count, after=()
):
    tok_len = received[0].shape[0]
    block = tok_len // 2
    seq_len = seg_row.shape[2]
    blocks = seq_len // block
    step = 256
    scaler = 1.0 / math.sqrt(HD)

    def body(here_ref, *rest):
        refs, grad_refs = rest[:5], rest[5:10]
        seg_ref, key_ref, lse_ref = rest[10:13]
        rest = rest[13 + len(earlier) :]
        outs = [ref.at[0] for ref in rest[:5]]
        q_all, k_all, k_turned, v_turned, g_all, result, dk_turned, dv_turned = rest[5:]
        me = here_ref[0]
        seq = me // heads
        for device, value in exchanged(refs, me):
            for half, place in enumerate(rows_of_device(device, block, blocks)):
                rows = value[half * block : (half + 1) * block]
                q_all[place] = rows[:, :HD]
                k_all[place] = rows[:, HD : 2 * HD]
                k_turned[:, place] = rows[:, HD : 2 * HD].T
                v_turned[:, place] = rows[:, 2 * HD :].T
        for device, value in exchanged(grad_refs, me):
            for half, place in enumerate(rows_of_device(device, block, blocks)):
                g_all[place] = value[half * block : (half + 1) * block]
        last = seq_len // step - 1
        for number in range(last, -1, -1):
            start, stop = number * step, (number + 1) * step
            segs = as_column(seg_ref[seq, :, start:stop])
            query, grad = q_all[start:stop], g_all[start:stop]
            scores = dot(query, k_turned[:, :stop]) * (scaler * LOG2E)
            scores = masked(scores, segs, key_ref, seq, start, stop)
            probs = jnp.exp2(scores - lse_ref[start:stop])
            grad_probs = dot(grad, v_turned[:, :stop])
            inner = jnp.sum(probs * grad_probs, axis=-1, keepdims=True)
            grad_scores = (probs * (grad_probs - inner)).astype(BF)
            dv_part = dot_tn(grad, probs.astype(BF))
            dk_part = dot_tn(query, grad_scores)
            if number == last:
                dv_turned[...] = dv_part
                dk_turned[...] = dk_part
            else:
                dv_turned[:, :stop] += dv_part
                dk_turned[:, :stop] += dk_part
            dq = dot(grad_scores, k_all[:stop]) * scaler
            result[start:stop, :HD] = dq.astype(BF)
        for number in range(last + 1):
            start, stop = number * step, (number + 1) * step
            result[start:stop, HD : 2 * HD] = (dk_turned[:, start:stop] * scaler).T.astype(BF)
            result[start:stop, 2 * HD :] = dv_turned[:, start:stop].T.astype(BF)

        def load(device):
            return jnp.concatenate(
                [result[place] for place in rows_of_device(device, block, blocks)], axis=0
            )

        emit_exchange(load, me, outs)

    shapes = exchange_shapes(tok_len, 3 * HD)
    args = [here, *received, *grads, seg_row, key_row, lse, *earlier]
    first = len(args) - len(earlier)
    return launch(
        body,
        operands_of(args),
        [pl.BlockSpec(memory_space=pltpu.SMEM)]
        + [whole_of(item.shape) for item in args[1:first]]
        + [pl.BlockSpec(memory_space=pl.ANY) for _ in earlier],
        [sds((count,) + item.shape) for item in shapes],
        [
            pl.BlockSpec((1,) + item.shape, lambda i, n=len(item.shape): (index,) + (0,) * n)
            for item in shapes
        ],
        [
            pltpu.VMEM((seq_len, HD), BF),
            pltpu.VMEM((seq_len, HD), BF),
            pltpu.VMEM((HD, seq_len), BF),
            pltpu.VMEM((HD, seq_len), BF),
            pltpu.VMEM((seq_len, HD), BF),
            pltpu.VMEM((seq_len, 3 * HD), BF),
            pltpu.VMEM((HD, seq_len), F32),
            pltpu.VMEM((HD, seq_len), F32),
        ],
        36 << 20,
        cost(5 * seq_len * seq_len * HD, 12 * seq_len * HD),
        "attention_back",
        after,
        grid=(1,),
        aliases={first + number: number for number in range(len(earlier))},
    )


def mix_heads(here, tp_here, received, weight, heads, direct, after=()):
    tok_len = received[0].shape[0]
    inner, width = weight.shape
    rows = len_units(received) * tok_len // heads
    size = rows // 4

    def body(here_ref, tp_ref, *rest):
        refs, weight_ref = rest[:5], rest[5]
        heads_ref, outs, held = rest[6], rest[7:11], rest[11]
        for unit_id, value in exchanged(refs, here_ref[0]):
            column = pl.multiple_of(unit_id % heads * HD, HD)
            heads_ref[rows_at(unit_id // heads * tok_len, tok_len), pl.ds(column, HD)] = value
        for start in range(0, width, 512):
            held[:, start : start + 512] = dot(
                heads_ref[...], weight_ref[:, start : start + 512]
            ).astype(BF)
        emit_messages(lambda place: held[place, :], tp_ref[0], outs, size)

    return run_kernel(
        body,
        [sds((rows, inner))] + message_shapes(size // 2, width, direct),
        [here, tp_here] + list(received) + [weight],
        flops=2 * rows * inner * width,
        scratch=[pltpu.VMEM((rows, width), BF)],
        after=after,
        name="mix_heads",
        limit=6,
    )


def len_units(received):
    return 2 * received[-1].shape[0]


def second_norm(sums, x_mine, mixer_bias, gain, shift, direct, after=()):
    size, width = x_mine.shape
    count = len(sums)

    def body(*rest):
        refs, (x_ref, bias_ref, gain_ref, shift_ref) = rest[:count], rest[count : count + 4]
        resid_ref, outs = rest[count + 4], rest[count + 5 :]
        resid = x_ref[...].astype(F32) + total_of(refs) + bias_ref[...]
        resid_ref[...] = resid
        unit, _ = normalized(resid)
        emit_shard((unit * gain_ref[...] + shift_ref[...]).astype(BF), outs)

    return run_kernel(
        body,
        [sds((size, width), F32)] + shard_shapes(size, width, direct),
        list(sums) + [x_mine, mixer_bias, gain, shift],
        name="second_norm",
        limit=8,
        after=after,
    )


def feed_forward(
    tp_here, pieces, cot, up_weight, up_bias, down_weight, earlier, index, count, direct, after=()
):
    rows, width = cot.shape
    hidden = up_weight.shape[1]
    size = rows // 4
    step = 512
    blocks = hidden // step

    def body(tp_ref, *rest):
        refs, rest = rest[: len(pieces)], rest[len(pieces) :]
        cot_ref, up_hbm, bias_ref, down_hbm = rest[:4]
        rest = rest[4 + len(earlier) :]
        norm_ref, act_ref, pre_ref, sum_ref, cot_sum_ref = rest[:5]
        feed_outs, grad_outs = rest[5:9], rest[9:13]
        up, down, held, sems = rest[13:]

        def part(number):
            return pl.ds(pl.multiple_of(number * step, step), step)

        def copies(number):
            place = part(number)
            return (
                pltpu.make_async_copy(up_hbm.at[:, place], up.at[:, place], sems.at[0, number]),
                pltpu.make_async_copy(down_hbm.at[place, :], down.at[place, :], sems.at[1, number]),
            )

        for number in range(blocks):
            for copy in copies(number):
                copy.start()

        def store(place, value):
            norm_ref[place, :] = value

        place_gathered(store, tp_ref[0], refs, size)
        cot_sum_ref[...] = jnp.sum(cot_ref[...].astype(F32), axis=0, keepdims=True)

        @pl.loop(0, blocks)
        def _(number):
            for copy in copies(number):
                copy.wait()
            place = part(number)
            pre = dot(norm_ref[...], up[:, place]) + bias_ref[:, place]
            grad_act = dot_nt(cot_ref[...], down[place, :])
            spread = 0.5 + 0.5 * lax.erf(pre * math.sqrt(0.5))
            dense = jnp.exp(-0.5 * pre * pre) * (1.0 / math.sqrt(2.0 * math.pi))
            act_ref[:, place] = (pre * spread).astype(BF)
            grad_pre = (grad_act * (spread + pre * dense)).astype(BF)
            pre_ref[:, place] = grad_pre
            sum_ref[:, place] = jnp.sum(grad_pre.astype(F32), axis=0, keepdims=True)

        @pl.loop(0, width // step)
        def _(number):
            place = part(number)
            held[:, place] = dot_nt(pre_ref[...], up[place, :]).astype(BF)

        emit_messages(lambda at: held[at, :], tp_ref[0], grad_outs, size)

        @pl.loop(0, width // step)
        def _(number):
            place = part(number)
            held[:, place] = dot(act_ref[...], down[:, place]).astype(BF)

        emit_messages(lambda at: held[at, :], tp_ref[0], [ref.at[0] for ref in feed_outs], size)

    message = (2, size // 2, width)
    args = [tp_here, *pieces, cot, up_weight, up_bias, down_weight, *earlier]
    first = len(args) - len(earlier)
    outs = [
        sds((rows, width)),
        sds((rows, hidden)),
        sds((rows, hidden)),
        sds((1, hidden), F32),
        sds((1, width), F32),
    ]
    messages = message_shapes(size // 2, width, direct)
    return launch(
        body,
        operands_of(args),
        [pl.BlockSpec(memory_space=pltpu.SMEM)]
        + [whole_of(piece.shape) for piece in pieces]
        + [cot.spec(), pl.BlockSpec(memory_space=pl.ANY), whole_of(up_bias.shape)]
        + [pl.BlockSpec(memory_space=pl.ANY)] * (1 + len(earlier)),
        outs + [sds((count,) + message)] * 4 + messages,
        [whole_of(item.shape) for item in outs]
        + [pl.BlockSpec((1,) + message, lambda i: (index, 0, 0, 0))] * 4
        + [whole_of(item.shape) for item in messages],
        [
            pltpu.VMEM((width, hidden), BF),
            pltpu.VMEM((hidden, width), BF),
            pltpu.VMEM((rows, width), BF),
            pltpu.SemaphoreType.DMA((2, blocks)),
        ],
        50 << 20,
        cost(8 * rows * width * hidden, 4 * width * hidden + 20 * rows * width),
        "feed_forward",
        after,
        grid=(1,),
        aliases={first + number: 5 + number for number in range(len(earlier))},
    )


def second_norm_back(sums, resid, cot_mine, gain, direct, after=()):
    size, width = resid.shape
    count = len(sums)

    def body(*rest):
        refs, (resid_ref, cot_ref, gain_ref) = rest[:count], rest[count : count + 3]
        grad_ref, gain_out, shift_out, *outs = rest[count + 3 :]
        back, gain_sum, shift_sum = norm_back(resid_ref[...], gain_ref[...], total_of(refs))
        grad = back + cot_ref[...].astype(F32)
        grad_ref[...] = grad
        emit_shard(grad.astype(BF), outs)
        gain_out[...] = gain_sum
        shift_out[...] = shift_sum

    return run_kernel(
        body,
        [sds((size, width), F32)]
        + [sds((1, width), F32)] * 2
        + shard_shapes(size, width, direct),
        list(sums) + [resid, cot_mine, gain],
        name="second_norm_back",
        limit=10,
        after=after,
    )


def first_norm_back(sums, x_mine, grad_resids, gain, after=()):
    count = len(x_mine)
    size, width = grad_resids[0].shape

    def body(*rest):
        refs, rest = rest[:6], rest[6:]
        x_refs, grad_refs, gain_ref = rest[:count], rest[count : 2 * count], rest[2 * count]
        gain_out, shift_out, *outs = rest[2 * count + 1 :]
        for index in range(count):
            back, gain_sum, shift_sum = norm_back(
                x_refs[index][...].astype(F32),
                gain_ref[...],
                total_of([ref.at[index] for ref in refs]),
            )
            emit_shard(
                (back + grad_refs[index][...]).astype(BF), [ref.at[index] for ref in outs]
            )
            gain_out[...] = gain_sum if index == 0 else gain_out[...] + gain_sum
            shift_out[...] = shift_sum if index == 0 else shift_out[...] + shift_sum

    return run_kernel(
        body,
        [sds((1, width), F32)] * 2
        + [sds((count,) + item.shape) for item in shard_shapes(size, width)],
        list(sums) + list(x_mine) + list(grad_resids) + [gain],
        name="first_norm_back",
        limit=10,
        after=after,
    )


def finish_outputs(sums, resids, bias, after=()):
    size, width = resids[0].shape
    half = size // 2
    count = len(resids)

    def body(*rest):
        refs, resid_refs, bias_ref = rest[:6], rest[6 : 6 + count], rest[6 + count]
        low_ref, high_ref = rest[7 + count :]
        for index in range(count):
            ours = [ref.at[index] for ref in refs]
            value = (resid_refs[index][...] + total_of(ours) + bias_ref[...]).astype(BF)
            low_ref[index] = value[:half]
            high_ref[index] = value[half:]

    return run_kernel(
        body,
        [sds((count, half, width))] * 2,
        list(sums) + list(resids) + [bias],
        after=after,
        name="finish_outputs",
        limit=8,
    )


def assemble_outputs(tp_here, pieces, dtype, after=()):
    count, half, width = pieces[0].shape
    size = 2 * half
    rows = 4 * size

    def block_of(shape):
        return pl.BlockSpec((1,) + shape[1:], lambda i, n=len(shape) - 1: (i,) + (0,) * n)

    def body(tp_ref, *rest):
        refs, out_ref = rest[:6], rest[6]

        def store(place, value):
            out_ref[0, place, :] = value.astype(dtype)

        place_gathered(store, tp_ref[0], [ref.at[0] for ref in refs], size)

    results, done = launch(
        body,
        [tp_here] + list(pieces),
        [pl.BlockSpec(memory_space=pltpu.SMEM)] + [block_of(piece.shape) for piece in pieces],
        [HBM((count, rows, width), dtype)],
        [block_of((count, rows, width))],
        (),
        24 << 20,
        cost(0, count * rows * width * 6),
        "assemble_outputs",
        after,
        grid=(count,),
    )
    return results[0], done


def widen(part, turned, after=()):
    rows, wide = part.shape

    def body(part_ref, out_ref):
        value = part_ref[...].astype(F32)
        out_ref[...] = value.T if turned else value

    shape = (wide, rows) if turned else (rows, wide)
    return run_kernel(body, [sds(shape, F32)], [part], after=after, name="widen", limit=6)


def widen_last(part, inner, after=()):
    rows, _ = part.shape

    def body(part_ref, proj_ref, mixer_ref):
        for number in range(3):
            place = slice(number * inner, (number + 1) * inner)
            proj_ref[number] = part_ref[:, place].astype(F32)
        mixer_ref[...] = part_ref[:, 3 * inner :].astype(F32).T

    return run_kernel(
        body,
        [sds((3, rows, inner), F32), sds((inner, rows), F32)],
        [part],
        after=after,
        name="widen",
        limit=6,
    )


def heads_back(here, tp_here, pieces, weight, tok_len, after=()):
    inner, width = weight.shape
    heads = inner // HD
    count = len(pieces)
    size = pieces[0].shape[0] * (1 if count == 4 else 2)
    rows = 4 * size

    def body(here_ref, tp_ref, *rest):
        refs, weight_ref, rest = rest[:count], rest[count], rest[count + 1 :]
        mix_ref, sum_ref, outs, held = rest[0], rest[1], rest[2:7], rest[7]

        def store(place, value):
            mix_ref[place, :] = value

        place_gathered(store, tp_ref[0], refs, size)
        sum_ref[...] = jnp.sum(mix_ref[...].astype(F32), axis=0, keepdims=True)
        value = dot_nt(mix_ref[...], weight_ref[...]).astype(BF)
        for head in range(heads):
            held[head] = value[:, head * HD : (head + 1) * HD]

        def load(unit_id):
            return held[unit_id % heads, rows_at(unit_id // heads * tok_len, tok_len), :]

        emit_exchange(load, here_ref[0], outs)

    return run_kernel(
        body,
        [sds((rows, width)), sds((1, width), F32)] + exchange_shapes(tok_len, HD),
        [here, tp_here] + list(pieces) + [weight],
        flops=2 * rows * inner * width,
        scratch=[pltpu.VMEM((heads, rows, HD), BF)],
        after=after,
        name="heads_back",
        limit=8,
    )


def project_back(here, tp_here, received, weight, after=()):
    count, tok_len, _ = received[0].shape
    _, width, inner = weight.shape
    heads = inner // HD
    rows = 2 * received[-1].shape[1] * tok_len // heads
    size = rows // 4

    def body(here_ref, tp_ref, *rest):
        refs, weight_ref, rest = rest[:5], rest[5], rest[6:]
        proj_refs, sum_ref, outs, held = rest[:count], rest[count], rest[-5:-1], rest[-1]
        for index, proj_ref in enumerate(proj_refs):
            for unit_id, value in exchanged([ref.at[index] for ref in refs], here_ref[0]):
                place = rows_at(unit_id // heads * tok_len, tok_len)
                for part in range(3):
                    column = pl.multiple_of(part * inner + unit_id % heads * HD, HD)
                    proj_ref[place, pl.ds(column, HD)] = value[:, part * HD : (part + 1) * HD]
            part_sum = jnp.sum(proj_ref[...].astype(F32), axis=0, keepdims=True)
            sum_ref[...] = part_sum if index == 0 else sum_ref[...] + part_sum
            for start in range(0, width, 512):
                value = dot_nt(proj_ref[:, :inner], weight_ref[0, start : start + 512])
                for part in range(1, 3):
                    value += dot_nt(
                        proj_ref[:, part * inner : (part + 1) * inner],
                        weight_ref[part, start : start + 512],
                    )
                held[:, start : start + 512] = value.astype(BF)
            emit_messages(
                lambda place: held[place, :], tp_ref[0], [ref.at[index] for ref in outs], size
            )

    return run_kernel(
        body,
        [sds((rows, 3 * inner))] * count
        + [sds((1, 3 * inner), F32)]
        + [sds((count,) + item.shape) for item in message_shapes(size // 2, width)],
        [here, tp_here] + list(received) + [weight],
        flops=6 * count * rows * inner * width,
        scratch=[pltpu.VMEM((rows, width), BF)],
        name="project_back",
        limit=10,
        after=after,
    )


def weight_grad(groups, here=None, after=()):
    count = len(groups[0][0])
    rows, tall = groups[0][0][0].shape
    widths = [rights[0].shape[1] for _, rights in groups]
    total = sum(widths)
    split = here is not None
    steps = 8 if split else 4
    step = tall // steps
    half = steps // 2

    def block_of(number, *fixed):
        if not split:
            return number
        core = fixed[0][0] & 1
        mine = number // half
        return 2 * (number % half) + (core ^ 1 ^ mine)

    def product(refs, store):
        start = 0
        for place, wide in enumerate(widths):
            ours = refs[2 * count * place : 2 * count * (place + 1)]
            value = dot_tn(ours[0][...], ours[count][...])
            for number in range(1, count):
                value += dot_tn(ours[number][...], ours[count + number][...])
            store(slice(start, start + wide), value.astype(BF))
            start += wide

    def body(*refs):
        if not split:
            out_ref = refs[-1]

            def store(place, value):
                out_ref[:, place] = value

            product(refs, store)
            return
        refs, other_ref, own_ref = refs[1:-2], refs[-2], refs[-1]
        number = pl.program_id(0)

        def into(ref):
            def store(place, value):
                ref[0, :, place] = value

            return store

        @pl.when(number < half)
        def _():
            product(refs, into(other_ref))

        @pl.when(number >= half)
        def _():
            product(refs, into(own_ref))

    args, in_specs = [], []
    for (lefts, rights), wide in zip(groups, widths):
        for item in lefts:
            if isinstance(item, Part):
                in_specs.append(
                    pl.BlockSpec(
                        (None, rows, step),
                        lambda i, *fixed, k=item.index: (k, 0, block_of(i, *fixed)),
                    )
                )
            else:
                in_specs.append(
                    pl.BlockSpec((rows, step), lambda i, *fixed: (0, block_of(i, *fixed)))
                )
        in_specs += [pl.BlockSpec((rows, wide), lambda *_: (0, 0))] * count
        args += list(lefts) + list(rights)
    if split:
        outs = [HBM((half, step, total), BF)] * 2
        out_specs = [
            pl.BlockSpec((1, step, total), lambda i, *_: (jnp.minimum(i, half - 1), 0, 0)),
            pl.BlockSpec((1, step, total), lambda i, *_: (jnp.maximum(i - half, 0), 0, 0)),
        ]
    else:
        outs = [HBM((tall, total), BF)]
        out_specs = [pl.BlockSpec((step, total), lambda i: (i, 0))]
    return launch(
        body,
        operands_of(args),
        in_specs,
        outs,
        out_specs,
        (),
        40 << 20,
        cost(
            2 * count * rows * tall * total,
            2 * (count * rows * (tall * len(groups) + total) + tall * total),
        ),
        "weight_grad",
        after,
        grid=(steps,),
        scalars=(here,) if split else (),
    )


def add_halves(own, got, after=()):
    def body(own_ref, got_ref, out_ref):
        out_ref[...] = (own_ref[...].astype(F32) + got_ref[...].astype(F32)).astype(BF)

    block_spec = pl.BlockSpec((1,) + own.shape[1:], lambda i: (i, 0, 0))
    return launch(
        body,
        operands_of([own, got]),
        [block_spec] * 2,
        [HBM(own.shape, BF)],
        [block_spec],
        (),
        16 << 20,
        cost(0, 6 * math.prod(own.shape)),
        "add_halves",
        after,
        grid=(own.shape[0],),
    )


def small_sums(values):
    here = lax.axis_index("ctx")
    step = values.shape[0] // 2
    while step:
        pair = values.reshape((2, step) + values.shape[1:])
        bit = (here // step) % 2
        keep = lax.dynamic_index_in_dim(pair, bit, 0, False)
        send = lax.dynamic_index_in_dim(pair, 1 - bit, 0, False)
        values = keep + xor_permute(send, "ctx", step)
        step //= 2
    return values[0]


def per_device_exchanged(
    inputs,
    segments,
    keep_mask,
    first_gain,
    first_shift,
    proj_weight,
    proj_bias,
    mixer_weight,
    mixer_bias,
    second_gain,
    second_shift,
    up_weight,
    up_bias,
    down_weight,
    down_bias,
    out_cotangent,
):
    ctx_count = lax.axis_size("ctx")
    micro_count, seq_count, tok_len, width = inputs.shape
    inner = proj_bias.shape[1]
    heads = inner // HD
    rows = seq_count * tok_len
    here = lax.axis_index("ctx").astype(jnp.int32).reshape(1)
    tp_here = lax.axis_index("tp").astype(jnp.int32).reshape(1)
    weight_three = jnp.transpose(proj_weight, (1, 0, 2))
    bias_three = jnp.stack([proj_bias[0], jnp.zeros_like(proj_bias[0]), proj_bias[1]])
    x_all = inputs.reshape(micro_count, rows, width)
    cot_all = out_cotangent.reshape(micro_count, rows, width)
    key_rows = jnp.where(keep_mask > 0, segments, -1)[:, :, None, :]
    gain_one, shift_one = first_gain[None], first_shift[None]
    gain_two, shift_two = second_gain[None], second_shift[None]
    mix_bias, low_bias, high_bias = mixer_bias[None], down_bias[None], up_bias[None]
    micro = range(micro_count)

    key_rows = [key_rows[index] for index in micro]
    seg_rows = [segments[index][:, None, :] for index in micro]
    cots = [Part(cot_all, index) for index in micro]
    size = rows // lax.axis_size("tp")
    start = tp_here[0] * size
    x_mine = [lax.dynamic_slice(x_all, (index, start, 0), (1, size, width))[0] for index in micro]
    cot_mine = [
        lax.dynamic_slice(cot_all, (index, start, 0), (1, size, width))[0] for index in micro
    ]

    chips = [[core + 2 * chip for chip in range(ctx_count // 2)] for core in range(2)]

    def scattered(part):
        return lax.psum_scatter(part, "ctx", scatter_dimension=0, tiled=True)

    def scattered_chips(part):
        part = part.reshape(-1, part.shape[2])
        return lax.psum_scatter(
            part, "ctx", scatter_dimension=0, axis_index_groups=chips, tiled=True
        )

    def until(items, *points):
        held, _ = lax.optimization_barrier((items, points))
        return held

    norm_one, received, lses, heads_low, resids = [], [], [], [], []

    def project_micro(index, done):
        (normed, *sent), done = project(
            here, x_all, index, gain_one, shift_one, weight_three, bias_three, tok_len, after=done
        )
        norm_one.append(normed)
        return exchange_chips(*sent), done

    def attend_micro(index, got, done):
        received.append(got)
        (*sent, lse), done = attention(
            here, got, seg_rows[index], key_rows[index], heads, after=done
        )
        lses.append(lse)
        return exchange_chips(*sent), done

    def mix_micro(got, direct, done):
        (mixed, *messages), done = mix_heads(
            here, tp_here, got, mixer_weight, heads, direct, after=done
        )
        heads_low.append(mixed)
        return messages, done

    def norm_micro(index, sums, direct, done):
        (resid, *shard), done = second_norm(
            sums, x_mine[index], mix_bias, gain_two, shift_two, direct, after=done
        )
        resids.append(resid)
        return shard if direct else gather_first(shard), done

    norm_two, acts, grad_pres, up_sums, cot_sums = [], [], [], [], []

    def feed_micro(index, pieces, feeds, direct, done):
        (normed, act, grad_pre, up_sum, cot_sum, *messages), done = feed_forward(
            tp_here,
            pieces,
            cots[index],
            up_weight,
            high_bias,
            down_weight,
            feeds,
            index,
            micro_count,
            direct,
            after=done,
        )
        norm_two.append(normed)
        acts.append(act)
        grad_pres.append(grad_pre)
        up_sums.append(up_sum)
        cot_sums.append(cot_sum)
        messages, ours = messages[:4], messages[4:]
        return messages, reduce_direct(ours) if direct else ours, done

    grad_resids, gain_twos, shift_twos = [], [], []
    grad_mixes, mix_sums, states = [], [], []

    def norm_back_micro(index, sums, done):
        (grad_resid, gain_sum, shift_sum, *shard), done = second_norm_back(
            sums, resids[index], cot_mine[index], gain_two, False, after=done
        )
        grad_resids.append(grad_resid)
        gain_twos.append(gain_sum)
        shift_twos.append(shift_sum)
        return gather_first(shard), done

    def heads_back_micro(index, pieces, done):
        (grad_mix, mix_sum, *sent), done = heads_back(
            here, tp_here, pieces, mixer_weight, tok_len, after=done
        )
        grad_mixes.append(grad_mix)
        mix_sums.append(mix_sum)
        states.append(exchange_chips(*sent))
        return done

    def attend_back_micro(index, got, earlier, done):
        return attention_back(
            here,
            received[index],
            got,
            seg_rows[index],
            key_rows[index],
            lses[index],
            heads,
            earlier,
            index,
            micro_count,
            after=done,
        )

    state_a, done = project_micro(0, ())
    state_b, done = project_micro(1, done)
    got, done = exchange_cores(state_a, done)
    state_a, done = attend_micro(0, got, done)
    got, done = exchange_cores(state_b, done)
    state_b, done = attend_micro(1, got, done)
    got, done = exchange_cores(state_a, done)
    messages, done = mix_micro(got, False, done)
    state_a = reduce_first(messages)
    got, done = exchange_cores(state_b, done)
    messages, done = mix_micro(got, False, done)
    state_b = reduce_first(messages)
    sums_a, done = reduce_second(state_a, done)
    state_a, done = norm_micro(0, sums_a, False, done)
    sums_b, done = reduce_second(state_b, done)
    pieces_a, done = gather_second(state_a, done)
    state_b, done = norm_micro(1, sums_b, True, done)
    pieces_b = gather_direct(state_b[0])
    feeds, sums_a, done = feed_micro(0, pieces_a, [], True, done)
    feeds, messages, done = feed_micro(1, pieces_b, feeds, False, done)

    state_b = reduce_first(messages)
    state_a, done = norm_back_micro(0, sums_a, done)
    (down_part,), done = weight_grad([(cots, acts)], after=done)
    pieces_a, done = gather_second(state_a, done)
    sums_b, done = reduce_second(state_b, done)
    down_grad = scattered(until(down_part, done))
    (sent, own), done = weight_grad([(norm_two, grad_pres)], here, after=done)
    done = heads_back_micro(0, pieces_a, done)
    state_b, done = norm_back_micro(1, sums_b, done)
    got_up = xor_permute(until(sent, done), "ctx", 1)
    pieces_b, done = gather_second(state_b, done)
    got_a, done = exchange_cores(states[0], done)
    (up_part,), done = add_halves(own, got_up, after=done)
    done = heads_back_micro(1, pieces_b, done)
    state_feed = reduce_first(until(feeds, done))
    sent, done = attend_back_micro(0, got_a, [], done)
    got_b, done = exchange_cores(states[1], done)
    sums_feed, done = reduce_second(state_feed, done)
    sent, done = attend_back_micro(1, got_b, sent, done)
    state_back = exchange_chips(*sent)
    halves, done = finish_outputs(sums_feed, resids, low_bias, after=done)
    state_out = gather_first(halves)
    got, done = exchange_cores(state_back, done)
    up_grad = scattered_chips(until(up_part, done))
    (*grad_projs, proj_sum, first, second, third, fourth), done = project_back(
        here, tp_here, got, weight_three, after=done
    )
    state_one = reduce_first((first, second, third, fourth))
    last = [(norm_one, grad_projs), (grad_mixes, heads_low)]
    (sent, own), done = weight_grad(last, here, after=done)
    pieces_out, done = gather_second(state_out, done)
    got_last = xor_permute(until(sent, done), "ctx", 1)
    sums_one, done = reduce_second(state_one, done)
    (last_part,), done = add_halves(own, got_last, after=done)
    last_grad = scattered_chips(last_part)
    (gain_sum, shift_sum, *halves), done = first_norm_back(
        sums_one, x_mine, grad_resids, gain_one, after=done
    )
    outputs, done = assemble_outputs(tp_here, pieces_out, BF, after=done)
    gain_ones, shift_ones, proj_sums = [gain_sum], [shift_sum], [proj_sum]
    pieces_in, done = gather_second(gather_first(halves), done)
    input_grad, done = assemble_outputs(tp_here, pieces_in, F32, after=done)
    (down_grad,), done = widen(down_grad, True, after=done)
    (up_grad,), done = widen(up_grad, False, after=done)
    (proj_grad, mixer_grad), done = widen_last(last_grad, inner, after=done)
    proj_grad = jnp.transpose(proj_grad, (1, 0, 2))

    def over_micro(items):
        return sum(items[1:], items[0]).reshape(ctx_count, -1)

    proj_sum = sum(proj_sums[1:], proj_sums[0]).reshape(3, ctx_count, -1)
    pair_sum = jnp.concatenate([proj_sum[0], proj_sum[2]], axis=1)
    share = width // ctx_count
    pair_sum = jnp.pad(pair_sum, ((0, 0), (0, share - pair_sum.shape[1])))
    kinds = [
        over_micro(gain_ones),
        over_micro(shift_ones),
        over_micro(gain_twos),
        over_micro(shift_twos),
        over_micro(mix_sums),
        over_micro(cot_sums),
        over_micro(up_sums),
        pair_sum,
    ]
    small = small_sums(jnp.stack(kinds, axis=1))
    norms = small[:4]
    for step in (1, 2):
        norms = norms + xor_permute(norms, "tp", step)
    proj_bias_grad = small[7, : 2 * inner // ctx_count].reshape(2, -1)
    return (
        outputs.reshape(inputs.shape),
        input_grad.reshape(inputs.shape),
        norms[0],
        norms[1],
        proj_grad,
        proj_bias_grad,
        mixer_grad,
        small[4],
        norms[2],
        norms[3],
        up_grad,
        small[6],
        down_grad,
        small[5],
    )


def plan_for(mesh):
    sizes = dict(mesh.shape)

    def chosen(*args):
        micro, seq_count, _, width = args[0].shape
        units = seq_count * args[6].shape[1] // HD
        fits = sizes["ctx"] == 8 and sizes["tp"] == 4 and units == sizes["ctx"]
        fits = fits and args[12].shape[0] == width and micro == 2
        return (per_device_exchanged if fits else per_device)(*args)

    return chosen


def solution(mesh):
    in_specs = (
        P(None, None, "ctx", None),
        P(),
        P(),
        P(),
        P(),
        P(None, None, "tp"),
        P(None, "tp"),
        P("tp", None),
        P(),
        P(),
        P(),
        P(None, "tp"),
        P("tp"),
        P("tp", None),
        P(),
        P(None, None, "ctx", None),
    )
    out_specs = (
        P(None, None, "ctx", None),
        P(None, None, "ctx", None),
        P("ctx"),
        P("ctx"),
        P("ctx", None, "tp"),
        P(None, ("tp", "ctx")),
        P("tp", "ctx"),
        P("ctx"),
        P("ctx"),
        P("ctx"),
        P("ctx", "tp"),
        P(("tp", "ctx")),
        P("tp", "ctx"),
        P("ctx"),
    )
    return jax.shard_map(
        plan_for(mesh), mesh=mesh, in_specs=in_specs, out_specs=out_specs, check_vma=False
    )
```

```python
import math

import jax
import jax.numpy as jnp
from jax import lax
from jax.experimental import pallas as pl
from jax.experimental.pallas import tpu as pltpu
from jax.sharding import PartitionSpec as P

HD = 128


def storage_order(values, part_count):
    leading = values.shape[:-1]
    blocks = values.reshape(leading + (2 * part_count, -1))
    front_half = blocks[..., :part_count, :]
    back_half = jnp.flip(blocks[..., part_count:, :], axis=-2)
    return jnp.stack([front_half, back_half], axis=-2).reshape(leading + (-1,))


def layer_norm(values, norm_gain, norm_shift):
    center = values - jnp.mean(values, axis=-1, keepdims=True)
    spread = jnp.mean(center * center, axis=-1, keepdims=True)
    return center * lax.rsqrt(spread + 1e-05) * norm_gain + norm_shift


def gelu_exact(values):
    return jax.nn.gelu(values, approximate=False)


def split_heads(rows, heads_here):
    return rows.reshape(rows.shape[0], rows.shape[1], heads_here, -1)


def scores_of(queries, key_all, allowed, heads_here, scaler):
    raw = (
        jnp.einsum(
            "sqhd,skhd->shqk",
            split_heads(queries, heads_here),
            split_heads(key_all, heads_here),
            preferred_element_type=jnp.float32,
        )
        * scaler
    )
    return jnp.where(allowed[:, None], raw, -1000000000.0)


def attend(queries, key_all, value_all, allowed, heads_here, scaler):
    masked = scores_of(queries, key_all, allowed, heads_here, scaler)
    top = jnp.max(masked, axis=-1, keepdims=True)
    raised = jnp.exp(masked - top)
    totals = jnp.sum(raised, axis=-1, keepdims=True)
    probs = raised / totals
    mixed = jnp.einsum(
        "shqk,skhd->sqhd",
        probs.astype(jnp.bfloat16),
        split_heads(value_all, heads_here),
        preferred_element_type=jnp.float32,
    )
    return (mixed.reshape(queries.shape), top + jnp.log(totals))


def attend_back(queries, key_all, value_all, allowed, log_total, grad_heads, heads_here, scaler):
    masked = scores_of(queries, key_all, allowed, heads_here, scaler)
    probs = jnp.exp(masked - log_total)
    grad_four = split_heads(grad_heads, heads_here)
    grad_value = jnp.einsum(
        "shqk,sqhd->skhd", probs.astype(jnp.bfloat16), grad_four, preferred_element_type=jnp.float32
    )
    grad_probs = jnp.einsum(
        "sqhd,skhd->shqk",
        grad_four,
        split_heads(value_all, heads_here),
        preferred_element_type=jnp.float32,
    )
    inner_sum = jnp.sum(probs * grad_probs, axis=-1, keepdims=True)
    grad_scores = (probs * (grad_probs - inner_sum)).astype(jnp.bfloat16)
    grad_query = (
        jnp.einsum(
            "shqk,skhd->sqhd",
            grad_scores,
            split_heads(key_all, heads_here),
            preferred_element_type=jnp.float32,
        )
        * scaler
    )
    grad_key = (
        jnp.einsum(
            "shqk,sqhd->skhd",
            grad_scores,
            split_heads(queries, heads_here),
            preferred_element_type=jnp.float32,
        )
        * scaler
    )
    return (
        grad_query.reshape(queries.shape),
        grad_key.reshape(key_all.shape),
        grad_value.reshape(value_all.shape),
    )


def reduce_grads(grads):
    return (
        lax.psum_scatter(
            grads[0].astype(jnp.bfloat16), "ctx", scatter_dimension=0, tiled=True
        ).astype(jnp.float32),
        lax.psum_scatter(
            grads[1].astype(jnp.bfloat16), "ctx", scatter_dimension=0, tiled=True
        ).astype(jnp.float32),
        lax.psum_scatter(
            grads[2].astype(jnp.bfloat16), "ctx", scatter_dimension=0, tiled=True
        ).astype(jnp.float32),
        lax.psum_scatter(
            grads[3].astype(jnp.bfloat16), "ctx", scatter_dimension=1, tiled=True
        ).astype(jnp.float32),
        lax.psum_scatter(
            grads[4].astype(jnp.bfloat16), "ctx", scatter_dimension=1, tiled=True
        ).astype(jnp.float32),
        lax.psum_scatter(
            grads[5].astype(jnp.bfloat16), "ctx", scatter_dimension=0, tiled=True
        ).astype(jnp.float32),
        lax.psum_scatter(
            grads[6].astype(jnp.bfloat16), "ctx", scatter_dimension=0, tiled=True
        ).astype(jnp.float32),
        lax.psum_scatter(
            grads[7].astype(jnp.bfloat16), "ctx", scatter_dimension=0, tiled=True
        ).astype(jnp.float32),
        lax.psum_scatter(
            grads[8].astype(jnp.bfloat16), "ctx", scatter_dimension=0, tiled=True
        ).astype(jnp.float32),
        lax.psum_scatter(
            grads[9].astype(jnp.bfloat16), "ctx", scatter_dimension=0, tiled=True
        ).astype(jnp.float32),
        lax.psum_scatter(
            grads[10].astype(jnp.bfloat16), "ctx", scatter_dimension=1, tiled=True
        ).astype(jnp.float32),
        lax.psum_scatter(
            grads[11].astype(jnp.bfloat16), "ctx", scatter_dimension=0, tiled=True
        ).astype(jnp.float32),
    )


def per_device(
    inputs,
    segments,
    keep_mask,
    first_gain,
    first_shift,
    proj_weight,
    proj_bias,
    mixer_weight,
    mixer_bias,
    second_gain,
    second_shift,
    up_weight,
    up_bias,
    down_weight,
    down_bias,
    out_cotangent,
):
    ctx_count = lax.axis_size("ctx")
    micro_count, seq_count, tok_len, model_width = inputs.shape
    inner_width = proj_bias.shape[1]
    heads_here = inner_width // HD
    scaler = 1.0 / math.sqrt(HD)
    seq_len = tok_len * ctx_count
    places = storage_order(jnp.arange(seq_len, dtype=jnp.int32), ctx_count)
    offset = lax.axis_index("ctx") * tok_len
    my_places = lax.dynamic_slice_in_dim(places, offset, tok_len, 0)
    seg_store = storage_order(segments, ctx_count)
    keep_store = storage_order(keep_mask, ctx_count)
    proj_flat = proj_weight.reshape(model_width, 3 * inner_width)
    bias_three = jnp.stack([proj_bias[0], jnp.zeros_like(proj_bias[0]), proj_bias[1]])
    causal = places[None, :] <= my_places[:, None]
    itself = places[None, :] == my_places[:, None]
    shaped_like = (
        first_gain,
        first_shift,
        proj_weight,
        proj_bias,
        mixer_weight,
        mixer_bias,
        second_gain,
        second_shift,
        up_weight,
        up_bias,
        down_weight,
        down_bias,
    )
    running = tuple((jnp.zeros(item.shape, jnp.float32) for item in shaped_like))
    out_list = []
    grad_list = []
    for micro_index in range(micro_count):
        x_now = inputs[micro_index].astype(jnp.float32)
        seg_keys = seg_store[micro_index]
        seg_mine = lax.dynamic_slice_in_dim(seg_keys, offset, tok_len, 1)
        visible = (keep_store[micro_index] > 0)[:, None, :] | itself[None]
        allowed = causal[None] & (seg_keys[:, None, :] == seg_mine[:, :, None]) & visible
        normed_one = layer_norm(x_now, first_gain, first_shift).astype(jnp.bfloat16)
        projected = jnp.einsum(
            "std,dc->stc", normed_one, proj_flat, preferred_element_type=jnp.float32
        )
        projected = (projected.reshape(seq_count, tok_len, 3, inner_width) + bias_three).astype(
            jnp.bfloat16
        )
        queries = projected[:, :, 0]
        key_here = projected[:, :, 1]
        value_here = projected[:, :, 2]
        key_all, value_all = (
            lax.all_gather(key_here, "ctx", axis=1, tiled=True),
            lax.all_gather(value_here, "ctx", axis=1, tiled=True),
        )
        heads_out, log_total = attend(queries, key_all, value_all, allowed, heads_here, scaler)
        heads_low = heads_out.astype(jnp.bfloat16)
        mixed_part = jnp.einsum(
            "stn,nd->std", heads_low, mixer_weight, preferred_element_type=jnp.float32
        )
        resid = (
            x_now + lax.psum(mixed_part.astype(jnp.bfloat16), "tp").astype(jnp.float32) + mixer_bias
        )
        normed_two = layer_norm(resid, second_gain, second_shift).astype(jnp.bfloat16)
        pre_act = (
            jnp.einsum("std,df->stf", normed_two, up_weight, preferred_element_type=jnp.float32)
            + up_bias
        )
        act_low = gelu_exact(pre_act).astype(jnp.bfloat16)
        feed_part = jnp.einsum(
            "stf,fd->std", act_low, down_weight, preferred_element_type=jnp.float32
        )
        feed = lax.psum(feed_part.astype(jnp.bfloat16), "tp").astype(jnp.float32) + down_bias
        out_list.append((resid + feed).astype(jnp.bfloat16))
        cot_low = out_cotangent[micro_index]
        cot_full = cot_low.astype(jnp.float32)
        down_bias_part = jnp.sum(cot_full, axis=(0, 1))
        down_part = jnp.einsum("stf,std->fd", act_low, cot_low, preferred_element_type=jnp.float32)
        grad_act = jnp.einsum(
            "std,fd->stf", cot_low, down_weight, preferred_element_type=jnp.float32
        )
        grad_pre = jax.vjp(gelu_exact, pre_act)[1](grad_act)[0].astype(jnp.bfloat16)
        up_part = jnp.einsum(
            "std,stf->df", normed_two, grad_pre, preferred_element_type=jnp.float32
        )
        up_bias_part = jnp.sum(grad_pre.astype(jnp.float32), axis=(0, 1))
        grad_two_part = jnp.einsum(
            "stf,df->std", grad_pre, up_weight, preferred_element_type=jnp.float32
        )
        grad_two = lax.psum(grad_two_part.astype(jnp.bfloat16), "tp").astype(jnp.float32)
        resid_part, second_gain_part, second_shift_part = jax.vjp(
            layer_norm, resid, second_gain, second_shift
        )[1](grad_two)
        grad_resid = cot_full + resid_part
        grad_mix = grad_resid.astype(jnp.bfloat16)
        mixer_bias_part = jnp.sum(grad_mix.astype(jnp.float32), axis=(0, 1))
        mixer_part = jnp.einsum(
            "stn,std->nd", heads_low, grad_mix, preferred_element_type=jnp.float32
        )
        grad_heads = jnp.einsum(
            "std,nd->stn", grad_mix, mixer_weight, preferred_element_type=jnp.float32
        ).astype(jnp.bfloat16)
        key_back, value_back = (key_all, value_all)
        grad_query, grad_key, grad_value = attend_back(
            queries, key_back, value_back, allowed, log_total, grad_heads, heads_here, scaler
        )
        key_share, value_share = (
            lax.psum_scatter(
                grad_key.astype(jnp.bfloat16), "ctx", scatter_dimension=1, tiled=True
            ).astype(jnp.float32),
            lax.psum_scatter(
                grad_value.astype(jnp.bfloat16), "ctx", scatter_dimension=1, tiled=True
            ).astype(jnp.float32),
        )
        grad_proj = jnp.stack([grad_query, key_share, value_share], axis=2).astype(jnp.bfloat16)
        proj_part = jnp.einsum(
            "std,stcn->dcn", normed_one, grad_proj, preferred_element_type=jnp.float32
        )
        proj_sums = jnp.sum(grad_proj.astype(jnp.float32), axis=(0, 1))
        proj_bias_part = jnp.stack([proj_sums[0], proj_sums[2]])
        grad_one_part = jnp.einsum(
            "stc,dc->std",
            grad_proj.reshape(seq_count, tok_len, 3 * inner_width),
            proj_flat,
            preferred_element_type=jnp.float32,
        )
        grad_one = lax.psum(grad_one_part.astype(jnp.bfloat16), "tp").astype(jnp.float32)
        input_part, first_gain_part, first_shift_part = jax.vjp(
            layer_norm, x_now, first_gain, first_shift
        )[1](grad_one)
        grad_list.append(grad_resid + input_part)
        batch_grads = (
            first_gain_part,
            first_shift_part,
            proj_part,
            proj_bias_part,
            mixer_part,
            mixer_bias_part,
            second_gain_part,
            second_shift_part,
            up_part,
            up_bias_part,
            down_part,
            down_bias_part,
        )
        running = tuple((earlier + adding for earlier, adding in zip(running, batch_grads)))
    final = reduce_grads(running)
    return (
        jnp.stack(out_list),
        jnp.stack(grad_list),
        final[0],
        final[1],
        final[2],
        final[3],
        final[4],
        final[5],
        final[6],
        final[7],
        final[8],
        final[9],
        final[10],
        final[11],
    )


BF = jnp.bfloat16
F32 = jnp.float32
LOG2E = 1.4426950408889634
LOW = -1e30
ORDERS = ((1, 2), (2, 1))
COST_SHARE = 1.0


def xor_permute(values, axis, step):
    count = lax.axis_size(axis)
    return lax.ppermute(values, axis, [(i, i ^ step) for i in range(count)])


def sds(shape, dtype=BF):
    return jax.ShapeDtypeStruct(tuple(shape), dtype)


def cost(flops, moved, exps=0):
    return pl.CostEstimate(
        flops=int(flops * COST_SHARE),
        bytes_accessed=int(moved * COST_SHARE),
        transcendentals=int(exps * COST_SHARE),
    )


HBM = pltpu.MemorySpace.HBM


def launch(
    body,
    args,
    in_specs,
    outs,
    out_specs,
    scratch,
    limit,
    cost,
    name,
    after,
    grid=(),
    aliases=None,
    scalars=(),
):
    first, last = len(after), len(after) + len(args) + len(outs)

    def inner(*refs):
        fixed, refs = refs[: len(scalars)], refs[len(scalars) :]
        body(*fixed, *refs[first:last], *refs[last + 1 :])

    token = pl.BlockSpec(memory_space=HBM)
    *results, done = pl.pallas_call(
        inner,
        grid_spec=pltpu.PrefetchScalarGridSpec(
            num_scalar_prefetch=len(scalars),
            grid=grid,
            in_specs=[token] * first + list(in_specs),
            out_specs=(*out_specs, token),
            scratch_shapes=list(scratch),
        ),
        out_shape=(*outs, sds((8, 128), F32)),
        input_output_aliases={first + key: value for key, value in (aliases or {}).items()},
        compiler_params=pltpu.CompilerParams(vmem_limit_bytes=limit),
        cost_estimate=cost,
        name=name,
    )(*scalars, *after, *args)
    return results, (done,)


class Part:
    def __init__(self, array, index):
        self.array, self.index = array, index
        self.shape, self.dtype = array.shape[1:], array.dtype

    def spec(self):
        index, rest = self.index, (0,) * len(self.shape)
        return pl.BlockSpec((None,) + self.shape, lambda *_: (index,) + rest)


def operands_of(args):
    arrays = [arg.array if isinstance(arg, Part) else arg for arg in args]
    return [array if array.dtype == jnp.int32 else pinned(array) for array in arrays]


def pinned(array):
    return pltpu.with_memory_space_constraint(array, HBM)


def run_kernel(body, outs, args, flops=0, exps=0, scratch=(), limit=8, name=None, after=(), in_hbm=()):
    specs = []
    moved = 0
    for place, arg in enumerate(args):
        if arg.dtype == jnp.int32 and math.prod(arg.shape) <= 8:
            specs.append(pl.BlockSpec(memory_space=pltpu.SMEM))
        elif place in in_hbm:
            specs.append(pl.BlockSpec(memory_space=HBM))
        else:
            specs.append(pl.BlockSpec(memory_space=pltpu.VMEM))
            moved += math.prod(arg.shape) * arg.dtype.itemsize
    moved += sum(math.prod(o.shape) * o.dtype.itemsize for o in outs)
    kept = [item for item in scratch if item.dtype in (BF, F32)]
    held = moved + sum(math.prod(item.shape) * item.dtype.itemsize for item in kept)
    return launch(
        body,
        [pinned(arg) if place in in_hbm else arg for place, arg in enumerate(args)],
        specs,
        outs,
        [pl.BlockSpec(memory_space=pltpu.VMEM) for _ in outs],
        scratch,
        held + (limit << 20),
        cost(flops, moved, exps),
        name,
        after,
    )


def whole_of(shape):
    return pl.BlockSpec(shape, lambda *_, n=len(shape): (0,) * n)


def rows_at(start, count):
    return pl.ds(pl.multiple_of(start, count), count)


def reduce_first(messages):
    return [
        (messages[2 * part + 1], xor_permute(messages[2 * part], "tp", first))
        for part, (first, _) in enumerate(ORDERS)
    ]


def reduce_second(state, after=()):
    shape = state[0][0].shape[:-3] + state[0][0].shape[-2:]

    def body(*refs):
        for part in range(2):
            keep, got = refs[2 * part : 2 * part + 2]
            refs[4 + part][...] = keep[..., 0, :, :].astype(F32) + got[..., 0, :, :].astype(F32)
            value = keep[..., 1, :, :].astype(F32) + got[..., 1, :, :].astype(F32)
            refs[6 + part][...] = value.astype(BF)

    (*rest, low, high), done = run_kernel(
        body,
        [sds(shape, F32)] * 2 + [sds(shape)] * 2,
        [item for pair in state for item in pair],
        after=after,
        name="reduce_middle",
        limit=4,
    )
    sums = []
    for part, (_, second) in enumerate(ORDERS):
        sums += [rest[part], xor_permute((low, high)[part], "tp", second)]
    return sums, done


def reduce_direct(messages):
    mine, *sent = messages
    return [mine] + [xor_permute(item, "tp", 1 + step) for step, item in enumerate(sent)]


def gather_first(halves):
    return [
        (halves[part], xor_permute(halves[part], "tp", first))
        for part, (first, _) in enumerate(ORDERS)
    ]


def gather_second(state, after=()):
    half = state[0][0].shape
    pair_shape = half[:-2] + (2,) + half[-2:]

    def body(*refs):
        for part in range(2):
            for place in range(2):
                refs[4 + part][..., place, :, :] = refs[2 * part + place][...]

    pairs, done = run_kernel(
        body,
        [sds(pair_shape)] * 2,
        [item for pair in state for item in pair],
        after=after,
        name="gather_middle",
        limit=3,
    )
    pieces = []
    for part, (_, second) in enumerate(ORDERS):
        pieces += [*state[part], xor_permute(pairs[part], "tp", second)]
    return pieces, done


def gather_direct(mine):
    return [mine] + [xor_permute(mine, "tp", step) for step in (1, 2, 3)]


def total_of(refs):
    if refs[0].dtype == BF:
        return sum([ref[...].astype(F32) for ref in refs[1:]], refs[0][...].astype(F32))
    halves = [refs[2 * part][...] + refs[2 * part + 1][...].astype(F32) for part in range(2)]
    return jnp.concatenate(halves, axis=0)


def place_gathered(store, tp_here, refs, size):
    if len(refs) == 4:
        for step, ref in enumerate(refs):
            store(rows_at((tp_here ^ step) * size, size), ref[...])
        return
    half = size // 2
    for part, (first, second) in enumerate(ORDERS):
        mine, near, far = refs[3 * part : 3 * part + 3]
        parts = ((0, mine[...]), (first, near[...]), (second, far[0]), (first | second, far[1]))
        for step, value in parts:
            store(rows_at((tp_here ^ step) * size + part * half, half), value)


def emit_messages(load, tp_here, refs, size):
    if refs[0].shape[-2] == size:
        for step, ref in enumerate(refs):
            ref[...] = load(rows_at((tp_here ^ step) * size, size))
        return
    half = size // 2
    for part, (first, second) in enumerate(ORDERS):
        send, keep = refs[2 * part], refs[2 * part + 1]
        for ref, steps in ((send, (first, first | second)), (keep, (0, second))):
            for place, step in enumerate(steps):
                ref[place] = load(rows_at((tp_here ^ step) * size + part * half, half))


def emit_shard(value, refs):
    rows = value.shape[0] // len(refs)
    for place, ref in enumerate(refs):
        ref[...] = value[place * rows : (place + 1) * rows]


def shard_shapes(size, width, direct=False):
    return [sds((size, width))] if direct else [sds((size // 2, width))] * 2


def message_shapes(half, width, direct=False):
    return [sds((2 * half, width) if direct else (2, half, width))] * 4


def exchange_chips(local, cross, first, second, third):
    got = [
        xor_permute(item, "ctx", 2 * (place + 1))
        for place, item in enumerate((first, second, third))
    ]
    return [local, cross] + got


def exchange_cores(state, after):
    local, cross, *got = state

    lead = cross.shape[:-2]

    def body(cross_ref, first_ref, second_ref, third_ref, out_ref):
        out_ref[..., 0, :, :] = cross_ref[...]
        for place, ref in enumerate((first_ref, second_ref, third_ref)):
            out_ref[..., place + 1, :, :] = ref[..., 1, :, :]

    (packed,), done = run_kernel(
        body, [sds(lead + (4,) + cross.shape[-2:])], [cross] + got, after=after, limit=2, name="pack"
    )
    return [local] + got + [xor_permute(packed, "ctx", 1)], done


def exchanged(refs, here):
    local, first, second, third, packed = refs
    return (
        (here, local[...]),
        (here ^ 1, packed[0]),
        (here ^ 2, first[0]),
        (here ^ 3, packed[1]),
        (here ^ 4, second[0]),
        (here ^ 5, packed[2]),
        (here ^ 6, third[0]),
        (here ^ 7, packed[3]),
    )


def emit_exchange(load, here, refs):
    local, cross, first, second, third = refs
    local[...] = load(here)
    cross[...] = load(here ^ 1)
    for place, ref in enumerate((first, second, third)):
        other = here ^ (2 * (place + 1))
        ref[0] = load(other)
        ref[1] = load(other ^ 1)


def exchange_shapes(rows, width):
    return [sds((rows, width)), sds((rows, width))] + [sds((2, rows, width))] * 3


def normalized(values):
    center = values - jnp.mean(values, axis=-1, keepdims=True)
    spread = jnp.mean(center * center, axis=-1, keepdims=True)
    root = lax.rsqrt(spread + 1e-05)
    return center * root, root


def norm_back(values, gain, grad):
    unit, root = normalized(values)
    scaled = grad * gain
    back = root * (
        scaled
        - jnp.mean(scaled, axis=-1, keepdims=True)
        - unit * jnp.mean(scaled * unit, axis=-1, keepdims=True)
    )
    gain_sum = jnp.sum(grad * unit, axis=0, keepdims=True)
    shift_sum = jnp.sum(grad, axis=0, keepdims=True)
    return back, gain_sum, shift_sum


def dot(left, right):
    return jnp.dot(left, right, preferred_element_type=F32)


def dot_nt(left, right):
    return lax.dot_general(left, right, (((1,), (1,)), ((), ())), preferred_element_type=F32)


def dot_tn(left, right):
    return lax.dot_general(left, right, (((0,), (0,)), ((), ())), preferred_element_type=F32)


def project(here, x_all, index, gain, shift, weight, bias, tok_len, after=()):
    _, rows, width = x_all.shape
    inner = weight.shape[2]
    heads = inner // HD

    def body(here_ref, x_ref, gain_ref, shift_ref, weight_hbm, bias_ref, *rest):
        norm_ref, outs, (held, weight_ref, x_held, sems) = rest[0], rest[1:6], rest[6:]
        fetch = pltpu.make_async_copy(x_ref.at[index], x_held, sems.at[3])
        fetch.start()
        copies = [
            pltpu.make_async_copy(weight_hbm.at[part], weight_ref.at[part], sems.at[part])
            for part in range(3)
        ]
        for copy in copies:
            copy.start()
        fetch.wait()
        unit, _ = normalized(x_held[...].astype(F32))
        norm_ref[...] = (unit * gain_ref[...] + shift_ref[...]).astype(BF)
        for part in range(3):
            copies[part].wait()
            value = dot(norm_ref[...], weight_ref[part]) + bias_ref[part : part + 1]
            value = value.astype(BF)
            for head in range(heads):
                held[head, :, part * HD : (part + 1) * HD] = value[:, head * HD : (head + 1) * HD]

        def load(unit_id):
            return held[unit_id % heads, rows_at(unit_id // heads * tok_len, tok_len), :]

        emit_exchange(load, here_ref[0], outs)

    return run_kernel(
        body,
        [sds((rows, width))] + exchange_shapes(tok_len, 3 * HD),
        [here, x_all, gain, shift, weight, bias],
        flops=6 * rows * width * inner,
        scratch=[
            pltpu.VMEM((heads, rows, 3 * HD), BF),
            pltpu.VMEM(weight.shape, BF),
            pltpu.VMEM((rows, width), BF),
            pltpu.SemaphoreType.DMA((4,)),
        ],
        name="project",
        limit=14,
        after=after,
        in_hbm=(1, 4),
    )


def rows_of_device(device, block, blocks):
    return (
        rows_at(device * block, block),
        rows_at((blocks - 1 - device) * block, block),
    )


def attention(here, received, seg_row, key_row, heads, after=()):
    tok_len = received[0].shape[0]
    block = tok_len // 2
    seq_len = seg_row.shape[2]
    blocks = seq_len // block
    step = 256
    factor = LOG2E / math.sqrt(HD)

    def body(here_ref, *rest):
        refs, seg_ref, key_ref = rest[:5], rest[5], rest[6]
        outs, lse_ref = rest[7:12], rest[12]
        q_all, k_turned, v_all, mixed = rest[13:]
        me = here_ref[0]
        seq = me // heads
        for device, value in exchanged(refs, me):
            for half, place in enumerate(rows_of_device(device, block, blocks)):
                rows = value[half * block : (half + 1) * block]
                q_all[place] = rows[:, :HD]
                k_turned[:, place] = rows[:, HD : 2 * HD].T
                v_all[place] = rows[:, 2 * HD :]
        for number in range(seq_len // step):
            start, stop = number * step, (number + 1) * step
            segs = as_column(seg_ref[seq, :, start:stop])
            scores = dot(q_all[start:stop], k_turned[:, :stop]) * factor
            scores = masked(scores, segs, key_ref, seq, start, stop)
            top = jnp.max(scores, axis=-1, keepdims=True)
            raised = jnp.exp2(scores - top)
            total = jnp.sum(raised, axis=-1, keepdims=True)
            out = dot(raised.astype(BF), v_all[:stop]) / total
            mixed[start:stop] = out.astype(BF)
            lse_ref[start:stop] = top + jnp.log2(total)

        def load(device):
            return jnp.concatenate(
                [mixed[place] for place in rows_of_device(device, block, blocks)], axis=0
            )

        emit_exchange(load, me, outs)

    return run_kernel(
        body,
        exchange_shapes(tok_len, HD) + [sds((seq_len, 1), F32)],
        [here] + list(received) + [seg_row, key_row],
        flops=2 * 2 * seq_len * seq_len * HD,
        exps=seq_len * seq_len // 2,
        scratch=[
            pltpu.VMEM((seq_len, HD), BF),
            pltpu.VMEM((HD, seq_len), BF),
            pltpu.VMEM((seq_len, HD), BF),
            pltpu.VMEM((seq_len, HD), BF),
        ],
        after=after,
        name="attention",
        limit=16,
    )


def as_column(row):
    return jnp.broadcast_to(row, (128, row.shape[1])).T[:, :1]


def masked(scores, segs, key_ref, seq, start, stop):
    size = stop - start
    row = lax.broadcasted_iota(jnp.int32, (size, size), 0)
    column = lax.broadcasted_iota(jnp.int32, (size, size), 1)
    same = segs == key_ref[seq, :, start:stop]
    seen = (same & (column < row)) | (column == row)
    corner = jnp.where(seen, scores[:, start:], LOW)
    if start == 0:
        return corner
    left = jnp.where(segs == key_ref[seq, :, :start], scores[:, :start], LOW)
    return jnp.concatenate([left, corner], axis=1)


def attention_back(
    here, received, grads, seg_row, key_row, lse, heads, earlier, index, count, after=()
):
    tok_len = received[0].shape[0]
    block = tok_len // 2
    seq_len = seg_row.shape[2]
    blocks = seq_len // block
    step = 256
    scaler = 1.0 / math.sqrt(HD)

    def body(here_ref, *rest):
        refs, grad_refs = rest[:5], rest[5:10]
        seg_ref, key_ref, lse_ref = rest[10:13]
        rest = rest[13 + len(earlier) :]
        outs = [ref.at[0] for ref in rest[:5]]
        q_all, k_all, k_turned, v_turned, g_all, result, dk_turned, dv_turned = rest[5:]
        me = here_ref[0]
        seq = me // heads
        for device, value in exchanged(refs, me):
            for half, place in enumerate(rows_of_device(device, block, blocks)):
                rows = value[half * block : (half + 1) * block]
                q_all[place] = rows[:, :HD]
                k_all[place] = rows[:, HD : 2 * HD]
                k_turned[:, place] = rows[:, HD : 2 * HD].T
                v_turned[:, place] = rows[:, 2 * HD :].T
        for device, value in exchanged(grad_refs, me):
            for half, place in enumerate(rows_of_device(device, block, blocks)):
                g_all[place] = value[half * block : (half + 1) * block]
        last = seq_len // step - 1
        for number in range(last, -1, -1):
            start, stop = number * step, (number + 1) * step
            segs = as_column(seg_ref[seq, :, start:stop])
            query, grad = q_all[start:stop], g_all[start:stop]
            scores = dot(query, k_turned[:, :stop]) * (scaler * LOG2E)
            scores = masked(scores, segs, key_ref, seq, start, stop)
            probs = jnp.exp2(scores - lse_ref[start:stop])
            grad_probs = dot(grad, v_turned[:, :stop])
            inner = jnp.sum(probs * grad_probs, axis=-1, keepdims=True)
            grad_scores = (probs * (grad_probs - inner)).astype(BF)
            dv_part = dot_tn(grad, probs.astype(BF))
            dk_part = dot_tn(query, grad_scores)
            if number == last:
                dv_turned[...] = dv_part
                dk_turned[...] = dk_part
            else:
                dv_turned[:, :stop] += dv_part
                dk_turned[:, :stop] += dk_part
            dq = dot(grad_scores, k_all[:stop]) * scaler
            result[start:stop, :HD] = dq.astype(BF)
        for number in range(last + 1):
            start, stop = number * step, (number + 1) * step
            result[start:stop, HD : 2 * HD] = (dk_turned[:, start:stop] * scaler).T.astype(BF)
            result[start:stop, 2 * HD :] = dv_turned[:, start:stop].T.astype(BF)

        def load(device):
            return jnp.concatenate(
                [result[place] for place in rows_of_device(device, block, blocks)], axis=0
            )

        emit_exchange(load, me, outs)

    shapes = exchange_shapes(tok_len, 3 * HD)
    args = [here, *received, *grads, seg_row, key_row, lse, *earlier]
    first = len(args) - len(earlier)
    return launch(
        body,
        operands_of(args),
        [pl.BlockSpec(memory_space=pltpu.SMEM)]
        + [whole_of(item.shape) for item in args[1:first]]
        + [pl.BlockSpec(memory_space=pl.ANY) for _ in earlier],
        [sds((count,) + item.shape) for item in shapes],
        [
            pl.BlockSpec((1,) + item.shape, lambda i, n=len(item.shape): (index,) + (0,) * n)
            for item in shapes
        ],
        [
            pltpu.VMEM((seq_len, HD), BF),
            pltpu.VMEM((seq_len, HD), BF),
            pltpu.VMEM((HD, seq_len), BF),
            pltpu.VMEM((HD, seq_len), BF),
            pltpu.VMEM((seq_len, HD), BF),
            pltpu.VMEM((seq_len, 3 * HD), BF),
            pltpu.VMEM((HD, seq_len), F32),
            pltpu.VMEM((HD, seq_len), F32),
        ],
        36 << 20,
        cost(5 * seq_len * seq_len * HD, 12 * seq_len * HD),
        "attention_back",
        after,
        grid=(1,),
        aliases={first + number: number for number in range(len(earlier))},
    )


def mix_heads(here, tp_here, received, weight, heads, direct, after=()):
    tok_len = received[0].shape[0]
    inner, width = weight.shape
    rows = len_units(received) * tok_len // heads
    size = rows // 4

    def body(here_ref, tp_ref, *rest):
        refs, weight_ref = rest[:5], rest[5]
        heads_ref, outs, held = rest[6], rest[7:11], rest[11]
        for unit_id, value in exchanged(refs, here_ref[0]):
            column = pl.multiple_of(unit_id % heads * HD, HD)
            heads_ref[rows_at(unit_id // heads * tok_len, tok_len), pl.ds(column, HD)] = value
        for start in range(0, width, 512):
            held[:, start : start + 512] = dot(
                heads_ref[...], weight_ref[:, start : start + 512]
            ).astype(BF)
        emit_messages(lambda place: held[place, :], tp_ref[0], outs, size)

    return run_kernel(
        body,
        [sds((rows, inner))] + message_shapes(size // 2, width, direct),
        [here, tp_here] + list(received) + [weight],
        flops=2 * rows * inner * width,
        scratch=[pltpu.VMEM((rows, width), BF)],
        after=after,
        name="mix_heads",
        limit=6,
    )


def len_units(received):
    return 2 * received[-1].shape[0]


def second_norm(sums, x_mine, mixer_bias, gain, shift, direct, after=()):
    size, width = x_mine.shape
    count = len(sums)

    def body(*rest):
        refs, (x_ref, bias_ref, gain_ref, shift_ref) = rest[:count], rest[count : count + 4]
        resid_ref, outs = rest[count + 4], rest[count + 5 :]
        resid = x_ref[...].astype(F32) + total_of(refs) + bias_ref[...]
        resid_ref[...] = resid
        unit, _ = normalized(resid)
        emit_shard((unit * gain_ref[...] + shift_ref[...]).astype(BF), outs)

    return run_kernel(
        body,
        [sds((size, width), F32)] + shard_shapes(size, width, direct),
        list(sums) + [x_mine, mixer_bias, gain, shift],
        name="second_norm",
        limit=8,
        after=after,
    )


def feed_forward(
    tp_here, pieces, cot, up_weight, up_bias, down_weight, earlier, index, count, direct, after=()
):
    rows, width = cot.shape
    hidden = up_weight.shape[1]
    size = rows // 4
    step = 512
    blocks = hidden // step

    def body(tp_ref, *rest):
        refs, rest = rest[: len(pieces)], rest[len(pieces) :]
        cot_ref, up_hbm, bias_ref, down_hbm = rest[:4]
        rest = rest[4 + len(earlier) :]
        norm_ref, act_ref, pre_ref, sum_ref, cot_sum_ref = rest[:5]
        feed_outs, grad_outs = rest[5:9], rest[9:13]
        up, down, held, sems = rest[13:]

        def part(number):
            return pl.ds(pl.multiple_of(number * step, step), step)

        def copies(number):
            place = part(number)
            return (
                pltpu.make_async_copy(up_hbm.at[:, place], up.at[:, place], sems.at[0, number]),
                pltpu.make_async_copy(down_hbm.at[place, :], down.at[place, :], sems.at[1, number]),
            )

        for number in range(blocks):
            for copy in copies(number):
                copy.start()

        def store(place, value):
            norm_ref[place, :] = value

        place_gathered(store, tp_ref[0], refs, size)
        cot_sum_ref[...] = jnp.sum(cot_ref[...].astype(F32), axis=0, keepdims=True)

        @pl.loop(0, blocks)
        def _(number):
            for copy in copies(number):
                copy.wait()
            place = part(number)
            pre = dot(norm_ref[...], up[:, place]) + bias_ref[:, place]
            grad_act = dot_nt(cot_ref[...], down[place, :])
            spread = 0.5 + 0.5 * lax.erf(pre * math.sqrt(0.5))
            dense = jnp.exp(-0.5 * pre * pre) * (1.0 / math.sqrt(2.0 * math.pi))
            act_ref[:, place] = (pre * spread).astype(BF)
            grad_pre = (grad_act * (spread + pre * dense)).astype(BF)
            pre_ref[:, place] = grad_pre
            sum_ref[:, place] = jnp.sum(grad_pre.astype(F32), axis=0, keepdims=True)

        @pl.loop(0, width // step)
        def _(number):
            place = part(number)
            held[:, place] = dot_nt(pre_ref[...], up[place, :]).astype(BF)

        emit_messages(lambda at: held[at, :], tp_ref[0], grad_outs, size)

        @pl.loop(0, width // step)
        def _(number):
            place = part(number)
            held[:, place] = dot(act_ref[...], down[:, place]).astype(BF)

        emit_messages(lambda at: held[at, :], tp_ref[0], [ref.at[0] for ref in feed_outs], size)

    message = (2, size // 2, width)
    args = [tp_here, *pieces, cot, up_weight, up_bias, down_weight, *earlier]
    first = len(args) - len(earlier)
    outs = [
        sds((rows, width)),
        sds((rows, hidden)),
        sds((rows, hidden)),
        sds((1, hidden), F32),
        sds((1, width), F32),
    ]
    messages = message_shapes(size // 2, width, direct)
    return launch(
        body,
        operands_of(args),
        [pl.BlockSpec(memory_space=pltpu.SMEM)]
        + [whole_of(piece.shape) for piece in pieces]
        + [cot.spec(), pl.BlockSpec(memory_space=pl.ANY), whole_of(up_bias.shape)]
        + [pl.BlockSpec(memory_space=pl.ANY)] * (1 + len(earlier)),
        outs + [sds((count,) + message)] * 4 + messages,
        [whole_of(item.shape) for item in outs]
        + [pl.BlockSpec((1,) + message, lambda i: (index, 0, 0, 0))] * 4
        + [whole_of(item.shape) for item in messages],
        [
            pltpu.VMEM((width, hidden), BF),
            pltpu.VMEM((hidden, width), BF),
            pltpu.VMEM((rows, width), BF),
            pltpu.SemaphoreType.DMA((2, blocks)),
        ],
        50 << 20,
        cost(8 * rows * width * hidden, 4 * width * hidden + 20 * rows * width),
        "feed_forward",
        after,
        grid=(1,),
        aliases={first + number: 5 + number for number in range(len(earlier))},
    )


def second_norm_back(sums, resid, cot_mine, gain, direct, after=()):
    size, width = resid.shape
    count = len(sums)

    def body(*rest):
        refs, (resid_ref, cot_ref, gain_ref) = rest[:count], rest[count : count + 3]
        grad_ref, gain_out, shift_out, *outs = rest[count + 3 :]
        back, gain_sum, shift_sum = norm_back(resid_ref[...], gain_ref[...], total_of(refs))
        grad = back + cot_ref[...].astype(F32)
        grad_ref[...] = grad
        emit_shard(grad.astype(BF), outs)
        gain_out[...] = gain_sum
        shift_out[...] = shift_sum

    return run_kernel(
        body,
        [sds((size, width), F32)]
        + [sds((1, width), F32)] * 2
        + shard_shapes(size, width, direct),
        list(sums) + [resid, cot_mine, gain],
        name="second_norm_back",
        limit=10,
        after=after,
    )


def first_norm_back(sums, x_mine, grad_resids, gain, after=()):
    count = len(x_mine)
    size, width = grad_resids[0].shape

    def body(*rest):
        refs, rest = rest[:4], rest[4:]
        x_refs, grad_refs, gain_ref = rest[:count], rest[count : 2 * count], rest[2 * count]
        gain_out, shift_out, *outs = rest[2 * count + 1 :]
        for index in range(count):
            back, gain_sum, shift_sum = norm_back(
                x_refs[index][...].astype(F32),
                gain_ref[...],
                total_of([ref.at[index] for ref in refs]),
            )
            emit_shard(
                (back + grad_refs[index][...]).astype(BF), [ref.at[index] for ref in outs]
            )
            gain_out[...] = gain_sum if index == 0 else gain_out[...] + gain_sum
            shift_out[...] = shift_sum if index == 0 else shift_out[...] + shift_sum

    return run_kernel(
        body,
        [sds((1, width), F32)] * 2
        + [sds((count,) + item.shape) for item in shard_shapes(size, width)],
        list(sums) + list(x_mine) + list(grad_resids) + [gain],
        name="first_norm_back",
        limit=10,
        after=after,
    )


def finish_outputs(sums, resids, bias, after=()):
    size, width = resids[0].shape
    half = size // 2
    count = len(resids)

    def body(*rest):
        refs, resid_refs, bias_ref = rest[:4], rest[4 : 4 + count], rest[4 + count]
        low_ref, high_ref = rest[5 + count :]
        for index in range(count):
            ours = [ref.at[index] for ref in refs]
            value = (resid_refs[index][...] + total_of(ours) + bias_ref[...]).astype(BF)
            low_ref[index] = value[:half]
            high_ref[index] = value[half:]

    return run_kernel(
        body,
        [sds((count, half, width))] * 2,
        list(sums) + list(resids) + [bias],
        after=after,
        name="finish_outputs",
        limit=8,
    )


def assemble_outputs(tp_here, pieces, dtype, after=()):
    count, half, width = pieces[0].shape
    size = 2 * half
    rows = 4 * size

    def block_of(shape):
        return pl.BlockSpec((1,) + shape[1:], lambda i, n=len(shape) - 1: (i,) + (0,) * n)

    def body(tp_ref, *rest):
        refs, out_ref = rest[:6], rest[6]

        def store(place, value):
            out_ref[0, place, :] = value.astype(dtype)

        place_gathered(store, tp_ref[0], [ref.at[0] for ref in refs], size)

    results, done = launch(
        body,
        [tp_here] + list(pieces),
        [pl.BlockSpec(memory_space=pltpu.SMEM)] + [block_of(piece.shape) for piece in pieces],
        [HBM((count, rows, width), dtype)],
        [block_of((count, rows, width))],
        (),
        24 << 20,
        cost(0, count * rows * width * 6),
        "assemble_outputs",
        after,
        grid=(count,),
    )
    return results[0], done


def widen(part, turned, after=()):
    rows, wide = part.shape

    def body(part_ref, out_ref):
        value = part_ref[...].astype(F32)
        out_ref[...] = value.T if turned else value

    shape = (wide, rows) if turned else (rows, wide)
    return run_kernel(body, [sds(shape, F32)], [part], after=after, name="widen", limit=6)


def widen_last(part, inner, after=()):
    rows, _ = part.shape

    def body(part_ref, proj_ref, mixer_ref):
        for number in range(3):
            place = slice(number * inner, (number + 1) * inner)
            proj_ref[number] = part_ref[:, place].astype(F32)
        mixer_ref[...] = part_ref[:, 3 * inner :].astype(F32).T

    return run_kernel(
        body,
        [sds((3, rows, inner), F32), sds((inner, rows), F32)],
        [part],
        after=after,
        name="widen",
        limit=6,
    )


def heads_back(here, tp_here, pieces, weight, tok_len, after=()):
    inner, width = weight.shape
    heads = inner // HD
    count = len(pieces)
    size = pieces[0].shape[0] * (1 if count == 4 else 2)
    rows = 4 * size

    def body(here_ref, tp_ref, *rest):
        refs, weight_ref, rest = rest[:count], rest[count], rest[count + 1 :]
        mix_ref, sum_ref, outs, held = rest[0], rest[1], rest[2:7], rest[7]

        def store(place, value):
            mix_ref[place, :] = value

        place_gathered(store, tp_ref[0], refs, size)
        sum_ref[...] = jnp.sum(mix_ref[...].astype(F32), axis=0, keepdims=True)
        value = dot_nt(mix_ref[...], weight_ref[...]).astype(BF)
        for head in range(heads):
            held[head] = value[:, head * HD : (head + 1) * HD]

        def load(unit_id):
            return held[unit_id % heads, rows_at(unit_id // heads * tok_len, tok_len), :]

        emit_exchange(load, here_ref[0], outs)

    return run_kernel(
        body,
        [sds((rows, width)), sds((1, width), F32)] + exchange_shapes(tok_len, HD),
        [here, tp_here] + list(pieces) + [weight],
        flops=2 * rows * inner * width,
        scratch=[pltpu.VMEM((heads, rows, HD), BF)],
        after=after,
        name="heads_back",
        limit=8,
    )


def project_back(here, tp_here, received, weight, after=()):
    count, tok_len, _ = received[0].shape
    _, width, inner = weight.shape
    heads = inner // HD
    rows = 2 * received[-1].shape[1] * tok_len // heads
    size = rows // 4

    def body(here_ref, tp_ref, *rest):
        refs, weight_ref, rest = rest[:5], rest[5], rest[6:]
        proj_refs, sum_ref, outs, held = rest[:count], rest[count], rest[-5:-1], rest[-1]
        for index, proj_ref in enumerate(proj_refs):
            for unit_id, value in exchanged([ref.at[index] for ref in refs], here_ref[0]):
                place = rows_at(unit_id // heads * tok_len, tok_len)
                for part in range(3):
                    column = pl.multiple_of(part * inner + unit_id % heads * HD, HD)
                    proj_ref[place, pl.ds(column, HD)] = value[:, part * HD : (part + 1) * HD]
            part_sum = jnp.sum(proj_ref[...].astype(F32), axis=0, keepdims=True)
            sum_ref[...] = part_sum if index == 0 else sum_ref[...] + part_sum
            for start in range(0, width, 512):
                value = dot_nt(proj_ref[:, :inner], weight_ref[0, start : start + 512])
                for part in range(1, 3):
                    value += dot_nt(
                        proj_ref[:, part * inner : (part + 1) * inner],
                        weight_ref[part, start : start + 512],
                    )
                held[:, start : start + 512] = value.astype(BF)
            emit_messages(
                lambda place: held[place, :], tp_ref[0], [ref.at[index] for ref in outs], size
            )

    return run_kernel(
        body,
        [sds((rows, 3 * inner))] * count
        + [sds((1, 3 * inner), F32)]
        + [sds((count,) + item.shape) for item in message_shapes(size // 2, width)],
        [here, tp_here] + list(received) + [weight],
        flops=6 * count * rows * inner * width,
        scratch=[pltpu.VMEM((rows, width), BF)],
        name="project_back",
        limit=10,
        after=after,
    )


def weight_grad(groups, here=None, after=()):
    count = len(groups[0][0])
    rows, tall = groups[0][0][0].shape
    widths = [rights[0].shape[1] for _, rights in groups]
    total = sum(widths)
    split = here is not None
    steps = 8 if split else 4
    step = tall // steps
    half = steps // 2

    def block_of(number, *fixed):
        if not split:
            return number
        core = fixed[0][0] & 1
        mine = number // half
        return 2 * (number % half) + (core ^ 1 ^ mine)

    def product(refs, store):
        start = 0
        for place, wide in enumerate(widths):
            ours = refs[2 * count * place : 2 * count * (place + 1)]
            value = dot_tn(ours[0][...], ours[count][...])
            for number in range(1, count):
                value += dot_tn(ours[number][...], ours[count + number][...])
            store(slice(start, start + wide), value.astype(BF))
            start += wide

    def body(*refs):
        if not split:
            out_ref = refs[-1]

            def store(place, value):
                out_ref[:, place] = value

            product(refs, store)
            return
        refs, other_ref, own_ref = refs[1:-2], refs[-2], refs[-1]
        number = pl.program_id(0)

        def into(ref):
            def store(place, value):
                ref[0, :, place] = value

            return store

        @pl.when(number < half)
        def _():
            product(refs, into(other_ref))

        @pl.when(number >= half)
        def _():
            product(refs, into(own_ref))

    args, in_specs = [], []
    for (lefts, rights), wide in zip(groups, widths):
        for item in lefts:
            if isinstance(item, Part):
                in_specs.append(
                    pl.BlockSpec(
                        (None, rows, step),
                        lambda i, *fixed, k=item.index: (k, 0, block_of(i, *fixed)),
                    )
                )
            else:
                in_specs.append(
                    pl.BlockSpec((rows, step), lambda i, *fixed: (0, block_of(i, *fixed)))
                )
        in_specs += [pl.BlockSpec((rows, wide), lambda *_: (0, 0))] * count
        args += list(lefts) + list(rights)
    if split:
        outs = [HBM((half, step, total), BF)] * 2
        out_specs = [
            pl.BlockSpec((1, step, total), lambda i, *_: (jnp.minimum(i, half - 1), 0, 0)),
            pl.BlockSpec((1, step, total), lambda i, *_: (jnp.maximum(i - half, 0), 0, 0)),
        ]
    else:
        outs = [HBM((tall, total), BF)]
        out_specs = [pl.BlockSpec((step, total), lambda i: (i, 0))]
    return launch(
        body,
        operands_of(args),
        in_specs,
        outs,
        out_specs,
        (),
        40 << 20,
        cost(
            2 * count * rows * tall * total,
            2 * (count * rows * (tall * len(groups) + total) + tall * total),
        ),
        "weight_grad",
        after,
        grid=(steps,),
        scalars=(here,) if split else (),
    )


def add_halves(own, got, after=()):
    def body(own_ref, got_ref, out_ref):
        out_ref[...] = (own_ref[...].astype(F32) + got_ref[...].astype(F32)).astype(BF)

    block_spec = pl.BlockSpec((1,) + own.shape[1:], lambda i: (i, 0, 0))
    return launch(
        body,
        operands_of([own, got]),
        [block_spec] * 2,
        [HBM(own.shape, BF)],
        [block_spec],
        (),
        16 << 20,
        cost(0, 6 * math.prod(own.shape)),
        "add_halves",
        after,
        grid=(own.shape[0],),
    )


def small_sums(values):
    here = lax.axis_index("ctx")
    step = values.shape[0] // 2
    while step:
        pair = values.reshape((2, step) + values.shape[1:])
        bit = (here // step) % 2
        keep = lax.dynamic_index_in_dim(pair, bit, 0, False)
        send = lax.dynamic_index_in_dim(pair, 1 - bit, 0, False)
        values = keep + xor_permute(send, "ctx", step)
        step //= 2
    return values[0]


def per_device_exchanged(
    inputs,
    segments,
    keep_mask,
    first_gain,
    first_shift,
    proj_weight,
    proj_bias,
    mixer_weight,
    mixer_bias,
    second_gain,
    second_shift,
    up_weight,
    up_bias,
    down_weight,
    down_bias,
    out_cotangent,
):
    ctx_count = lax.axis_size("ctx")
    micro_count, seq_count, tok_len, width = inputs.shape
    inner = proj_bias.shape[1]
    heads = inner // HD
    rows = seq_count * tok_len
    here = lax.axis_index("ctx").astype(jnp.int32).reshape(1)
    tp_here = lax.axis_index("tp").astype(jnp.int32).reshape(1)
    weight_three = jnp.transpose(proj_weight, (1, 0, 2))
    bias_three = jnp.stack([proj_bias[0], jnp.zeros_like(proj_bias[0]), proj_bias[1]])
    x_all = inputs.reshape(micro_count, rows, width)
    cot_all = out_cotangent.reshape(micro_count, rows, width)
    key_rows = jnp.where(keep_mask > 0, segments, -1)[:, :, None, :]
    gain_one, shift_one = first_gain[None], first_shift[None]
    gain_two, shift_two = second_gain[None], second_shift[None]
    mix_bias, low_bias, high_bias = mixer_bias[None], down_bias[None], up_bias[None]
    micro = range(micro_count)

    key_rows = [key_rows[index] for index in micro]
    seg_rows = [segments[index][:, None, :] for index in micro]
    cots = [Part(cot_all, index) for index in micro]
    size = rows // lax.axis_size("tp")
    start = tp_here[0] * size
    x_mine = [lax.dynamic_slice(x_all, (index, start, 0), (1, size, width))[0] for index in micro]
    cot_mine = [
        lax.dynamic_slice(cot_all, (index, start, 0), (1, size, width))[0] for index in micro
    ]

    chips = [[core + 2 * chip for chip in range(ctx_count // 2)] for core in range(2)]

    def scattered(part):
        return lax.psum_scatter(part, "ctx", scatter_dimension=0, tiled=True)

    def scattered_chips(part):
        part = part.reshape(-1, part.shape[2])
        return lax.psum_scatter(
            part, "ctx", scatter_dimension=0, axis_index_groups=chips, tiled=True
        )

    def until(items, *points):
        held, _ = lax.optimization_barrier((items, points))
        return held

    norm_one, received, lses, heads_low, resids = [], [], [], [], []

    def project_micro(index, done):
        (normed, *sent), done = project(
            here, x_all, index, gain_one, shift_one, weight_three, bias_three, tok_len, after=done
        )
        norm_one.append(normed)
        return exchange_chips(*sent), done

    def attend_micro(index, got, done):
        received.append(got)
        (*sent, lse), done = attention(
            here, got, seg_rows[index], key_rows[index], heads, after=done
        )
        lses.append(lse)
        return exchange_chips(*sent), done

    def mix_micro(got, direct, done):
        (mixed, *messages), done = mix_heads(
            here, tp_here, got, mixer_weight, heads, direct, after=done
        )
        heads_low.append(mixed)
        return messages, done

    def norm_micro(index, sums, direct, done):
        (resid, *shard), done = second_norm(
            sums, x_mine[index], mix_bias, gain_two, shift_two, direct, after=done
        )
        resids.append(resid)
        return shard if direct else gather_first(shard), done

    norm_two, acts, grad_pres, up_sums, cot_sums = [], [], [], [], []

    def feed_micro(index, pieces, feeds, direct, done):
        (normed, act, grad_pre, up_sum, cot_sum, *messages), done = feed_forward(
            tp_here,
            pieces,
            cots[index],
            up_weight,
            high_bias,
            down_weight,
            feeds,
            index,
            micro_count,
            direct,
            after=done,
        )
        norm_two.append(normed)
        acts.append(act)
        grad_pres.append(grad_pre)
        up_sums.append(up_sum)
        cot_sums.append(cot_sum)
        messages, ours = messages[:4], messages[4:]
        return messages, reduce_direct(ours) if direct else ours, done

    grad_resids, gain_twos, shift_twos = [], [], []
    grad_mixes, mix_sums, states = [], [], []

    def norm_back_micro(index, sums, done):
        (grad_resid, gain_sum, shift_sum, *shard), done = second_norm_back(
            sums, resids[index], cot_mine[index], gain_two, False, after=done
        )
        grad_resids.append(grad_resid)
        gain_twos.append(gain_sum)
        shift_twos.append(shift_sum)
        return gather_first(shard), done

    def heads_back_micro(index, pieces, done):
        (grad_mix, mix_sum, *sent), done = heads_back(
            here, tp_here, pieces, mixer_weight, tok_len, after=done
        )
        grad_mixes.append(grad_mix)
        mix_sums.append(mix_sum)
        states.append(exchange_chips(*sent))
        return done

    def attend_back_micro(index, got, earlier, done):
        return attention_back(
            here,
            received[index],
            got,
            seg_rows[index],
            key_rows[index],
            lses[index],
            heads,
            earlier,
            index,
            micro_count,
            after=done,
        )

    state_a, done = project_micro(0, ())
    state_b, done = project_micro(1, done)
    got, done = exchange_cores(state_a, done)
    state_a, done = attend_micro(0, got, done)
    got, done = exchange_cores(state_b, done)
    state_b, done = attend_micro(1, got, done)
    got, done = exchange_cores(state_a, done)
    messages, done = mix_micro(got, False, done)
    sums_a, done = reduce_second(reduce_first(messages), done)
    got, done = exchange_cores(state_b, done)
    messages, done = mix_micro(got, False, done)
    state_b = reduce_first(messages)
    state_a, done = norm_micro(0, sums_a, False, done)
    pieces_a, done = gather_second(state_a, done)
    sums_b, done = reduce_second(state_b, done)
    state_b, done = norm_micro(1, sums_b, True, done)
    pieces_b = gather_direct(state_b[0])
    feeds, sums_a, done = feed_micro(0, pieces_a, [], True, done)
    feeds, messages, done = feed_micro(1, pieces_b, feeds, False, done)

    state_b = reduce_first(messages)
    state_a, done = norm_back_micro(0, sums_a, done)
    (down_part,), done = weight_grad([(cots, acts)], after=done)
    pieces_a, done = gather_second(state_a, done)
    sums_b, done = reduce_second(state_b, done)
    down_grad = scattered(until(down_part, done))
    done = heads_back_micro(0, pieces_a, done)
    state_b, done = norm_back_micro(1, sums_b, done)
    pieces_b, done = gather_second(state_b, done)
    (sent, own), done = weight_grad([(norm_two, grad_pres)], here, after=done)
    got_a, done = exchange_cores(states[0], done)
    done = heads_back_micro(1, pieces_b, done)
    state_feed = reduce_first(until(feeds, done))
    sent_back, done = attend_back_micro(0, got_a, [], done)
    got_b, done = exchange_cores(states[1], done)
    sums_feed, done = reduce_second(state_feed, done)
    got_up = xor_permute(until(sent, done), "ctx", 1)
    sent_back, done = attend_back_micro(1, got_b, sent_back, done)
    state_back = exchange_chips(*sent_back)
    halves, done = finish_outputs(sums_feed, resids, low_bias, after=done)
    (up_part,), done = add_halves(own, got_up, after=done)
    pieces_out, done = gather_second(gather_first(halves), done)
    got, done = exchange_cores(state_back, done)
    outputs, done = assemble_outputs(tp_here, pieces_out, BF, after=done)
    up_grad = scattered_chips(until(up_part, done))
    (*grad_projs, proj_sum, first, second, third, fourth), done = project_back(
        here, tp_here, got, weight_three, after=done
    )
    state_one = reduce_first((first, second, third, fourth))
    last = [(norm_one, grad_projs), (grad_mixes, heads_low)]
    (sent, own), done = weight_grad(last, here, after=done)
    sums_one, done = reduce_second(state_one, done)
    got_last = xor_permute(until(sent, done), "ctx", 1)
    (last_part,), done = add_halves(own, got_last, after=done)
    (gain_sum, shift_sum, *halves), done = first_norm_back(
        sums_one, x_mine, grad_resids, gain_one, after=done
    )
    last_grad = scattered_chips(until(last_part, done))
    pieces_in, done = gather_second(gather_first(halves), done)
    gain_ones, shift_ones, proj_sums = [gain_sum], [shift_sum], [proj_sum]
    (down_grad,), done = widen(down_grad, True, after=done)
    input_grad, done = assemble_outputs(tp_here, pieces_in, F32, after=done)
    (up_grad,), done = widen(up_grad, False, after=done)
    (proj_grad, mixer_grad), done = widen_last(last_grad, inner, after=done)
    proj_grad = jnp.transpose(proj_grad, (1, 0, 2))

    def over_micro(items):
        return sum(items[1:], items[0]).reshape(ctx_count, -1)

    proj_sum = sum(proj_sums[1:], proj_sums[0]).reshape(3, ctx_count, -1)
    pair_sum = jnp.concatenate([proj_sum[0], proj_sum[2]], axis=1)
    share = width // ctx_count
    pair_sum = jnp.pad(pair_sum, ((0, 0), (0, share - pair_sum.shape[1])))
    kinds = [
        over_micro(gain_ones),
        over_micro(shift_ones),
        over_micro(gain_twos),
        over_micro(shift_twos),
        over_micro(mix_sums),
        over_micro(cot_sums),
        over_micro(up_sums),
        pair_sum,
    ]
    small = small_sums(jnp.stack(kinds, axis=1))
    norms = small[:4]
    for step in (1, 2):
        norms = norms + xor_permute(norms, "tp", step)
    proj_bias_grad = small[7, : 2 * inner // ctx_count].reshape(2, -1)
    return (
        outputs.reshape(inputs.shape),
        input_grad.reshape(inputs.shape),
        norms[0],
        norms[1],
        proj_grad,
        proj_bias_grad,
        mixer_grad,
        small[4],
        norms[2],
        norms[3],
        up_grad,
        small[6],
        down_grad,
        small[5],
    )


def plan_for(mesh):
    sizes = dict(mesh.shape)

    def chosen(*args):
        micro, seq_count, _, width = args[0].shape
        units = seq_count * args[6].shape[1] // HD
        fits = sizes["ctx"] == 8 and sizes["tp"] == 4 and units == sizes["ctx"]
        fits = fits and args[12].shape[0] == width and micro == 2
        return (per_device_exchanged if fits else per_device)(*args)

    return chosen


def solution(mesh):
    in_specs = (
        P(None, None, "ctx", None),
        P(),
        P(),
        P(),
        P(),
        P(None, None, "tp"),
        P(None, "tp"),
        P("tp", None),
        P(),
        P(),
        P(),
        P(None, "tp"),
        P("tp"),
        P("tp", None),
        P(),
        P(None, None, "ctx", None),
    )
    out_specs = (
        P(None, None, "ctx", None),
        P(None, None, "ctx", None),
        P("ctx"),
        P("ctx"),
        P("ctx", None, "tp"),
        P(None, ("tp", "ctx")),
        P("tp", "ctx"),
        P("ctx"),
        P("ctx"),
        P("ctx"),
        P("ctx", "tp"),
        P(("tp", "ctx")),
        P("tp", "ctx"),
        P("ctx"),
    )
    return jax.shard_map(
        plan_for(mesh), mesh=mesh, in_specs=in_specs, out_specs=out_specs, check_vma=False
    )
```

```python
import math

import jax
import jax.numpy as jnp
from jax import lax
from jax.experimental import pallas as pl
from jax.experimental.pallas import tpu as pltpu
from jax.sharding import PartitionSpec as P

HD = 128


def storage_order(values, part_count):
    leading = values.shape[:-1]
    blocks = values.reshape(leading + (2 * part_count, -1))
    front_half = blocks[..., :part_count, :]
    back_half = jnp.flip(blocks[..., part_count:, :], axis=-2)
    return jnp.stack([front_half, back_half], axis=-2).reshape(leading + (-1,))


def layer_norm(values, norm_gain, norm_shift):
    center = values - jnp.mean(values, axis=-1, keepdims=True)
    spread = jnp.mean(center * center, axis=-1, keepdims=True)
    return center * lax.rsqrt(spread + 1e-05) * norm_gain + norm_shift


def gelu_exact(values):
    return jax.nn.gelu(values, approximate=False)


def split_heads(rows, heads_here):
    return rows.reshape(rows.shape[0], rows.shape[1], heads_here, -1)


def scores_of(queries, key_all, allowed, heads_here, scaler):
    raw = (
        jnp.einsum(
            "sqhd,skhd->shqk",
            split_heads(queries, heads_here),
            split_heads(key_all, heads_here),
            preferred_element_type=jnp.float32,
        )
        * scaler
    )
    return jnp.where(allowed[:, None], raw, -1000000000.0)


def attend(queries, key_all, value_all, allowed, heads_here, scaler):
    masked = scores_of(queries, key_all, allowed, heads_here, scaler)
    top = jnp.max(masked, axis=-1, keepdims=True)
    raised = jnp.exp(masked - top)
    totals = jnp.sum(raised, axis=-1, keepdims=True)
    probs = raised / totals
    mixed = jnp.einsum(
        "shqk,skhd->sqhd",
        probs.astype(jnp.bfloat16),
        split_heads(value_all, heads_here),
        preferred_element_type=jnp.float32,
    )
    return (mixed.reshape(queries.shape), top + jnp.log(totals))


def attend_back(queries, key_all, value_all, allowed, log_total, grad_heads, heads_here, scaler):
    masked = scores_of(queries, key_all, allowed, heads_here, scaler)
    probs = jnp.exp(masked - log_total)
    grad_four = split_heads(grad_heads, heads_here)
    grad_value = jnp.einsum(
        "shqk,sqhd->skhd", probs.astype(jnp.bfloat16), grad_four, preferred_element_type=jnp.float32
    )
    grad_probs = jnp.einsum(
        "sqhd,skhd->shqk",
        grad_four,
        split_heads(value_all, heads_here),
        preferred_element_type=jnp.float32,
    )
    inner_sum = jnp.sum(probs * grad_probs, axis=-1, keepdims=True)
    grad_scores = (probs * (grad_probs - inner_sum)).astype(jnp.bfloat16)
    grad_query = (
        jnp.einsum(
            "shqk,skhd->sqhd",
            grad_scores,
            split_heads(key_all, heads_here),
            preferred_element_type=jnp.float32,
        )
        * scaler
    )
    grad_key = (
        jnp.einsum(
            "shqk,sqhd->skhd",
            grad_scores,
            split_heads(queries, heads_here),
            preferred_element_type=jnp.float32,
        )
        * scaler
    )
    return (
        grad_query.reshape(queries.shape),
        grad_key.reshape(key_all.shape),
        grad_value.reshape(value_all.shape),
    )


def reduce_grads(grads):
    return (
        lax.psum_scatter(
            grads[0].astype(jnp.bfloat16), "ctx", scatter_dimension=0, tiled=True
        ).astype(jnp.float32),
        lax.psum_scatter(
            grads[1].astype(jnp.bfloat16), "ctx", scatter_dimension=0, tiled=True
        ).astype(jnp.float32),
        lax.psum_scatter(
            grads[2].astype(jnp.bfloat16), "ctx", scatter_dimension=0, tiled=True
        ).astype(jnp.float32),
        lax.psum_scatter(
            grads[3].astype(jnp.bfloat16), "ctx", scatter_dimension=1, tiled=True
        ).astype(jnp.float32),
        lax.psum_scatter(
            grads[4].astype(jnp.bfloat16), "ctx", scatter_dimension=1, tiled=True
        ).astype(jnp.float32),
        lax.psum_scatter(
            grads[5].astype(jnp.bfloat16), "ctx", scatter_dimension=0, tiled=True
        ).astype(jnp.float32),
        lax.psum_scatter(
            grads[6].astype(jnp.bfloat16), "ctx", scatter_dimension=0, tiled=True
        ).astype(jnp.float32),
        lax.psum_scatter(
            grads[7].astype(jnp.bfloat16), "ctx", scatter_dimension=0, tiled=True
        ).astype(jnp.float32),
        lax.psum_scatter(
            grads[8].astype(jnp.bfloat16), "ctx", scatter_dimension=0, tiled=True
        ).astype(jnp.float32),
        lax.psum_scatter(
            grads[9].astype(jnp.bfloat16), "ctx", scatter_dimension=0, tiled=True
        ).astype(jnp.float32),
        lax.psum_scatter(
            grads[10].astype(jnp.bfloat16), "ctx", scatter_dimension=1, tiled=True
        ).astype(jnp.float32),
        lax.psum_scatter(
            grads[11].astype(jnp.bfloat16), "ctx", scatter_dimension=0, tiled=True
        ).astype(jnp.float32),
    )


def per_device(
    inputs,
    segments,
    keep_mask,
    first_gain,
    first_shift,
    proj_weight,
    proj_bias,
    mixer_weight,
    mixer_bias,
    second_gain,
    second_shift,
    up_weight,
    up_bias,
    down_weight,
    down_bias,
    out_cotangent,
):
    ctx_count = lax.axis_size("ctx")
    micro_count, seq_count, tok_len, model_width = inputs.shape
    inner_width = proj_bias.shape[1]
    heads_here = inner_width // HD
    scaler = 1.0 / math.sqrt(HD)
    seq_len = tok_len * ctx_count
    places = storage_order(jnp.arange(seq_len, dtype=jnp.int32), ctx_count)
    offset = lax.axis_index("ctx") * tok_len
    my_places = lax.dynamic_slice_in_dim(places, offset, tok_len, 0)
    seg_store = storage_order(segments, ctx_count)
    keep_store = storage_order(keep_mask, ctx_count)
    proj_flat = proj_weight.reshape(model_width, 3 * inner_width)
    bias_three = jnp.stack([proj_bias[0], jnp.zeros_like(proj_bias[0]), proj_bias[1]])
    causal = places[None, :] <= my_places[:, None]
    itself = places[None, :] == my_places[:, None]
    shaped_like = (
        first_gain,
        first_shift,
        proj_weight,
        proj_bias,
        mixer_weight,
        mixer_bias,
        second_gain,
        second_shift,
        up_weight,
        up_bias,
        down_weight,
        down_bias,
    )
    running = tuple((jnp.zeros(item.shape, jnp.float32) for item in shaped_like))
    out_list = []
    grad_list = []
    for micro_index in range(micro_count):
        x_now = inputs[micro_index].astype(jnp.float32)
        seg_keys = seg_store[micro_index]
        seg_mine = lax.dynamic_slice_in_dim(seg_keys, offset, tok_len, 1)
        visible = (keep_store[micro_index] > 0)[:, None, :] | itself[None]
        allowed = causal[None] & (seg_keys[:, None, :] == seg_mine[:, :, None]) & visible
        normed_one = layer_norm(x_now, first_gain, first_shift).astype(jnp.bfloat16)
        projected = jnp.einsum(
            "std,dc->stc", normed_one, proj_flat, preferred_element_type=jnp.float32
        )
        projected = (projected.reshape(seq_count, tok_len, 3, inner_width) + bias_three).astype(
            jnp.bfloat16
        )
        queries = projected[:, :, 0]
        key_here = projected[:, :, 1]
        value_here = projected[:, :, 2]
        key_all, value_all = (
            lax.all_gather(key_here, "ctx", axis=1, tiled=True),
            lax.all_gather(value_here, "ctx", axis=1, tiled=True),
        )
        heads_out, log_total = attend(queries, key_all, value_all, allowed, heads_here, scaler)
        heads_low = heads_out.astype(jnp.bfloat16)
        mixed_part = jnp.einsum(
            "stn,nd->std", heads_low, mixer_weight, preferred_element_type=jnp.float32
        )
        resid = (
            x_now + lax.psum(mixed_part.astype(jnp.bfloat16), "tp").astype(jnp.float32) + mixer_bias
        )
        normed_two = layer_norm(resid, second_gain, second_shift).astype(jnp.bfloat16)
        pre_act = (
            jnp.einsum("std,df->stf", normed_two, up_weight, preferred_element_type=jnp.float32)
            + up_bias
        )
        act_low = gelu_exact(pre_act).astype(jnp.bfloat16)
        feed_part = jnp.einsum(
            "stf,fd->std", act_low, down_weight, preferred_element_type=jnp.float32
        )
        feed = lax.psum(feed_part.astype(jnp.bfloat16), "tp").astype(jnp.float32) + down_bias
        out_list.append((resid + feed).astype(jnp.bfloat16))
        cot_low = out_cotangent[micro_index]
        cot_full = cot_low.astype(jnp.float32)
        down_bias_part = jnp.sum(cot_full, axis=(0, 1))
        down_part = jnp.einsum("stf,std->fd", act_low, cot_low, preferred_element_type=jnp.float32)
        grad_act = jnp.einsum(
            "std,fd->stf", cot_low, down_weight, preferred_element_type=jnp.float32
        )
        grad_pre = jax.vjp(gelu_exact, pre_act)[1](grad_act)[0].astype(jnp.bfloat16)
        up_part = jnp.einsum(
            "std,stf->df", normed_two, grad_pre, preferred_element_type=jnp.float32
        )
        up_bias_part = jnp.sum(grad_pre.astype(jnp.float32), axis=(0, 1))
        grad_two_part = jnp.einsum(
            "stf,df->std", grad_pre, up_weight, preferred_element_type=jnp.float32
        )
        grad_two = lax.psum(grad_two_part.astype(jnp.bfloat16), "tp").astype(jnp.float32)
        resid_part, second_gain_part, second_shift_part = jax.vjp(
            layer_norm, resid, second_gain, second_shift
        )[1](grad_two)
        grad_resid = cot_full + resid_part
        grad_mix = grad_resid.astype(jnp.bfloat16)
        mixer_bias_part = jnp.sum(grad_mix.astype(jnp.float32), axis=(0, 1))
        mixer_part = jnp.einsum(
            "stn,std->nd", heads_low, grad_mix, preferred_element_type=jnp.float32
        )
        grad_heads = jnp.einsum(
            "std,nd->stn", grad_mix, mixer_weight, preferred_element_type=jnp.float32
        ).astype(jnp.bfloat16)
        key_back, value_back = (key_all, value_all)
        grad_query, grad_key, grad_value = attend_back(
            queries, key_back, value_back, allowed, log_total, grad_heads, heads_here, scaler
        )
        key_share, value_share = (
            lax.psum_scatter(
                grad_key.astype(jnp.bfloat16), "ctx", scatter_dimension=1, tiled=True
            ).astype(jnp.float32),
            lax.psum_scatter(
                grad_value.astype(jnp.bfloat16), "ctx", scatter_dimension=1, tiled=True
            ).astype(jnp.float32),
        )
        grad_proj = jnp.stack([grad_query, key_share, value_share], axis=2).astype(jnp.bfloat16)
        proj_part = jnp.einsum(
            "std,stcn->dcn", normed_one, grad_proj, preferred_element_type=jnp.float32
        )
        proj_sums = jnp.sum(grad_proj.astype(jnp.float32), axis=(0, 1))
        proj_bias_part = jnp.stack([proj_sums[0], proj_sums[2]])
        grad_one_part = jnp.einsum(
            "stc,dc->std",
            grad_proj.reshape(seq_count, tok_len, 3 * inner_width),
            proj_flat,
            preferred_element_type=jnp.float32,
        )
        grad_one = lax.psum(grad_one_part.astype(jnp.bfloat16), "tp").astype(jnp.float32)
        input_part, first_gain_part, first_shift_part = jax.vjp(
            layer_norm, x_now, first_gain, first_shift
        )[1](grad_one)
        grad_list.append(grad_resid + input_part)
        batch_grads = (
            first_gain_part,
            first_shift_part,
            proj_part,
            proj_bias_part,
            mixer_part,
            mixer_bias_part,
            second_gain_part,
            second_shift_part,
            up_part,
            up_bias_part,
            down_part,
            down_bias_part,
        )
        running = tuple((earlier + adding for earlier, adding in zip(running, batch_grads)))
    final = reduce_grads(running)
    return (
        jnp.stack(out_list),
        jnp.stack(grad_list),
        final[0],
        final[1],
        final[2],
        final[3],
        final[4],
        final[5],
        final[6],
        final[7],
        final[8],
        final[9],
        final[10],
        final[11],
    )


BF = jnp.bfloat16
F32 = jnp.float32
LOG2E = 1.4426950408889634
LOW = -1e30
ORDERS = ((1, 2), (2, 1))
COST_SHARE = 1.0


def xor_permute(values, axis, step):
    count = lax.axis_size(axis)
    return lax.ppermute(values, axis, [(i, i ^ step) for i in range(count)])


def sds(shape, dtype=BF):
    return jax.ShapeDtypeStruct(tuple(shape), dtype)


def cost(flops, moved, exps=0):
    return pl.CostEstimate(
        flops=int(flops * COST_SHARE),
        bytes_accessed=int(moved * COST_SHARE),
        transcendentals=int(exps * COST_SHARE),
    )


HBM = pltpu.MemorySpace.HBM


def launch(
    body,
    args,
    in_specs,
    outs,
    out_specs,
    scratch,
    limit,
    cost,
    name,
    after,
    grid=(),
    aliases=None,
    scalars=(),
):
    first, last = len(after), len(after) + len(args) + len(outs)

    def inner(*refs):
        fixed, refs = refs[: len(scalars)], refs[len(scalars) :]
        body(*fixed, *refs[first:last], *refs[last + 1 :])

    token = pl.BlockSpec(memory_space=HBM)
    *results, done = pl.pallas_call(
        inner,
        grid_spec=pltpu.PrefetchScalarGridSpec(
            num_scalar_prefetch=len(scalars),
            grid=grid,
            in_specs=[token] * first + list(in_specs),
            out_specs=(*out_specs, token),
            scratch_shapes=list(scratch),
        ),
        out_shape=(*outs, sds((8, 128), F32)),
        input_output_aliases={first + key: value for key, value in (aliases or {}).items()},
        compiler_params=pltpu.CompilerParams(vmem_limit_bytes=limit),
        cost_estimate=cost,
        name=name,
    )(*scalars, *after, *args)
    return results, (done,)


class Part:
    def __init__(self, array, index):
        self.array, self.index = array, index
        self.shape, self.dtype = array.shape[1:], array.dtype

    def spec(self):
        index, rest = self.index, (0,) * len(self.shape)
        return pl.BlockSpec((None,) + self.shape, lambda *_: (index,) + rest)


def operands_of(args):
    arrays = [arg.array if isinstance(arg, Part) else arg for arg in args]
    return [array if array.dtype == jnp.int32 else pinned(array) for array in arrays]


def pinned(array):
    return pltpu.with_memory_space_constraint(array, HBM)


def run_kernel(body, outs, args, flops=0, exps=0, scratch=(), limit=8, name=None, after=(), in_hbm=()):
    specs = []
    moved = 0
    for place, arg in enumerate(args):
        if arg.dtype == jnp.int32 and math.prod(arg.shape) <= 8:
            specs.append(pl.BlockSpec(memory_space=pltpu.SMEM))
        elif place in in_hbm:
            specs.append(pl.BlockSpec(memory_space=HBM))
        else:
            specs.append(pl.BlockSpec(memory_space=pltpu.VMEM))
            moved += math.prod(arg.shape) * arg.dtype.itemsize
    moved += sum(math.prod(o.shape) * o.dtype.itemsize for o in outs)
    kept = [item for item in scratch if item.dtype in (BF, F32)]
    held = moved + sum(math.prod(item.shape) * item.dtype.itemsize for item in kept)
    return launch(
        body,
        [pinned(arg) if place in in_hbm else arg for place, arg in enumerate(args)],
        specs,
        outs,
        [pl.BlockSpec(memory_space=pltpu.VMEM) for _ in outs],
        scratch,
        held + (limit << 20),
        cost(flops, moved, exps),
        name,
        after,
    )


def whole_of(shape):
    return pl.BlockSpec(shape, lambda *_, n=len(shape): (0,) * n)


def rows_at(start, count):
    return pl.ds(pl.multiple_of(start, count), count)


def reduce_first(messages):
    return [
        (messages[2 * part + 1], xor_permute(messages[2 * part], "tp", first))
        for part, (first, _) in enumerate(ORDERS)
    ]


def reduce_second(state, after=()):
    shape = state[0][0].shape[:-3] + state[0][0].shape[-2:]

    def body(*refs):
        for part in range(2):
            keep, got = refs[2 * part : 2 * part + 2]
            refs[4 + part][...] = keep[..., 0, :, :].astype(F32) + got[..., 0, :, :].astype(F32)
            value = keep[..., 1, :, :].astype(F32) + got[..., 1, :, :].astype(F32)
            refs[6 + part][...] = value.astype(BF)

    (*rest, low, high), done = run_kernel(
        body,
        [sds(shape, F32)] * 2 + [sds(shape)] * 2,
        [item for pair in state for item in pair],
        after=after,
        name="reduce_middle",
        limit=4,
    )
    sums = []
    for part, (_, second) in enumerate(ORDERS):
        sums += [rest[part], xor_permute((low, high)[part], "tp", second)]
    return sums, done


def reduce_direct(messages):
    mine, *sent = messages
    return [mine] + [xor_permute(item, "tp", 1 + step) for step, item in enumerate(sent)]


def gather_first(halves):
    return [
        (halves[part], xor_permute(halves[part], "tp", first))
        for part, (first, _) in enumerate(ORDERS)
    ]


def gather_second(state, after=()):
    half = state[0][0].shape
    pair_shape = half[:-2] + (2,) + half[-2:]

    def body(*refs):
        for part in range(2):
            for place in range(2):
                refs[4 + part][..., place, :, :] = refs[2 * part + place][...]

    pairs, done = run_kernel(
        body,
        [sds(pair_shape)] * 2,
        [item for pair in state for item in pair],
        after=after,
        name="gather_middle",
        limit=3,
    )
    pieces = []
    for part, (_, second) in enumerate(ORDERS):
        pieces += [*state[part], xor_permute(pairs[part], "tp", second)]
    return pieces, done


def gather_direct(mine):
    return [mine] + [xor_permute(mine, "tp", step) for step in (1, 2, 3)]


def total_of(refs):
    if refs[0].dtype == BF:
        return sum([ref[...].astype(F32) for ref in refs[1:]], refs[0][...].astype(F32))
    halves = [refs[2 * part][...] + refs[2 * part + 1][...].astype(F32) for part in range(2)]
    return jnp.concatenate(halves, axis=0)


def place_gathered(store, tp_here, refs, size):
    if len(refs) == 4:
        for step, ref in enumerate(refs):
            store(rows_at((tp_here ^ step) * size, size), ref[...])
        return
    half = size // 2
    for part, (first, second) in enumerate(ORDERS):
        mine, near, far = refs[3 * part : 3 * part + 3]
        parts = ((0, mine[...]), (first, near[...]), (second, far[0]), (first | second, far[1]))
        for step, value in parts:
            store(rows_at((tp_here ^ step) * size + part * half, half), value)


def emit_messages(load, tp_here, refs, size):
    if refs[0].shape[-2] == size:
        for step, ref in enumerate(refs):
            ref[...] = load(rows_at((tp_here ^ step) * size, size))
        return
    half = size // 2
    for part, (first, second) in enumerate(ORDERS):
        send, keep = refs[2 * part], refs[2 * part + 1]
        for ref, steps in ((send, (first, first | second)), (keep, (0, second))):
            for place, step in enumerate(steps):
                ref[place] = load(rows_at((tp_here ^ step) * size + part * half, half))


def emit_shard(value, refs):
    rows = value.shape[0] // len(refs)
    for place, ref in enumerate(refs):
        ref[...] = value[place * rows : (place + 1) * rows]


def shard_shapes(size, width, direct=False):
    return [sds((size, width))] if direct else [sds((size // 2, width))] * 2


def message_shapes(half, width, direct=False):
    return [sds((2 * half, width) if direct else (2, half, width))] * 4


def exchange_chips(local, cross, first, second, third):
    got = [
        xor_permute(item, "ctx", 2 * (place + 1))
        for place, item in enumerate((first, second, third))
    ]
    return [local, cross] + got


def exchange_cores(state, after):
    local, cross, *got = state

    lead = cross.shape[:-2]

    def body(cross_ref, first_ref, second_ref, third_ref, out_ref):
        out_ref[..., 0, :, :] = cross_ref[...]
        for place, ref in enumerate((first_ref, second_ref, third_ref)):
            out_ref[..., place + 1, :, :] = ref[..., 1, :, :]

    (packed,), done = run_kernel(
        body, [sds(lead + (4,) + cross.shape[-2:])], [cross] + got, after=after, limit=2, name="pack"
    )
    return [local] + got + [xor_permute(packed, "ctx", 1)], done


def exchanged(refs, here):
    local, first, second, third, packed = refs
    return (
        (here, local[...]),
        (here ^ 1, packed[0]),
        (here ^ 2, first[0]),
        (here ^ 3, packed[1]),
        (here ^ 4, second[0]),
        (here ^ 5, packed[2]),
        (here ^ 6, third[0]),
        (here ^ 7, packed[3]),
    )


def emit_exchange(load, here, refs):
    local, cross, first, second, third = refs
    local[...] = load(here)
    cross[...] = load(here ^ 1)
    for place, ref in enumerate((first, second, third)):
        other = here ^ (2 * (place + 1))
        ref[0] = load(other)
        ref[1] = load(other ^ 1)


def exchange_shapes(rows, width):
    return [sds((rows, width)), sds((rows, width))] + [sds((2, rows, width))] * 3


def normalized(values):
    center = values - jnp.mean(values, axis=-1, keepdims=True)
    spread = jnp.mean(center * center, axis=-1, keepdims=True)
    root = lax.rsqrt(spread + 1e-05)
    return center * root, root


def norm_back(values, gain, grad):
    unit, root = normalized(values)
    scaled = grad * gain
    back = root * (
        scaled
        - jnp.mean(scaled, axis=-1, keepdims=True)
        - unit * jnp.mean(scaled * unit, axis=-1, keepdims=True)
    )
    gain_sum = jnp.sum(grad * unit, axis=0, keepdims=True)
    shift_sum = jnp.sum(grad, axis=0, keepdims=True)
    return back, gain_sum, shift_sum


def dot(left, right):
    return jnp.dot(left, right, preferred_element_type=F32)


def dot_nt(left, right):
    return lax.dot_general(left, right, (((1,), (1,)), ((), ())), preferred_element_type=F32)


def dot_tn(left, right):
    return lax.dot_general(left, right, (((0,), (0,)), ((), ())), preferred_element_type=F32)


def project(here, x_all, index, gain, shift, weight, bias, tok_len, after=()):
    _, rows, width = x_all.shape
    inner = weight.shape[2]
    heads = inner // HD

    def body(here_ref, x_ref, gain_ref, shift_ref, weight_hbm, bias_ref, *rest):
        norm_ref, outs, (held, weight_ref, x_held, sems) = rest[0], rest[1:6], rest[6:]
        fetch = pltpu.make_async_copy(x_ref.at[index], x_held, sems.at[3])
        fetch.start()
        copies = [
            pltpu.make_async_copy(weight_hbm.at[part], weight_ref.at[part], sems.at[part])
            for part in range(3)
        ]
        for copy in copies:
            copy.start()
        fetch.wait()
        unit, _ = normalized(x_held[...].astype(F32))
        norm_ref[...] = (unit * gain_ref[...] + shift_ref[...]).astype(BF)
        for part in range(3):
            copies[part].wait()
            value = dot(norm_ref[...], weight_ref[part]) + bias_ref[part : part + 1]
            value = value.astype(BF)
            for head in range(heads):
                held[head, :, part * HD : (part + 1) * HD] = value[:, head * HD : (head + 1) * HD]

        def load(unit_id):
            return held[unit_id % heads, rows_at(unit_id // heads * tok_len, tok_len), :]

        emit_exchange(load, here_ref[0], outs)

    return run_kernel(
        body,
        [sds((rows, width))] + exchange_shapes(tok_len, 3 * HD),
        [here, x_all, gain, shift, weight, bias],
        flops=6 * rows * width * inner,
        scratch=[
            pltpu.VMEM((heads, rows, 3 * HD), BF),
            pltpu.VMEM(weight.shape, BF),
            pltpu.VMEM((rows, width), BF),
            pltpu.SemaphoreType.DMA((4,)),
        ],
        name="project",
        limit=14,
        after=after,
        in_hbm=(1, 4),
    )


def rows_of_device(device, block, blocks):
    return (
        rows_at(device * block, block),
        rows_at((blocks - 1 - device) * block, block),
    )


def attention(here, received, seg_row, key_row, heads, after=()):
    tok_len = received[0].shape[0]
    block = tok_len // 2
    seq_len = seg_row.shape[2]
    blocks = seq_len // block
    step = 256
    factor = LOG2E / math.sqrt(HD)

    def body(here_ref, *rest):
        refs, seg_ref, key_ref = rest[:5], rest[5], rest[6]
        outs, lse_ref = rest[7:12], rest[12]
        q_all, k_turned, v_all, mixed = rest[13:]
        me = here_ref[0]
        seq = me // heads
        for device, value in exchanged(refs, me):
            for half, place in enumerate(rows_of_device(device, block, blocks)):
                rows = value[half * block : (half + 1) * block]
                q_all[place] = rows[:, :HD]
                k_turned[:, place] = rows[:, HD : 2 * HD].T
                v_all[place] = rows[:, 2 * HD :]
        for number in range(seq_len // step):
            start, stop = number * step, (number + 1) * step
            segs = as_column(seg_ref[seq, :, start:stop])
            scores = dot(q_all[start:stop], k_turned[:, :stop]) * factor
            scores = masked(scores, segs, key_ref, seq, start, stop)
            top = jnp.max(scores, axis=-1, keepdims=True)
            raised = jnp.exp2(scores - top)
            total = jnp.sum(raised, axis=-1, keepdims=True)
            out = dot(raised.astype(BF), v_all[:stop]) / total
            mixed[start:stop] = out.astype(BF)
            lse_ref[start:stop] = top + jnp.log2(total)

        def load(device):
            return jnp.concatenate(
                [mixed[place] for place in rows_of_device(device, block, blocks)], axis=0
            )

        emit_exchange(load, me, outs)

    return run_kernel(
        body,
        exchange_shapes(tok_len, HD) + [sds((seq_len, 1), F32)],
        [here] + list(received) + [seg_row, key_row],
        flops=2 * 2 * seq_len * seq_len * HD,
        exps=seq_len * seq_len // 2,
        scratch=[
            pltpu.VMEM((seq_len, HD), BF),
            pltpu.VMEM((HD, seq_len), BF),
            pltpu.VMEM((seq_len, HD), BF),
            pltpu.VMEM((seq_len, HD), BF),
        ],
        after=after,
        name="attention",
        limit=16,
    )


def as_column(row):
    return jnp.broadcast_to(row, (128, row.shape[1])).T[:, :1]


def masked(scores, segs, key_ref, seq, start, stop):
    size = stop - start
    row = lax.broadcasted_iota(jnp.int32, (size, size), 0)
    column = lax.broadcasted_iota(jnp.int32, (size, size), 1)
    same = segs == key_ref[seq, :, start:stop]
    seen = (same & (column < row)) | (column == row)
    corner = jnp.where(seen, scores[:, start:], LOW)
    if start == 0:
        return corner
    left = jnp.where(segs == key_ref[seq, :, :start], scores[:, :start], LOW)
    return jnp.concatenate([left, corner], axis=1)


def attention_back(
    here, received, grads, seg_row, key_row, lse, heads, earlier, index, count, after=()
):
    tok_len = received[0].shape[0]
    block = tok_len // 2
    seq_len = seg_row.shape[2]
    blocks = seq_len // block
    step = 256
    scaler = 1.0 / math.sqrt(HD)

    def body(here_ref, *rest):
        refs, grad_refs = rest[:5], rest[5:10]
        seg_ref, key_ref, lse_ref = rest[10:13]
        rest = rest[13 + len(earlier) :]
        outs = [ref.at[0] for ref in rest[:5]]
        q_all, k_all, k_turned, v_turned, g_all, result, dk_turned, dv_turned = rest[5:]
        me = here_ref[0]
        seq = me // heads
        for device, value in exchanged(refs, me):
            for half, place in enumerate(rows_of_device(device, block, blocks)):
                rows = value[half * block : (half + 1) * block]
                q_all[place] = rows[:, :HD]
                k_all[place] = rows[:, HD : 2 * HD]
                k_turned[:, place] = rows[:, HD : 2 * HD].T
                v_turned[:, place] = rows[:, 2 * HD :].T
        for device, value in exchanged(grad_refs, me):
            for half, place in enumerate(rows_of_device(device, block, blocks)):
                g_all[place] = value[half * block : (half + 1) * block]
        last = seq_len // step - 1
        for number in range(last, -1, -1):
            start, stop = number * step, (number + 1) * step
            segs = as_column(seg_ref[seq, :, start:stop])
            query, grad = q_all[start:stop], g_all[start:stop]
            scores = dot(query, k_turned[:, :stop]) * (scaler * LOG2E)
            scores = masked(scores, segs, key_ref, seq, start, stop)
            probs = jnp.exp2(scores - lse_ref[start:stop])
            grad_probs = dot(grad, v_turned[:, :stop])
            inner = jnp.sum(probs * grad_probs, axis=-1, keepdims=True)
            grad_scores = (probs * (grad_probs - inner)).astype(BF)
            dv_part = dot_tn(grad, probs.astype(BF))
            dk_part = dot_tn(query, grad_scores)
            if number == last:
                dv_turned[...] = dv_part
                dk_turned[...] = dk_part
            else:
                dv_turned[:, :stop] += dv_part
                dk_turned[:, :stop] += dk_part
            dq = dot(grad_scores, k_all[:stop]) * scaler
            result[start:stop, :HD] = dq.astype(BF)
        for number in range(last + 1):
            start, stop = number * step, (number + 1) * step
            result[start:stop, HD : 2 * HD] = (dk_turned[:, start:stop] * scaler).T.astype(BF)
            result[start:stop, 2 * HD :] = dv_turned[:, start:stop].T.astype(BF)

        def load(device):
            return jnp.concatenate(
                [result[place] for place in rows_of_device(device, block, blocks)], axis=0
            )

        emit_exchange(load, me, outs)

    shapes = exchange_shapes(tok_len, 3 * HD)
    args = [here, *received, *grads, seg_row, key_row, lse, *earlier]
    first = len(args) - len(earlier)
    return launch(
        body,
        operands_of(args),
        [pl.BlockSpec(memory_space=pltpu.SMEM)]
        + [whole_of(item.shape) for item in args[1:first]]
        + [pl.BlockSpec(memory_space=pl.ANY) for _ in earlier],
        [sds((count,) + item.shape) for item in shapes],
        [
            pl.BlockSpec((1,) + item.shape, lambda i, n=len(item.shape): (index,) + (0,) * n)
            for item in shapes
        ],
        [
            pltpu.VMEM((seq_len, HD), BF),
            pltpu.VMEM((seq_len, HD), BF),
            pltpu.VMEM((HD, seq_len), BF),
            pltpu.VMEM((HD, seq_len), BF),
            pltpu.VMEM((seq_len, HD), BF),
            pltpu.VMEM((seq_len, 3 * HD), BF),
            pltpu.VMEM((HD, seq_len), F32),
            pltpu.VMEM((HD, seq_len), F32),
        ],
        36 << 20,
        cost(5 * seq_len * seq_len * HD, 12 * seq_len * HD),
        "attention_back",
        after,
        grid=(1,),
        aliases={first + number: number for number in range(len(earlier))},
    )


def mix_heads(here, tp_here, received, weight, heads, direct, after=()):
    tok_len = received[0].shape[0]
    inner, width = weight.shape
    rows = len_units(received) * tok_len // heads
    size = rows // 4

    def body(here_ref, tp_ref, *rest):
        refs, weight_ref = rest[:5], rest[5]
        heads_ref, outs, held = rest[6], rest[7:11], rest[11]
        for unit_id, value in exchanged(refs, here_ref[0]):
            column = pl.multiple_of(unit_id % heads * HD, HD)
            heads_ref[rows_at(unit_id // heads * tok_len, tok_len), pl.ds(column, HD)] = value
        for start in range(0, width, 512):
            held[:, start : start + 512] = dot(
                heads_ref[...], weight_ref[:, start : start + 512]
            ).astype(BF)
        emit_messages(lambda place: held[place, :], tp_ref[0], outs, size)

    return run_kernel(
        body,
        [sds((rows, inner))] + message_shapes(size // 2, width, direct),
        [here, tp_here] + list(received) + [weight],
        flops=2 * rows * inner * width,
        scratch=[pltpu.VMEM((rows, width), BF)],
        after=after,
        name="mix_heads",
        limit=6,
    )


def len_units(received):
    return 2 * received[-1].shape[0]


def second_norm(sums, x_mine, mixer_bias, gain, shift, direct, after=()):
    size, width = x_mine.shape
    count = len(sums)

    def body(*rest):
        refs, (x_ref, bias_ref, gain_ref, shift_ref) = rest[:count], rest[count : count + 4]
        resid_ref, outs = rest[count + 4], rest[count + 5 :]
        resid = x_ref[...].astype(F32) + total_of(refs) + bias_ref[...]
        resid_ref[...] = resid
        unit, _ = normalized(resid)
        emit_shard((unit * gain_ref[...] + shift_ref[...]).astype(BF), outs)

    return run_kernel(
        body,
        [sds((size, width), F32)] + shard_shapes(size, width, direct),
        list(sums) + [x_mine, mixer_bias, gain, shift],
        name="second_norm",
        limit=8,
        after=after,
    )


def feed_inner(tp_here, pieces, cot, up_weight, up_bias, down_weight, with_grad, after=()):
    rows, width = cot.shape
    hidden = up_weight.shape[1]
    size = rows // 4
    step = 512
    blocks = hidden // step

    def body(tp_ref, *rest):
        refs, rest = rest[: len(pieces)], rest[len(pieces) :]
        cot_ref, up_hbm, bias_ref, down_hbm = rest[:4]
        norm_ref, act_ref, pre_ref, sum_ref, cot_sum_ref = rest[4:9]
        grad_outs = rest[9:13] if with_grad else ()
        up, down, held, sems = rest[-4:]

        def part(number):
            return pl.ds(pl.multiple_of(number * step, step), step)

        def copies(number):
            place = part(number)
            return (
                pltpu.make_async_copy(up_hbm.at[:, place], up.at[:, place], sems.at[0, number]),
                pltpu.make_async_copy(down_hbm.at[place, :], down.at[place, :], sems.at[1, number]),
            )

        for number in range(blocks):
            for copy in copies(number):
                copy.start()

        def store(place, value):
            norm_ref[place, :] = value

        place_gathered(store, tp_ref[0], refs, size)
        cot_sum_ref[...] = jnp.sum(cot_ref[...].astype(F32), axis=0, keepdims=True)

        @pl.loop(0, blocks)
        def _(number):
            for copy in copies(number):
                copy.wait()
            place = part(number)
            pre = dot(norm_ref[...], up[:, place]) + bias_ref[:, place]
            grad_act = dot_nt(cot_ref[...], down[place, :])
            spread = 0.5 + 0.5 * lax.erf(pre * math.sqrt(0.5))
            dense = jnp.exp(-0.5 * pre * pre) * (1.0 / math.sqrt(2.0 * math.pi))
            act_ref[:, place] = (pre * spread).astype(BF)
            grad_pre = (grad_act * (spread + pre * dense)).astype(BF)
            pre_ref[:, place] = grad_pre
            sum_ref[:, place] = jnp.sum(grad_pre.astype(F32), axis=0, keepdims=True)

        if with_grad:

            @pl.loop(0, width // step)
            def _(number):
                place = part(number)
                held[:, place] = dot_nt(pre_ref[...], up[place, :]).astype(BF)

            emit_messages(lambda at: held[at, :], tp_ref[0], grad_outs, size)

    args = [tp_here, *pieces, cot, up_weight, up_bias, down_weight]
    outs = [
        sds((rows, width)),
        sds((rows, hidden)),
        sds((rows, hidden)),
        sds((1, hidden), F32),
        sds((1, width), F32),
    ] + (message_shapes(size // 2, width, True) if with_grad else [])
    return launch(
        body,
        operands_of(args),
        [pl.BlockSpec(memory_space=pltpu.SMEM)]
        + [whole_of(piece.shape) for piece in pieces]
        + [cot.spec(), pl.BlockSpec(memory_space=HBM), whole_of(up_bias.shape)]
        + [pl.BlockSpec(memory_space=HBM)],
        outs,
        [whole_of(item.shape) for item in outs],
        [
            pltpu.VMEM((width, hidden), BF),
            pltpu.VMEM((hidden, width), BF),
            pltpu.VMEM((rows, width), BF),
            pltpu.SemaphoreType.DMA((2, blocks)),
        ],
        50 << 20,
        cost(6 * rows * width * hidden, 4 * width * hidden + 20 * rows * width),
        "feed_inner",
        after,
        grid=(1,),
    )


def feed_grad(tp_here, grad_pre, up_weight, after=()):
    rows, hidden = grad_pre.shape
    width = up_weight.shape[0]
    size = rows // 4
    step = 512
    blocks = width // step

    def body(tp_ref, pre_ref, up_ref, *rest):
        outs, held = rest[:4], rest[4]
        number = pl.program_id(0)
        place = pl.ds(pl.multiple_of(number * step, step), step)
        held[:, place] = dot_nt(pre_ref[...], up_ref[...]).astype(BF)

        @pl.when(number == blocks - 1)
        def _():
            emit_messages(lambda at: held[at, :], tp_ref[0], outs, size)

    outs = message_shapes(size // 2, width)
    return launch(
        body,
        operands_of([tp_here, grad_pre, up_weight]),
        [
            pl.BlockSpec(memory_space=pltpu.SMEM),
            whole_of(grad_pre.shape),
            pl.BlockSpec((step, hidden), lambda i: (i, 0)),
        ],
        outs,
        [whole_of(item.shape) for item in outs],
        [pltpu.VMEM((rows, width), BF)],
        24 << 20,
        cost(2 * rows * width * hidden, 2 * width * hidden + 6 * rows * width),
        "feed_grad",
        after,
        grid=(blocks,),
    )


def feed_out(tp_here, acts, down_weight, after=()):
    count = len(acts)
    rows, hidden = acts[0].shape
    width = down_weight.shape[1]
    size = rows // 4
    step = 512
    blocks = width // step

    def body(tp_ref, *rest):
        act_refs, down_ref, outs, held = rest[:count], rest[count], rest[-5:-1], rest[-1]
        number = pl.program_id(0)
        place = pl.ds(pl.multiple_of(number * step, step), step)
        for index in range(count):
            held[index, :, place] = dot(act_refs[index][...], down_ref[...]).astype(BF)

        @pl.when(number == blocks - 1)
        def _():
            for index in range(count):
                emit_messages(
                    lambda at: held[index, at, :],
                    tp_ref[0],
                    [ref.at[index] for ref in outs],
                    size,
                )

    outs = [sds((count,) + item.shape) for item in message_shapes(size // 2, width)]
    return launch(
        body,
        operands_of([tp_here, *acts, down_weight]),
        [pl.BlockSpec(memory_space=pltpu.SMEM)]
        + [whole_of(act.shape) for act in acts]
        + [pl.BlockSpec((hidden, step), lambda i: (0, i))],
        outs,
        [whole_of(item.shape) for item in outs],
        [pltpu.VMEM((count, rows, width), BF)],
        36 << 20,
        cost(2 * count * rows * width * hidden, 2 * width * hidden + 12 * rows * width),
        "feed_out",
        after,
        grid=(blocks,),
    )


def second_norm_back(sums, resid, cot_mine, gain, direct, after=()):
    size, width = resid.shape
    count = len(sums)

    def body(*rest):
        refs, (resid_ref, cot_ref, gain_ref) = rest[:count], rest[count : count + 3]
        grad_ref, gain_out, shift_out, *outs = rest[count + 3 :]
        back, gain_sum, shift_sum = norm_back(resid_ref[...], gain_ref[...], total_of(refs))
        grad = back + cot_ref[...].astype(F32)
        grad_ref[...] = grad
        emit_shard(grad.astype(BF), outs)
        gain_out[...] = gain_sum
        shift_out[...] = shift_sum

    return run_kernel(
        body,
        [sds((size, width), F32)]
        + [sds((1, width), F32)] * 2
        + shard_shapes(size, width, direct),
        list(sums) + [resid, cot_mine, gain],
        name="second_norm_back",
        limit=10,
        after=after,
    )


def first_norm_back(sums, x_mine, grad_resids, gain, after=()):
    count = len(x_mine)
    size, width = grad_resids[0].shape

    def body(*rest):
        refs, rest = rest[:4], rest[4:]
        x_refs, grad_refs, gain_ref = rest[:count], rest[count : 2 * count], rest[2 * count]
        gain_out, shift_out, *outs = rest[2 * count + 1 :]
        for index in range(count):
            back, gain_sum, shift_sum = norm_back(
                x_refs[index][...].astype(F32),
                gain_ref[...],
                total_of([ref.at[index] for ref in refs]),
            )
            emit_shard(
                (back + grad_refs[index][...]).astype(BF), [ref.at[index] for ref in outs]
            )
            gain_out[...] = gain_sum if index == 0 else gain_out[...] + gain_sum
            shift_out[...] = shift_sum if index == 0 else shift_out[...] + shift_sum

    return run_kernel(
        body,
        [sds((1, width), F32)] * 2
        + [sds((count,) + item.shape) for item in shard_shapes(size, width)],
        list(sums) + list(x_mine) + list(grad_resids) + [gain],
        name="first_norm_back",
        limit=10,
        after=after,
    )


def finish_outputs(sums, resids, bias, after=()):
    size, width = resids[0].shape
    half = size // 2
    count = len(resids)

    def body(*rest):
        refs, resid_refs, bias_ref = rest[:4], rest[4 : 4 + count], rest[4 + count]
        low_ref, high_ref = rest[5 + count :]
        for index in range(count):
            ours = [ref.at[index] for ref in refs]
            value = (resid_refs[index][...] + total_of(ours) + bias_ref[...]).astype(BF)
            low_ref[index] = value[:half]
            high_ref[index] = value[half:]

    return run_kernel(
        body,
        [sds((count, half, width))] * 2,
        list(sums) + list(resids) + [bias],
        after=after,
        name="finish_outputs",
        limit=8,
    )


def assemble_outputs(tp_here, pieces, dtype, after=()):
    count, half, width = pieces[0].shape
    size = 2 * half
    rows = 4 * size

    def block_of(shape):
        return pl.BlockSpec((1,) + shape[1:], lambda i, n=len(shape) - 1: (i,) + (0,) * n)

    def body(tp_ref, *rest):
        refs, out_ref = rest[:6], rest[6]

        def store(place, value):
            out_ref[0, place, :] = value.astype(dtype)

        place_gathered(store, tp_ref[0], [ref.at[0] for ref in refs], size)

    results, done = launch(
        body,
        [tp_here] + list(pieces),
        [pl.BlockSpec(memory_space=pltpu.SMEM)] + [block_of(piece.shape) for piece in pieces],
        [HBM((count, rows, width), dtype)],
        [block_of((count, rows, width))],
        (),
        24 << 20,
        cost(0, count * rows * width * 6),
        "assemble_outputs",
        after,
        grid=(count,),
    )
    return results[0], done


def widen(part, turned, after=()):
    rows, wide = part.shape

    def body(part_ref, out_ref):
        value = part_ref[...].astype(F32)
        out_ref[...] = value.T if turned else value

    shape = (wide, rows) if turned else (rows, wide)
    return run_kernel(body, [sds(shape, F32)], [part], after=after, name="widen", limit=6)


def widen_last(part, inner, after=()):
    rows, _ = part.shape

    def body(part_ref, proj_ref, mixer_ref):
        for number in range(3):
            place = slice(number * inner, (number + 1) * inner)
            proj_ref[number] = part_ref[:, place].astype(F32)
        mixer_ref[...] = part_ref[:, 3 * inner :].astype(F32).T

    return run_kernel(
        body,
        [sds((3, rows, inner), F32), sds((inner, rows), F32)],
        [part],
        after=after,
        name="widen",
        limit=6,
    )


def heads_back(here, tp_here, pieces, weight, tok_len, after=()):
    inner, width = weight.shape
    heads = inner // HD
    count = len(pieces)
    size = pieces[0].shape[0] * (1 if count == 4 else 2)
    rows = 4 * size

    def body(here_ref, tp_ref, *rest):
        refs, weight_ref, rest = rest[:count], rest[count], rest[count + 1 :]
        mix_ref, sum_ref, outs, held = rest[0], rest[1], rest[2:7], rest[7]

        def store(place, value):
            mix_ref[place, :] = value

        place_gathered(store, tp_ref[0], refs, size)
        sum_ref[...] = jnp.sum(mix_ref[...].astype(F32), axis=0, keepdims=True)
        value = dot_nt(mix_ref[...], weight_ref[...]).astype(BF)
        for head in range(heads):
            held[head] = value[:, head * HD : (head + 1) * HD]

        def load(unit_id):
            return held[unit_id % heads, rows_at(unit_id // heads * tok_len, tok_len), :]

        emit_exchange(load, here_ref[0], outs)

    return run_kernel(
        body,
        [sds((rows, width)), sds((1, width), F32)] + exchange_shapes(tok_len, HD),
        [here, tp_here] + list(pieces) + [weight],
        flops=2 * rows * inner * width,
        scratch=[pltpu.VMEM((heads, rows, HD), BF)],
        after=after,
        name="heads_back",
        limit=8,
    )


def project_back(here, tp_here, received, weight, after=()):
    count, tok_len, _ = received[0].shape
    _, width, inner = weight.shape
    heads = inner // HD
    rows = 2 * received[-1].shape[1] * tok_len // heads
    size = rows // 4

    def body(here_ref, tp_ref, *rest):
        refs, weight_ref, rest = rest[:5], rest[5], rest[6:]
        proj_refs, sum_ref, outs, held = rest[:count], rest[count], rest[-5:-1], rest[-1]
        for index, proj_ref in enumerate(proj_refs):
            for unit_id, value in exchanged([ref.at[index] for ref in refs], here_ref[0]):
                place = rows_at(unit_id // heads * tok_len, tok_len)
                for part in range(3):
                    column = pl.multiple_of(part * inner + unit_id % heads * HD, HD)
                    proj_ref[place, pl.ds(column, HD)] = value[:, part * HD : (part + 1) * HD]
            part_sum = jnp.sum(proj_ref[...].astype(F32), axis=0, keepdims=True)
            sum_ref[...] = part_sum if index == 0 else sum_ref[...] + part_sum
            for start in range(0, width, 512):
                value = dot_nt(proj_ref[:, :inner], weight_ref[0, start : start + 512])
                for part in range(1, 3):
                    value += dot_nt(
                        proj_ref[:, part * inner : (part + 1) * inner],
                        weight_ref[part, start : start + 512],
                    )
                held[:, start : start + 512] = value.astype(BF)
            emit_messages(
                lambda place: held[place, :], tp_ref[0], [ref.at[index] for ref in outs], size
            )

    return run_kernel(
        body,
        [sds((rows, 3 * inner))] * count
        + [sds((1, 3 * inner), F32)]
        + [sds((count,) + item.shape) for item in message_shapes(size // 2, width)],
        [here, tp_here] + list(received) + [weight],
        flops=6 * count * rows * inner * width,
        scratch=[pltpu.VMEM((rows, width), BF)],
        name="project_back",
        limit=10,
        after=after,
    )


def weight_grad(groups, here=None, after=()):
    count = len(groups[0][0])
    rows, tall = groups[0][0][0].shape
    widths = [rights[0].shape[1] for _, rights in groups]
    total = sum(widths)
    split = here is not None
    steps = 8 if split else 4
    step = tall // steps
    half = steps // 2

    def block_of(number, *fixed):
        if not split:
            return number
        core = fixed[0][0] & 1
        mine = number // half
        return 2 * (number % half) + (core ^ 1 ^ mine)

    def product(refs, store):
        start = 0
        for place, wide in enumerate(widths):
            ours = refs[2 * count * place : 2 * count * (place + 1)]
            value = dot_tn(ours[0][...], ours[count][...])
            for number in range(1, count):
                value += dot_tn(ours[number][...], ours[count + number][...])
            store(slice(start, start + wide), value.astype(BF))
            start += wide

    def body(*refs):
        if not split:
            out_ref = refs[-1]

            def store(place, value):
                out_ref[:, place] = value

            product(refs, store)
            return
        refs, other_ref, own_ref = refs[1:-2], refs[-2], refs[-1]
        number = pl.program_id(0)

        def into(ref):
            def store(place, value):
                ref[0, :, place] = value

            return store

        @pl.when(number < half)
        def _():
            product(refs, into(other_ref))

        @pl.when(number >= half)
        def _():
            product(refs, into(own_ref))

    args, in_specs = [], []
    for (lefts, rights), wide in zip(groups, widths):
        for item in lefts:
            if isinstance(item, Part):
                in_specs.append(
                    pl.BlockSpec(
                        (None, rows, step),
                        lambda i, *fixed, k=item.index: (k, 0, block_of(i, *fixed)),
                    )
                )
            else:
                in_specs.append(
                    pl.BlockSpec((rows, step), lambda i, *fixed: (0, block_of(i, *fixed)))
                )
        in_specs += [pl.BlockSpec((rows, wide), lambda *_: (0, 0))] * count
        args += list(lefts) + list(rights)
    if split:
        outs = [HBM((half, step, total), BF)] * 2
        out_specs = [
            pl.BlockSpec((1, step, total), lambda i, *_: (jnp.minimum(i, half - 1), 0, 0)),
            pl.BlockSpec((1, step, total), lambda i, *_: (jnp.maximum(i - half, 0), 0, 0)),
        ]
    else:
        outs = [HBM((tall, total), BF)]
        out_specs = [pl.BlockSpec((step, total), lambda i: (i, 0))]
    return launch(
        body,
        operands_of(args),
        in_specs,
        outs,
        out_specs,
        (),
        40 << 20,
        cost(
            2 * count * rows * tall * total,
            2 * (count * rows * (tall * len(groups) + total) + tall * total),
        ),
        "weight_grad",
        after,
        grid=(steps,),
        scalars=(here,) if split else (),
    )


def add_halves(own, got, after=()):
    def body(own_ref, got_ref, out_ref):
        out_ref[...] = (own_ref[...].astype(F32) + got_ref[...].astype(F32)).astype(BF)

    block_spec = pl.BlockSpec((1,) + own.shape[1:], lambda i: (i, 0, 0))
    return launch(
        body,
        operands_of([own, got]),
        [block_spec] * 2,
        [HBM(own.shape, BF)],
        [block_spec],
        (),
        16 << 20,
        cost(0, 6 * math.prod(own.shape)),
        "add_halves",
        after,
        grid=(own.shape[0],),
    )


def small_sums(values):
    here = lax.axis_index("ctx")
    step = values.shape[0] // 2
    while step:
        pair = values.reshape((2, step) + values.shape[1:])
        bit = (here // step) % 2
        keep = lax.dynamic_index_in_dim(pair, bit, 0, False)
        send = lax.dynamic_index_in_dim(pair, 1 - bit, 0, False)
        values = keep + xor_permute(send, "ctx", step)
        step //= 2
    return values[0]


def per_device_exchanged(
    inputs,
    segments,
    keep_mask,
    first_gain,
    first_shift,
    proj_weight,
    proj_bias,
    mixer_weight,
    mixer_bias,
    second_gain,
    second_shift,
    up_weight,
    up_bias,
    down_weight,
    down_bias,
    out_cotangent,
):
    ctx_count = lax.axis_size("ctx")
    micro_count, seq_count, tok_len, width = inputs.shape
    inner = proj_bias.shape[1]
    heads = inner // HD
    rows = seq_count * tok_len
    here = lax.axis_index("ctx").astype(jnp.int32).reshape(1)
    tp_here = lax.axis_index("tp").astype(jnp.int32).reshape(1)
    weight_three = jnp.transpose(proj_weight, (1, 0, 2))
    bias_three = jnp.stack([proj_bias[0], jnp.zeros_like(proj_bias[0]), proj_bias[1]])
    x_all = inputs.reshape(micro_count, rows, width)
    cot_all = out_cotangent.reshape(micro_count, rows, width)
    key_rows = jnp.where(keep_mask > 0, segments, -1)[:, :, None, :]
    gain_one, shift_one = first_gain[None], first_shift[None]
    gain_two, shift_two = second_gain[None], second_shift[None]
    mix_bias, low_bias, high_bias = mixer_bias[None], down_bias[None], up_bias[None]
    micro = range(micro_count)

    key_rows = [key_rows[index] for index in micro]
    seg_rows = [segments[index][:, None, :] for index in micro]
    cots = [Part(cot_all, index) for index in micro]
    size = rows // lax.axis_size("tp")
    start = tp_here[0] * size
    x_mine = [lax.dynamic_slice(x_all, (index, start, 0), (1, size, width))[0] for index in micro]
    cot_mine = [
        lax.dynamic_slice(cot_all, (index, start, 0), (1, size, width))[0] for index in micro
    ]

    chips = [[core + 2 * chip for chip in range(ctx_count // 2)] for core in range(2)]

    def scattered(part):
        return lax.psum_scatter(part, "ctx", scatter_dimension=0, tiled=True)

    def scattered_chips(part):
        part = part.reshape(-1, part.shape[2])
        return lax.psum_scatter(
            part, "ctx", scatter_dimension=0, axis_index_groups=chips, tiled=True
        )

    def until(items, *points):
        held, _ = lax.optimization_barrier((items, points))
        return held

    norm_one, received, lses, heads_low, resids = [], [], [], [], []

    def project_micro(index, done):
        (normed, *sent), done = project(
            here, x_all, index, gain_one, shift_one, weight_three, bias_three, tok_len, after=done
        )
        norm_one.append(normed)
        return exchange_chips(*sent), done

    def attend_micro(index, got, done):
        received.append(got)
        (*sent, lse), done = attention(
            here, got, seg_rows[index], key_rows[index], heads, after=done
        )
        lses.append(lse)
        return exchange_chips(*sent), done

    def mix_micro(got, direct, done):
        (mixed, *messages), done = mix_heads(
            here, tp_here, got, mixer_weight, heads, direct, after=done
        )
        heads_low.append(mixed)
        return messages, done

    def norm_micro(index, sums, direct, done):
        (resid, *shard), done = second_norm(
            sums, x_mine[index], mix_bias, gain_two, shift_two, direct, after=done
        )
        resids.append(resid)
        return shard if direct else gather_first(shard), done

    norm_two, acts, grad_pres, up_sums, cot_sums = [], [], [], [], []

    def feed_micro(index, pieces, with_grad, done):
        (normed, act, grad_pre, up_sum, cot_sum, *messages), done = feed_inner(
            tp_here,
            pieces,
            cots[index],
            up_weight,
            high_bias,
            down_weight,
            with_grad,
            after=done,
        )
        norm_two.append(normed)
        acts.append(act)
        grad_pres.append(grad_pre)
        up_sums.append(up_sum)
        cot_sums.append(cot_sum)
        return messages, done

    grad_resids, gain_twos, shift_twos = [], [], []
    grad_mixes, mix_sums, states = [], [], []

    def norm_back_micro(index, sums, done):
        (grad_resid, gain_sum, shift_sum, *shard), done = second_norm_back(
            sums, resids[index], cot_mine[index], gain_two, False, after=done
        )
        grad_resids.append(grad_resid)
        gain_twos.append(gain_sum)
        shift_twos.append(shift_sum)
        return gather_first(shard), done

    def heads_back_micro(index, pieces, done):
        (grad_mix, mix_sum, *sent), done = heads_back(
            here, tp_here, pieces, mixer_weight, tok_len, after=done
        )
        grad_mixes.append(grad_mix)
        mix_sums.append(mix_sum)
        states.append(exchange_chips(*sent))
        return done

    def attend_back_micro(index, got, earlier, done):
        return attention_back(
            here,
            received[index],
            got,
            seg_rows[index],
            key_rows[index],
            lses[index],
            heads,
            earlier,
            index,
            micro_count,
            after=done,
        )

    state_a, done = project_micro(0, ())
    state_b, done = project_micro(1, done)
    got, done = exchange_cores(state_a, done)
    state_a, done = attend_micro(0, got, done)
    got, done = exchange_cores(state_b, done)
    state_b, done = attend_micro(1, got, done)
    got, done = exchange_cores(state_a, done)
    messages, done = mix_micro(got, False, done)
    sums_a, done = reduce_second(reduce_first(messages), done)
    got, done = exchange_cores(state_b, done)
    messages, done = mix_micro(got, False, done)
    state_b = reduce_first(messages)
    state_a, done = norm_micro(0, sums_a, False, done)
    pieces_a, done = gather_second(state_a, done)
    sums_b, done = reduce_second(state_b, done)
    state_b, done = norm_micro(1, sums_b, True, done)
    pieces_b = gather_direct(state_b[0])
    messages, done = feed_micro(0, pieces_a, True, done)
    sums_a = reduce_direct(messages)
    _, done = feed_micro(1, pieces_b, False, done)
    (down_part,), done = weight_grad([(cots, acts)], after=done)
    state_a, done = norm_back_micro(0, sums_a, done)
    down_grad = scattered(until(down_part, done))
    messages, done = feed_grad(tp_here, grad_pres[1], up_weight, after=done)
    state_b = reduce_first(messages)
    pieces_a, done = gather_second(state_a, done)
    feeds, done = feed_out(tp_here, acts, down_weight, after=done)
    sums_b, done = reduce_second(state_b, done)
    done = heads_back_micro(0, pieces_a, done)
    state_b, done = norm_back_micro(1, sums_b, done)
    pieces_b, done = gather_second(state_b, done)
    (sent, own), done = weight_grad([(norm_two, grad_pres)], here, after=done)
    got_a, done = exchange_cores(states[0], done)
    done = heads_back_micro(1, pieces_b, done)
    state_feed = reduce_first(until(feeds, done))
    sent_back, done = attend_back_micro(0, got_a, [], done)
    got_b, done = exchange_cores(states[1], done)
    sums_feed, done = reduce_second(state_feed, done)
    got_up = xor_permute(until(sent, done), "ctx", 1)
    sent_back, done = attend_back_micro(1, got_b, sent_back, done)
    state_back = exchange_chips(*sent_back)
    halves, done = finish_outputs(sums_feed, resids, low_bias, after=done)
    (up_part,), done = add_halves(own, got_up, after=done)
    got, done = exchange_cores(state_back, done)
    up_grad = scattered_chips(until(up_part, done))
    (*grad_projs, proj_sum, first, second, third, fourth), done = project_back(
        here, tp_here, got, weight_three, after=done
    )
    state_one = reduce_first((first, second, third, fourth))
    last = [(norm_one, grad_projs), (grad_mixes, heads_low)]
    (sent, own), done = weight_grad(last, here, after=done)
    sums_one, done = reduce_second(state_one, done)
    got_last = xor_permute(until(sent, done), "ctx", 1)
    pieces_out, done = gather_second(gather_first(halves), done)
    (last_part,), done = add_halves(own, got_last, after=done)
    (gain_sum, shift_sum, *halves), done = first_norm_back(
        sums_one, x_mine, grad_resids, gain_one, after=done
    )
    last_grad = scattered_chips(until(last_part, done))
    pieces_in, done = gather_second(gather_first(halves), done)
    outputs, done = assemble_outputs(tp_here, pieces_out, BF, after=done)
    gain_ones, shift_ones, proj_sums = [gain_sum], [shift_sum], [proj_sum]
    (down_grad,), done = widen(down_grad, True, after=done)
    input_grad, done = assemble_outputs(tp_here, pieces_in, F32, after=done)
    (up_grad,), done = widen(up_grad, False, after=done)
    (proj_grad, mixer_grad), done = widen_last(last_grad, inner, after=done)
    proj_grad = jnp.transpose(proj_grad, (1, 0, 2))

    def over_micro(items):
        return sum(items[1:], items[0]).reshape(ctx_count, -1)

    proj_sum = sum(proj_sums[1:], proj_sums[0]).reshape(3, ctx_count, -1)
    pair_sum = jnp.concatenate([proj_sum[0], proj_sum[2]], axis=1)
    share = width // ctx_count
    pair_sum = jnp.pad(pair_sum, ((0, 0), (0, share - pair_sum.shape[1])))
    kinds = [
        over_micro(gain_ones),
        over_micro(shift_ones),
        over_micro(gain_twos),
        over_micro(shift_twos),
        over_micro(mix_sums),
        over_micro(cot_sums),
        over_micro(up_sums),
        pair_sum,
    ]
    small = small_sums(jnp.stack(kinds, axis=1))
    norms = small[:4]
    for step in (1, 2):
        norms = norms + xor_permute(norms, "tp", step)
    proj_bias_grad = small[7, : 2 * inner // ctx_count].reshape(2, -1)
    return (
        outputs.reshape(inputs.shape),
        input_grad.reshape(inputs.shape),
        norms[0],
        norms[1],
        proj_grad,
        proj_bias_grad,
        mixer_grad,
        small[4],
        norms[2],
        norms[3],
        up_grad,
        small[6],
        down_grad,
        small[5],
    )


def plan_for(mesh):
    sizes = dict(mesh.shape)

    def chosen(*args):
        micro, seq_count, _, width = args[0].shape
        units = seq_count * args[6].shape[1] // HD
        fits = sizes["ctx"] == 8 and sizes["tp"] == 4 and units == sizes["ctx"]
        fits = fits and args[12].shape[0] == width and micro == 2
        return (per_device_exchanged if fits else per_device)(*args)

    return chosen


def solution(mesh):
    in_specs = (
        P(None, None, "ctx", None),
        P(),
        P(),
        P(),
        P(),
        P(None, None, "tp"),
        P(None, "tp"),
        P("tp", None),
        P(),
        P(),
        P(),
        P(None, "tp"),
        P("tp"),
        P("tp", None),
        P(),
        P(None, None, "ctx", None),
    )
    out_specs = (
        P(None, None, "ctx", None),
        P(None, None, "ctx", None),
        P("ctx"),
        P("ctx"),
        P("ctx", None, "tp"),
        P(None, ("tp", "ctx")),
        P("tp", "ctx"),
        P("ctx"),
        P("ctx"),
        P("ctx"),
        P("ctx", "tp"),
        P(("tp", "ctx")),
        P("tp", "ctx"),
        P("ctx"),
    )
    return jax.shard_map(
        plan_for(mesh), mesh=mesh, in_specs=in_specs, out_specs=out_specs, check_vma=False
    )
```

```python
import math

import jax
import jax.numpy as jnp
from jax import lax
from jax.experimental import pallas as pl
from jax.experimental.pallas import tpu as pltpu
from jax.sharding import PartitionSpec as P

HD = 128


def storage_order(values, part_count):
    leading = values.shape[:-1]
    blocks = values.reshape(leading + (2 * part_count, -1))
    front_half = blocks[..., :part_count, :]
    back_half = jnp.flip(blocks[..., part_count:, :], axis=-2)
    return jnp.stack([front_half, back_half], axis=-2).reshape(leading + (-1,))


def layer_norm(values, norm_gain, norm_shift):
    center = values - jnp.mean(values, axis=-1, keepdims=True)
    spread = jnp.mean(center * center, axis=-1, keepdims=True)
    return center * lax.rsqrt(spread + 1e-05) * norm_gain + norm_shift


def gelu_exact(values):
    return jax.nn.gelu(values, approximate=False)


def split_heads(rows, heads_here):
    return rows.reshape(rows.shape[0], rows.shape[1], heads_here, -1)


def scores_of(queries, key_all, allowed, heads_here, scaler):
    raw = (
        jnp.einsum(
            "sqhd,skhd->shqk",
            split_heads(queries, heads_here),
            split_heads(key_all, heads_here),
            preferred_element_type=jnp.float32,
        )
        * scaler
    )
    return jnp.where(allowed[:, None], raw, -1000000000.0)


def attend(queries, key_all, value_all, allowed, heads_here, scaler):
    masked = scores_of(queries, key_all, allowed, heads_here, scaler)
    top = jnp.max(masked, axis=-1, keepdims=True)
    raised = jnp.exp(masked - top)
    totals = jnp.sum(raised, axis=-1, keepdims=True)
    probs = raised / totals
    mixed = jnp.einsum(
        "shqk,skhd->sqhd",
        probs.astype(jnp.bfloat16),
        split_heads(value_all, heads_here),
        preferred_element_type=jnp.float32,
    )
    return (mixed.reshape(queries.shape), top + jnp.log(totals))


def attend_back(queries, key_all, value_all, allowed, log_total, grad_heads, heads_here, scaler):
    masked = scores_of(queries, key_all, allowed, heads_here, scaler)
    probs = jnp.exp(masked - log_total)
    grad_four = split_heads(grad_heads, heads_here)
    grad_value = jnp.einsum(
        "shqk,sqhd->skhd", probs.astype(jnp.bfloat16), grad_four, preferred_element_type=jnp.float32
    )
    grad_probs = jnp.einsum(
        "sqhd,skhd->shqk",
        grad_four,
        split_heads(value_all, heads_here),
        preferred_element_type=jnp.float32,
    )
    inner_sum = jnp.sum(probs * grad_probs, axis=-1, keepdims=True)
    grad_scores = (probs * (grad_probs - inner_sum)).astype(jnp.bfloat16)
    grad_query = (
        jnp.einsum(
            "shqk,skhd->sqhd",
            grad_scores,
            split_heads(key_all, heads_here),
            preferred_element_type=jnp.float32,
        )
        * scaler
    )
    grad_key = (
        jnp.einsum(
            "shqk,sqhd->skhd",
            grad_scores,
            split_heads(queries, heads_here),
            preferred_element_type=jnp.float32,
        )
        * scaler
    )
    return (
        grad_query.reshape(queries.shape),
        grad_key.reshape(key_all.shape),
        grad_value.reshape(value_all.shape),
    )


def reduce_grads(grads):
    return (
        lax.psum_scatter(
            grads[0].astype(jnp.bfloat16), "ctx", scatter_dimension=0, tiled=True
        ).astype(jnp.float32),
        lax.psum_scatter(
            grads[1].astype(jnp.bfloat16), "ctx", scatter_dimension=0, tiled=True
        ).astype(jnp.float32),
        lax.psum_scatter(
            grads[2].astype(jnp.bfloat16), "ctx", scatter_dimension=0, tiled=True
        ).astype(jnp.float32),
        lax.psum_scatter(
            grads[3].astype(jnp.bfloat16), "ctx", scatter_dimension=1, tiled=True
        ).astype(jnp.float32),
        lax.psum_scatter(
            grads[4].astype(jnp.bfloat16), "ctx", scatter_dimension=1, tiled=True
        ).astype(jnp.float32),
        lax.psum_scatter(
            grads[5].astype(jnp.bfloat16), "ctx", scatter_dimension=0, tiled=True
        ).astype(jnp.float32),
        lax.psum_scatter(
            grads[6].astype(jnp.bfloat16), "ctx", scatter_dimension=0, tiled=True
        ).astype(jnp.float32),
        lax.psum_scatter(
            grads[7].astype(jnp.bfloat16), "ctx", scatter_dimension=0, tiled=True
        ).astype(jnp.float32),
        lax.psum_scatter(
            grads[8].astype(jnp.bfloat16), "ctx", scatter_dimension=0, tiled=True
        ).astype(jnp.float32),
        lax.psum_scatter(
            grads[9].astype(jnp.bfloat16), "ctx", scatter_dimension=0, tiled=True
        ).astype(jnp.float32),
        lax.psum_scatter(
            grads[10].astype(jnp.bfloat16), "ctx", scatter_dimension=1, tiled=True
        ).astype(jnp.float32),
        lax.psum_scatter(
            grads[11].astype(jnp.bfloat16), "ctx", scatter_dimension=0, tiled=True
        ).astype(jnp.float32),
    )


def per_device(
    inputs,
    segments,
    keep_mask,
    first_gain,
    first_shift,
    proj_weight,
    proj_bias,
    mixer_weight,
    mixer_bias,
    second_gain,
    second_shift,
    up_weight,
    up_bias,
    down_weight,
    down_bias,
    out_cotangent,
):
    ctx_count = lax.axis_size("ctx")
    micro_count, seq_count, tok_len, model_width = inputs.shape
    inner_width = proj_bias.shape[1]
    heads_here = inner_width // HD
    scaler = 1.0 / math.sqrt(HD)
    seq_len = tok_len * ctx_count
    places = storage_order(jnp.arange(seq_len, dtype=jnp.int32), ctx_count)
    offset = lax.axis_index("ctx") * tok_len
    my_places = lax.dynamic_slice_in_dim(places, offset, tok_len, 0)
    seg_store = storage_order(segments, ctx_count)
    keep_store = storage_order(keep_mask, ctx_count)
    proj_flat = proj_weight.reshape(model_width, 3 * inner_width)
    bias_three = jnp.stack([proj_bias[0], jnp.zeros_like(proj_bias[0]), proj_bias[1]])
    causal = places[None, :] <= my_places[:, None]
    itself = places[None, :] == my_places[:, None]
    shaped_like = (
        first_gain,
        first_shift,
        proj_weight,
        proj_bias,
        mixer_weight,
        mixer_bias,
        second_gain,
        second_shift,
        up_weight,
        up_bias,
        down_weight,
        down_bias,
    )
    running = tuple((jnp.zeros(item.shape, jnp.float32) for item in shaped_like))
    out_list = []
    grad_list = []
    for micro_index in range(micro_count):
        x_now = inputs[micro_index].astype(jnp.float32)
        seg_keys = seg_store[micro_index]
        seg_mine = lax.dynamic_slice_in_dim(seg_keys, offset, tok_len, 1)
        visible = (keep_store[micro_index] > 0)[:, None, :] | itself[None]
        allowed = causal[None] & (seg_keys[:, None, :] == seg_mine[:, :, None]) & visible
        normed_one = layer_norm(x_now, first_gain, first_shift).astype(jnp.bfloat16)
        projected = jnp.einsum(
            "std,dc->stc", normed_one, proj_flat, preferred_element_type=jnp.float32
        )
        projected = (projected.reshape(seq_count, tok_len, 3, inner_width) + bias_three).astype(
            jnp.bfloat16
        )
        queries = projected[:, :, 0]
        key_here = projected[:, :, 1]
        value_here = projected[:, :, 2]
        key_all, value_all = (
            lax.all_gather(key_here, "ctx", axis=1, tiled=True),
            lax.all_gather(value_here, "ctx", axis=1, tiled=True),
        )
        heads_out, log_total = attend(queries, key_all, value_all, allowed, heads_here, scaler)
        heads_low = heads_out.astype(jnp.bfloat16)
        mixed_part = jnp.einsum(
            "stn,nd->std", heads_low, mixer_weight, preferred_element_type=jnp.float32
        )
        resid = (
            x_now + lax.psum(mixed_part.astype(jnp.bfloat16), "tp").astype(jnp.float32) + mixer_bias
        )
        normed_two = layer_norm(resid, second_gain, second_shift).astype(jnp.bfloat16)
        pre_act = (
            jnp.einsum("std,df->stf", normed_two, up_weight, preferred_element_type=jnp.float32)
            + up_bias
        )
        act_low = gelu_exact(pre_act).astype(jnp.bfloat16)
        feed_part = jnp.einsum(
            "stf,fd->std", act_low, down_weight, preferred_element_type=jnp.float32
        )
        feed = lax.psum(feed_part.astype(jnp.bfloat16), "tp").astype(jnp.float32) + down_bias
        out_list.append((resid + feed).astype(jnp.bfloat16))
        cot_low = out_cotangent[micro_index]
        cot_full = cot_low.astype(jnp.float32)
        down_bias_part = jnp.sum(cot_full, axis=(0, 1))
        down_part = jnp.einsum("stf,std->fd", act_low, cot_low, preferred_element_type=jnp.float32)
        grad_act = jnp.einsum(
            "std,fd->stf", cot_low, down_weight, preferred_element_type=jnp.float32
        )
        grad_pre = jax.vjp(gelu_exact, pre_act)[1](grad_act)[0].astype(jnp.bfloat16)
        up_part = jnp.einsum(
            "std,stf->df", normed_two, grad_pre, preferred_element_type=jnp.float32
        )
        up_bias_part = jnp.sum(grad_pre.astype(jnp.float32), axis=(0, 1))
        grad_two_part = jnp.einsum(
            "stf,df->std", grad_pre, up_weight, preferred_element_type=jnp.float32
        )
        grad_two = lax.psum(grad_two_part.astype(jnp.bfloat16), "tp").astype(jnp.float32)
        resid_part, second_gain_part, second_shift_part = jax.vjp(
            layer_norm, resid, second_gain, second_shift
        )[1](grad_two)
        grad_resid = cot_full + resid_part
        grad_mix = grad_resid.astype(jnp.bfloat16)
        mixer_bias_part = jnp.sum(grad_mix.astype(jnp.float32), axis=(0, 1))
        mixer_part = jnp.einsum(
            "stn,std->nd", heads_low, grad_mix, preferred_element_type=jnp.float32
        )
        grad_heads = jnp.einsum(
            "std,nd->stn", grad_mix, mixer_weight, preferred_element_type=jnp.float32
        ).astype(jnp.bfloat16)
        key_back, value_back = (key_all, value_all)
        grad_query, grad_key, grad_value = attend_back(
            queries, key_back, value_back, allowed, log_total, grad_heads, heads_here, scaler
        )
        key_share, value_share = (
            lax.psum_scatter(
                grad_key.astype(jnp.bfloat16), "ctx", scatter_dimension=1, tiled=True
            ).astype(jnp.float32),
            lax.psum_scatter(
                grad_value.astype(jnp.bfloat16), "ctx", scatter_dimension=1, tiled=True
            ).astype(jnp.float32),
        )
        grad_proj = jnp.stack([grad_query, key_share, value_share], axis=2).astype(jnp.bfloat16)
        proj_part = jnp.einsum(
            "std,stcn->dcn", normed_one, grad_proj, preferred_element_type=jnp.float32
        )
        proj_sums = jnp.sum(grad_proj.astype(jnp.float32), axis=(0, 1))
        proj_bias_part = jnp.stack([proj_sums[0], proj_sums[2]])
        grad_one_part = jnp.einsum(
            "stc,dc->std",
            grad_proj.reshape(seq_count, tok_len, 3 * inner_width),
            proj_flat,
            preferred_element_type=jnp.float32,
        )
        grad_one = lax.psum(grad_one_part.astype(jnp.bfloat16), "tp").astype(jnp.float32)
        input_part, first_gain_part, first_shift_part = jax.vjp(
            layer_norm, x_now, first_gain, first_shift
        )[1](grad_one)
        grad_list.append(grad_resid + input_part)
        batch_grads = (
            first_gain_part,
            first_shift_part,
            proj_part,
            proj_bias_part,
            mixer_part,
            mixer_bias_part,
            second_gain_part,
            second_shift_part,
            up_part,
            up_bias_part,
            down_part,
            down_bias_part,
        )
        running = tuple((earlier + adding for earlier, adding in zip(running, batch_grads)))
    final = reduce_grads(running)
    return (
        jnp.stack(out_list),
        jnp.stack(grad_list),
        final[0],
        final[1],
        final[2],
        final[3],
        final[4],
        final[5],
        final[6],
        final[7],
        final[8],
        final[9],
        final[10],
        final[11],
    )


BF = jnp.bfloat16
F32 = jnp.float32
LOG2E = 1.4426950408889634
LOW = -1e30
ORDERS = ((1, 2), (2, 1))
COST_SHARE = 1.0


def xor_permute(values, axis, step):
    count = lax.axis_size(axis)
    return lax.ppermute(values, axis, [(i, i ^ step) for i in range(count)])


def sds(shape, dtype=BF):
    return jax.ShapeDtypeStruct(tuple(shape), dtype)


def cost(flops, moved, exps=0):
    return pl.CostEstimate(
        flops=int(flops * COST_SHARE),
        bytes_accessed=int(moved * COST_SHARE),
        transcendentals=int(exps * COST_SHARE),
    )


HBM = pltpu.MemorySpace.HBM


def launch(
    body,
    args,
    in_specs,
    outs,
    out_specs,
    scratch,
    limit,
    cost,
    name,
    after,
    grid=(),
    aliases=None,
    scalars=(),
):
    first, last = len(after), len(after) + len(args) + len(outs)

    def inner(*refs):
        fixed, refs = refs[: len(scalars)], refs[len(scalars) :]
        body(*fixed, *refs[first:last], *refs[last + 1 :])

    token = pl.BlockSpec(memory_space=HBM)
    *results, done = pl.pallas_call(
        inner,
        grid_spec=pltpu.PrefetchScalarGridSpec(
            num_scalar_prefetch=len(scalars),
            grid=grid,
            in_specs=[token] * first + list(in_specs),
            out_specs=(*out_specs, token),
            scratch_shapes=list(scratch),
        ),
        out_shape=(*outs, sds((8, 128), F32)),
        input_output_aliases={first + key: value for key, value in (aliases or {}).items()},
        compiler_params=pltpu.CompilerParams(vmem_limit_bytes=limit),
        cost_estimate=cost,
        name=name,
    )(*scalars, *after, *args)
    return results, (done,)


class Part:
    def __init__(self, array, index):
        self.array, self.index = array, index
        self.shape, self.dtype = array.shape[1:], array.dtype

    def spec(self):
        index, rest = self.index, (0,) * len(self.shape)
        return pl.BlockSpec((None,) + self.shape, lambda *_: (index,) + rest)


def operands_of(args):
    arrays = [arg.array if isinstance(arg, Part) else arg for arg in args]
    return [array if array.dtype == jnp.int32 else pinned(array) for array in arrays]


def pinned(array):
    return pltpu.with_memory_space_constraint(array, HBM)


def run_kernel(body, outs, args, flops=0, exps=0, scratch=(), limit=8, name=None, after=(), in_hbm=()):
    specs = []
    moved = 0
    for place, arg in enumerate(args):
        if arg.dtype == jnp.int32 and math.prod(arg.shape) <= 8:
            specs.append(pl.BlockSpec(memory_space=pltpu.SMEM))
        elif place in in_hbm:
            specs.append(pl.BlockSpec(memory_space=HBM))
        else:
            specs.append(pl.BlockSpec(memory_space=pltpu.VMEM))
            moved += math.prod(arg.shape) * arg.dtype.itemsize
    moved += sum(math.prod(o.shape) * o.dtype.itemsize for o in outs)
    kept = [item for item in scratch if item.dtype in (BF, F32)]
    held = moved + sum(math.prod(item.shape) * item.dtype.itemsize for item in kept)
    return launch(
        body,
        [pinned(arg) if place in in_hbm else arg for place, arg in enumerate(args)],
        specs,
        outs,
        [pl.BlockSpec(memory_space=pltpu.VMEM) for _ in outs],
        scratch,
        held + (limit << 20),
        cost(flops, moved, exps),
        name,
        after,
    )


def whole_of(shape):
    return pl.BlockSpec(shape, lambda *_, n=len(shape): (0,) * n)


def rows_at(start, count):
    return pl.ds(pl.multiple_of(start, count), count)


def reduce_first(messages):
    return [
        (messages[2 * part + 1], xor_permute(messages[2 * part], "tp", first))
        for part, (first, _) in enumerate(ORDERS)
    ]


def reduce_second(state, after=()):
    shape = state[0][0].shape[:-3] + state[0][0].shape[-2:]

    def body(*refs):
        for part in range(2):
            keep, got = refs[2 * part : 2 * part + 2]
            refs[4 + part][...] = keep[..., 0, :, :].astype(F32) + got[..., 0, :, :].astype(F32)
            value = keep[..., 1, :, :].astype(F32) + got[..., 1, :, :].astype(F32)
            refs[6 + part][...] = value.astype(BF)

    (*rest, low, high), done = run_kernel(
        body,
        [sds(shape, F32)] * 2 + [sds(shape)] * 2,
        [item for pair in state for item in pair],
        after=after,
        name="reduce_middle",
        limit=4,
    )
    sums = []
    for part, (_, second) in enumerate(ORDERS):
        sums += [rest[part], xor_permute((low, high)[part], "tp", second)]
    return sums, done


def reduce_direct(messages):
    mine, *sent = messages
    return [mine] + [xor_permute(item, "tp", 1 + step) for step, item in enumerate(sent)]


def gather_first(halves):
    return [
        (halves[part], xor_permute(halves[part], "tp", first))
        for part, (first, _) in enumerate(ORDERS)
    ]


def gather_second(state, after=()):
    half = state[0][0].shape
    pair_shape = half[:-2] + (2,) + half[-2:]

    def body(*refs):
        for part in range(2):
            for place in range(2):
                refs[4 + part][..., place, :, :] = refs[2 * part + place][...]

    pairs, done = run_kernel(
        body,
        [sds(pair_shape)] * 2,
        [item for pair in state for item in pair],
        after=after,
        name="gather_middle",
        limit=3,
    )
    pieces = []
    for part, (_, second) in enumerate(ORDERS):
        pieces += [*state[part], xor_permute(pairs[part], "tp", second)]
    return pieces, done


def gather_direct(mine):
    return [mine] + [xor_permute(mine, "tp", step) for step in (1, 2, 3)]


def total_of(refs):
    if refs[0].dtype == BF:
        return sum([ref[...].astype(F32) for ref in refs[1:]], refs[0][...].astype(F32))
    halves = [refs[2 * part][...] + refs[2 * part + 1][...].astype(F32) for part in range(2)]
    return jnp.concatenate(halves, axis=0)


def place_gathered(store, tp_here, refs, size):
    if len(refs) == 4:
        for step, ref in enumerate(refs):
            store(rows_at((tp_here ^ step) * size, size), ref[...])
        return
    half = size // 2
    for part, (first, second) in enumerate(ORDERS):
        mine, near, far = refs[3 * part : 3 * part + 3]
        parts = ((0, mine[...]), (first, near[...]), (second, far[0]), (first | second, far[1]))
        for step, value in parts:
            store(rows_at((tp_here ^ step) * size + part * half, half), value)


def emit_messages(load, tp_here, refs, size):
    if refs[0].shape[-2] == size:
        for step, ref in enumerate(refs):
            ref[...] = load(rows_at((tp_here ^ step) * size, size))
        return
    half = size // 2
    for part, (first, second) in enumerate(ORDERS):
        send, keep = refs[2 * part], refs[2 * part + 1]
        for ref, steps in ((send, (first, first | second)), (keep, (0, second))):
            for place, step in enumerate(steps):
                ref[place] = load(rows_at((tp_here ^ step) * size + part * half, half))


def emit_shard(value, refs):
    rows = value.shape[0] // len(refs)
    for place, ref in enumerate(refs):
        ref[...] = value[place * rows : (place + 1) * rows]


def shard_shapes(size, width, direct=False):
    return [sds((size, width))] if direct else [sds((size // 2, width))] * 2


def message_shapes(half, width, direct=False):
    return [sds((2 * half, width) if direct else (2, half, width))] * 4


def exchange_chips(local, cross, first, second, third):
    got = [
        xor_permute(item, "ctx", 2 * (place + 1))
        for place, item in enumerate((first, second, third))
    ]
    return [local, cross] + got


def exchange_cores(state, after):
    local, cross, *got = state

    lead = cross.shape[:-2]

    def body(cross_ref, first_ref, second_ref, third_ref, out_ref):
        out_ref[..., 0, :, :] = cross_ref[...]
        for place, ref in enumerate((first_ref, second_ref, third_ref)):
            out_ref[..., place + 1, :, :] = ref[..., 1, :, :]

    (packed,), done = run_kernel(
        body, [sds(lead + (4,) + cross.shape[-2:])], [cross] + got, after=after, limit=2, name="pack"
    )
    return [local] + got + [xor_permute(packed, "ctx", 1)], done


def exchanged(refs, here):
    local, first, second, third, packed = refs
    return (
        (here, local[...]),
        (here ^ 1, packed[0]),
        (here ^ 2, first[0]),
        (here ^ 3, packed[1]),
        (here ^ 4, second[0]),
        (here ^ 5, packed[2]),
        (here ^ 6, third[0]),
        (here ^ 7, packed[3]),
    )


def emit_exchange(load, here, refs):
    local, cross, first, second, third = refs
    local[...] = load(here)
    cross[...] = load(here ^ 1)
    for place, ref in enumerate((first, second, third)):
        other = here ^ (2 * (place + 1))
        ref[0] = load(other)
        ref[1] = load(other ^ 1)


def exchange_shapes(rows, width):
    return [sds((rows, width)), sds((rows, width))] + [sds((2, rows, width))] * 3


def normalized(values):
    center = values - jnp.mean(values, axis=-1, keepdims=True)
    spread = jnp.mean(center * center, axis=-1, keepdims=True)
    root = lax.rsqrt(spread + 1e-05)
    return center * root, root


def norm_back(values, gain, grad):
    unit, root = normalized(values)
    scaled = grad * gain
    back = root * (
        scaled
        - jnp.mean(scaled, axis=-1, keepdims=True)
        - unit * jnp.mean(scaled * unit, axis=-1, keepdims=True)
    )
    gain_sum = jnp.sum(grad * unit, axis=0, keepdims=True)
    shift_sum = jnp.sum(grad, axis=0, keepdims=True)
    return back, gain_sum, shift_sum


def dot(left, right):
    return jnp.dot(left, right, preferred_element_type=F32)


def dot_nt(left, right):
    return lax.dot_general(left, right, (((1,), (1,)), ((), ())), preferred_element_type=F32)


def dot_tn(left, right):
    return lax.dot_general(left, right, (((0,), (0,)), ((), ())), preferred_element_type=F32)


def project(here, x_all, index, gain, shift, weight, bias, tok_len, after=()):
    _, rows, width = x_all.shape
    inner = weight.shape[2]
    heads = inner // HD

    def body(here_ref, x_ref, gain_ref, shift_ref, weight_hbm, bias_ref, *rest):
        norm_ref, outs = rest[0], rest[1:6]
        held, weight_ref, x_held, gain_held, shift_held, bias_held, sems = rest[6:]
        fetches = [
            pltpu.make_async_copy(source, target, sems.at[3 + number])
            for number, (source, target) in enumerate(
                (
                    (x_ref.at[index], x_held),
                    (gain_ref, gain_held),
                    (shift_ref, shift_held),
                    (bias_ref, bias_held),
                )
            )
        ]
        for fetch in fetches:
            fetch.start()
        copies = [
            pltpu.make_async_copy(weight_hbm.at[part], weight_ref.at[part], sems.at[part])
            for part in range(3)
        ]
        for copy in copies:
            copy.start()
        for fetch in fetches:
            fetch.wait()
        unit, _ = normalized(x_held[...].astype(F32))
        norm_ref[...] = (unit * gain_held[...] + shift_held[...]).astype(BF)
        for part in range(3):
            copies[part].wait()
            value = dot(norm_ref[...], weight_ref[part])
            if part != 1:
                value += bias_held[part // 2 : part // 2 + 1]
            value = value.astype(BF)
            for head in range(heads):
                held[head, :, part * HD : (part + 1) * HD] = value[:, head * HD : (head + 1) * HD]

        def load(unit_id):
            return held[unit_id % heads, rows_at(unit_id // heads * tok_len, tok_len), :]

        emit_exchange(load, here_ref[0], outs)

    return run_kernel(
        body,
        [sds((rows, width))] + exchange_shapes(tok_len, 3 * HD),
        [here, x_all, gain, shift, weight, bias],
        flops=6 * rows * width * inner,
        scratch=[
            pltpu.VMEM((heads, rows, 3 * HD), BF),
            pltpu.VMEM(weight.shape, BF),
            pltpu.VMEM((rows, width), BF),
            pltpu.VMEM(gain.shape, F32),
            pltpu.VMEM(shift.shape, F32),
            pltpu.VMEM(bias.shape, F32),
            pltpu.SemaphoreType.DMA((7,)),
        ],
        name="project",
        limit=14,
        after=after,
        in_hbm=(1, 2, 3, 4, 5),
    )


def rows_of_device(device, block, blocks):
    return (
        rows_at(device * block, block),
        rows_at((blocks - 1 - device) * block, block),
    )


def attention(here, received, seg_row, key_row, heads, after=()):
    tok_len = received[0].shape[0]
    block = tok_len // 2
    seq_len = seg_row.shape[2]
    blocks = seq_len // block
    step = 256
    factor = LOG2E / math.sqrt(HD)

    def body(here_ref, *rest):
        refs, seg_ref, key_ref = rest[:5], rest[5], rest[6]
        outs, lse_ref = rest[7:12], rest[12]
        q_all, k_turned, v_all, mixed = rest[13:]
        me = here_ref[0]
        seq = me // heads
        for device, value in exchanged(refs, me):
            for half, place in enumerate(rows_of_device(device, block, blocks)):
                rows = value[half * block : (half + 1) * block]
                q_all[place] = rows[:, :HD]
                k_turned[:, place] = rows[:, HD : 2 * HD].T
                v_all[place] = rows[:, 2 * HD :]
        for number in range(seq_len // step):
            start, stop = number * step, (number + 1) * step
            segs = as_column(seg_ref[seq, :, start:stop])
            scores = dot(q_all[start:stop], k_turned[:, :stop]) * factor
            scores = masked(scores, segs, key_ref, seq, start, stop)
            top = jnp.max(scores, axis=-1, keepdims=True)
            raised = jnp.exp2(scores - top)
            total = jnp.sum(raised, axis=-1, keepdims=True)
            out = dot(raised.astype(BF), v_all[:stop]) / total
            mixed[start:stop] = out.astype(BF)
            lse_ref[start:stop] = top + jnp.log2(total)

        def load(device):
            return jnp.concatenate(
                [mixed[place] for place in rows_of_device(device, block, blocks)], axis=0
            )

        emit_exchange(load, me, outs)

    return run_kernel(
        body,
        exchange_shapes(tok_len, HD) + [sds((seq_len, 1), F32)],
        [here] + list(received) + [seg_row, key_row],
        flops=2 * 2 * seq_len * seq_len * HD,
        exps=seq_len * seq_len // 2,
        scratch=[
            pltpu.VMEM((seq_len, HD), BF),
            pltpu.VMEM((HD, seq_len), BF),
            pltpu.VMEM((seq_len, HD), BF),
            pltpu.VMEM((seq_len, HD), BF),
        ],
        after=after,
        name="attention",
        limit=16,
    )


def as_column(row):
    return jnp.broadcast_to(row, (128, row.shape[1])).T[:, :1]


def masked(scores, segs, key_ref, seq, start, stop):
    size = stop - start
    row = lax.broadcasted_iota(jnp.int32, (size, size), 0)
    column = lax.broadcasted_iota(jnp.int32, (size, size), 1)
    same = segs == key_ref[seq, :, start:stop]
    seen = (same & (column < row)) | (column == row)
    corner = jnp.where(seen, scores[:, start:], LOW)
    if start == 0:
        return corner
    left = jnp.where(segs == key_ref[seq, :, :start], scores[:, :start], LOW)
    return jnp.concatenate([left, corner], axis=1)


def attention_back(
    here, received, grads, seg_row, key_row, lse, heads, earlier, index, count, after=()
):
    tok_len = received[0].shape[0]
    block = tok_len // 2
    seq_len = seg_row.shape[2]
    blocks = seq_len // block
    step = 256
    scaler = 1.0 / math.sqrt(HD)

    def body(here_ref, *rest):
        refs, grad_refs = rest[:5], rest[5:10]
        seg_ref, key_ref, lse_ref = rest[10:13]
        rest = rest[13 + len(earlier) :]
        outs = [ref.at[0] for ref in rest[:5]]
        q_all, k_all, k_turned, v_turned, g_all, result, dk_turned, dv_turned = rest[5:]
        me = here_ref[0]
        seq = me // heads
        for device, value in exchanged(refs, me):
            for half, place in enumerate(rows_of_device(device, block, blocks)):
                rows = value[half * block : (half + 1) * block]
                q_all[place] = rows[:, :HD]
                k_all[place] = rows[:, HD : 2 * HD]
                k_turned[:, place] = rows[:, HD : 2 * HD].T
                v_turned[:, place] = rows[:, 2 * HD :].T
        for device, value in exchanged(grad_refs, me):
            for half, place in enumerate(rows_of_device(device, block, blocks)):
                g_all[place] = value[half * block : (half + 1) * block]
        last = seq_len // step - 1
        for number in range(last, -1, -1):
            start, stop = number * step, (number + 1) * step
            segs = as_column(seg_ref[seq, :, start:stop])
            query, grad = q_all[start:stop], g_all[start:stop]
            scores = dot(query, k_turned[:, :stop]) * (scaler * LOG2E)
            scores = masked(scores, segs, key_ref, seq, start, stop)
            probs = jnp.exp2(scores - lse_ref[start:stop])
            grad_probs = dot(grad, v_turned[:, :stop])
            inner = jnp.sum(probs * grad_probs, axis=-1, keepdims=True)
            grad_scores = (probs * (grad_probs - inner)).astype(BF)
            dv_part = dot_tn(grad, probs.astype(BF))
            dk_part = dot_tn(query, grad_scores)
            if number == last:
                dv_turned[...] = dv_part
                dk_turned[...] = dk_part
            else:
                dv_turned[:, :stop] += dv_part
                dk_turned[:, :stop] += dk_part
            dq = dot(grad_scores, k_all[:stop]) * scaler
            result[start:stop, :HD] = dq.astype(BF)
        for number in range(last + 1):
            start, stop = number * step, (number + 1) * step
            result[start:stop, HD : 2 * HD] = (dk_turned[:, start:stop] * scaler).T.astype(BF)
            result[start:stop, 2 * HD :] = dv_turned[:, start:stop].T.astype(BF)

        def load(device):
            return jnp.concatenate(
                [result[place] for place in rows_of_device(device, block, blocks)], axis=0
            )

        emit_exchange(load, me, outs)

    shapes = exchange_shapes(tok_len, 3 * HD)
    args = [here, *received, *grads, seg_row, key_row, lse, *earlier]
    first = len(args) - len(earlier)
    return launch(
        body,
        operands_of(args),
        [pl.BlockSpec(memory_space=pltpu.SMEM)]
        + [whole_of(item.shape) for item in args[1:first]]
        + [pl.BlockSpec(memory_space=pl.ANY) for _ in earlier],
        [sds((count,) + item.shape) for item in shapes],
        [
            pl.BlockSpec((1,) + item.shape, lambda i, n=len(item.shape): (index,) + (0,) * n)
            for item in shapes
        ],
        [
            pltpu.VMEM((seq_len, HD), BF),
            pltpu.VMEM((seq_len, HD), BF),
            pltpu.VMEM((HD, seq_len), BF),
            pltpu.VMEM((HD, seq_len), BF),
            pltpu.VMEM((seq_len, HD), BF),
            pltpu.VMEM((seq_len, 3 * HD), BF),
            pltpu.VMEM((HD, seq_len), F32),
            pltpu.VMEM((HD, seq_len), F32),
        ],
        36 << 20,
        cost(5 * seq_len * seq_len * HD, 12 * seq_len * HD),
        "attention_back",
        after,
        grid=(1,),
        aliases={first + number: number for number in range(len(earlier))},
    )


def mix_heads(here, tp_here, received, weight, heads, direct, after=()):
    tok_len = received[0].shape[0]
    inner, width = weight.shape
    rows = len_units(received) * tok_len // heads
    size = rows // 4

    def body(here_ref, tp_ref, *rest):
        refs, weight_ref = rest[:5], rest[5]
        heads_ref, outs, held = rest[6], rest[7:11], rest[11]
        for unit_id, value in exchanged(refs, here_ref[0]):
            column = pl.multiple_of(unit_id % heads * HD, HD)
            heads_ref[rows_at(unit_id // heads * tok_len, tok_len), pl.ds(column, HD)] = value
        for start in range(0, width, 512):
            held[:, start : start + 512] = dot(
                heads_ref[...], weight_ref[:, start : start + 512]
            ).astype(BF)
        emit_messages(lambda place: held[place, :], tp_ref[0], outs, size)

    return run_kernel(
        body,
        [sds((rows, inner))] + message_shapes(size // 2, width, direct),
        [here, tp_here] + list(received) + [weight],
        flops=2 * rows * inner * width,
        scratch=[pltpu.VMEM((rows, width), BF)],
        after=after,
        name="mix_heads",
        limit=6,
    )


def len_units(received):
    return 2 * received[-1].shape[0]


def second_norm(sums, x_mine, mixer_bias, gain, shift, direct, after=()):
    size, width = x_mine.shape
    count = len(sums)

    def body(*rest):
        refs, (x_ref, bias_ref, gain_ref, shift_ref) = rest[:count], rest[count : count + 4]
        resid_ref, outs = rest[count + 4], rest[count + 5 :]
        resid = x_ref[...].astype(F32) + total_of(refs) + bias_ref[...]
        resid_ref[...] = resid
        unit, _ = normalized(resid)
        emit_shard((unit * gain_ref[...] + shift_ref[...]).astype(BF), outs)

    return run_kernel(
        body,
        [sds((size, width), F32)] + shard_shapes(size, width, direct),
        list(sums) + [x_mine, mixer_bias, gain, shift],
        name="second_norm",
        limit=8,
        after=after,
    )


def feed_inner(
    tp_here, pieces, cot, up_weight, up_bias, down_weight, earlier, index, with_grad, after=()
):
    rows, width = cot.shape
    hidden = up_weight.shape[1]
    size = rows // 4
    step = 512
    blocks = hidden // step

    def body(tp_ref, *rest):
        refs, rest = rest[: len(pieces)], rest[len(pieces) :]
        cot_ref, up_hbm, bias_ref, down_hbm = rest[:4]
        rest = rest[4 + len(earlier) :]
        norm_ref, act_ref, pre_ref = [ref.at[0] for ref in rest[:3]]
        sum_ref, cot_sum_ref = rest[3:5]
        grad_outs = rest[5:9] if with_grad else ()
        up, down, held, sems = rest[-4:]

        def part(number):
            return pl.ds(pl.multiple_of(number * step, step), step)

        def copies(number):
            place = part(number)
            return (
                pltpu.make_async_copy(up_hbm.at[:, place], up.at[:, place], sems.at[0, number]),
                pltpu.make_async_copy(down_hbm.at[place, :], down.at[place, :], sems.at[1, number]),
            )

        for number in range(blocks):
            for copy in copies(number):
                copy.start()

        def store(place, value):
            norm_ref[place, :] = value

        place_gathered(store, tp_ref[0], refs, size)
        cot_sum_ref[...] = jnp.sum(cot_ref[...].astype(F32), axis=0, keepdims=True)

        @pl.loop(0, blocks)
        def _(number):
            for copy in copies(number):
                copy.wait()
            place = part(number)
            pre = dot(norm_ref[...], up[:, place]) + bias_ref[:, place]
            grad_act = dot_nt(cot_ref[...], down[place, :])
            spread = 0.5 + 0.5 * lax.erf(pre * math.sqrt(0.5))
            dense = jnp.exp(-0.5 * pre * pre) * (1.0 / math.sqrt(2.0 * math.pi))
            act_ref[:, place] = (pre * spread).astype(BF)
            grad_pre = (grad_act * (spread + pre * dense)).astype(BF)
            pre_ref[:, place] = grad_pre
            sum_ref[:, place] = jnp.sum(grad_pre.astype(F32), axis=0, keepdims=True)

        if with_grad:

            @pl.loop(0, width // step)
            def _(number):
                place = part(number)
                held[:, place] = dot_nt(pre_ref[...], up[place, :]).astype(BF)

            emit_messages(lambda at: held[at, :], tp_ref[0], grad_outs, size)

    args = [tp_here, *pieces, cot, up_weight, up_bias, down_weight]
    count = cot.array.shape[0]
    wide = [(1, rows, width), (1, rows, hidden), (1, rows, hidden)]
    outs = [sds((1, hidden), F32), sds((1, width), F32)]
    outs += message_shapes(size // 2, width, True) if with_grad else []
    return launch(
        body,
        operands_of(args) + list(earlier),
        [pl.BlockSpec(memory_space=pltpu.SMEM)]
        + [whole_of(piece.shape) for piece in pieces]
        + [cot.spec(), pl.BlockSpec(memory_space=HBM), whole_of(up_bias.shape)]
        + [pl.BlockSpec(memory_space=HBM)] * (1 + len(earlier)),
        [HBM((count,) + shape[1:], BF) for shape in wide] + outs,
        [pl.BlockSpec(shape, lambda i: (index, 0, 0)) for shape in wide]
        + [whole_of(item.shape) for item in outs],
        [
            pltpu.VMEM((width, hidden), BF),
            pltpu.VMEM((hidden, width), BF),
            pltpu.VMEM((rows, width), BF),
            pltpu.SemaphoreType.DMA((2, blocks)),
        ],
        50 << 20,
        cost(6 * rows * width * hidden, 4 * width * hidden + 20 * rows * width),
        "feed_inner",
        after,
        grid=(1,),
        aliases={len(args) + number: number for number in range(len(earlier))},
    )


def stacked(array):
    return array.reshape((-1, array.shape[-1]))


def feed_grad(tp_here, grad_pre, up_weight, after=()):
    rows, hidden = grad_pre.shape
    width = up_weight.shape[0]
    size = rows // 4
    step = 512
    blocks = width // step

    def body(tp_ref, pre_ref, up_ref, *rest):
        outs, held = rest[:4], rest[4]
        number = pl.program_id(0)
        place = pl.ds(pl.multiple_of(number * step, step), step)
        held[:, place] = dot_nt(pre_ref[...], up_ref[...]).astype(BF)

        @pl.when(number == blocks - 1)
        def _():
            emit_messages(lambda at: held[at, :], tp_ref[0], outs, size)

    outs = message_shapes(size // 2, width)
    return launch(
        body,
        operands_of([tp_here, grad_pre, up_weight]),
        [
            pl.BlockSpec(memory_space=pltpu.SMEM),
            grad_pre.spec(),
            pl.BlockSpec((step, hidden), lambda i: (i, 0)),
        ],
        outs,
        [whole_of(item.shape) for item in outs],
        [pltpu.VMEM((rows, width), BF)],
        24 << 20,
        cost(2 * rows * width * hidden, 2 * width * hidden + 6 * rows * width),
        "feed_grad",
        after,
        grid=(blocks,),
    )


def feed_out(tp_here, acts, down_weight, after=()):
    count = len(acts)
    rows, hidden = acts[0].shape
    width = down_weight.shape[1]
    size = rows // 4
    step = 512
    blocks = width // step

    def body(tp_ref, *rest):
        act_refs, down_ref, outs, held = rest[:count], rest[count], rest[-5:-1], rest[-1]
        number = pl.program_id(0)
        place = pl.ds(pl.multiple_of(number * step, step), step)
        for index in range(count):
            held[index, :, place] = dot(act_refs[index][...], down_ref[...]).astype(BF)

        @pl.when(number == blocks - 1)
        def _():
            for index in range(count):
                emit_messages(
                    lambda at: held[index, at, :],
                    tp_ref[0],
                    [ref.at[index] for ref in outs],
                    size,
                )

    outs = [sds((count,) + item.shape) for item in message_shapes(size // 2, width)]
    return launch(
        body,
        operands_of([tp_here, *acts, down_weight]),
        [pl.BlockSpec(memory_space=pltpu.SMEM)]
        + [act.spec() for act in acts]
        + [pl.BlockSpec((hidden, step), lambda i: (0, i))],
        outs,
        [whole_of(item.shape) for item in outs],
        [pltpu.VMEM((count, rows, width), BF)],
        36 << 20,
        cost(2 * count * rows * width * hidden, 2 * width * hidden + 12 * rows * width),
        "feed_out",
        after,
        grid=(blocks,),
    )


def second_norm_back(sums, resid, cot_mine, gain, direct, after=()):
    size, width = resid.shape
    count = len(sums)

    def body(*rest):
        refs, (resid_ref, cot_ref, gain_ref) = rest[:count], rest[count : count + 3]
        grad_ref, gain_out, shift_out, *outs = rest[count + 3 :]
        back, gain_sum, shift_sum = norm_back(resid_ref[...], gain_ref[...], total_of(refs))
        grad = back + cot_ref[...].astype(F32)
        grad_ref[...] = grad
        emit_shard(grad.astype(BF), outs)
        gain_out[...] = gain_sum
        shift_out[...] = shift_sum

    return run_kernel(
        body,
        [sds((size, width), F32)]
        + [sds((1, width), F32)] * 2
        + shard_shapes(size, width, direct),
        list(sums) + [resid, cot_mine, gain],
        name="second_norm_back",
        limit=10,
        after=after,
    )


def first_norm_back(sums, x_mine, grad_resids, gain, after=()):
    count = len(x_mine)
    size, width = grad_resids[0].shape

    def body(*rest):
        refs, rest = rest[:4], rest[4:]
        x_refs, grad_refs, gain_ref = rest[:count], rest[count : 2 * count], rest[2 * count]
        gain_out, shift_out, *outs = rest[2 * count + 1 :]
        for index in range(count):
            back, gain_sum, shift_sum = norm_back(
                x_refs[index][...].astype(F32),
                gain_ref[...],
                total_of([ref.at[index] for ref in refs]),
            )
            emit_shard(
                (back + grad_refs[index][...]).astype(BF), [ref.at[index] for ref in outs]
            )
            gain_out[...] = gain_sum if index == 0 else gain_out[...] + gain_sum
            shift_out[...] = shift_sum if index == 0 else shift_out[...] + shift_sum

    return run_kernel(
        body,
        [sds((1, width), F32)] * 2
        + [sds((count,) + item.shape) for item in shard_shapes(size, width)],
        list(sums) + list(x_mine) + list(grad_resids) + [gain],
        name="first_norm_back",
        limit=10,
        after=after,
    )


def finish_outputs(sums, resids, bias, after=()):
    size, width = resids[0].shape
    half = size // 2
    count = len(resids)

    def body(*rest):
        refs, resid_refs, bias_ref = rest[:4], rest[4 : 4 + count], rest[4 + count]
        low_ref, high_ref = rest[5 + count :]
        for index in range(count):
            ours = [ref.at[index] for ref in refs]
            value = (resid_refs[index][...] + total_of(ours) + bias_ref[...]).astype(BF)
            low_ref[index] = value[:half]
            high_ref[index] = value[half:]

    return run_kernel(
        body,
        [sds((count, half, width))] * 2,
        list(sums) + list(resids) + [bias],
        after=after,
        name="finish_outputs",
        limit=8,
    )


def assemble_outputs(tp_here, pieces, dtype, after=()):
    count, half, width = pieces[0].shape
    size = 2 * half
    rows = 4 * size

    def block_of(shape):
        return pl.BlockSpec((1,) + shape[1:], lambda i, n=len(shape) - 1: (i,) + (0,) * n)

    def body(tp_ref, *rest):
        refs, out_ref = rest[:6], rest[6]

        def store(place, value):
            out_ref[0, place, :] = value.astype(dtype)

        place_gathered(store, tp_ref[0], [ref.at[0] for ref in refs], size)

    results, done = launch(
        body,
        [tp_here] + list(pieces),
        [pl.BlockSpec(memory_space=pltpu.SMEM)] + [block_of(piece.shape) for piece in pieces],
        [HBM((count, rows, width), dtype)],
        [block_of((count, rows, width))],
        (),
        24 << 20,
        cost(0, count * rows * width * 6),
        "assemble_outputs",
        after,
        grid=(count,),
    )
    return results[0], done


def widen(part, turned, after=()):
    rows, wide = part.shape

    def body(part_ref, out_ref):
        value = part_ref[...].astype(F32)
        out_ref[...] = value.T if turned else value

    shape = (wide, rows) if turned else (rows, wide)
    return run_kernel(body, [sds(shape, F32)], [part], after=after, name="widen", limit=6)


def widen_last(part, inner, after=()):
    rows, _ = part.shape

    def body(part_ref, proj_ref, mixer_ref):
        for number in range(3):
            place = slice(number * inner, (number + 1) * inner)
            proj_ref[number] = part_ref[:, place].astype(F32)
        mixer_ref[...] = part_ref[:, 3 * inner :].astype(F32).T

    outs = [sds((3, rows, inner), F32), sds((inner, rows), F32)]
    return launch(
        body,
        operands_of([part]),
        [whole_of(part.shape)],
        outs,
        [whole_of(item.shape) for item in outs],
        (),
        16 << 20,
        cost(0, 16 * rows * inner),
        "widen",
        after,
        grid=(1,),
    )


def heads_back(here, tp_here, pieces, weight, tok_len, after=()):
    inner, width = weight.shape
    heads = inner // HD
    count = len(pieces)
    size = pieces[0].shape[0] * (1 if count == 4 else 2)
    rows = 4 * size

    def body(here_ref, tp_ref, *rest):
        refs, weight_ref, rest = rest[:count], rest[count], rest[count + 1 :]
        mix_ref, sum_ref, outs, held = rest[0], rest[1], rest[2:7], rest[7]

        def store(place, value):
            mix_ref[place, :] = value

        place_gathered(store, tp_ref[0], refs, size)
        sum_ref[...] = jnp.sum(mix_ref[...].astype(F32), axis=0, keepdims=True)
        value = dot_nt(mix_ref[...], weight_ref[...]).astype(BF)
        for head in range(heads):
            held[head] = value[:, head * HD : (head + 1) * HD]

        def load(unit_id):
            return held[unit_id % heads, rows_at(unit_id // heads * tok_len, tok_len), :]

        emit_exchange(load, here_ref[0], outs)

    return run_kernel(
        body,
        [sds((rows, width)), sds((1, width), F32)] + exchange_shapes(tok_len, HD),
        [here, tp_here] + list(pieces) + [weight],
        flops=2 * rows * inner * width,
        scratch=[pltpu.VMEM((heads, rows, HD), BF)],
        after=after,
        name="heads_back",
        limit=8,
    )


def project_back(here, tp_here, received, weight, after=()):
    count, tok_len, _ = received[0].shape
    _, width, inner = weight.shape
    heads = inner // HD
    rows = 2 * received[-1].shape[1] * tok_len // heads
    size = rows // 4

    def body(here_ref, tp_ref, *rest):
        refs, weight_ref, rest = rest[:5], rest[5], rest[6:]
        proj_refs, sum_ref, outs, held = rest[:count], rest[count], rest[-5:-1], rest[-1]
        for index, proj_ref in enumerate(proj_refs):
            for unit_id, value in exchanged([ref.at[index] for ref in refs], here_ref[0]):
                place = rows_at(unit_id // heads * tok_len, tok_len)
                for part in range(3):
                    column = pl.multiple_of(part * inner + unit_id % heads * HD, HD)
                    proj_ref[place, pl.ds(column, HD)] = value[:, part * HD : (part + 1) * HD]
            part_sum = jnp.sum(proj_ref[...].astype(F32), axis=0, keepdims=True)
            sum_ref[...] = part_sum if index == 0 else sum_ref[...] + part_sum
            for start in range(0, width, 512):
                value = dot_nt(proj_ref[:, :inner], weight_ref[0, start : start + 512])
                for part in range(1, 3):
                    value += dot_nt(
                        proj_ref[:, part * inner : (part + 1) * inner],
                        weight_ref[part, start : start + 512],
                    )
                held[:, start : start + 512] = value.astype(BF)
            emit_messages(
                lambda place: held[place, :], tp_ref[0], [ref.at[index] for ref in outs], size
            )

    return run_kernel(
        body,
        [sds((rows, 3 * inner))] * count
        + [sds((1, 3 * inner), F32)]
        + [sds((count,) + item.shape) for item in message_shapes(size // 2, width)],
        [here, tp_here] + list(received) + [weight],
        flops=6 * count * rows * inner * width,
        scratch=[pltpu.VMEM((rows, width), BF)],
        name="project_back",
        limit=10,
        after=after,
    )


def weight_grad(groups, here=None, after=()):
    count = len(groups[0][0])
    rows, tall = groups[0][0][0].shape
    widths = [rights[0].shape[1] for _, rights in groups]
    total = sum(widths)
    split = here is not None
    steps = 8 if split else 4
    step = tall // steps
    half = steps // 2

    def block_of(number, *fixed):
        if not split:
            return number
        core = fixed[0][0] & 1
        mine = number // half
        return 2 * (number % half) + (core ^ 1 ^ mine)

    def product(refs, store):
        start = 0
        for place, wide in enumerate(widths):
            ours = refs[2 * count * place : 2 * count * (place + 1)]
            value = dot_tn(ours[0][...], ours[count][...])
            for number in range(1, count):
                value += dot_tn(ours[number][...], ours[count + number][...])
            store(slice(start, start + wide), value.astype(BF))
            start += wide

    def body(*refs):
        if not split:
            out_ref = refs[-1]

            def store(place, value):
                out_ref[:, place] = value

            product(refs, store)
            return
        refs, other_ref, own_ref = refs[1:-2], refs[-2], refs[-1]
        number = pl.program_id(0)

        def into(ref):
            def store(place, value):
                ref[0, :, place] = value

            return store

        @pl.when(number < half)
        def _():
            product(refs, into(other_ref))

        @pl.when(number >= half)
        def _():
            product(refs, into(own_ref))

    args, in_specs = [], []
    for (lefts, rights), wide in zip(groups, widths):
        for item in lefts:
            if isinstance(item, Part):
                in_specs.append(
                    pl.BlockSpec(
                        (None, rows, step),
                        lambda i, *fixed, k=item.index: (k, 0, block_of(i, *fixed)),
                    )
                )
            else:
                in_specs.append(
                    pl.BlockSpec((rows, step), lambda i, *fixed: (0, block_of(i, *fixed)))
                )
        in_specs += [pl.BlockSpec((rows, wide), lambda *_: (0, 0))] * count
        args += list(lefts) + list(rights)
    if split:
        outs = [HBM((half, step, total), BF)] * 2
        out_specs = [
            pl.BlockSpec((1, step, total), lambda i, *_: (jnp.minimum(i, half - 1), 0, 0)),
            pl.BlockSpec((1, step, total), lambda i, *_: (jnp.maximum(i - half, 0), 0, 0)),
        ]
    else:
        outs = [HBM((tall, total), BF)]
        out_specs = [pl.BlockSpec((step, total), lambda i: (i, 0))]
    return launch(
        body,
        operands_of(args),
        in_specs,
        outs,
        out_specs,
        (),
        40 << 20,
        cost(
            2 * count * rows * tall * total,
            2 * (count * rows * (tall * len(groups) + total) + tall * total),
        ),
        "weight_grad",
        after,
        grid=(steps,),
        scalars=(here,) if split else (),
    )


def add_halves(own, got, after=()):
    def body(own_ref, got_ref, out_ref):
        out_ref[...] = (own_ref[...].astype(F32) + got_ref[...].astype(F32)).astype(BF)

    block_spec = pl.BlockSpec((1,) + own.shape[1:], lambda i: (i, 0, 0))
    return launch(
        body,
        operands_of([own, got]),
        [block_spec] * 2,
        [HBM(own.shape, BF)],
        [block_spec],
        (),
        16 << 20,
        cost(0, 6 * math.prod(own.shape)),
        "add_halves",
        after,
        grid=(own.shape[0],),
    )


def small_sums(values):
    here = lax.axis_index("ctx")
    step = values.shape[0] // 2
    while step:
        pair = values.reshape((2, step) + values.shape[1:])
        bit = (here // step) % 2
        keep = lax.dynamic_index_in_dim(pair, bit, 0, False)
        send = lax.dynamic_index_in_dim(pair, 1 - bit, 0, False)
        values = keep + xor_permute(send, "ctx", step)
        step //= 2
    return values[0]


def per_device_exchanged(
    inputs,
    segments,
    keep_mask,
    first_gain,
    first_shift,
    proj_weight,
    proj_bias,
    mixer_weight,
    mixer_bias,
    second_gain,
    second_shift,
    up_weight,
    up_bias,
    down_weight,
    down_bias,
    out_cotangent,
):
    ctx_count = lax.axis_size("ctx")
    micro_count, seq_count, tok_len, width = inputs.shape
    inner = proj_bias.shape[1]
    heads = inner // HD
    rows = seq_count * tok_len
    here = lax.axis_index("ctx").astype(jnp.int32).reshape(1)
    tp_here = lax.axis_index("tp").astype(jnp.int32).reshape(1)
    weight_three = jnp.transpose(proj_weight, (1, 0, 2))
    x_all = inputs.reshape(micro_count, rows, width)
    cot_all = out_cotangent.reshape(micro_count, rows, width)
    key_rows = jnp.where(keep_mask > 0, segments, -1)[:, :, None, :]
    gain_one, shift_one = first_gain[None], first_shift[None]
    gain_two, shift_two = second_gain[None], second_shift[None]
    mix_bias, low_bias, high_bias = mixer_bias[None], down_bias[None], up_bias[None]
    micro = range(micro_count)

    key_rows = [key_rows[index] for index in micro]
    seg_rows = [segments[index][:, None, :] for index in micro]
    cots = [Part(cot_all, index) for index in micro]
    size = rows // lax.axis_size("tp")
    start = tp_here[0] * size
    x_mine = [lax.dynamic_slice(x_all, (index, start, 0), (1, size, width))[0] for index in micro]
    cot_mine = [
        lax.dynamic_slice(cot_all, (index, start, 0), (1, size, width))[0] for index in micro
    ]

    chips = [[core + 2 * chip for chip in range(ctx_count // 2)] for core in range(2)]

    def scattered(part):
        return lax.psum_scatter(part, "ctx", scatter_dimension=0, tiled=True)

    def scattered_chips(part):
        part = part.reshape(-1, part.shape[2])
        return lax.psum_scatter(
            part, "ctx", scatter_dimension=0, axis_index_groups=chips, tiled=True
        )

    def until(items, *points):
        held, _ = lax.optimization_barrier((items, points))
        return held

    norm_one, received, lses, heads_low, resids = [], [], [], [], []

    def project_micro(index, done):
        (normed, *sent), done = project(
            here, x_all, index, gain_one, shift_one, weight_three, proj_bias, tok_len, after=done
        )
        norm_one.append(normed)
        return exchange_chips(*sent), done

    def attend_micro(index, got, done):
        received.append(got)
        (*sent, lse), done = attention(
            here, got, seg_rows[index], key_rows[index], heads, after=done
        )
        lses.append(lse)
        return exchange_chips(*sent), done

    def mix_micro(got, direct, done):
        (mixed, *messages), done = mix_heads(
            here, tp_here, got, mixer_weight, heads, direct, after=done
        )
        heads_low.append(mixed)
        return messages, done

    def norm_micro(index, sums, direct, done):
        (resid, *shard), done = second_norm(
            sums, x_mine[index], mix_bias, gain_two, shift_two, direct, after=done
        )
        resids.append(resid)
        return shard if direct else gather_first(shard), done

    up_sums, cot_sums = [], []

    def feed_micro(index, pieces, earlier, with_grad, done):
        (norms, acts, pres, up_sum, cot_sum, *messages), done = feed_inner(
            tp_here,
            pieces,
            cots[index],
            up_weight,
            high_bias,
            down_weight,
            earlier,
            index,
            with_grad,
            after=done,
        )
        up_sums.append(up_sum)
        cot_sums.append(cot_sum)
        return (norms, acts, pres), messages, done

    grad_resids, gain_twos, shift_twos = [], [], []
    grad_mixes, mix_sums, states = [], [], []

    def norm_back_micro(index, sums, done):
        (grad_resid, gain_sum, shift_sum, *shard), done = second_norm_back(
            sums, resids[index], cot_mine[index], gain_two, False, after=done
        )
        grad_resids.append(grad_resid)
        gain_twos.append(gain_sum)
        shift_twos.append(shift_sum)
        return gather_first(shard), done

    def heads_back_micro(index, pieces, done):
        (grad_mix, mix_sum, *sent), done = heads_back(
            here, tp_here, pieces, mixer_weight, tok_len, after=done
        )
        grad_mixes.append(grad_mix)
        mix_sums.append(mix_sum)
        states.append(exchange_chips(*sent))
        return done

    def attend_back_micro(index, got, earlier, done):
        return attention_back(
            here,
            received[index],
            got,
            seg_rows[index],
            key_rows[index],
            lses[index],
            heads,
            earlier,
            index,
            micro_count,
            after=done,
        )

    state_a, done = project_micro(0, ())
    state_b, done = project_micro(1, done)
    got, done = exchange_cores(state_a, done)
    state_a, done = attend_micro(0, got, done)
    got, done = exchange_cores(state_b, done)
    state_b, done = attend_micro(1, got, done)
    got, done = exchange_cores(state_a, done)
    messages, done = mix_micro(got, False, done)
    sums_a, done = reduce_second(reduce_first(messages), done)
    got, done = exchange_cores(state_b, done)
    messages, done = mix_micro(got, False, done)
    state_b = reduce_first(messages)
    state_a, done = norm_micro(0, sums_a, False, done)
    pieces_a, done = gather_second(state_a, done)
    sums_b, done = reduce_second(state_b, done)
    state_b, done = norm_micro(1, sums_b, True, done)
    pieces_b = gather_direct(state_b[0])
    kept, messages, done = feed_micro(0, pieces_a, (), True, done)
    sums_a = reduce_direct(messages)
    (norm_two, acts, grad_pres), _, done = feed_micro(1, pieces_b, kept, False, done)
    (down_part,), done = weight_grad([([stacked(cot_all)], [stacked(acts)])], after=done)
    state_a, done = norm_back_micro(0, sums_a, done)
    down_grad = scattered(until(down_part, done))
    messages, done = feed_grad(tp_here, Part(grad_pres, 1), up_weight, after=done)
    state_b = reduce_first(messages)
    pieces_a, done = gather_second(state_a, done)
    acts = [Part(acts, index) for index in micro]
    feeds, done = feed_out(tp_here, acts, down_weight, after=done)
    sums_b, done = reduce_second(state_b, done)
    done = heads_back_micro(0, pieces_a, done)
    state_b, done = norm_back_micro(1, sums_b, done)
    pieces_b, done = gather_second(state_b, done)
    (sent, own), done = weight_grad(
        [([stacked(norm_two)], [stacked(grad_pres)])], here, after=done
    )
    got_a, done = exchange_cores(states[0], done)
    done = heads_back_micro(1, pieces_b, done)
    state_feed = reduce_first(until(feeds, done))
    sent_back, done = attend_back_micro(0, got_a, [], done)
    got_b, done = exchange_cores(states[1], done)
    sums_feed, done = reduce_second(state_feed, done)
    sent_back, done = attend_back_micro(1, got_b, sent_back, done)
    got_up = xor_permute(until(sent, done), "ctx", 1)
    state_back = exchange_chips(*sent_back)
    halves, done = finish_outputs(sums_feed, resids, low_bias, after=done)
    (up_part,), done = add_halves(own, got_up, after=done)
    got, done = exchange_cores(state_back, done)
    up_grad = scattered_chips(until(up_part, done))
    (*grad_projs, proj_sum, first, second, third, fourth), done = project_back(
        here, tp_here, got, weight_three, after=done
    )
    state_one = reduce_first((first, second, third, fourth))
    last = [(norm_one, grad_projs), (grad_mixes, heads_low)]
    (sent, own), done = weight_grad(last, here, after=done)
    sums_one, done = reduce_second(state_one, done)
    got_last = xor_permute(until(sent, done), "ctx", 1)
    pieces_out, done = gather_second(gather_first(halves), done)
    (last_part,), done = add_halves(own, got_last, after=done)
    (gain_sum, shift_sum, *halves), done = first_norm_back(
        sums_one, x_mine, grad_resids, gain_one, after=done
    )
    last_grad = scattered_chips(until(last_part, done))
    pieces_in, done = gather_second(gather_first(halves), done)
    outputs, done = assemble_outputs(tp_here, pieces_out, BF, after=done)
    gain_ones, shift_ones, proj_sums = [gain_sum], [shift_sum], [proj_sum]
    (down_grad,), done = widen(down_grad, True, after=done)
    input_grad, done = assemble_outputs(tp_here, pieces_in, F32, after=done)
    (up_grad,), done = widen(up_grad, False, after=done)
    (proj_grad, mixer_grad), done = widen_last(last_grad, inner, after=done)
    proj_grad = jnp.transpose(proj_grad, (1, 0, 2))

    def over_micro(items):
        return sum(items[1:], items[0]).reshape(ctx_count, -1)

    proj_sum = sum(proj_sums[1:], proj_sums[0]).reshape(3, ctx_count, -1)
    pair_sum = jnp.concatenate([proj_sum[0], proj_sum[2]], axis=1)
    share = width // ctx_count
    pair_sum = jnp.pad(pair_sum, ((0, 0), (0, share - pair_sum.shape[1])))
    kinds = [
        over_micro(gain_ones),
        over_micro(shift_ones),
        over_micro(gain_twos),
        over_micro(shift_twos),
        over_micro(mix_sums),
        over_micro(cot_sums),
        over_micro(up_sums),
        pair_sum,
    ]
    small = small_sums(jnp.stack(kinds, axis=1))
    norms = small[:4]
    for step in (1, 2):
        norms = norms + xor_permute(norms, "tp", step)
    proj_bias_grad = small[7, : 2 * inner // ctx_count].reshape(2, -1)
    return (
        outputs.reshape(inputs.shape),
        input_grad.reshape(inputs.shape),
        norms[0],
        norms[1],
        proj_grad,
        proj_bias_grad,
        mixer_grad,
        small[4],
        norms[2],
        norms[3],
        up_grad,
        small[6],
        down_grad,
        small[5],
    )


def plan_for(mesh):
    sizes = dict(mesh.shape)

    def chosen(*args):
        micro, seq_count, _, width = args[0].shape
        units = seq_count * args[6].shape[1] // HD
        fits = sizes["ctx"] == 8 and sizes["tp"] == 4 and units == sizes["ctx"]
        fits = fits and args[12].shape[0] == width and micro == 2
        return (per_device_exchanged if fits else per_device)(*args)

    return chosen


def solution(mesh):
    in_specs = (
        P(None, None, "ctx", None),
        P(),
        P(),
        P(),
        P(),
        P(None, None, "tp"),
        P(None, "tp"),
        P("tp", None),
        P(),
        P(),
        P(),
        P(None, "tp"),
        P("tp"),
        P("tp", None),
        P(),
        P(None, None, "ctx", None),
    )
    out_specs = (
        P(None, None, "ctx", None),
        P(None, None, "ctx", None),
        P("ctx"),
        P("ctx"),
        P("ctx", None, "tp"),
        P(None, ("tp", "ctx")),
        P("tp", "ctx"),
        P("ctx"),
        P("ctx"),
        P("ctx"),
        P("ctx", "tp"),
        P(("tp", "ctx")),
        P("tp", "ctx"),
        P("ctx"),
    )
    return jax.shard_map(
        plan_for(mesh), mesh=mesh, in_specs=in_specs, out_specs=out_specs, check_vma=False
    )
```

```python
import math

import jax
import jax.numpy as jnp
from jax import lax
from jax.experimental import pallas as pl
from jax.experimental.pallas import tpu as pltpu
from jax.sharding import PartitionSpec as P

HD = 128


def storage_order(values, part_count):
    leading = values.shape[:-1]
    blocks = values.reshape(leading + (2 * part_count, -1))
    front_half = blocks[..., :part_count, :]
    back_half = jnp.flip(blocks[..., part_count:, :], axis=-2)
    return jnp.stack([front_half, back_half], axis=-2).reshape(leading + (-1,))


def layer_norm(values, norm_gain, norm_shift):
    center = values - jnp.mean(values, axis=-1, keepdims=True)
    spread = jnp.mean(center * center, axis=-1, keepdims=True)
    return center * lax.rsqrt(spread + 1e-05) * norm_gain + norm_shift


def gelu_exact(values):
    return jax.nn.gelu(values, approximate=False)


def split_heads(rows, heads_here):
    return rows.reshape(rows.shape[0], rows.shape[1], heads_here, -1)


def scores_of(queries, key_all, allowed, heads_here, scaler):
    raw = (
        jnp.einsum(
            "sqhd,skhd->shqk",
            split_heads(queries, heads_here),
            split_heads(key_all, heads_here),
            preferred_element_type=jnp.float32,
        )
        * scaler
    )
    return jnp.where(allowed[:, None], raw, -1000000000.0)


def attend(queries, key_all, value_all, allowed, heads_here, scaler):
    masked = scores_of(queries, key_all, allowed, heads_here, scaler)
    top = jnp.max(masked, axis=-1, keepdims=True)
    raised = jnp.exp(masked - top)
    totals = jnp.sum(raised, axis=-1, keepdims=True)
    probs = raised / totals
    mixed = jnp.einsum(
        "shqk,skhd->sqhd",
        probs.astype(jnp.bfloat16),
        split_heads(value_all, heads_here),
        preferred_element_type=jnp.float32,
    )
    return (mixed.reshape(queries.shape), top + jnp.log(totals))


def attend_back(queries, key_all, value_all, allowed, log_total, grad_heads, heads_here, scaler):
    masked = scores_of(queries, key_all, allowed, heads_here, scaler)
    probs = jnp.exp(masked - log_total)
    grad_four = split_heads(grad_heads, heads_here)
    grad_value = jnp.einsum(
        "shqk,sqhd->skhd", probs.astype(jnp.bfloat16), grad_four, preferred_element_type=jnp.float32
    )
    grad_probs = jnp.einsum(
        "sqhd,skhd->shqk",
        grad_four,
        split_heads(value_all, heads_here),
        preferred_element_type=jnp.float32,
    )
    inner_sum = jnp.sum(probs * grad_probs, axis=-1, keepdims=True)
    grad_scores = (probs * (grad_probs - inner_sum)).astype(jnp.bfloat16)
    grad_query = (
        jnp.einsum(
            "shqk,skhd->sqhd",
            grad_scores,
            split_heads(key_all, heads_here),
            preferred_element_type=jnp.float32,
        )
        * scaler
    )
    grad_key = (
        jnp.einsum(
            "shqk,sqhd->skhd",
            grad_scores,
            split_heads(queries, heads_here),
            preferred_element_type=jnp.float32,
        )
        * scaler
    )
    return (
        grad_query.reshape(queries.shape),
        grad_key.reshape(key_all.shape),
        grad_value.reshape(value_all.shape),
    )


def reduce_grads(grads):
    return (
        lax.psum_scatter(
            grads[0].astype(jnp.bfloat16), "ctx", scatter_dimension=0, tiled=True
        ).astype(jnp.float32),
        lax.psum_scatter(
            grads[1].astype(jnp.bfloat16), "ctx", scatter_dimension=0, tiled=True
        ).astype(jnp.float32),
        lax.psum_scatter(
            grads[2].astype(jnp.bfloat16), "ctx", scatter_dimension=0, tiled=True
        ).astype(jnp.float32),
        lax.psum_scatter(
            grads[3].astype(jnp.bfloat16), "ctx", scatter_dimension=1, tiled=True
        ).astype(jnp.float32),
        lax.psum_scatter(
            grads[4].astype(jnp.bfloat16), "ctx", scatter_dimension=1, tiled=True
        ).astype(jnp.float32),
        lax.psum_scatter(
            grads[5].astype(jnp.bfloat16), "ctx", scatter_dimension=0, tiled=True
        ).astype(jnp.float32),
        lax.psum_scatter(
            grads[6].astype(jnp.bfloat16), "ctx", scatter_dimension=0, tiled=True
        ).astype(jnp.float32),
        lax.psum_scatter(
            grads[7].astype(jnp.bfloat16), "ctx", scatter_dimension=0, tiled=True
        ).astype(jnp.float32),
        lax.psum_scatter(
            grads[8].astype(jnp.bfloat16), "ctx", scatter_dimension=0, tiled=True
        ).astype(jnp.float32),
        lax.psum_scatter(
            grads[9].astype(jnp.bfloat16), "ctx", scatter_dimension=0, tiled=True
        ).astype(jnp.float32),
        lax.psum_scatter(
            grads[10].astype(jnp.bfloat16), "ctx", scatter_dimension=1, tiled=True
        ).astype(jnp.float32),
        lax.psum_scatter(
            grads[11].astype(jnp.bfloat16), "ctx", scatter_dimension=0, tiled=True
        ).astype(jnp.float32),
    )


def per_device(
    inputs,
    segments,
    keep_mask,
    first_gain,
    first_shift,
    proj_weight,
    proj_bias,
    mixer_weight,
    mixer_bias,
    second_gain,
    second_shift,
    up_weight,
    up_bias,
    down_weight,
    down_bias,
    out_cotangent,
):
    ctx_count = lax.axis_size("ctx")
    micro_count, seq_count, tok_len, model_width = inputs.shape
    inner_width = proj_bias.shape[1]
    heads_here = inner_width // HD
    scaler = 1.0 / math.sqrt(HD)
    seq_len = tok_len * ctx_count
    places = storage_order(jnp.arange(seq_len, dtype=jnp.int32), ctx_count)
    offset = lax.axis_index("ctx") * tok_len
    my_places = lax.dynamic_slice_in_dim(places, offset, tok_len, 0)
    seg_store = storage_order(segments, ctx_count)
    keep_store = storage_order(keep_mask, ctx_count)
    proj_flat = proj_weight.reshape(model_width, 3 * inner_width)
    bias_three = jnp.stack([proj_bias[0], jnp.zeros_like(proj_bias[0]), proj_bias[1]])
    causal = places[None, :] <= my_places[:, None]
    itself = places[None, :] == my_places[:, None]
    shaped_like = (
        first_gain,
        first_shift,
        proj_weight,
        proj_bias,
        mixer_weight,
        mixer_bias,
        second_gain,
        second_shift,
        up_weight,
        up_bias,
        down_weight,
        down_bias,
    )
    running = tuple((jnp.zeros(item.shape, jnp.float32) for item in shaped_like))
    out_list = []
    grad_list = []
    for micro_index in range(micro_count):
        x_now = inputs[micro_index].astype(jnp.float32)
        seg_keys = seg_store[micro_index]
        seg_mine = lax.dynamic_slice_in_dim(seg_keys, offset, tok_len, 1)
        visible = (keep_store[micro_index] > 0)[:, None, :] | itself[None]
        allowed = causal[None] & (seg_keys[:, None, :] == seg_mine[:, :, None]) & visible
        normed_one = layer_norm(x_now, first_gain, first_shift).astype(jnp.bfloat16)
        projected = jnp.einsum(
            "std,dc->stc", normed_one, proj_flat, preferred_element_type=jnp.float32
        )
        projected = (projected.reshape(seq_count, tok_len, 3, inner_width) + bias_three).astype(
            jnp.bfloat16
        )
        queries = projected[:, :, 0]
        key_here = projected[:, :, 1]
        value_here = projected[:, :, 2]
        key_all, value_all = (
            lax.all_gather(key_here, "ctx", axis=1, tiled=True),
            lax.all_gather(value_here, "ctx", axis=1, tiled=True),
        )
        heads_out, log_total = attend(queries, key_all, value_all, allowed, heads_here, scaler)
        heads_low = heads_out.astype(jnp.bfloat16)
        mixed_part = jnp.einsum(
            "stn,nd->std", heads_low, mixer_weight, preferred_element_type=jnp.float32
        )
        resid = (
            x_now + lax.psum(mixed_part.astype(jnp.bfloat16), "tp").astype(jnp.float32) + mixer_bias
        )
        normed_two = layer_norm(resid, second_gain, second_shift).astype(jnp.bfloat16)
        pre_act = (
            jnp.einsum("std,df->stf", normed_two, up_weight, preferred_element_type=jnp.float32)
            + up_bias
        )
        act_low = gelu_exact(pre_act).astype(jnp.bfloat16)
        feed_part = jnp.einsum(
            "stf,fd->std", act_low, down_weight, preferred_element_type=jnp.float32
        )
        feed = lax.psum(feed_part.astype(jnp.bfloat16), "tp").astype(jnp.float32) + down_bias
        out_list.append((resid + feed).astype(jnp.bfloat16))
        cot_low = out_cotangent[micro_index]
        cot_full = cot_low.astype(jnp.float32)
        down_bias_part = jnp.sum(cot_full, axis=(0, 1))
        down_part = jnp.einsum("stf,std->fd", act_low, cot_low, preferred_element_type=jnp.float32)
        grad_act = jnp.einsum(
            "std,fd->stf", cot_low, down_weight, preferred_element_type=jnp.float32
        )
        grad_pre = jax.vjp(gelu_exact, pre_act)[1](grad_act)[0].astype(jnp.bfloat16)
        up_part = jnp.einsum(
            "std,stf->df", normed_two, grad_pre, preferred_element_type=jnp.float32
        )
        up_bias_part = jnp.sum(grad_pre.astype(jnp.float32), axis=(0, 1))
        grad_two_part = jnp.einsum(
            "stf,df->std", grad_pre, up_weight, preferred_element_type=jnp.float32
        )
        grad_two = lax.psum(grad_two_part.astype(jnp.bfloat16), "tp").astype(jnp.float32)
        resid_part, second_gain_part, second_shift_part = jax.vjp(
            layer_norm, resid, second_gain, second_shift
        )[1](grad_two)
        grad_resid = cot_full + resid_part
        grad_mix = grad_resid.astype(jnp.bfloat16)
        mixer_bias_part = jnp.sum(grad_mix.astype(jnp.float32), axis=(0, 1))
        mixer_part = jnp.einsum(
            "stn,std->nd", heads_low, grad_mix, preferred_element_type=jnp.float32
        )
        grad_heads = jnp.einsum(
            "std,nd->stn", grad_mix, mixer_weight, preferred_element_type=jnp.float32
        ).astype(jnp.bfloat16)
        key_back, value_back = (key_all, value_all)
        grad_query, grad_key, grad_value = attend_back(
            queries, key_back, value_back, allowed, log_total, grad_heads, heads_here, scaler
        )
        key_share, value_share = (
            lax.psum_scatter(
                grad_key.astype(jnp.bfloat16), "ctx", scatter_dimension=1, tiled=True
            ).astype(jnp.float32),
            lax.psum_scatter(
                grad_value.astype(jnp.bfloat16), "ctx", scatter_dimension=1, tiled=True
            ).astype(jnp.float32),
        )
        grad_proj = jnp.stack([grad_query, key_share, value_share], axis=2).astype(jnp.bfloat16)
        proj_part = jnp.einsum(
            "std,stcn->dcn", normed_one, grad_proj, preferred_element_type=jnp.float32
        )
        proj_sums = jnp.sum(grad_proj.astype(jnp.float32), axis=(0, 1))
        proj_bias_part = jnp.stack([proj_sums[0], proj_sums[2]])
        grad_one_part = jnp.einsum(
            "stc,dc->std",
            grad_proj.reshape(seq_count, tok_len, 3 * inner_width),
            proj_flat,
            preferred_element_type=jnp.float32,
        )
        grad_one = lax.psum(grad_one_part.astype(jnp.bfloat16), "tp").astype(jnp.float32)
        input_part, first_gain_part, first_shift_part = jax.vjp(
            layer_norm, x_now, first_gain, first_shift
        )[1](grad_one)
        grad_list.append(grad_resid + input_part)
        batch_grads = (
            first_gain_part,
            first_shift_part,
            proj_part,
            proj_bias_part,
            mixer_part,
            mixer_bias_part,
            second_gain_part,
            second_shift_part,
            up_part,
            up_bias_part,
            down_part,
            down_bias_part,
        )
        running = tuple((earlier + adding for earlier, adding in zip(running, batch_grads)))
    final = reduce_grads(running)
    return (
        jnp.stack(out_list),
        jnp.stack(grad_list),
        final[0],
        final[1],
        final[2],
        final[3],
        final[4],
        final[5],
        final[6],
        final[7],
        final[8],
        final[9],
        final[10],
        final[11],
    )


BF = jnp.bfloat16
F32 = jnp.float32
LOG2E = 1.4426950408889634
LOW = -1e30
ORDERS = ((1, 2), (2, 1))
COST_SHARE = 1.0


def xor_permute(values, axis, step):
    count = lax.axis_size(axis)
    return lax.ppermute(values, axis, [(i, i ^ step) for i in range(count)])


def sds(shape, dtype=BF):
    return jax.ShapeDtypeStruct(tuple(shape), dtype)


def cost(flops, moved, exps=0):
    return pl.CostEstimate(
        flops=int(flops * COST_SHARE),
        bytes_accessed=int(moved * COST_SHARE),
        transcendentals=int(exps * COST_SHARE),
    )


HBM = pltpu.MemorySpace.HBM


def launch(
    body,
    args,
    in_specs,
    outs,
    out_specs,
    scratch,
    limit,
    cost,
    name,
    after,
    grid=(),
    aliases=None,
    scalars=(),
):
    first, last = len(after), len(after) + len(args) + len(outs)

    def inner(*refs):
        fixed, refs = refs[: len(scalars)], refs[len(scalars) :]
        body(*fixed, *refs[first:last], *refs[last + 1 :])

    token = pl.BlockSpec(memory_space=HBM)
    *results, done = pl.pallas_call(
        inner,
        grid_spec=pltpu.PrefetchScalarGridSpec(
            num_scalar_prefetch=len(scalars),
            grid=grid,
            in_specs=[token] * first + list(in_specs),
            out_specs=(*out_specs, token),
            scratch_shapes=list(scratch),
        ),
        out_shape=(*outs, sds((8, 128), F32)),
        input_output_aliases={first + key: value for key, value in (aliases or {}).items()},
        compiler_params=pltpu.CompilerParams(vmem_limit_bytes=limit),
        cost_estimate=cost,
        name=name,
    )(*scalars, *after, *args)
    return results, (done,)


class Part:
    def __init__(self, array, index):
        self.array, self.index = array, index
        self.shape, self.dtype = array.shape[1:], array.dtype

    def spec(self):
        index, rest = self.index, (0,) * len(self.shape)
        return pl.BlockSpec((None,) + self.shape, lambda *_: (index,) + rest)


def operands_of(args):
    arrays = [arg.array if isinstance(arg, Part) else arg for arg in args]
    return [array if array.dtype == jnp.int32 else pinned(array) for array in arrays]


def pinned(array):
    return pltpu.with_memory_space_constraint(array, HBM)


def run_kernel(body, outs, args, flops=0, exps=0, scratch=(), limit=8, name=None, after=(), in_hbm=()):
    specs = []
    moved = 0
    for place, arg in enumerate(args):
        if arg.dtype == jnp.int32 and math.prod(arg.shape) <= 8:
            specs.append(pl.BlockSpec(memory_space=pltpu.SMEM))
        elif place in in_hbm:
            specs.append(pl.BlockSpec(memory_space=HBM))
        else:
            specs.append(pl.BlockSpec(memory_space=pltpu.VMEM))
            moved += math.prod(arg.shape) * arg.dtype.itemsize
    moved += sum(math.prod(o.shape) * o.dtype.itemsize for o in outs)
    kept = [item for item in scratch if item.dtype in (BF, F32)]
    held = moved + sum(math.prod(item.shape) * item.dtype.itemsize for item in kept)
    return launch(
        body,
        [pinned(arg) if place in in_hbm else arg for place, arg in enumerate(args)],
        specs,
        outs,
        [pl.BlockSpec(memory_space=pltpu.VMEM) for _ in outs],
        scratch,
        held + (limit << 20),
        cost(flops, moved, exps),
        name,
        after,
    )


def whole_of(shape):
    return pl.BlockSpec(shape, lambda *_, n=len(shape): (0,) * n)


def rows_at(start, count):
    return pl.ds(pl.multiple_of(start, count), count)


def reduce_first(messages):
    return [
        (messages[2 * part + 1], xor_permute(messages[2 * part], "tp", first))
        for part, (first, _) in enumerate(ORDERS)
    ]


def reduce_second(state, after=()):
    shape = state[0][0].shape[:-3] + state[0][0].shape[-2:]

    def body(*refs):
        for part in range(2):
            keep, got = refs[2 * part : 2 * part + 2]
            refs[4 + part][...] = keep[..., 0, :, :].astype(F32) + got[..., 0, :, :].astype(F32)
            value = keep[..., 1, :, :].astype(F32) + got[..., 1, :, :].astype(F32)
            refs[6 + part][...] = value.astype(BF)

    (*rest, low, high), done = run_kernel(
        body,
        [sds(shape, F32)] * 2 + [sds(shape)] * 2,
        [item for pair in state for item in pair],
        after=after,
        name="reduce_middle",
        limit=4,
    )
    sums = []
    for part, (_, second) in enumerate(ORDERS):
        sums += [rest[part], xor_permute((low, high)[part], "tp", second)]
    return sums, done


def reduce_direct(messages):
    mine, *sent = messages
    return [mine] + [xor_permute(item, "tp", 1 + step) for step, item in enumerate(sent)]


def gather_first(halves):
    return [
        (halves[part], xor_permute(halves[part], "tp", first))
        for part, (first, _) in enumerate(ORDERS)
    ]


def gather_second(state, after=()):
    half = state[0][0].shape
    pair_shape = half[:-2] + (2,) + half[-2:]

    def body(*refs):
        for part in range(2):
            for place in range(2):
                refs[4 + part][..., place, :, :] = refs[2 * part + place][...]

    pairs, done = run_kernel(
        body,
        [sds(pair_shape)] * 2,
        [item for pair in state for item in pair],
        after=after,
        name="gather_middle",
        limit=3,
    )
    pieces = []
    for part, (_, second) in enumerate(ORDERS):
        pieces += [*state[part], xor_permute(pairs[part], "tp", second)]
    return pieces, done


def gather_direct(mine):
    return [mine] + [xor_permute(mine, "tp", step) for step in (1, 2, 3)]


def total_of(refs):
    if refs[0].dtype == BF:
        return sum([ref[...].astype(F32) for ref in refs[1:]], refs[0][...].astype(F32))
    halves = [refs[2 * part][...] + refs[2 * part + 1][...].astype(F32) for part in range(2)]
    return jnp.concatenate(halves, axis=0)


def place_gathered(store, tp_here, refs, size):
    if len(refs) == 4:
        for step, ref in enumerate(refs):
            store(rows_at((tp_here ^ step) * size, size), ref[...])
        return
    half = size // 2
    for part, (first, second) in enumerate(ORDERS):
        mine, near, far = refs[3 * part : 3 * part + 3]
        parts = ((0, mine[...]), (first, near[...]), (second, far[0]), (first | second, far[1]))
        for step, value in parts:
            store(rows_at((tp_here ^ step) * size + part * half, half), value)


def emit_messages(load, tp_here, refs, size):
    if refs[0].shape[-2] == size:
        for step, ref in enumerate(refs):
            ref[...] = load(rows_at((tp_here ^ step) * size, size))
        return
    half = size // 2
    for part, (first, second) in enumerate(ORDERS):
        send, keep = refs[2 * part], refs[2 * part + 1]
        for ref, steps in ((send, (first, first | second)), (keep, (0, second))):
            for place, step in enumerate(steps):
                ref[place] = load(rows_at((tp_here ^ step) * size + part * half, half))


def emit_shard(value, refs):
    rows = value.shape[0] // len(refs)
    for place, ref in enumerate(refs):
        ref[...] = value[place * rows : (place + 1) * rows]


def shard_shapes(size, width, direct=False):
    return [sds((size, width))] if direct else [sds((size // 2, width))] * 2


def message_shapes(half, width, direct=False):
    return [sds((2 * half, width) if direct else (2, half, width))] * 4


def exchange_chips(local, cross, first, second, third):
    got = [
        xor_permute(item, "ctx", 2 * (place + 1))
        for place, item in enumerate((first, second, third))
    ]
    return [local, cross] + got


def exchange_cores(state, after):
    local, cross, *got = state

    lead = cross.shape[:-2]

    def body(cross_ref, first_ref, second_ref, third_ref, out_ref):
        out_ref[..., 0, :, :] = cross_ref[...]
        for place, ref in enumerate((first_ref, second_ref, third_ref)):
            out_ref[..., place + 1, :, :] = ref[..., 1, :, :]

    (packed,), done = run_kernel(
        body, [sds(lead + (4,) + cross.shape[-2:])], [cross] + got, after=after, limit=2, name="pack"
    )
    return [local] + got + [xor_permute(packed, "ctx", 1)], done


def exchanged(refs, here):
    local, first, second, third, packed = refs
    return (
        (here, local[...]),
        (here ^ 1, packed[0]),
        (here ^ 2, first[0]),
        (here ^ 3, packed[1]),
        (here ^ 4, second[0]),
        (here ^ 5, packed[2]),
        (here ^ 6, third[0]),
        (here ^ 7, packed[3]),
    )


def emit_exchange(load, here, refs):
    local, cross, first, second, third = refs
    local[...] = load(here)
    cross[...] = load(here ^ 1)
    for place, ref in enumerate((first, second, third)):
        other = here ^ (2 * (place + 1))
        ref[0] = load(other)
        ref[1] = load(other ^ 1)


def exchange_shapes(rows, width):
    return [sds((rows, width)), sds((rows, width))] + [sds((2, rows, width))] * 3


def normalized(values):
    center = values - jnp.mean(values, axis=-1, keepdims=True)
    spread = jnp.mean(center * center, axis=-1, keepdims=True)
    root = lax.rsqrt(spread + 1e-05)
    return center * root, root


def norm_back(values, gain, grad):
    unit, root = normalized(values)
    scaled = grad * gain
    back = root * (
        scaled
        - jnp.mean(scaled, axis=-1, keepdims=True)
        - unit * jnp.mean(scaled * unit, axis=-1, keepdims=True)
    )
    gain_sum = jnp.sum(grad * unit, axis=0, keepdims=True)
    shift_sum = jnp.sum(grad, axis=0, keepdims=True)
    return back, gain_sum, shift_sum


def dot(left, right):
    return jnp.dot(left, right, preferred_element_type=F32)


def dot_nt(left, right):
    return lax.dot_general(left, right, (((1,), (1,)), ((), ())), preferred_element_type=F32)


def dot_tn(left, right):
    return lax.dot_general(left, right, (((0,), (0,)), ((), ())), preferred_element_type=F32)


def project(here, x_all, index, gain, shift, weight, bias, tok_len, after=()):
    _, rows, width = x_all.shape
    inner = weight.shape[2]
    heads = inner // HD

    def body(here_ref, x_ref, gain_ref, shift_ref, weight_hbm, bias_ref, *rest):
        norm_ref, outs = rest[0], rest[1:6]
        held, weight_ref, x_held, gain_held, shift_held, bias_held, sems = rest[6:]
        fetches = [
            pltpu.make_async_copy(source, target, sems.at[3 + number])
            for number, (source, target) in enumerate(
                (
                    (x_ref.at[index], x_held),
                    (gain_ref, gain_held),
                    (shift_ref, shift_held),
                    (bias_ref, bias_held),
                )
            )
        ]
        for fetch in fetches:
            fetch.start()
        copies = [
            pltpu.make_async_copy(weight_hbm.at[part], weight_ref.at[part], sems.at[part])
            for part in range(3)
        ]
        for copy in copies:
            copy.start()
        for fetch in fetches:
            fetch.wait()
        for start in range(0, rows, tok_len):
            place = slice(start, start + tok_len)
            unit, _ = normalized(x_held[place].astype(F32))
            norm_ref[place] = (unit * gain_held[...] + shift_held[...]).astype(BF)
            for part in range(3):
                if start == 0:
                    copies[part].wait()
                value = dot(norm_ref[place], weight_ref[part])
                if part != 1:
                    value += bias_held[part // 2 : part // 2 + 1]
                value = value.astype(BF)
                for head in range(heads):
                    held[head, place, part * HD : (part + 1) * HD] = value[
                        :, head * HD : (head + 1) * HD
                    ]

        def load(unit_id):
            return held[unit_id % heads, rows_at(unit_id // heads * tok_len, tok_len), :]

        emit_exchange(load, here_ref[0], outs)

    return run_kernel(
        body,
        [sds((rows, width))] + exchange_shapes(tok_len, 3 * HD),
        [here, x_all, gain, shift, weight, bias],
        flops=6 * rows * width * inner,
        scratch=[
            pltpu.VMEM((heads, rows, 3 * HD), BF),
            pltpu.VMEM(weight.shape, BF),
            pltpu.VMEM((rows, width), BF),
            pltpu.VMEM(gain.shape, F32),
            pltpu.VMEM(shift.shape, F32),
            pltpu.VMEM(bias.shape, F32),
            pltpu.SemaphoreType.DMA((7,)),
        ],
        name="project",
        limit=14,
        after=after,
        in_hbm=(1, 2, 3, 4, 5),
    )


def rows_of_device(device, block, blocks):
    return (
        rows_at(device * block, block),
        rows_at((blocks - 1 - device) * block, block),
    )


def attention(here, received, seg_row, key_row, heads, after=()):
    tok_len = received[0].shape[0]
    block = tok_len // 2
    seq_len = seg_row.shape[2]
    blocks = seq_len // block
    step = 256
    factor = LOG2E / math.sqrt(HD)

    def body(here_ref, *rest):
        refs, seg_ref, key_ref = rest[:5], rest[5], rest[6]
        outs, lse_ref = rest[7:12], rest[12]
        q_all, k_turned, v_all, mixed = rest[13:]
        me = here_ref[0]
        seq = me // heads
        for device, value in exchanged(refs, me):
            for half, place in enumerate(rows_of_device(device, block, blocks)):
                rows = value[half * block : (half + 1) * block]
                q_all[place] = rows[:, :HD]
                k_turned[:, place] = rows[:, HD : 2 * HD].T
                v_all[place] = rows[:, 2 * HD :]
        for number in range(seq_len // step):
            start, stop = number * step, (number + 1) * step
            segs = as_column(seg_ref[seq, :, start:stop])
            scores = dot(q_all[start:stop], k_turned[:, :stop]) * factor
            scores = masked(scores, segs, key_ref, seq, start, stop)
            top = jnp.max(scores, axis=-1, keepdims=True)
            raised = jnp.exp2(scores - top)
            total = jnp.sum(raised, axis=-1, keepdims=True)
            out = dot(raised.astype(BF), v_all[:stop]) / total
            mixed[start:stop] = out.astype(BF)
            lse_ref[start:stop] = top + jnp.log2(total)

        def load(device):
            return jnp.concatenate(
                [mixed[place] for place in rows_of_device(device, block, blocks)], axis=0
            )

        emit_exchange(load, me, outs)

    return run_kernel(
        body,
        exchange_shapes(tok_len, HD) + [sds((seq_len, 1), F32)],
        [here] + list(received) + [seg_row, key_row],
        flops=2 * 2 * seq_len * seq_len * HD,
        exps=seq_len * seq_len // 2,
        scratch=[
            pltpu.VMEM((seq_len, HD), BF),
            pltpu.VMEM((HD, seq_len), BF),
            pltpu.VMEM((seq_len, HD), BF),
            pltpu.VMEM((seq_len, HD), BF),
        ],
        after=after,
        name="attention",
        limit=16,
    )


def as_column(row):
    return jnp.broadcast_to(row, (128, row.shape[1])).T[:, :1]


def masked(scores, segs, key_ref, seq, start, stop):
    size = stop - start
    row = lax.broadcasted_iota(jnp.int32, (size, size), 0)
    column = lax.broadcasted_iota(jnp.int32, (size, size), 1)
    same = segs == key_ref[seq, :, start:stop]
    seen = (same & (column < row)) | (column == row)
    corner = jnp.where(seen, scores[:, start:], LOW)
    if start == 0:
        return corner
    left = jnp.where(segs == key_ref[seq, :, :start], scores[:, :start], LOW)
    return jnp.concatenate([left, corner], axis=1)


def attention_back(
    here, received, grads, seg_row, key_row, lse, heads, earlier, index, count, after=()
):
    tok_len = received[0].shape[0]
    block = tok_len // 2
    seq_len = seg_row.shape[2]
    blocks = seq_len // block
    step = 256
    scaler = 1.0 / math.sqrt(HD)

    def body(here_ref, *rest):
        refs, grad_refs = rest[:5], rest[5:10]
        seg_ref, key_ref, lse_ref = rest[10:13]
        rest = rest[13 + len(earlier) :]
        outs = [ref.at[0] for ref in rest[:5]]
        q_all, k_all, k_turned, v_turned, g_all, result, dk_turned, dv_turned = rest[5:]
        me = here_ref[0]
        seq = me // heads
        for device, value in exchanged(refs, me):
            for half, place in enumerate(rows_of_device(device, block, blocks)):
                rows = value[half * block : (half + 1) * block]
                q_all[place] = rows[:, :HD]
                k_all[place] = rows[:, HD : 2 * HD]
                k_turned[:, place] = rows[:, HD : 2 * HD].T
                v_turned[:, place] = rows[:, 2 * HD :].T
        for device, value in exchanged(grad_refs, me):
            for half, place in enumerate(rows_of_device(device, block, blocks)):
                g_all[place] = value[half * block : (half + 1) * block]
        last = seq_len // step - 1
        for number in range(last, -1, -1):
            start, stop = number * step, (number + 1) * step
            segs = as_column(seg_ref[seq, :, start:stop])
            query, grad = q_all[start:stop], g_all[start:stop]
            scores = dot(query, k_turned[:, :stop]) * (scaler * LOG2E)
            scores = masked(scores, segs, key_ref, seq, start, stop)
            probs = jnp.exp2(scores - lse_ref[start:stop])
            grad_probs = dot(grad, v_turned[:, :stop])
            inner = jnp.sum(probs * grad_probs, axis=-1, keepdims=True)
            grad_scores = (probs * (grad_probs - inner)).astype(BF)
            dv_part = dot_tn(grad, probs.astype(BF))
            dk_part = dot_tn(query, grad_scores)
            if number == last:
                dv_turned[...] = dv_part
                dk_turned[...] = dk_part
            else:
                dv_turned[:, :stop] += dv_part
                dk_turned[:, :stop] += dk_part
            dq = dot(grad_scores, k_all[:stop]) * scaler
            result[start:stop, :HD] = dq.astype(BF)
        for number in range(last + 1):
            start, stop = number * step, (number + 1) * step
            result[start:stop, HD : 2 * HD] = (dk_turned[:, start:stop] * scaler).T.astype(BF)
            result[start:stop, 2 * HD :] = dv_turned[:, start:stop].T.astype(BF)

        def load(device):
            return jnp.concatenate(
                [result[place] for place in rows_of_device(device, block, blocks)], axis=0
            )

        emit_exchange(load, me, outs)

    shapes = exchange_shapes(tok_len, 3 * HD)
    args = [here, *received, *grads, seg_row, key_row, lse, *earlier]
    first = len(args) - len(earlier)
    return launch(
        body,
        operands_of(args),
        [pl.BlockSpec(memory_space=pltpu.SMEM)]
        + [whole_of(item.shape) for item in args[1:first]]
        + [pl.BlockSpec(memory_space=pl.ANY) for _ in earlier],
        [sds((count,) + item.shape) for item in shapes],
        [
            pl.BlockSpec((1,) + item.shape, lambda i, n=len(item.shape): (index,) + (0,) * n)
            for item in shapes
        ],
        [
            pltpu.VMEM((seq_len, HD), BF),
            pltpu.VMEM((seq_len, HD), BF),
            pltpu.VMEM((HD, seq_len), BF),
            pltpu.VMEM((HD, seq_len), BF),
            pltpu.VMEM((seq_len, HD), BF),
            pltpu.VMEM((seq_len, 3 * HD), BF),
            pltpu.VMEM((HD, seq_len), F32),
            pltpu.VMEM((HD, seq_len), F32),
        ],
        36 << 20,
        cost(5 * seq_len * seq_len * HD, 12 * seq_len * HD),
        "attention_back",
        after,
        grid=(1,),
        aliases={first + number: number for number in range(len(earlier))},
    )


def mix_heads(here, tp_here, received, weight, heads, direct, after=()):
    tok_len = received[0].shape[0]
    inner, width = weight.shape
    rows = len_units(received) * tok_len // heads
    size = rows // 4

    def body(here_ref, tp_ref, *rest):
        refs, weight_ref = rest[:5], rest[5]
        heads_ref, outs, held = rest[6], rest[7:11], rest[11]
        for unit_id, value in exchanged(refs, here_ref[0]):
            column = pl.multiple_of(unit_id % heads * HD, HD)
            heads_ref[rows_at(unit_id // heads * tok_len, tok_len), pl.ds(column, HD)] = value
        for start in range(0, width, 512):
            held[:, start : start + 512] = dot(
                heads_ref[...], weight_ref[:, start : start + 512]
            ).astype(BF)
        emit_messages(lambda place: held[place, :], tp_ref[0], outs, size)

    return run_kernel(
        body,
        [sds((rows, inner))] + message_shapes(size // 2, width, direct),
        [here, tp_here] + list(received) + [weight],
        flops=2 * rows * inner * width,
        scratch=[pltpu.VMEM((rows, width), BF)],
        after=after,
        name="mix_heads",
        limit=6,
    )


def len_units(received):
    return 2 * received[-1].shape[0]


def second_norm(sums, x_mine, mixer_bias, gain, shift, direct, after=()):
    size, width = x_mine.shape
    count = len(sums)

    def body(*rest):
        refs, (x_ref, bias_ref, gain_ref, shift_ref) = rest[:count], rest[count : count + 4]
        resid_ref, outs = rest[count + 4], rest[count + 5 :]
        resid = x_ref[...].astype(F32) + total_of(refs) + bias_ref[...]
        resid_ref[...] = resid
        unit, _ = normalized(resid)
        emit_shard((unit * gain_ref[...] + shift_ref[...]).astype(BF), outs)

    return run_kernel(
        body,
        [sds((size, width), F32)] + shard_shapes(size, width, direct),
        list(sums) + [x_mine, mixer_bias, gain, shift],
        name="second_norm",
        limit=8,
        after=after,
    )


def feed_inner(
    tp_here, pieces, cot, up_weight, up_bias, down_weight, earlier, index, with_grad, after=()
):
    rows, width = cot.shape
    hidden = up_weight.shape[1]
    size = rows // 4
    step = 512
    blocks = hidden // step

    def body(tp_ref, *rest):
        refs, rest = rest[: len(pieces)], rest[len(pieces) :]
        cot_ref, up_hbm, bias_ref, down_hbm = rest[:4]
        rest = rest[4 + len(earlier) :]
        norm_ref, act_ref, pre_ref = [ref.at[0] for ref in rest[:3]]
        sum_ref, cot_sum_ref = rest[3:5]
        grad_outs = rest[5:9] if with_grad else ()
        up, down, held, sems = rest[-4:]

        def part(number):
            return pl.ds(pl.multiple_of(number * step, step), step)

        def copies(number):
            place = part(number)
            return (
                pltpu.make_async_copy(up_hbm.at[:, place], up.at[:, place], sems.at[0, number]),
                pltpu.make_async_copy(down_hbm.at[place, :], down.at[place, :], sems.at[1, number]),
            )

        for number in range(blocks):
            for copy in copies(number):
                copy.start()

        def store(place, value):
            norm_ref[place, :] = value

        place_gathered(store, tp_ref[0], refs, size)
        cot_sum_ref[...] = jnp.sum(cot_ref[...].astype(F32), axis=0, keepdims=True)

        @pl.loop(0, blocks)
        def _(number):
            for copy in copies(number):
                copy.wait()
            place = part(number)
            pre = dot(norm_ref[...], up[:, place]) + bias_ref[:, place]
            grad_act = dot_nt(cot_ref[...], down[place, :])
            spread = 0.5 + 0.5 * lax.erf(pre * math.sqrt(0.5))
            dense = jnp.exp(-0.5 * pre * pre) * (1.0 / math.sqrt(2.0 * math.pi))
            act_ref[:, place] = (pre * spread).astype(BF)
            grad_pre = (grad_act * (spread + pre * dense)).astype(BF)
            pre_ref[:, place] = grad_pre
            sum_ref[:, place] = jnp.sum(grad_pre.astype(F32), axis=0, keepdims=True)

        if with_grad:

            @pl.loop(0, width // step)
            def _(number):
                place = part(number)
                held[:, place] = dot_nt(pre_ref[...], up[place, :]).astype(BF)

            emit_messages(lambda at: held[at, :], tp_ref[0], grad_outs, size)

    args = [tp_here, *pieces, cot, up_weight, up_bias, down_weight]
    count = cot.array.shape[0]
    wide = [(1, rows, width), (1, rows, hidden), (1, rows, hidden)]
    outs = [sds((1, hidden), F32), sds((1, width), F32)]
    outs += message_shapes(size // 2, width, True) if with_grad else []
    return launch(
        body,
        operands_of(args) + list(earlier),
        [pl.BlockSpec(memory_space=pltpu.SMEM)]
        + [whole_of(piece.shape) for piece in pieces]
        + [cot.spec(), pl.BlockSpec(memory_space=HBM), whole_of(up_bias.shape)]
        + [pl.BlockSpec(memory_space=HBM)] * (1 + len(earlier)),
        [HBM((count,) + shape[1:], BF) for shape in wide] + outs,
        [pl.BlockSpec(shape, lambda i: (index, 0, 0)) for shape in wide]
        + [whole_of(item.shape) for item in outs],
        [
            pltpu.VMEM((width, hidden), BF),
            pltpu.VMEM((hidden, width), BF),
            pltpu.VMEM((rows, width), BF),
            pltpu.SemaphoreType.DMA((2, blocks)),
        ],
        50 << 20,
        cost(6 * rows * width * hidden, 4 * width * hidden + 20 * rows * width),
        "feed_inner",
        after,
        grid=(1,),
        aliases={len(args) + number: number for number in range(len(earlier))},
    )


def stacked(array):
    return array.reshape((-1, array.shape[-1]))


def feed_grad(tp_here, grad_pre, up_weight, after=()):
    rows, hidden = grad_pre.shape
    width = up_weight.shape[0]
    size = rows // 4
    step = 512
    blocks = width // step

    def body(tp_ref, pre_ref, up_ref, *rest):
        outs, held = rest[:4], rest[4]
        number = pl.program_id(0)
        place = pl.ds(pl.multiple_of(number * step, step), step)
        held[:, place] = dot_nt(pre_ref[...], up_ref[...]).astype(BF)

        @pl.when(number == blocks - 1)
        def _():
            emit_messages(lambda at: held[at, :], tp_ref[0], outs, size)

    outs = message_shapes(size // 2, width)
    return launch(
        body,
        operands_of([tp_here, grad_pre, up_weight]),
        [
            pl.BlockSpec(memory_space=pltpu.SMEM),
            grad_pre.spec(),
            pl.BlockSpec((step, hidden), lambda i: (i, 0)),
        ],
        outs,
        [whole_of(item.shape) for item in outs],
        [pltpu.VMEM((rows, width), BF)],
        24 << 20,
        cost(2 * rows * width * hidden, 2 * width * hidden + 6 * rows * width),
        "feed_grad",
        after,
        grid=(blocks,),
    )


def feed_out(tp_here, acts, down_weight, after=()):
    count = len(acts)
    rows, hidden = acts[0].shape
    width = down_weight.shape[1]
    size = rows // 4
    step = 512
    blocks = width // step

    def body(tp_ref, *rest):
        act_refs, down_ref, outs, held = rest[:count], rest[count], rest[-5:-1], rest[-1]
        number = pl.program_id(0)
        place = pl.ds(pl.multiple_of(number * step, step), step)
        for index in range(count):
            held[index, :, place] = dot(act_refs[index][...], down_ref[...]).astype(BF)

        @pl.when(number == blocks - 1)
        def _():
            for index in range(count):
                emit_messages(
                    lambda at: held[index, at, :],
                    tp_ref[0],
                    [ref.at[index] for ref in outs],
                    size,
                )

    outs = [sds((count,) + item.shape) for item in message_shapes(size // 2, width)]
    return launch(
        body,
        operands_of([tp_here, *acts, down_weight]),
        [pl.BlockSpec(memory_space=pltpu.SMEM)]
        + [act.spec() for act in acts]
        + [pl.BlockSpec((hidden, step), lambda i: (0, i))],
        outs,
        [whole_of(item.shape) for item in outs],
        [pltpu.VMEM((count, rows, width), BF)],
        36 << 20,
        cost(2 * count * rows * width * hidden, 2 * width * hidden + 12 * rows * width),
        "feed_out",
        after,
        grid=(blocks,),
    )


def second_norm_back(sums, resid, cot_mine, gain, direct, after=()):
    size, width = resid.shape
    count = len(sums)

    def body(*rest):
        refs, (resid_ref, cot_ref, gain_ref) = rest[:count], rest[count : count + 3]
        grad_ref, gain_out, shift_out, *outs = rest[count + 3 :]
        back, gain_sum, shift_sum = norm_back(resid_ref[...], gain_ref[...], total_of(refs))
        grad = back + cot_ref[...].astype(F32)
        grad_ref[...] = grad
        emit_shard(grad.astype(BF), outs)
        gain_out[...] = gain_sum
        shift_out[...] = shift_sum

    return run_kernel(
        body,
        [sds((size, width), F32)]
        + [sds((1, width), F32)] * 2
        + shard_shapes(size, width, direct),
        list(sums) + [resid, cot_mine, gain],
        name="second_norm_back",
        limit=10,
        after=after,
    )


def first_norm_back(sums, x_mine, grad_resids, gain, after=()):
    count = len(x_mine)
    size, width = grad_resids[0].shape

    def body(*rest):
        refs, rest = rest[:4], rest[4:]
        x_refs, grad_refs, gain_ref = rest[:count], rest[count : 2 * count], rest[2 * count]
        gain_out, shift_out, *outs = rest[2 * count + 1 :]
        for index in range(count):
            back, gain_sum, shift_sum = norm_back(
                x_refs[index][...].astype(F32),
                gain_ref[...],
                total_of([ref.at[index] for ref in refs]),
            )
            emit_shard(
                (back + grad_refs[index][...]).astype(BF), [ref.at[index] for ref in outs]
            )
            gain_out[...] = gain_sum if index == 0 else gain_out[...] + gain_sum
            shift_out[...] = shift_sum if index == 0 else shift_out[...] + shift_sum

    return run_kernel(
        body,
        [sds((1, width), F32)] * 2
        + [sds((count,) + item.shape) for item in shard_shapes(size, width)],
        list(sums) + list(x_mine) + list(grad_resids) + [gain],
        name="first_norm_back",
        limit=10,
        after=after,
    )


def finish_outputs(sums, resids, bias, after=()):
    size, width = resids[0].shape
    half = size // 2
    count = len(resids)

    def body(*rest):
        refs, resid_refs, bias_ref = rest[:4], rest[4 : 4 + count], rest[4 + count]
        low_ref, high_ref = rest[5 + count :]
        for index in range(count):
            ours = [ref.at[index] for ref in refs]
            value = (resid_refs[index][...] + total_of(ours) + bias_ref[...]).astype(BF)
            low_ref[index] = value[:half]
            high_ref[index] = value[half:]

    return run_kernel(
        body,
        [sds((count, half, width))] * 2,
        list(sums) + list(resids) + [bias],
        after=after,
        name="finish_outputs",
        limit=8,
    )


def assemble_outputs(tp_here, pieces, dtype, after=()):
    count, half, width = pieces[0].shape
    size = 2 * half
    rows = 4 * size

    def block_of(shape):
        return pl.BlockSpec((1,) + shape[1:], lambda i, n=len(shape) - 1: (i,) + (0,) * n)

    def body(tp_ref, *rest):
        refs, out_ref = rest[:6], rest[6]

        def store(place, value):
            out_ref[0, place, :] = value.astype(dtype)

        place_gathered(store, tp_ref[0], [ref.at[0] for ref in refs], size)

    results, done = launch(
        body,
        [tp_here] + list(pieces),
        [pl.BlockSpec(memory_space=pltpu.SMEM)] + [block_of(piece.shape) for piece in pieces],
        [HBM((count, rows, width), dtype)],
        [block_of((count, rows, width))],
        (),
        24 << 20,
        cost(0, count * rows * width * 6),
        "assemble_outputs",
        after,
        grid=(count,),
    )
    return results[0], done


def widen(part, turned, after=()):
    rows, wide = part.shape

    def body(part_ref, out_ref):
        value = part_ref[...].astype(F32)
        out_ref[...] = value.T if turned else value

    shape = (wide, rows) if turned else (rows, wide)
    return run_kernel(body, [sds(shape, F32)], [part], after=after, name="widen", limit=6)


def widen_last(part, inner, after=()):
    rows, _ = part.shape

    def body(part_ref, proj_ref, mixer_ref):
        for number in range(3):
            place = slice(number * inner, (number + 1) * inner)
            proj_ref[number] = part_ref[:, place].astype(F32)
        mixer_ref[...] = part_ref[:, 3 * inner :].astype(F32).T

    outs = [sds((3, rows, inner), F32), sds((inner, rows), F32)]
    return launch(
        body,
        operands_of([part]),
        [whole_of(part.shape)],
        outs,
        [whole_of(item.shape) for item in outs],
        (),
        16 << 20,
        cost(0, 16 * rows * inner),
        "widen",
        after,
        grid=(1,),
    )


def heads_back(here, tp_here, pieces, weight, tok_len, after=()):
    inner, width = weight.shape
    heads = inner // HD
    count = len(pieces)
    size = pieces[0].shape[0] * (1 if count == 4 else 2)
    rows = 4 * size

    def body(here_ref, tp_ref, *rest):
        refs, weight_ref, rest = rest[:count], rest[count], rest[count + 1 :]
        mix_ref, sum_ref, outs, held = rest[0], rest[1], rest[2:7], rest[7]

        def store(place, value):
            mix_ref[place, :] = value

        place_gathered(store, tp_ref[0], refs, size)
        sum_ref[...] = jnp.sum(mix_ref[...].astype(F32), axis=0, keepdims=True)
        value = dot_nt(mix_ref[...], weight_ref[...]).astype(BF)
        for head in range(heads):
            held[head] = value[:, head * HD : (head + 1) * HD]

        def load(unit_id):
            return held[unit_id % heads, rows_at(unit_id // heads * tok_len, tok_len), :]

        emit_exchange(load, here_ref[0], outs)

    return run_kernel(
        body,
        [sds((rows, width)), sds((1, width), F32)] + exchange_shapes(tok_len, HD),
        [here, tp_here] + list(pieces) + [weight],
        flops=2 * rows * inner * width,
        scratch=[pltpu.VMEM((heads, rows, HD), BF)],
        after=after,
        name="heads_back",
        limit=8,
    )


def project_back(here, tp_here, received, weight, after=()):
    count, tok_len, _ = received[0].shape
    _, width, inner = weight.shape
    heads = inner // HD
    rows = 2 * received[-1].shape[1] * tok_len // heads
    size = rows // 4

    def body(here_ref, tp_ref, *rest):
        refs, weight_ref, rest = rest[:5], rest[5], rest[6:]
        proj_refs, sum_ref, outs, held = rest[:count], rest[count], rest[-5:-1], rest[-1]
        for index, proj_ref in enumerate(proj_refs):
            for unit_id, value in exchanged([ref.at[index] for ref in refs], here_ref[0]):
                place = rows_at(unit_id // heads * tok_len, tok_len)
                for part in range(3):
                    column = pl.multiple_of(part * inner + unit_id % heads * HD, HD)
                    proj_ref[place, pl.ds(column, HD)] = value[:, part * HD : (part + 1) * HD]
            part_sum = jnp.sum(proj_ref[...].astype(F32), axis=0, keepdims=True)
            sum_ref[...] = part_sum if index == 0 else sum_ref[...] + part_sum
            for start in range(0, width, 512):
                value = dot_nt(proj_ref[:, :inner], weight_ref[0, start : start + 512])
                for part in range(1, 3):
                    value += dot_nt(
                        proj_ref[:, part * inner : (part + 1) * inner],
                        weight_ref[part, start : start + 512],
                    )
                held[:, start : start + 512] = value.astype(BF)
            emit_messages(
                lambda place: held[place, :], tp_ref[0], [ref.at[index] for ref in outs], size
            )

    return run_kernel(
        body,
        [sds((rows, 3 * inner))] * count
        + [sds((1, 3 * inner), F32)]
        + [sds((count,) + item.shape) for item in message_shapes(size // 2, width)],
        [here, tp_here] + list(received) + [weight],
        flops=6 * count * rows * inner * width,
        scratch=[pltpu.VMEM((rows, width), BF)],
        name="project_back",
        limit=10,
        after=after,
    )


def weight_grad(groups, here=None, after=()):
    count = len(groups[0][0])
    rows, tall = groups[0][0][0].shape
    widths = [rights[0].shape[1] for _, rights in groups]
    total = sum(widths)
    split = here is not None
    steps = 8 if split else 4
    step = tall // steps
    half = steps // 2

    def block_of(number, *fixed):
        if not split:
            return number
        core = fixed[0][0] & 1
        mine = number // half
        return 2 * (number % half) + (core ^ 1 ^ mine)

    def product(refs, store):
        start = 0
        for place, wide in enumerate(widths):
            ours = refs[2 * count * place : 2 * count * (place + 1)]
            value = dot_tn(ours[0][...], ours[count][...])
            for number in range(1, count):
                value += dot_tn(ours[number][...], ours[count + number][...])
            store(slice(start, start + wide), value.astype(BF))
            start += wide

    def body(*refs):
        if not split:
            out_ref = refs[-1]

            def store(place, value):
                out_ref[:, place] = value

            product(refs, store)
            return
        refs, other_ref, own_ref = refs[1:-2], refs[-2], refs[-1]
        number = pl.program_id(0)

        def into(ref):
            def store(place, value):
                ref[0, :, place] = value

            return store

        @pl.when(number < half)
        def _():
            product(refs, into(other_ref))

        @pl.when(number >= half)
        def _():
            product(refs, into(own_ref))

    args, in_specs = [], []
    for (lefts, rights), wide in zip(groups, widths):
        for item in lefts:
            if isinstance(item, Part):
                in_specs.append(
                    pl.BlockSpec(
                        (None, rows, step),
                        lambda i, *fixed, k=item.index: (k, 0, block_of(i, *fixed)),
                    )
                )
            else:
                in_specs.append(
                    pl.BlockSpec((rows, step), lambda i, *fixed: (0, block_of(i, *fixed)))
                )
        in_specs += [pl.BlockSpec((rows, wide), lambda *_: (0, 0))] * count
        args += list(lefts) + list(rights)
    if split:
        outs = [HBM((half, step, total), BF)] * 2
        out_specs = [
            pl.BlockSpec((1, step, total), lambda i, *_: (jnp.minimum(i, half - 1), 0, 0)),
            pl.BlockSpec((1, step, total), lambda i, *_: (jnp.maximum(i - half, 0), 0, 0)),
        ]
    else:
        outs = [HBM((tall, total), BF)]
        out_specs = [pl.BlockSpec((step, total), lambda i: (i, 0))]
    return launch(
        body,
        operands_of(args),
        in_specs,
        outs,
        out_specs,
        (),
        40 << 20,
        cost(
            2 * count * rows * tall * total,
            2 * (count * rows * (tall * len(groups) + total) + tall * total),
        ),
        "weight_grad",
        after,
        grid=(steps,),
        scalars=(here,) if split else (),
    )


def add_halves(own, got, after=()):
    def body(own_ref, got_ref, out_ref):
        out_ref[...] = (own_ref[...].astype(F32) + got_ref[...].astype(F32)).astype(BF)

    block_spec = pl.BlockSpec((1,) + own.shape[1:], lambda i: (i, 0, 0))
    return launch(
        body,
        operands_of([own, got]),
        [block_spec] * 2,
        [HBM(own.shape, BF)],
        [block_spec],
        (),
        16 << 20,
        cost(0, 6 * math.prod(own.shape)),
        "add_halves",
        after,
        grid=(own.shape[0],),
    )


def small_sums(values):
    here = lax.axis_index("ctx")
    step = values.shape[0] // 2
    while step:
        pair = values.reshape((2, step) + values.shape[1:])
        bit = (here // step) % 2
        keep = lax.dynamic_index_in_dim(pair, bit, 0, False)
        send = lax.dynamic_index_in_dim(pair, 1 - bit, 0, False)
        values = keep + xor_permute(send, "ctx", step)
        step //= 2
    return values[0]


def per_device_exchanged(
    inputs,
    segments,
    keep_mask,
    first_gain,
    first_shift,
    proj_weight,
    proj_bias,
    mixer_weight,
    mixer_bias,
    second_gain,
    second_shift,
    up_weight,
    up_bias,
    down_weight,
    down_bias,
    out_cotangent,
):
    ctx_count = lax.axis_size("ctx")
    micro_count, seq_count, tok_len, width = inputs.shape
    inner = proj_bias.shape[1]
    heads = inner // HD
    rows = seq_count * tok_len
    here = lax.axis_index("ctx").astype(jnp.int32).reshape(1)
    tp_here = lax.axis_index("tp").astype(jnp.int32).reshape(1)
    weight_three = jnp.transpose(proj_weight, (1, 0, 2))
    x_all = inputs.reshape(micro_count, rows, width)
    cot_all = out_cotangent.reshape(micro_count, rows, width)
    key_rows = jnp.where(keep_mask > 0, segments, -1)[:, :, None, :]
    gain_one, shift_one = first_gain[None], first_shift[None]
    gain_two, shift_two = second_gain[None], second_shift[None]
    mix_bias, low_bias, high_bias = mixer_bias[None], down_bias[None], up_bias[None]
    micro = range(micro_count)

    key_rows = [key_rows[index] for index in micro]
    seg_rows = [segments[index][:, None, :] for index in micro]
    cots = [Part(cot_all, index) for index in micro]
    size = rows // lax.axis_size("tp")
    start = tp_here[0] * size
    x_mine = [lax.dynamic_slice(x_all, (index, start, 0), (1, size, width))[0] for index in micro]
    cot_mine = [
        lax.dynamic_slice(cot_all, (index, start, 0), (1, size, width))[0] for index in micro
    ]

    chips = [[core + 2 * chip for chip in range(ctx_count // 2)] for core in range(2)]

    def scattered(part):
        return lax.psum_scatter(part, "ctx", scatter_dimension=0, tiled=True)

    def scattered_chips(part):
        part = part.reshape(-1, part.shape[2])
        return lax.psum_scatter(
            part, "ctx", scatter_dimension=0, axis_index_groups=chips, tiled=True
        )

    def until(items, *points):
        held, _ = lax.optimization_barrier((items, points))
        return held

    norm_one, received, lses, heads_low, resids = [], [], [], [], []

    def project_micro(index, done):
        (normed, *sent), done = project(
            here, x_all, index, gain_one, shift_one, weight_three, proj_bias, tok_len, after=done
        )
        norm_one.append(normed)
        return exchange_chips(*sent), done

    def attend_micro(index, got, done):
        received.append(got)
        (*sent, lse), done = attention(
            here, got, seg_rows[index], key_rows[index], heads, after=done
        )
        lses.append(lse)
        return exchange_chips(*sent), done

    def mix_micro(got, direct, done):
        (mixed, *messages), done = mix_heads(
            here, tp_here, got, mixer_weight, heads, direct, after=done
        )
        heads_low.append(mixed)
        return messages, done

    def norm_micro(index, sums, direct, done):
        (resid, *shard), done = second_norm(
            sums, x_mine[index], mix_bias, gain_two, shift_two, direct, after=done
        )
        resids.append(resid)
        return shard if direct else gather_first(shard), done

    up_sums, cot_sums = [], []

    def feed_micro(index, pieces, earlier, with_grad, done):
        (norms, acts, pres, up_sum, cot_sum, *messages), done = feed_inner(
            tp_here,
            pieces,
            cots[index],
            up_weight,
            high_bias,
            down_weight,
            earlier,
            index,
            with_grad,
            after=done,
        )
        up_sums.append(up_sum)
        cot_sums.append(cot_sum)
        return (norms, acts, pres), messages, done

    grad_resids, gain_twos, shift_twos = [], [], []
    grad_mixes, mix_sums, states = [], [], []

    def norm_back_micro(index, sums, done):
        (grad_resid, gain_sum, shift_sum, *shard), done = second_norm_back(
            sums, resids[index], cot_mine[index], gain_two, False, after=done
        )
        grad_resids.append(grad_resid)
        gain_twos.append(gain_sum)
        shift_twos.append(shift_sum)
        return gather_first(shard), done

    def heads_back_micro(index, pieces, done):
        (grad_mix, mix_sum, *sent), done = heads_back(
            here, tp_here, pieces, mixer_weight, tok_len, after=done
        )
        grad_mixes.append(grad_mix)
        mix_sums.append(mix_sum)
        states.append(exchange_chips(*sent))
        return done

    def attend_back_micro(index, got, earlier, done):
        return attention_back(
            here,
            received[index],
            got,
            seg_rows[index],
            key_rows[index],
            lses[index],
            heads,
            earlier,
            index,
            micro_count,
            after=done,
        )

    state_a, done = project_micro(0, ())
    state_b, done = project_micro(1, done)
    got, done = exchange_cores(state_a, done)
    state_a, done = attend_micro(0, got, done)
    got, done = exchange_cores(state_b, done)
    state_b, done = attend_micro(1, got, done)
    got, done = exchange_cores(state_a, done)
    messages, done = mix_micro(got, False, done)
    sums_a, done = reduce_second(reduce_first(messages), done)
    got, done = exchange_cores(state_b, done)
    messages, done = mix_micro(got, False, done)
    state_b = reduce_first(messages)
    state_a, done = norm_micro(0, sums_a, False, done)
    pieces_a, done = gather_second(state_a, done)
    sums_b, done = reduce_second(state_b, done)
    state_b, done = norm_micro(1, sums_b, True, done)
    pieces_b = gather_direct(state_b[0])
    kept, messages, done = feed_micro(0, pieces_a, (), True, done)
    sums_a = reduce_direct(messages)
    (norm_two, acts, grad_pres), _, done = feed_micro(1, pieces_b, kept, False, done)
    (down_part,), done = weight_grad([([stacked(cot_all)], [stacked(acts)])], after=done)
    state_a, done = norm_back_micro(0, sums_a, done)
    down_grad = scattered(until(down_part, done))
    messages, done = feed_grad(tp_here, Part(grad_pres, 1), up_weight, after=done)
    state_b = reduce_first(messages)
    pieces_a, done = gather_second(state_a, done)
    acts = [Part(acts, index) for index in micro]
    feeds, done = feed_out(tp_here, acts, down_weight, after=done)
    sums_b, done = reduce_second(state_b, done)
    done = heads_back_micro(0, pieces_a, done)
    state_b, done = norm_back_micro(1, sums_b, done)
    pieces_b, done = gather_second(state_b, done)
    (sent, own), done = weight_grad(
        [([stacked(norm_two)], [stacked(grad_pres)])], here, after=done
    )
    got_a, done = exchange_cores(states[0], done)
    done = heads_back_micro(1, pieces_b, done)
    state_feed = reduce_first(until(feeds, done))
    sent_back, done = attend_back_micro(0, got_a, [], done)
    got_b, done = exchange_cores(states[1], done)
    sums_feed, done = reduce_second(state_feed, done)
    sent_back, done = attend_back_micro(1, got_b, sent_back, done)
    got_up = xor_permute(until(sent, done), "ctx", 1)
    state_back = exchange_chips(*sent_back)
    halves, done = finish_outputs(sums_feed, resids, low_bias, after=done)
    (up_part,), done = add_halves(own, got_up, after=done)
    got, done = exchange_cores(state_back, done)
    up_grad = scattered_chips(until(up_part, done))
    (*grad_projs, proj_sum, first, second, third, fourth), done = project_back(
        here, tp_here, got, weight_three, after=done
    )
    state_one = reduce_first((first, second, third, fourth))
    last = [(norm_one, grad_projs), (grad_mixes, heads_low)]
    (sent, own), done = weight_grad(last, here, after=done)
    sums_one, done = reduce_second(state_one, done)
    got_last = xor_permute(until(sent, done), "ctx", 1)
    pieces_out, done = gather_second(gather_first(halves), done)
    (last_part,), done = add_halves(own, got_last, after=done)
    (gain_sum, shift_sum, *halves), done = first_norm_back(
        sums_one, x_mine, grad_resids, gain_one, after=done
    )
    last_grad = scattered_chips(until(last_part, done))
    pieces_in, done = gather_second(gather_first(halves), done)
    outputs, done = assemble_outputs(tp_here, pieces_out, BF, after=done)
    gain_ones, shift_ones, proj_sums = [gain_sum], [shift_sum], [proj_sum]
    (down_grad,), done = widen(down_grad, True, after=done)
    input_grad, done = assemble_outputs(tp_here, pieces_in, F32, after=done)
    (up_grad,), done = widen(up_grad, False, after=done)
    (proj_grad, mixer_grad), done = widen_last(last_grad, inner, after=done)
    proj_grad = jnp.transpose(proj_grad, (1, 0, 2))

    def over_micro(items):
        return sum(items[1:], items[0]).reshape(ctx_count, -1)

    proj_sum = sum(proj_sums[1:], proj_sums[0]).reshape(3, ctx_count, -1)
    pair_sum = jnp.concatenate([proj_sum[0], proj_sum[2]], axis=1)
    share = width // ctx_count
    pair_sum = jnp.pad(pair_sum, ((0, 0), (0, share - pair_sum.shape[1])))
    kinds = [
        over_micro(gain_ones),
        over_micro(shift_ones),
        over_micro(gain_twos),
        over_micro(shift_twos),
        over_micro(mix_sums),
        over_micro(cot_sums),
        over_micro(up_sums),
        pair_sum,
    ]
    small = small_sums(jnp.stack(kinds, axis=1))
    norms = small[:4]
    for step in (1, 2):
        norms = norms + xor_permute(norms, "tp", step)
    proj_bias_grad = small[7, : 2 * inner // ctx_count].reshape(2, -1)
    return (
        outputs.reshape(inputs.shape),
        input_grad.reshape(inputs.shape),
        norms[0],
        norms[1],
        proj_grad,
        proj_bias_grad,
        mixer_grad,
        small[4],
        norms[2],
        norms[3],
        up_grad,
        small[6],
        down_grad,
        small[5],
    )


def plan_for(mesh):
    sizes = dict(mesh.shape)

    def chosen(*args):
        micro, seq_count, _, width = args[0].shape
        units = seq_count * args[6].shape[1] // HD
        fits = sizes["ctx"] == 8 and sizes["tp"] == 4 and units == sizes["ctx"]
        fits = fits and args[12].shape[0] == width and micro == 2
        return (per_device_exchanged if fits else per_device)(*args)

    return chosen


def solution(mesh):
    in_specs = (
        P(None, None, "ctx", None),
        P(),
        P(),
        P(),
        P(),
        P(None, None, "tp"),
        P(None, "tp"),
        P("tp", None),
        P(),
        P(),
        P(),
        P(None, "tp"),
        P("tp"),
        P("tp", None),
        P(),
        P(None, None, "ctx", None),
    )
    out_specs = (
        P(None, None, "ctx", None),
        P(None, None, "ctx", None),
        P("ctx"),
        P("ctx"),
        P("ctx", None, "tp"),
        P(None, ("tp", "ctx")),
        P("tp", "ctx"),
        P("ctx"),
        P("ctx"),
        P("ctx"),
        P("ctx", "tp"),
        P(("tp", "ctx")),
        P("tp", "ctx"),
        P("ctx"),
    )
    return jax.shard_map(
        plan_for(mesh), mesh=mesh, in_specs=in_specs, out_specs=out_specs, check_vma=False
    )
```
